32 devices in a mesh: dom: 8 (over z, x), sub: 4 (over y, core).
Axes of the slice: x: 2, y: 2, z: 4, core: 2. Of those that a mesh axis runs over, the one named last changes fastest.
Arguments:
- positions: float32 [3, 262144], P(None, ('dom', 'sub')), may hold values from 0 to 1
- masses: float32 [262144], P(('dom', 'sub')), may hold values from 0.00029296876 to 0.0029296875
- cell_mass: float32 [4096], P(('dom', 'sub')), may hold values from 0.00234375 to 0.0234375
- cell_center: float32 [3, 4096], P(None, ('dom', 'sub')), may hold values from 0 to 1
- cell_quad: float32 [6, 4096], P(None, ('dom', 'sub')), may hold values from -0.0046875 to 0.0046875
- cell_list: int32 [4096, 128], P(('dom', 'sub')), may hold values from 0 to 4095
- leaf_list: int32 [4096, 16], P(('dom', 'sub')), may hold values from 0 to 575, as said below
- send_list: int32 [8, 4, 8, 8], P('dom', 'sub'), may hold values from 0 to 127
- send_count: int32 [8, 4, 8], P('dom', 'sub'), may hold values from 1 to 8, as said below
Outputs:
- accel: float32 [3, 262144], P(None, ('dom', 'sub'))
The draws below stay inside these ranges and needn't reach their ends.
Inputs may be any that keep to these rules, and one draw needn't show every extreme that they name: `send_count`: counts fall off with the distance along the curve: an offset of one domain always carries 8 blocks, an offset of d domains at most max(1, 8 // d). `leaf_list`: each id names a block of the group's own domain or a slot of the far part that carries a block.
All inputs are finite; a program needn't handle non-finite values.
Results may differ from the reference program's by a relative error of at most 0.0003.
Values sent between devices are 32-bit elements; how exact they have to be, the bound alone decides.
No kernel may reach another device: no remote copies, remote signals or barrier semaphores. Data moves between devices by JAX's collectives and lax.ppermute only.
A program may use at most 128 MiB of HBM per device.

```python
import math
import jax
import jax.numpy as jnp
from jax import lax

LEAF = 64
LEAF_DEV = 128
NCELL = 128
NLEAF = 16
RANGE = 4
CAP = 8
PARTICLES = 262144
CELLS = 4096
GROUPS = 4096
N_DOM = 8
N_SUB = 4


def curve_counts(key):
    offsets = jnp.concatenate([jnp.arange(-RANGE, 0, dtype=jnp.int32), jnp.arange(1, RANGE + 1, dtype=jnp.int32)])
    reach = jnp.abs(offsets)
    top = jnp.maximum(2, CAP // reach + 1)
    drawn = jax.random.randint(key, (N_DOM, N_SUB, 2 * RANGE), 1, top[None, None, :])
    return jnp.where(reach[None, None, :] == 1, CAP, drawn).astype(jnp.int32)


def draw_send_count(key, part):
    return curve_counts(key)


def draw_leaf_list(key, part):
    counts = curve_counts(key)
    key = jax.random.fold_in(key, 11)
    key_near, key_slot, key_pick, key_side = jax.random.split(key, 4)
    offsets = jnp.concatenate([jnp.arange(-RANGE, 0, dtype=jnp.int32), jnp.arange(1, RANGE + 1, dtype=jnp.int32)])
    groups = jnp.arange(GROUPS, dtype=jnp.int32)
    device = groups // LEAF_DEV
    domain = (device // N_SUB)[:, None]
    segment = (device % N_SUB)[:, None]
    near = jax.random.randint(key_near, (GROUPS, NLEAF), 0, N_SUB * LEAF_DEV)
    slot = jax.random.randint(key_slot, (GROUPS, NLEAF), 0, 2 * RANGE)
    source = domain - offsets[slot]
    bad = (source < 0) | (source >= N_DOM)
    slot = jnp.where(bad, 2 * RANGE - 1 - slot, slot)
    source = domain - offsets[slot]
    count = counts[source, jnp.broadcast_to(segment, slot.shape), slot]
    pick = jax.random.randint(key_pick, (GROUPS, NLEAF), 0, CAP) % count
    far = N_SUB * LEAF_DEV + slot * CAP + pick
    side = jax.random.randint(key_side, (GROUPS, NLEAF), 0, 2)
    return jnp.where(side == 1, far, near).astype(jnp.int32)


def set_ends(array, rng, smallest, high):
    longest = array.shape.index(max(array.shape))
    spots = []
    for shift in (0, 1):
        where = [jax.random.randint(jax.random.fold_in(rng, axis), (), 0, length) for axis, length in enumerate(array.shape)]
        where[longest] = (where[longest] + shift) % array.shape[longest]
        spots.append(tuple(where))
    return array.at[spots[0]].set(smallest).at[spots[1]].set(high)


def levels(key, shape, cuts, smallest, top_value):
    gain = 1.0
    for dim, parts in cuts:
        draws = jax.random.uniform(jax.random.fold_in(jax.random.fold_in(key, 6), dim), (parts,), jnp.float32, smallest / len(cuts), top_value / len(cuts))
        gain = gain * jnp.repeat(jnp.exp(draws), shape[dim] // parts).reshape((-1,) + (1,) * (len(shape) - 1 - dim))
    return gain


def noise(own_key, shape, spread, most, cuts=(), kind=jnp.bfloat16):
    array = jax.random.normal(own_key, shape, jnp.float32) * spread
    if len(cuts) > 0:
        array = levels(own_key, shape, cuts, -0.22, 0.18) * array
    return jnp.clip(array, min=-most, max=most).astype(kind)


def setup_inputs(seed: int = 0) -> dict:
    streams_of = jax.random.split(jax.random.key(seed), 10)
    return {
        "positions": jnp.clip(1.0 * jax.random.uniform(streams_of[0], (3, PARTICLES), jnp.float32) ** levels(streams_of[0], (3, PARTICLES), ((1, 32),), -0.2, 0.2), 0.0, 1.0),
        "masses": jnp.clip(jnp.exp(math.log(0.0029296875) - 2.3025851 * jax.random.uniform(streams_of[1], (PARTICLES,), jnp.float32) ** levels(streams_of[1], (PARTICLES,), ((0, 32),), -0.2, 0.2)), 0.00029296876, 0.0029296875),
        "cell_mass": jnp.clip(jnp.exp(math.log(0.0234375) - 2.3025851 * jax.random.uniform(streams_of[2], (CELLS,), jnp.float32) ** levels(streams_of[2], (CELLS,), ((0, 32),), -0.2, 0.2)), 0.00234375, 0.0234375),
        "cell_center": jnp.clip(1.0 * jax.random.uniform(streams_of[3], (3, CELLS), jnp.float32) ** levels(streams_of[3], (3, CELLS), ((1, 32),), -0.2, 0.2), 0.0, 1.0),
        "cell_quad": noise(streams_of[4], (6, CELLS), (0.1 / NCELL), 0.0046875, ((1, 32),), jnp.float32),
        "cell_list": set_ends(jax.random.randint(streams_of[5], (GROUPS, NCELL), 0, CELLS), jax.random.fold_in(streams_of[5], 1), 0, CELLS - 1).astype(jnp.int32),
        "leaf_list": draw_leaf_list(jax.random.fold_in(streams_of[9], 71), 0),
        "send_list": set_ends(jax.random.randint(streams_of[7], (N_DOM, N_SUB, 2 * RANGE, CAP), 0, LEAF_DEV), jax.random.fold_in(streams_of[7], 1), 0, LEAF_DEV - 1).astype(jnp.int32),
        "send_count": draw_send_count(jax.random.fold_in(streams_of[9], 71), 0),
    }


softening_sq = 0.0025

def direct_pull(targets, sources, weights):
    offset = sources[:, :, None, :] - targets[:, :, :, None]
    dist_sq = lax.optimization_barrier(jnp.sum(offset * offset, axis=0)) + softening_sq
    factor = weights[:, None, :] / (dist_sq * jnp.sqrt(dist_sq))
    return lax.optimization_barrier(jnp.sum(offset * factor[None], axis=-1))

def multipole_pull(targets, moments):
    offset = targets[:, :, :, None] - moments[1:4, :, None, :]
    dist_sq = lax.optimization_barrier(jnp.sum(offset * offset, axis=0)) + softening_sq
    inv_one = 1.0 / jnp.sqrt(dist_sq)
    inv_two = inv_one * inv_one
    inv_three = inv_one * inv_two
    inv_five = inv_three * inv_two
    inv_seven = inv_five * inv_two
    quad_part = moments[4:10, :, None, :]
    q_times_x = quad_part[0] * offset[0] + quad_part[3] * offset[1] + quad_part[4] * offset[2]
    q_times_y = quad_part[3] * offset[0] + quad_part[1] * offset[1] + quad_part[5] * offset[2]
    q_times_z = quad_part[4] * offset[0] + quad_part[5] * offset[1] + quad_part[2] * offset[2]
    q_times = jnp.stack([q_times_x, q_times_y, q_times_z])
    quad_form = lax.optimization_barrier(jnp.sum(offset * q_times, axis=0))
    mass_part = moments[0, :, None, :]
    accel_terms = -mass_part * inv_three * offset + inv_five * q_times - 2.5 * inv_seven * quad_form * offset
    return lax.optimization_barrier(jnp.sum(accel_terms, axis=-1))

def group_pull(targets, essential, leaf_ids, cell_table, cell_ids):
    groups_here = leaf_ids.shape[0]
    particle_ids = (leaf_ids[:, :, None] * LEAF + jnp.arange(LEAF, dtype=jnp.int32)[None, None, :]).reshape(groups_here, -1)
    picked = essential[:, particle_ids]
    moments = cell_table[:, cell_ids]
    return direct_pull(targets, picked[0:3], picked[3]) + multipole_pull(targets, moments)

def reference(positions, masses, cell_mass, cell_center, cell_quad, cell_list, leaf_list, send_list, send_count):
    packed = jnp.concatenate([positions, masses[None]], axis=0).reshape(4, N_DOM, N_SUB, LEAF_DEV * LEAF)
    cell_table = jnp.concatenate([cell_mass[None], cell_center, cell_quad], axis=0)
    cell_lists = cell_list.reshape(N_DOM, N_SUB, LEAF_DEV, NCELL)
    leaf_lists = leaf_list.reshape(N_DOM, N_SUB, LEAF_DEV, NLEAF)
    offsets = jnp.concatenate([jnp.arange(-RANGE, 0, dtype=jnp.int32), jnp.arange(1, RANGE + 1, dtype=jnp.int32)])
    slot_index = jnp.arange(2 * RANGE, dtype=jnp.int32)

    def one_domain(linear):
        domain = linear // N_SUB
        segment = linear % N_SUB
        nearby = packed[:, domain].reshape(4, N_SUB * LEAF_DEV * LEAF)
        column = packed[:, :, segment].reshape(4, N_DOM * LEAF_DEV * LEAF)
        source = domain - offsets
        inside = (source >= 0) & (source < N_DOM)
        clipped = jnp.clip(source, 0, N_DOM - 1).astype(jnp.int32)
        chosen = send_list[clipped, segment, slot_index, :]
        counts = send_count[clipped, segment, slot_index]
        live = inside[:, None] & (jnp.arange(CAP, dtype=jnp.int32)[None, :] < counts[:, None])
        block_ids = clipped[:, None] * LEAF_DEV + chosen
        flat_ids = (block_ids[:, :, None] * LEAF + jnp.arange(LEAF, dtype=jnp.int32)[None, None, :]).reshape(-1)
        weight = jnp.repeat(live.astype(jnp.float32).reshape(-1), LEAF)
        remote = column[:, flat_ids] * weight[None, :]
        essential = jnp.concatenate([nearby, remote], axis=1)
        targets = packed[0:3, domain, segment].reshape(3, LEAF_DEV, LEAF)
        pulled = group_pull(targets, essential, leaf_lists[domain, segment], cell_table, cell_lists[domain, segment])
        return pulled.reshape(3, LEAF_DEV * LEAF)
    result = lax.map(one_domain, jnp.arange(N_DOM * N_SUB, dtype=jnp.int32))
    return result.transpose(1, 0, 2).reshape(3, N_DOM * N_SUB * LEAF_DEV * LEAF)
```

```python
import functools

import jax
import jax.numpy as jnp
from jax import lax
from jax.experimental import pallas as pl
from jax.experimental.pallas import tpu as pltpu
from jax.sharding import PartitionSpec as P

LEAF = 64
LEAF_DEV = 128
NCELL = 128
NLEAF = 16
RANGE = 4
CAP = 8
PAIRS = LEAF_DEV // 2
CELL_UNITS = 3
OUT_UNITS = CAP // 2
OFFSETS = list(range(-RANGE, 0)) + list(range(1, RANGE + 1))

softening_sq = 0.0025
GRID_ROUND = 49152.0
F32 = jnp.float32
BF16 = jnp.bfloat16

H_ROWS = 32
Q_ROWS = 64
V_ROWS = 16
U_ROWS = 48
Q_AT = H_ROWS
V_AT = Q_AT + Q_ROWS
U_AT = V_AT + V_ROWS
CELL_ROWS = U_AT + U_ROWS
SOURCE_ROWS = H_ROWS + V_ROWS


def rounded(value):
    return value.astype(BF16).astype(F32)


def three_parts(value):
    first = rounded(value)
    rest = value - first
    second = rounded(rest)
    return first, second, rest - second


def two_parts(value):
    first = value.astype(BF16)
    return first, (value - first.astype(F32)).astype(BF16)


def grid_parts(value):
    high = (value + GRID_ROUND) - GRID_ROUND
    low = value - high
    first = rounded(low)
    return high, low, first, low - first


def norm_parts(parts, extra=None):
    big = sum(high * high for high, _, _, _ in parts)
    small = sum(low * (2.0 * high + low) for high, low, _, _ in parts)
    if extra is not None:
        small = small + extra
    return three_parts(big), three_parts(small)


def pack_kernel(pos_ref, mass_ref, cmass_ref, center_ref, quad_ref, out_ref):
    for pair in range(PAIRS):
        lanes = pl.ds(128 * pair, 128)
        out_ref[pair, 0:3, :] = pos_ref[:, lanes]
        out_ref[pair, 3:4, :] = mass_ref[:, lanes]
    out_ref[PAIRS, 0:1, :] = cmass_ref[...]
    out_ref[PAIRS, 1:4, :] = center_ref[...]
    out_ref[PAIRS + 1] = quad_ref[0:4, :]
    out_ref[PAIRS + 2, 0:2, :] = quad_ref[4:6, :]
    out_ref[PAIRS + 2, 2:4, :] = jnp.zeros((2, 128), F32)


def outgoing_kernel(n_dom, n_sub, own_ref, all_ref, list_ref, count_ref, out_ref):
    me = lax.axis_index("dom")
    left = lax.broadcasted_iota(jnp.int32, (4, 128), 1) < LEAF
    zero = jnp.zeros((OUT_UNITS, 4, 128), F32)

    def one_target(target, carry):
        out_ref[target, 0:OUT_UNITS] = zero
        for seg in range(n_sub):
            at = OUT_UNITS + CELL_UNITS * seg
            out_ref[target, at : at + CELL_UNITS] = all_ref[seg, PAIRS : PAIRS + CELL_UNITS]
        return carry

    lax.fori_loop(0, n_dom, one_target, 0)

    def half(slot, j, right):
        block = list_ref[slot, j]
        value = own_ref[block // 2]
        value = jnp.where(j < count_ref[0, slot], value, 0.0)
        return jnp.where((block & 1) == right, value, pltpu.roll(value, LEAF, 1))

    for slot in range(2 * RANGE):
        target = me + OFFSETS[slot]

        @pl.when((target >= 0) & (target < n_dom))
        def _():
            for unit in range(OUT_UNITS):
                out_ref[target, unit] = jnp.where(left, half(slot, 2 * unit, 0), half(slot, 2 * unit + 1, 1))


def build_table(n_dom, n_sub, all_ref, recv_ref, tab_ref):
    left = lax.broadcasted_iota(jnp.int32, (4, 128), 1) < LEAF

    def put(at, value):
        turned = pltpu.roll(value, LEAF, 1)
        tab_ref[at] = jnp.where(left, value, turned)
        tab_ref[at + 1] = jnp.where(left, turned, value)

    for seg in range(n_sub):

        def near(step, carry):
            for sub in range(8):
                pair = step * 8 + sub
                put(seg * LEAF_DEV + 2 * pair, all_ref[seg, pair])
            return carry

        lax.fori_loop(0, PAIRS // 8, near, 0)
    me = lax.axis_index("dom")
    for slot in range(2 * RANGE):
        source = me - OFFSETS[slot]
        inside = (source >= 0) & (source < n_dom)
        source = jnp.clip(source, 0, n_dom - 1)
        for unit in range(OUT_UNITS):
            value = jnp.where(inside, recv_ref[source, unit], 0.0)
            put(n_sub * LEAF_DEV + slot * CAP + 2 * unit, value)


def target_features(all_ref, tg_ref, ce_ref, feat_ref, ah_ref, aq_ref):
    me = lax.axis_index("sub")
    left = lax.broadcasted_iota(jnp.int32, (8, 128), 1) < LEAF
    one = jnp.ones((8, 128), F32)
    zero = jnp.zeros((8, 128), F32)
    raw_ref = tg_ref

    def copy_in(pair, carry):
        raw_ref[pl.ds(pl.multiple_of(4 * pair, 4), 4), :] = all_ref[me, pair]
        return carry

    lax.fori_loop(0, PAIRS, copy_in, 0)

    def one_octet(octet, carry):
        parts, centred = [], []
        for comp in range(3):
            rows = pl.ds(octet * 32 + comp, 8, stride=4)
            value = raw_ref[rows, :]
            first = jnp.broadcast_to(value[:, 0:1], (8, 128))
            second = jnp.broadcast_to(value[:, LEAF : LEAF + 1], (8, 128))
            ce_ref[comp, pl.ds(octet * 16, 8, stride=2), :] = first
            ce_ref[comp, pl.ds(octet * 16 + 1, 8, stride=2), :] = second
            value = value - jnp.where(left, first, second)
            raw_ref[rows, :] = value
            centred.append(value)
            parts.append(grid_parts(value))
        big, small = norm_parts(parts, softening_sq)
        minus_high = [-2.0 * part[0] for part in parts]
        minus_one = [-2.0 * part[2] for part in parts]
        minus_two = [-2.0 * part[3] for part in parts]
        rows = minus_high + [one] * 3 + list(big) + minus_high + minus_one + minus_high
        rows += minus_two + minus_one + [one] * 3 + list(small) + [zero] * 2
        x, y, z = centred
        split = [three_parts(v) for v in (x, y, z, x * x, y * y, z * z, x * y, x * z, y * z)]
        for which in (0, 0, 1, 0, 1, 2):
            rows += [part[which] for part in split]
        rows += [one] * 3 + [zero] * 7
        for at, value in enumerate(rows):
            feat_ref[8 * at : 8 * at + 8, :] = value
        for sub in range(8):
            pair = octet * 8 + sub
            ah_ref[pair] = feat_ref[pl.ds(sub, H_ROWS, stride=8), :].T.astype(BF16)
            aq_ref[pair] = feat_ref[pl.ds(8 * H_ROWS + sub, Q_ROWS, stride=8), :].T.astype(BF16)
        return carry

    lax.fori_loop(0, PAIRS // 8, one_octet, 0)


def source_h_rows(parts):
    (p1, p2, p3), (s1, s2, s3) = norm_parts(parts)
    high = [part[0] for part in parts]
    one = [part[2] for part in parts]
    two = [part[3] for part in parts]
    rows = dict(enumerate(high + [p1, p2, p3]))
    rows.update(enumerate(one + high + two + high + one + [s1, s2, s3], 9))
    return rows


def put_rows(ref, rows):
    for at, value in rows.items():
        ref[8 * at : 8 * at + 8, :] = value


def fill_constant_rows(ref, count):
    one = jnp.ones((8, 128), F32)
    zero = jnp.zeros((8, 128), F32)
    for at in range(count):
        ones = at in (6, 7, 8, 27, 28, 29) or (count == CELL_ROWS and at == V_AT + 3)
        ref[8 * at : 8 * at + 8, :] = one if ones else zero


def cell_features(n_dom, n_sub, octet, cl_ref, recv_ref, ce_ref, cf_ref, cm_ref):
    ids = cl_ref[pl.ds(pl.multiple_of(8 * octet, 8), 8), :]
    lane = ids & 127
    owner = ids >> 7

    def one_domain(dom, found):
        for seg in range(n_sub):
            here = owner == dom * n_sub + seg
            at = OUT_UNITS + CELL_UNITS * seg
            new = []
            for comp in range(10):
                row = recv_ref[dom, at + comp // 4, comp % 4 : comp % 4 + 1, :]
                value = jnp.take_along_axis(jnp.broadcast_to(row, (8, 128)), lane, axis=1, mode="promise_in_bounds")
                new.append(jnp.where(here, value, found[comp]))
            found = tuple(new)
        return found

    start = tuple(jnp.zeros((8, 128), F32) for _ in range(10))
    mass, cx, cy, cz, xx, yy, zz, xy, xz, yz = lax.fori_loop(0, n_dom, one_domain, start)
    cm_ref[...] = mass
    rows8 = pl.ds(pl.multiple_of(8 * octet, 8), 8)
    cx, cy, cz = [value - ce_ref[comp, rows8, :] for comp, value in enumerate((cx, cy, cz))]
    put_rows(cf_ref, source_h_rows([grid_parts(value) for value in (cx, cy, cz)]))
    qx = xx * cx + xy * cy + xz * cz
    qy = xy * cx + yy * cy + yz * cz
    qz = xz * cx + yz * cy + zz * cz
    const = three_parts(2.5 * (qx * cx + qy * cy + qz * cz))
    linear = [-5.0 * qx, -5.0 * qy, -5.0 * qz]
    square = [2.5 * xx, 2.5 * yy, 2.5 * zz, 5.0 * xy, 5.0 * xz, 5.0 * yz]
    split = [three_parts(value) for value in linear + square]
    rows = []
    for which in (0, 1, 0, 2, 1, 0):
        rows += [part[which] for part in split]
    rows += list(const)
    put_rows(cf_ref, dict(enumerate(rows, Q_AT)))
    for comp, value in enumerate((cx, cy, cz)):
        for which, part in enumerate(three_parts(value)):
            cf_ref[8 * (V_AT + 4 * which + comp) : 8 * (V_AT + 4 * which + comp) + 8, :] = part
    columns = {name: three_parts(value) for name, value in dict(xx=xx, yy=yy, zz=zz, xy=xy, xz=xz, yz=yz, cx=qx, cy=qy, cz=qz).items()}
    order = (("xx", "xy", "xz"), ("xy", "yy", "yz"), ("xz", "yz", "zz"), ("cx", "cy", "cz"))
    for which in range(3):
        for column, names in enumerate(order):
            for row, name in enumerate(names):
                at = U_AT + 16 * which + 4 * column + row
                cf_ref[8 * at : 8 * at + 8, :] = columns[name][which]


def source_features(group, ll_ref, tab_ref, ce_ref, raw_ref, sf_ref):
    left = lax.broadcasted_iota(jnp.int32, (4, 128), 1) < LEAF
    for pair in range(NLEAF // 2):
        first = tab_ref[ll_ref[group, 2 * pair]]
        second = tab_ref[ll_ref[group, 2 * pair + 1]]
        raw_ref[4 * pair : 4 * pair + 4, :] = jnp.where(left, first, second)
    value = [raw_ref[pl.ds(comp, 8, stride=4), :] for comp in range(4)]
    mass = value[3]
    centred = [value[comp] - ce_ref[comp, pl.ds(group, 1), :] for comp in range(3)]
    put_rows(sf_ref, source_h_rows([grid_parts(v) for v in centred]))
    for comp, v in enumerate([mass * v for v in centred] + [mass]):
        for which, part in enumerate(three_parts(v)):
            at = H_ROWS + 4 * which + comp
            sf_ref[8 * at : 8 * at + 8, :] = part


def transposed_dot(rows, weights):
    return lax.dot_general(rows, weights, (((1,), (1,)), ((), ())), preferred_element_type=F32)


def summed(rows, value):
    high, low = two_parts(value)
    return transposed_dot(rows, high) + transposed_dot(rows, low)


def one_group(sub, target_h, target_q, sf_ref, cf_ref, cm_ref):
    total = jnp.zeros((V_ROWS, LEAF), F32)
    for block in range(4):
        pieces = [sf_ref[pl.ds(2 * block + half, H_ROWS, stride=8), :].astype(BF16) for half in range(2)]
        dist_sq = jnp.dot(target_h, jnp.concatenate(pieces, axis=1), preferred_element_type=F32)
        inv = lax.rsqrt(dist_sq)
        weights = [sf_ref[pl.ds(8 * H_ROWS + 2 * block + half, V_ROWS, stride=8), :].astype(BF16) for half in range(2)]
        total += summed(jnp.concatenate(weights, axis=1), inv * inv * inv)

    def cell_rows(at, count):
        return cf_ref[pl.ds(8 * at + sub, count, stride=8), :].astype(BF16)

    dist_sq = jnp.dot(target_h, cell_rows(0, H_ROWS), preferred_element_type=F32)
    quad_form = jnp.dot(target_q, cell_rows(Q_AT, Q_ROWS), preferred_element_type=F32)
    inv = lax.rsqrt(dist_sq)
    inv_two = inv * inv
    inv_three = inv * inv_two
    pull = inv_three * (cm_ref[pl.ds(sub, 1), :] + quad_form * (inv_two * inv_two))
    total += summed(cell_rows(V_AT, V_ROWS), pull)
    quad = summed(cell_rows(U_AT, U_ROWS), inv_three * inv_two)
    return total[0:8] + total[8:16], quad[0:16] + quad[16:32] + quad[32:48]


def pull_kernel(n_dom, n_sub, all_ref, recv_ref, cl_ref, ll_ref, out_ref, tab_ref, tg_ref, ce_ref, feat_ref, ah_ref, aq_ref, cf_ref, cm_ref, raw_ref, sf_ref):
    build_table(n_dom, n_sub, all_ref, recv_ref, tab_ref)
    target_features(all_ref, tg_ref, ce_ref, feat_ref, ah_ref, aq_ref)
    fill_constant_rows(cf_ref, CELL_ROWS)
    for half in range(2):
        fill_constant_rows(sf_ref.at[half], SOURCE_ROWS)
    upper = lax.broadcasted_iota(jnp.int32, (8, 128), 0) < 4

    def one_octet(octet, carry):
        cell_features(n_dom, n_sub, octet, cl_ref, recv_ref, ce_ref, cf_ref, cm_ref)

        def one_pair(inner, carry):
            pair = octet * 4 + inner
            sums, quads = [], []
            for half in range(2):
                source_features(2 * pair + half, ll_ref, tab_ref, ce_ref, raw_ref.at[half], sf_ref.at[half])
            for half in range(2):
                rows = pl.ds(LEAF * half, LEAF)
                sums_half, quads_half = one_group(
                    2 * inner + half, ah_ref[pair, rows, :], aq_ref[pair, rows, :], sf_ref.at[half], cf_ref, cm_ref
                )
                sums.append(sums_half)
                quads.append(quads_half)
            sums = jnp.concatenate(sums, axis=1)
            quads = jnp.concatenate(quads, axis=1)
            sums = sums + pltpu.roll(sums, 4, 0)
            place = tg_ref[pl.ds(pl.multiple_of(4 * pair, 4), 4), :]
            x, y, z = [place[comp : comp + 1, :] for comp in range(3)]
            turned = quads[0:8] * jnp.where(upper, x, y) + quads[8:16] * jnp.where(upper, z, -1.0)
            turned = turned + pltpu.roll(turned, 4, 0)
            result = sums + turned
            lanes = pl.ds(pl.multiple_of(128 * pair, 128), 128)
            out_ref[:, lanes] = result[0:3] - place[0:3] * sums[3:4]
            return carry

        lax.fori_loop(0, 4, one_pair, 0)
        return carry

    lax.fori_loop(0, LEAF_DEV // 8, one_octet, 0)


def on_device(n_dom, n_sub, positions, masses, cell_mass, cell_center, cell_quad, cell_list, leaf_list, send_list, send_count):
    vmem = pl.BlockSpec(memory_space=pltpu.VMEM)
    smem = pl.BlockSpec(memory_space=pltpu.SMEM)
    params = pltpu.CompilerParams(vmem_limit_bytes=48 * 1024 * 1024)
    packed = pl.pallas_call(
        pack_kernel,
        out_shape=jax.ShapeDtypeStruct((PAIRS + CELL_UNITS, 4, 128), F32),
        in_specs=[vmem] * 5,
        out_specs=vmem,
        compiler_params=params,
        name="pack_own",
    )(positions, masses.reshape(1, -1), cell_mass.reshape(1, -1), cell_center, cell_quad)
    nearby = lax.all_gather(packed, "sub", axis=0, tiled=False)
    units = OUT_UNITS + CELL_UNITS * n_sub
    outgoing = pl.pallas_call(
        functools.partial(outgoing_kernel, n_dom, n_sub),
        out_shape=jax.ShapeDtypeStruct((n_dom, units, 4, 128), F32),
        in_specs=[vmem, vmem, smem, smem],
        out_specs=vmem,
        compiler_params=params,
        name="pack_outgoing",
    )(packed, nearby, send_list.reshape(2 * RANGE, CAP), send_count.reshape(1, 2 * RANGE))
    received = lax.all_to_all(outgoing, "dom", split_axis=0, concat_axis=0, tiled=True)
    return pl.pallas_call(
        functools.partial(pull_kernel, n_dom, n_sub),
        out_shape=jax.ShapeDtypeStruct((3, LEAF_DEV * LEAF), F32),
        in_specs=[vmem, vmem, vmem, smem],
        out_specs=vmem,
        scratch_shapes=[
            pltpu.VMEM((n_sub * LEAF_DEV + 2 * RANGE * CAP, 4, 128), F32),
            pltpu.VMEM((4 * PAIRS, 128), F32),
            pltpu.VMEM((3, LEAF_DEV, 128), F32),
            pltpu.VMEM((8 * (H_ROWS + Q_ROWS), 128), F32),
            pltpu.VMEM((PAIRS, 128, H_ROWS), BF16),
            pltpu.VMEM((PAIRS, 128, Q_ROWS), BF16),
            pltpu.VMEM((8 * CELL_ROWS, 128), F32),
            pltpu.VMEM((8, 128), F32),
            pltpu.VMEM((2, 32, 128), F32),
            pltpu.VMEM((2, 8 * SOURCE_ROWS, 128), F32),
        ],
        compiler_params=params,
        name="pull",
    )(nearby, received, cell_list, leaf_list)


def solution(mesh):
    sharded = P(("dom", "sub"))
    return jax.shard_map(
        functools.partial(on_device, mesh.shape["dom"], mesh.shape["sub"]),
        mesh=mesh,
        in_specs=(
            P(None, ("dom", "sub")),
            sharded,
            sharded,
            P(None, ("dom", "sub")),
            P(None, ("dom", "sub")),
            P(("dom", "sub"), None),
            P(("dom", "sub"), None),
            P("dom", "sub", None, None),
            P("dom", "sub", None),
        ),
        out_specs=P(None, ("dom", "sub")),
        check_vma=False,
    )
```

```python
import functools

import jax
import jax.numpy as jnp
from jax import lax
from jax.experimental import pallas as pl
from jax.experimental.pallas import tpu as pltpu
from jax.sharding import PartitionSpec as P

LEAF = 64
LEAF_DEV = 128
NCELL = 128
NLEAF = 16
RANGE = 4
CAP = 8
PAIRS = LEAF_DEV // 2
CELL_UNITS = 3
OUT_UNITS = CAP // 2
OFFSETS = list(range(-RANGE, 0)) + list(range(1, RANGE + 1))

softening_sq = 0.0025
GRID_ROUND = 49152.0
F32 = jnp.float32
BF16 = jnp.bfloat16

H_ROWS = 32
Q_ROWS = 64
V_ROWS = 16
U_ROWS = 48
Q_AT = H_ROWS
V_AT = Q_AT + Q_ROWS
U_AT = V_AT + V_ROWS
CELL_ROWS = U_AT + U_ROWS
SOURCE_ROWS = H_ROWS + V_ROWS


def rounded(value):
    return value.astype(BF16).astype(F32)


def three_parts(value):
    first = rounded(value)
    rest = value - first
    second = rounded(rest)
    return first, second, rest - second


def two_parts(value):
    first = value.astype(BF16)
    return first, (value - first.astype(F32)).astype(BF16)


def grid_parts(value):
    high = (value + GRID_ROUND) - GRID_ROUND
    low = value - high
    first = rounded(low)
    return high, low, first, low - first


def norm_parts(parts, extra=None):
    big = sum(high * high for high, _, _, _ in parts)
    small = sum(low * (2.0 * high + low) for high, low, _, _ in parts)
    if extra is not None:
        small = small + extra
    return three_parts(big), three_parts(small)


def pack_kernel(pos_ref, mass_ref, cmass_ref, center_ref, quad_ref, out_ref):
    for pair in range(PAIRS):
        lanes = pl.ds(128 * pair, 128)
        out_ref[pair, 0:3, :] = pos_ref[:, lanes]
        out_ref[pair, 3:4, :] = mass_ref[:, lanes]
    out_ref[PAIRS, 0:1, :] = cmass_ref[...]
    out_ref[PAIRS, 1:4, :] = center_ref[...]
    out_ref[PAIRS + 1] = quad_ref[0:4, :]
    out_ref[PAIRS + 2, 0:2, :] = quad_ref[4:6, :]
    out_ref[PAIRS + 2, 2:4, :] = jnp.zeros((2, 128), F32)


def outgoing_kernel(n_dom, n_sub, own_ref, all_ref, list_ref, count_ref, out_ref):
    me = lax.axis_index("dom")
    left = lax.broadcasted_iota(jnp.int32, (4, 128), 1) < LEAF
    zero = jnp.zeros((OUT_UNITS, 4, 128), F32)

    def one_target(target, carry):
        out_ref[target, 0:OUT_UNITS] = zero
        for seg in range(n_sub):
            at = OUT_UNITS + CELL_UNITS * seg
            out_ref[target, at : at + CELL_UNITS] = all_ref[seg, PAIRS : PAIRS + CELL_UNITS]
        return carry

    lax.fori_loop(0, n_dom, one_target, 0)

    def half(slot, j, right):
        block = list_ref[slot, j]
        value = own_ref[block // 2]
        value = jnp.where(j < count_ref[0, slot], value, 0.0)
        return jnp.where((block & 1) == right, value, pltpu.roll(value, LEAF, 1))

    for slot in range(2 * RANGE):
        target = me + OFFSETS[slot]

        @pl.when((target >= 0) & (target < n_dom))
        def _():
            for unit in range(OUT_UNITS):
                out_ref[target, unit] = jnp.where(left, half(slot, 2 * unit, 0), half(slot, 2 * unit + 1, 1))


def build_table(n_dom, n_sub, all_ref, recv_ref, tab_ref):
    left = lax.broadcasted_iota(jnp.int32, (4, 128), 1) < LEAF

    def put(at, value):
        turned = pltpu.roll(value, LEAF, 1)
        tab_ref[at] = jnp.where(left, value, turned)
        tab_ref[at + 1] = jnp.where(left, turned, value)

    for seg in range(n_sub):

        def near(step, carry):
            for sub in range(8):
                pair = step * 8 + sub
                put(seg * LEAF_DEV + 2 * pair, all_ref[seg, pair])
            return carry

        lax.fori_loop(0, PAIRS // 8, near, 0)
    me = lax.axis_index("dom")
    for slot in range(2 * RANGE):
        source = me - OFFSETS[slot]
        inside = (source >= 0) & (source < n_dom)
        source = jnp.clip(source, 0, n_dom - 1)
        for unit in range(OUT_UNITS):
            value = jnp.where(inside, recv_ref[source, unit], 0.0)
            put(n_sub * LEAF_DEV + slot * CAP + 2 * unit, value)


def target_features(all_ref, tg_ref, ce_ref, feat_ref, ah_ref, aq_ref):
    me = lax.axis_index("sub")
    left = lax.broadcasted_iota(jnp.int32, (8, 128), 1) < LEAF
    one = jnp.ones((8, 128), F32)
    zero = jnp.zeros((8, 128), F32)
    raw_ref = tg_ref

    def copy_in(pair, carry):
        raw_ref[pl.ds(pl.multiple_of(4 * pair, 4), 4), :] = all_ref[me, pair]
        return carry

    lax.fori_loop(0, PAIRS, copy_in, 0)

    def one_octet(octet, carry):
        parts, centred = [], []
        for comp in range(3):
            rows = pl.ds(octet * 32 + comp, 8, stride=4)
            value = raw_ref[rows, :]
            first = jnp.broadcast_to(value[:, 0:1], (8, 128))
            second = jnp.broadcast_to(value[:, LEAF : LEAF + 1], (8, 128))
            ce_ref[comp, pl.ds(octet * 16, 8, stride=2), :] = first
            ce_ref[comp, pl.ds(octet * 16 + 1, 8, stride=2), :] = second
            value = value - jnp.where(left, first, second)
            raw_ref[rows, :] = value
            centred.append(value)
            parts.append(grid_parts(value))
        big, small = norm_parts(parts, softening_sq)
        minus_high = [-2.0 * part[0] for part in parts]
        minus_one = [-2.0 * part[2] for part in parts]
        minus_two = [-2.0 * part[3] for part in parts]
        rows = minus_high + [one] * 3 + list(big) + minus_high + minus_one + minus_high
        rows += minus_two + minus_one + [one] * 3 + list(small) + [zero] * 2
        x, y, z = centred
        split = [three_parts(v) for v in (x, y, z, x * x, y * y, z * z, x * y, x * z, y * z)]
        for which in (0, 0, 1, 0, 1, 2):
            rows += [part[which] for part in split]
        rows += [one] * 3 + [zero] * 7
        for at, value in enumerate(rows):
            feat_ref[8 * at : 8 * at + 8, :] = value
        for sub in range(8):
            pair = octet * 8 + sub
            ah_ref[pair] = feat_ref[pl.ds(sub, H_ROWS, stride=8), :].T.astype(BF16)
            aq_ref[pair] = feat_ref[pl.ds(8 * H_ROWS + sub, Q_ROWS, stride=8), :].T.astype(BF16)
        return carry

    lax.fori_loop(0, PAIRS // 8, one_octet, 0)


def source_h_rows(parts):
    (p1, p2, p3), (s1, s2, s3) = norm_parts(parts)
    high = [part[0] for part in parts]
    one = [part[2] for part in parts]
    two = [part[3] for part in parts]
    rows = dict(enumerate(high + [p1, p2, p3]))
    rows.update(enumerate(one + high + two + high + one + [s1, s2, s3], 9))
    return rows


def put_rows(ref, rows):
    for at, value in rows.items():
        ref[8 * at : 8 * at + 8, :] = value


def fill_constant_rows(ref, count):
    one = jnp.ones((8, 128), F32)
    zero = jnp.zeros((8, 128), F32)
    for at in range(count):
        ones = at in (6, 7, 8, 27, 28, 29) or (count == CELL_ROWS and at == V_AT + 3)
        ref[8 * at : 8 * at + 8, :] = one if ones else zero


def cell_features(n_dom, n_sub, octet, cl_ref, recv_ref, ce_ref, cf_ref, cm_ref):
    ids = cl_ref[pl.ds(pl.multiple_of(8 * octet, 8), 8), :]
    lane = ids & 127
    owner = ids >> 7

    def one_domain(dom, found):
        for seg in range(n_sub):
            here = owner == dom * n_sub + seg
            at = OUT_UNITS + CELL_UNITS * seg
            new = []
            for comp in range(10):
                row = recv_ref[dom, at + comp // 4, comp % 4 : comp % 4 + 1, :]
                value = jnp.take_along_axis(jnp.broadcast_to(row, (8, 128)), lane, axis=1, mode="promise_in_bounds")
                new.append(jnp.where(here, value, found[comp]))
            found = tuple(new)
        return found

    start = tuple(jnp.zeros((8, 128), F32) for _ in range(10))
    mass, cx, cy, cz, xx, yy, zz, xy, xz, yz = lax.fori_loop(0, n_dom, one_domain, start)
    cm_ref[...] = mass
    rows8 = pl.ds(pl.multiple_of(8 * octet, 8), 8)
    cx, cy, cz = [value - ce_ref[comp, rows8, :] for comp, value in enumerate((cx, cy, cz))]
    put_rows(cf_ref, source_h_rows([grid_parts(value) for value in (cx, cy, cz)]))
    qx = xx * cx + xy * cy + xz * cz
    qy = xy * cx + yy * cy + yz * cz
    qz = xz * cx + yz * cy + zz * cz
    const = three_parts(2.5 * (qx * cx + qy * cy + qz * cz))
    linear = [-5.0 * qx, -5.0 * qy, -5.0 * qz]
    square = [2.5 * xx, 2.5 * yy, 2.5 * zz, 5.0 * xy, 5.0 * xz, 5.0 * yz]
    split = [three_parts(value) for value in linear + square]
    rows = []
    for which in (0, 1, 0, 2, 1, 0):
        rows += [part[which] for part in split]
    rows += list(const)
    put_rows(cf_ref, dict(enumerate(rows, Q_AT)))
    for comp, value in enumerate((cx, cy, cz)):
        for which, part in enumerate(three_parts(value)):
            cf_ref[8 * (V_AT + 4 * which + comp) : 8 * (V_AT + 4 * which + comp) + 8, :] = part
    columns = {name: three_parts(value) for name, value in dict(xx=xx, yy=yy, zz=zz, xy=xy, xz=xz, yz=yz, cx=qx, cy=qy, cz=qz).items()}
    order = (("xx", "xy", "xz"), ("xy", "yy", "yz"), ("xz", "yz", "zz"), ("cx", "cy", "cz"))
    for which in range(3):
        for column, names in enumerate(order):
            for row, name in enumerate(names):
                at = U_AT + 16 * which + 4 * column + row
                cf_ref[8 * at : 8 * at + 8, :] = columns[name][which]


def source_features(group, ll_ref, tab_ref, ce_ref, raw_ref, sf_ref):
    left = lax.broadcasted_iota(jnp.int32, (4, 128), 1) < LEAF
    for pair in range(NLEAF // 2):
        first = tab_ref[ll_ref[group, 2 * pair]]
        second = tab_ref[ll_ref[group, 2 * pair + 1]]
        raw_ref[4 * pair : 4 * pair + 4, :] = jnp.where(left, first, second)
    value = [raw_ref[pl.ds(comp, 8, stride=4), :] for comp in range(4)]
    mass = value[3]
    centred = [value[comp] - ce_ref[comp, pl.ds(group, 1), :] for comp in range(3)]
    put_rows(sf_ref, source_h_rows([grid_parts(v) for v in centred]))
    for comp, v in enumerate([mass * v for v in centred] + [mass]):
        for which, part in enumerate(three_parts(v)):
            at = H_ROWS + 4 * which + comp
            sf_ref[8 * at : 8 * at + 8, :] = part


def transposed_dot(rows, weights):
    return lax.dot_general(rows, weights, (((1,), (1,)), ((), ())), preferred_element_type=F32)


def stacked(value):
    return jnp.concatenate(two_parts(value), axis=0)


def cell_group(sub, target_h, target_q, cf_ref, cm_ref):
    def cell_rows(at, count):
        return cf_ref[pl.ds(8 * at + sub, count, stride=8), :].astype(BF16)

    dist_sq = jnp.dot(target_h, cell_rows(0, H_ROWS), preferred_element_type=F32)
    quad_form = jnp.dot(target_q, cell_rows(Q_AT, Q_ROWS), preferred_element_type=F32)
    inv = lax.rsqrt(dist_sq)
    inv_two = inv * inv
    inv_three = inv * inv_two
    pull = inv_three * (cm_ref[pl.ds(sub, 1), :] + quad_form * (inv_two * inv_two))
    moments = jnp.concatenate(
        [
            jnp.concatenate([cell_rows(V_AT, V_ROWS), jnp.zeros((V_ROWS, 128), BF16)], axis=1),
            jnp.concatenate([jnp.zeros((U_ROWS, 128), BF16), cell_rows(U_AT, U_ROWS)], axis=1),
        ],
        axis=0,
    )
    both = jnp.concatenate([stacked(pull), stacked(inv_three * inv_two)], axis=1)
    sums = transposed_dot(both, moments)
    return sums[0:LEAF] + sums[LEAF:]


def direct_group(target_h, sf_ref):
    def source_rows(at, count, chunk):
        return sf_ref[pl.ds(8 * at + chunk, count, stride=8), :].astype(BF16)

    weights = []
    for block in range(4):
        pieces = [source_rows(0, H_ROWS, 2 * block + half) for half in range(2)]
        dist_sq = jnp.dot(target_h, jnp.concatenate(pieces, axis=1), preferred_element_type=F32)
        inv = lax.rsqrt(dist_sq)
        weights.append(stacked(inv * inv * inv))
    moments = jnp.concatenate([source_rows(H_ROWS, V_ROWS, chunk) for chunk in range(8)], axis=1)
    sums = transposed_dot(jnp.concatenate(weights, axis=1), moments)
    return sums[0:LEAF] + sums[LEAF:]


def pair_lanes(pair):
    return pl.ds(pl.multiple_of(128 * pair, 128), 128)


def pair_place(tg_ref, pair):
    return tg_ref[pl.ds(pl.multiple_of(4 * pair, 4), 4), :]


def point_sums(sums, place):
    sums = sums[0:8] + sums[8:16]
    sums = sums + pltpu.roll(sums, 4, 0)
    return sums[0:3] - place[0:3] * sums[3:4]


def cell_kernel(n_dom, n_sub, all_ref, recv_ref, cl_ref, out_ref, tg_ref, ce_ref, ah_ref, feat_ref, aq_ref, cf_ref, cm_ref):
    target_features(all_ref, tg_ref, ce_ref, feat_ref, ah_ref, aq_ref)
    fill_constant_rows(cf_ref, CELL_ROWS)
    upper = lax.broadcasted_iota(jnp.int32, (8, 128), 0) < 4

    def one_octet(octet, carry):
        cell_features(n_dom, n_sub, octet, cl_ref, recv_ref, ce_ref, cf_ref, cm_ref)
        for inner in range(4):
            pair = octet * 4 + inner
            sums = []
            for half in range(2):
                rows = pl.ds(LEAF * half, LEAF)
                sums.append(cell_group(2 * inner + half, ah_ref[pair, rows, :], aq_ref[pair, rows, :], cf_ref, cm_ref))
            sums = jnp.concatenate(sums, axis=0).T
            place = pair_place(tg_ref, pair)
            x, y, z = [place[comp : comp + 1, :] for comp in range(3)]
            quads = sums[16:32] + sums[32:48] + sums[48:64]
            turned = quads[0:8] * jnp.where(upper, x, y) + quads[8:16] * jnp.where(upper, z, -1.0)
            turned = turned + pltpu.roll(turned, 4, 0)
            out_ref[:, pair_lanes(pair)] = point_sums(sums[0:16], place) + turned[0:3]
        return carry

    lax.fori_loop(0, LEAF_DEV // 8, one_octet, 0)


def direct_kernel(n_dom, n_sub, all_ref, recv_ref, ll_ref, tg_ref, ce_ref, ah_ref, cell_ref, out_ref, tab_ref, raw_ref, even_ref, odd_ref):
    build_table(n_dom, n_sub, all_ref, recv_ref, tab_ref)
    for half in range(2):
        fill_constant_rows(even_ref.at[half], SOURCE_ROWS)
        fill_constant_rows(odd_ref.at[half], SOURCE_ROWS)

    def features(pair, raw_at, slot_ref):
        for half in range(2):
            source_features(2 * pair + half, ll_ref, tab_ref, ce_ref, raw_ref.at[raw_at + half], slot_ref.at[half])

    def pull(pair, slot_ref):
        sums = [direct_group(ah_ref[pair, pl.ds(LEAF * half, LEAF), :], slot_ref.at[half]) for half in range(2)]
        lanes = pair_lanes(pair)
        sums = jnp.concatenate(sums, axis=0).T
        out_ref[:, lanes] = cell_ref[:, lanes] + point_sums(sums, pair_place(tg_ref, pair))

    features(0, 0, even_ref)

    def two_pairs(step, carry):
        pair = 2 * step
        features(pair + 1, 2, odd_ref)
        pull(pair, even_ref)
        features(jnp.minimum(pair + 2, PAIRS - 1), 0, even_ref)
        pull(pair + 1, odd_ref)
        return carry

    lax.fori_loop(0, PAIRS // 2, two_pairs, 0)


def on_device(n_dom, n_sub, positions, masses, cell_mass, cell_center, cell_quad, cell_list, leaf_list, send_list, send_count):
    vmem = pl.BlockSpec(memory_space=pltpu.VMEM)
    smem = pl.BlockSpec(memory_space=pltpu.SMEM)
    params = pltpu.CompilerParams(vmem_limit_bytes=48 * 1024 * 1024)
    packed = pl.pallas_call(
        pack_kernel,
        out_shape=jax.ShapeDtypeStruct((PAIRS + CELL_UNITS, 4, 128), F32),
        in_specs=[vmem] * 5,
        out_specs=vmem,
        compiler_params=params,
        name="pack_own",
    )(positions, masses.reshape(1, -1), cell_mass.reshape(1, -1), cell_center, cell_quad)
    nearby = lax.all_gather(packed, "sub", axis=0, tiled=False)
    units = OUT_UNITS + CELL_UNITS * n_sub
    outgoing = pl.pallas_call(
        functools.partial(outgoing_kernel, n_dom, n_sub),
        out_shape=jax.ShapeDtypeStruct((n_dom, units, 4, 128), F32),
        in_specs=[vmem, vmem, smem, smem],
        out_specs=vmem,
        compiler_params=params,
        name="pack_outgoing",
    )(packed, nearby, send_list.reshape(2 * RANGE, CAP), send_count.reshape(1, 2 * RANGE))
    received = lax.all_to_all(outgoing, "dom", split_axis=0, concat_axis=0, tiled=True)
    cell_part, places, centres, features = pl.pallas_call(
        functools.partial(cell_kernel, n_dom, n_sub),
        out_shape=(
            jax.ShapeDtypeStruct((3, LEAF_DEV * LEAF), F32),
            jax.ShapeDtypeStruct((4 * PAIRS, 128), F32),
            jax.ShapeDtypeStruct((3, LEAF_DEV, 128), F32),
            jax.ShapeDtypeStruct((PAIRS, 128, H_ROWS), BF16),
        ),
        in_specs=[vmem] * 3,
        out_specs=[vmem] * 4,
        scratch_shapes=[
            pltpu.VMEM((8 * (H_ROWS + Q_ROWS), 128), F32),
            pltpu.VMEM((PAIRS, 128, Q_ROWS), BF16),
            pltpu.VMEM((8 * CELL_ROWS, 128), F32),
            pltpu.VMEM((8, 128), F32),
        ],
        compiler_params=params,
        name="cells",
    )(nearby, received, cell_list)
    return pl.pallas_call(
        functools.partial(direct_kernel, n_dom, n_sub),
        out_shape=jax.ShapeDtypeStruct((3, LEAF_DEV * LEAF), F32),
        in_specs=[vmem, vmem, smem] + [vmem] * 4,
        out_specs=vmem,
        scratch_shapes=[
            pltpu.VMEM((n_sub * LEAF_DEV + 2 * RANGE * CAP, 4, 128), F32),
            pltpu.VMEM((4, 32, 128), F32),
            pltpu.VMEM((2, 8 * SOURCE_ROWS, 128), F32),
            pltpu.VMEM((2, 8 * SOURCE_ROWS, 128), F32),
        ],
        compiler_params=params,
        name="direct",
    )(nearby, received, leaf_list, places, centres, features, cell_part)


def solution(mesh):
    sharded = P(("dom", "sub"))
    return jax.shard_map(
        functools.partial(on_device, mesh.shape["dom"], mesh.shape["sub"]),
        mesh=mesh,
        in_specs=(
            P(None, ("dom", "sub")),
            sharded,
            sharded,
            P(None, ("dom", "sub")),
            P(None, ("dom", "sub")),
            P(("dom", "sub"), None),
            P(("dom", "sub"), None),
            P("dom", "sub", None, None),
            P("dom", "sub", None),
        ),
        out_specs=P(None, ("dom", "sub")),
        check_vma=False,
    )
```

```python
import functools

import jax
import jax.numpy as jnp
from jax import lax
from jax.experimental import pallas as pl
from jax.experimental.pallas import tpu as pltpu
from jax.sharding import PartitionSpec as P

LEAF = 64
LEAF_DEV = 128
NCELL = 128
NLEAF = 16
RANGE = 4
CAP = 8
PAIRS = LEAF_DEV // 2
OUT_UNITS = CAP // 2
OWN_ROWS = 4 * PAIRS + 16
OUT_ROWS = 4 * OUT_UNITS
CELL_AT = 4 * PAIRS
CELL_COMPS = 10
CELL_PAD = 12
OFFSETS = list(range(-RANGE, 0)) + list(range(1, RANGE + 1))

softening_sq = 0.0025
GRID_ROUND = 49152.0
F32 = jnp.float32
BF16 = jnp.bfloat16

H_ROWS = 32
Q_ROWS = 64
V_ROWS = 16
U_ROWS = 48
Q_AT = H_ROWS
V_AT = Q_AT + Q_ROWS
U_AT = V_AT + V_ROWS
CELL_ROWS = U_AT + U_ROWS
SOURCE_ROWS = H_ROWS + V_ROWS


def rounded(value):
    return value.astype(BF16).astype(F32)


def three_parts(value):
    first = rounded(value)
    rest = value - first
    second = rounded(rest)
    return first, second, rest - second


def two_parts(value):
    first = value.astype(BF16)
    return first, (value - first.astype(F32)).astype(BF16)


def grid_parts(value):
    high = (value + GRID_ROUND) - GRID_ROUND
    low = value - high
    first = rounded(low)
    return high, low, first, low - first


def norm_parts(parts, extra=None):
    big = sum(high * high for high, _, _, _ in parts)
    small = sum(low * (2.0 * high + low) for high, low, _, _ in parts)
    if extra is not None:
        small = small + extra
    return three_parts(big), three_parts(small)


def pack_kernel(pos_ref, mass_ref, cmass_ref, center_ref, quad_ref, out_ref):
    for pair in range(PAIRS):
        lanes = pl.ds(128 * pair, 128)
        out_ref[4 * pair : 4 * pair + 3, :] = pos_ref[:, lanes]
        out_ref[4 * pair + 3 : 4 * pair + 4, :] = mass_ref[:, lanes]
    out_ref[CELL_AT : CELL_AT + 1, :] = cmass_ref[...]
    out_ref[CELL_AT + 1 : CELL_AT + 4, :] = center_ref[...]
    out_ref[CELL_AT + 4 : CELL_AT + 10, :] = quad_ref[...]
    out_ref[CELL_AT + 10 : OWN_ROWS, :] = jnp.zeros((OWN_ROWS - CELL_AT - 10, 128), F32)


def outgoing_kernel(n_dom, n_sub, own_ref, all_ref, list_ref, count_ref, out_ref):
    me = lax.axis_index("dom")
    left = lax.broadcasted_iota(jnp.int32, (4, 128), 1) < LEAF
    zero = jnp.zeros((OUT_ROWS, 128), F32)

    def one_target(target, carry):
        out_ref[target, 0:OUT_ROWS, :] = zero
        for seg in range(n_sub):
            at = OUT_ROWS + CELL_PAD * seg
            first = seg * OWN_ROWS + CELL_AT
            out_ref[target, at : at + CELL_PAD, :] = all_ref[first : first + CELL_PAD, :]
        return carry

    lax.fori_loop(0, n_dom, one_target, 0)

    def half(slot, j, right):
        block = list_ref[slot, j]
        value = own_ref[pl.ds(pl.multiple_of(4 * (block // 2), 4), 4), :]
        value = jnp.where(j < count_ref[0, slot], value, 0.0)
        return jnp.where((block & 1) == right, value, pltpu.roll(value, LEAF, 1))

    for slot in range(2 * RANGE):
        target = me + OFFSETS[slot]

        @pl.when((target >= 0) & (target < n_dom))
        def _():
            for unit in range(OUT_UNITS):
                out_ref[target, 4 * unit : 4 * unit + 4, :] = jnp.where(left, half(slot, 2 * unit, 0), half(slot, 2 * unit + 1, 1))


def target_h_rows(parts, one, zero):
    big, small = norm_parts(parts, softening_sq)
    minus_high = [-2.0 * part[0] for part in parts]
    minus_one = [-2.0 * part[2] for part in parts]
    minus_two = [-2.0 * part[3] for part in parts]
    rows = minus_high + [one] * 3 + list(big) + minus_high + minus_one + minus_high
    return rows + minus_two + minus_one + [one] * 3 + list(small) + [zero] * 2


def target_features(all_ref, tg_ref, ce_ref, feat_ref, ah_ref, aq_ref):
    me = lax.axis_index("sub")
    left = lax.broadcasted_iota(jnp.int32, (8, 128), 1) < LEAF
    one = jnp.ones((8, 128), F32)
    zero = jnp.zeros((8, 128), F32)
    raw_ref = tg_ref

    raw_ref[...] = all_ref[pl.ds(pl.multiple_of(me * OWN_ROWS, 8), 4 * PAIRS), :]

    def one_octet(octet, carry):
        parts, centred = [], []
        for comp in range(3):
            rows = pl.ds(octet * 32 + comp, 8, stride=4)
            value = raw_ref[rows, :]
            first = jnp.broadcast_to(value[:, 0:1], (8, 128))
            second = jnp.broadcast_to(value[:, LEAF : LEAF + 1], (8, 128))
            ce_ref[comp, pl.ds(octet * 16, 8, stride=2), :] = first
            ce_ref[comp, pl.ds(octet * 16 + 1, 8, stride=2), :] = second
            value = value - jnp.where(left, first, second)
            raw_ref[rows, :] = value
            centred.append(value)
            parts.append(grid_parts(value))
        rows = target_h_rows(parts, one, zero)
        x, y, z = centred
        split = [three_parts(v) for v in (x, y, z, x * x, y * y, z * z, x * y, x * z, y * z)]
        for which in (0, 0, 1, 0, 1, 2):
            rows += [part[which] for part in split]
        rows += [one] * 3 + [zero] * 7
        for at, value in enumerate(rows):
            feat_ref[8 * at : 8 * at + 8, :] = value
        for sub in range(8):
            pair = octet * 8 + sub
            ah_ref[pair] = feat_ref[pl.ds(sub, H_ROWS, stride=8), :].T.astype(BF16)
            aq_ref[pair] = feat_ref[pl.ds(8 * H_ROWS + sub, Q_ROWS, stride=8), :].T.astype(BF16)
        return carry

    lax.fori_loop(0, PAIRS // 8, one_octet, 0)


def source_h_rows(parts):
    (p1, p2, p3), (s1, s2, s3) = norm_parts(parts)
    high = [part[0] for part in parts]
    one = [part[2] for part in parts]
    two = [part[3] for part in parts]
    rows = dict(enumerate(high + [p1, p2, p3]))
    rows.update(enumerate(one + high + two + high + one + [s1, s2, s3], 9))
    return rows


def put_rows(ref, rows):
    for at, value in rows.items():
        ref[8 * at : 8 * at + 8, :] = value


def fill_constant_rows(ref, count):
    one = jnp.ones((8, 128), F32)
    zero = jnp.zeros((8, 128), F32)
    for at in range(count):
        ones = at in (6, 7, 8, 27, 28, 29) or at == V_AT + 3
        ref[8 * at : 8 * at + 8, :] = one if ones else zero


def cell_features(n_dom, n_sub, octet, cl_ref, recv_ref, ce_ref, cf_ref, cm_ref):
    ids = cl_ref[pl.ds(pl.multiple_of(8 * octet, 8), 8), :]
    lane = ids & 127
    owner = ids >> 7

    def one_domain(dom, found):
        for seg in range(n_sub):
            here = owner == dom * n_sub + seg
            new = []
            for comp in range(CELL_COMPS):
                at = OUT_ROWS + CELL_PAD * seg + comp
                row = jnp.broadcast_to(recv_ref[dom, at : at + 1, :], (8, 128))
                value = jnp.take_along_axis(row, lane, axis=1, mode="promise_in_bounds")
                new.append(jnp.where(here, value, found[comp]))
            found = tuple(new)
        return found

    found = tuple(jnp.zeros((8, 128), F32) for _ in range(CELL_COMPS))
    if n_dom <= 8:
        for dom in range(n_dom):
            found = one_domain(dom, found)
    else:
        found = lax.fori_loop(0, n_dom, one_domain, found)
    mass, cx, cy, cz, xx, yy, zz, xy, xz, yz = found
    cm_ref[...] = mass
    rows8 = pl.ds(pl.multiple_of(8 * octet, 8), 8)
    cx, cy, cz = [value - ce_ref[comp, rows8, :] for comp, value in enumerate((cx, cy, cz))]
    put_rows(cf_ref, source_h_rows([grid_parts(value) for value in (cx, cy, cz)]))
    qx = xx * cx + xy * cy + xz * cz
    qy = xy * cx + yy * cy + yz * cz
    qz = xz * cx + yz * cy + zz * cz
    const = three_parts(2.5 * (qx * cx + qy * cy + qz * cz))
    linear = [-5.0 * qx, -5.0 * qy, -5.0 * qz]
    square = [2.5 * xx, 2.5 * yy, 2.5 * zz, 5.0 * xy, 5.0 * xz, 5.0 * yz]
    split = [three_parts(value) for value in linear + square]
    rows = []
    for which in (0, 1, 0, 2, 1, 0):
        rows += [part[which] for part in split]
    rows += list(const)
    put_rows(cf_ref, dict(enumerate(rows, Q_AT)))
    for comp, value in enumerate((cx, cy, cz)):
        for which, part in enumerate(three_parts(value)):
            cf_ref[8 * (V_AT + 4 * which + comp) : 8 * (V_AT + 4 * which + comp) + 8, :] = part
    columns = {name: three_parts(value) for name, value in dict(xx=xx, yy=yy, zz=zz, xy=xy, xz=xz, yz=yz, cx=qx, cy=qy, cz=qz).items()}
    order = (("xx", "xy", "xz"), ("xy", "yy", "yz"), ("xz", "yz", "zz"), ("cx", "cy", "cz"))
    for which in range(3):
        for column, names in enumerate(order):
            for row, name in enumerate(names):
                at = U_AT + 16 * which + 4 * column + row
                cf_ref[8 * at : 8 * at + 8, :] = columns[name][which]


def source_moments(group, ll_ref, tab_ref, ce_ref, raw_ref, sf_ref):
    left = lax.broadcasted_iota(jnp.int32, (4, 128), 1) < LEAF
    for pair in range(NLEAF // 2):
        first = tab_ref[ll_ref[group, 2 * pair]]
        second = tab_ref[ll_ref[group, 2 * pair + 1]]
        raw_ref[4 * pair : 4 * pair + 4, :] = jnp.where(left, first, second)
    value = [raw_ref[pl.ds(comp, 8, stride=4), :] for comp in range(4)]
    mass = value[3]
    centred = [value[comp] - ce_ref[comp, pl.ds(group, 1), :] for comp in range(3)]
    for comp, v in enumerate([mass * v for v in centred] + [mass]):
        for which, part in enumerate(three_parts(v)):
            at = 4 * which + comp
            sf_ref[8 * at : 8 * at + 8, :] = part


def transposed_dot(rows, weights):
    return lax.dot_general(rows, weights, (((1,), (1,)), ((), ())), preferred_element_type=F32)


def stacked(value):
    return jnp.concatenate(two_parts(value), axis=0)


def cell_group(sub, target_h, target_q, cf_ref, cm_ref):
    def cell_rows(at, count):
        return cf_ref[pl.ds(8 * at + sub, count, stride=8), :].astype(BF16)

    dist_sq = jnp.dot(target_h, cell_rows(0, H_ROWS), preferred_element_type=F32)
    quad_form = jnp.dot(target_q, cell_rows(Q_AT, Q_ROWS), preferred_element_type=F32)
    inv = lax.rsqrt(dist_sq)
    inv_two = inv * inv
    inv_three = inv * inv_two
    pull = inv_three * (cm_ref[pl.ds(sub, 1), :] + quad_form * (inv_two * inv_two))
    moments = jnp.concatenate(
        [
            jnp.concatenate([cell_rows(V_AT, V_ROWS), jnp.zeros((V_ROWS, 128), BF16)], axis=1),
            jnp.concatenate([jnp.zeros((U_ROWS, 128), BF16), cell_rows(U_AT, U_ROWS)], axis=1),
        ],
        axis=0,
    )
    both = jnp.concatenate([stacked(pull), stacked(inv_three * inv_two)], axis=1)
    sums = transposed_dot(both, moments)
    return sums[0:LEAF] + sums[LEAF:]


def pair_lanes(pair):
    return pl.ds(pl.multiple_of(128 * pair, 128), 128)


def pair_place(tg_ref, pair):
    return tg_ref[pl.ds(pl.multiple_of(4 * pair, 4), 4), :]


def point_sums(sums, place):
    sums = sums[0:8] + sums[8:16]
    sums = sums + pltpu.roll(sums, 4, 0)
    return sums[0:3] - place[0:3] * sums[3:4]


def cell_kernel(n_dom, n_sub, all_ref, recv_ref, cl_ref, out_ref, tg_ref, ce_ref, feat_ref, ah_ref, aq_ref, even_ref, odd_ref, cm_ref):
    target_features(all_ref, tg_ref, ce_ref, feat_ref, ah_ref, aq_ref)
    fill_constant_rows(even_ref, CELL_ROWS)
    fill_constant_rows(odd_ref, CELL_ROWS)
    upper = lax.broadcasted_iota(jnp.int32, (8, 128), 0) < 4

    def build(octet, slot, slot_ref):
        cell_features(n_dom, n_sub, octet, cl_ref, recv_ref, ce_ref, slot_ref, cm_ref.at[slot])

    def pull(octet, slot, slot_ref):
        for inner in range(4):
            pair = octet * 4 + inner
            sums = []
            for half in range(2):
                rows = pl.ds(LEAF * half, LEAF)
                sums.append(cell_group(2 * inner + half, ah_ref[pair, rows, :], aq_ref[pair, rows, :], slot_ref, cm_ref.at[slot]))
            sums = jnp.concatenate(sums, axis=0).T
            place = pair_place(tg_ref, pair)
            x, y, z = [place[comp : comp + 1, :] for comp in range(3)]
            quads = sums[16:32] + sums[32:48] + sums[48:64]
            turned = quads[0:8] * jnp.where(upper, x, y) + quads[8:16] * jnp.where(upper, z, -1.0)
            turned = turned + pltpu.roll(turned, 4, 0)
            out_ref[:, pair_lanes(pair)] = point_sums(sums[0:16], place) + turned[0:3]

    octets = LEAF_DEV // 8
    build(0, 0, even_ref)

    def two_octets(step, carry):
        octet = 2 * step
        build(octet + 1, 1, odd_ref)
        pull(octet, 0, even_ref)
        build(jnp.minimum(octet + 2, octets - 1), 0, even_ref)
        pull(octet + 1, 1, odd_ref)
        return carry

    lax.fori_loop(0, octets // 2, two_octets, 0)


def block_tables(n_dom, n_sub, all_ref, recv_ref, tab_ref, rows_ref, feat_ref):
    left = lax.broadcasted_iota(jnp.int32, (4, 128), 1) < LEAF
    copies = lax.broadcasted_iota(jnp.int32, (H_ROWS, 128), 1) % H_ROWS
    copies = jnp.where(copies == lax.broadcasted_iota(jnp.int32, (H_ROWS, 128), 0), 1.0, 0.0).astype(BF16)

    def put(block, value):
        turned = pltpu.roll(value, LEAF, 1)
        tab_ref[block] = jnp.where(left, value, turned)
        tab_ref[block + 1] = jnp.where(left, turned, value)

    def eight_pairs(block, coords):
        put_rows(feat_ref, source_h_rows([grid_parts(value) for value in coords]))
        for pair in range(8):
            spread = feat_ref[pl.ds(pair, H_ROWS, stride=8), :].T.astype(BF16)
            spread = jnp.dot(spread, copies, preferred_element_type=F32).astype(BF16)
            rows_ref[block + 2 * pair] = spread[0:LEAF]
            rows_ref[block + 2 * pair + 1] = spread[LEAF:]

    for seg in range(n_sub):

        def near(octet, carry):
            block = seg * LEAF_DEV + 16 * octet
            first = pl.multiple_of(seg * OWN_ROWS + 32 * octet, 8)
            for pair in range(8):
                put(block + 2 * pair, all_ref[pl.ds(pl.multiple_of(first + 4 * pair, 4), 4), :])
            eight_pairs(block, [all_ref[pl.ds(first + comp, 8, stride=4), :] for comp in range(3)])
            return carry

        lax.fori_loop(0, PAIRS // 8, near, 0)
    me = lax.axis_index("dom")
    for two in range(RANGE):
        halves = []
        for slot in (2 * two, 2 * two + 1):
            source = me - OFFSETS[slot]
            inside = (source >= 0) & (source < n_dom)
            source = jnp.clip(source, 0, n_dom - 1)
            for unit in range(OUT_UNITS):
                value = jnp.where(inside, recv_ref[source, 4 * unit : 4 * unit + 4, :], 0.0)
                put(n_sub * LEAF_DEV + slot * CAP + 2 * unit, value)
            halves.append([jnp.where(inside, recv_ref[source, pl.ds(comp, OUT_UNITS, stride=4), :], 0.0) for comp in range(3)])
        coords = [jnp.concatenate([one, other], axis=0) for one, other in zip(*halves)]
        eight_pairs(n_sub * LEAF_DEV + 2 * two * CAP, coords)


def target_rows(all_ref, feat_ref, at_ref):
    first = lax.axis_index("sub") * OWN_ROWS
    one = jnp.ones((8, 128), F32)
    zero = jnp.zeros((8, 128), F32)

    def one_octet(octet, carry):
        parts = [grid_parts(all_ref[pl.ds(first + octet * 32 + comp, 8, stride=4), :]) for comp in range(3)]
        for at, value in enumerate(target_h_rows(parts, one, zero)):
            feat_ref[8 * at : 8 * at + 8, :] = value
        for pair in range(8):
            at_ref[octet * 8 + pair] = feat_ref[pl.ds(pair, H_ROWS, stride=8), :].astype(BF16)
        return carry

    lax.fori_loop(0, PAIRS // 8, one_octet, 0)


def direct_kernel(n_dom, n_sub, all_ref, recv_ref, ll_ref, tg_ref, ce_ref, cell_ref, out_ref, tab_ref, rows_ref, feat_ref, at_ref, raw_ref, even_ref, odd_ref):
    target_rows(all_ref, feat_ref, at_ref)
    fill_constant_rows(feat_ref, H_ROWS)
    block_tables(n_dom, n_sub, all_ref, recv_ref, tab_ref, rows_ref, feat_ref)
    nothing = jnp.zeros((8, 128), F32)
    for group in range(4):
        for at in range(12, V_ROWS):
            even_ref[group, 8 * at : 8 * at + 8, :] = nothing
            odd_ref[group, 8 * at : 8 * at + 8, :] = nothing
    left = lax.broadcasted_iota(jnp.int32, (V_ROWS, 128), 1) < LEAF
    left_target = lax.broadcasted_iota(jnp.int32, (H_ROWS, 128), 1) < LEAF
    owner = lax.broadcasted_iota(jnp.int32, (LEAF, 128), 1) // H_ROWS

    def features(quad, raw_at, slot_ref):
        for group in range(4):
            source_moments(4 * quad + group, ll_ref, tab_ref, ce_ref, raw_ref.at[raw_at + group], slot_ref.at[group])

    def pull(quad, slot_ref):
        nothing = jnp.zeros((H_ROWS, 128), BF16)
        first, second = at_ref[2 * quad], at_ref[2 * quad + 1]
        targets = jnp.concatenate(
            [
                jnp.concatenate([jnp.where(left_target, first, nothing), nothing], axis=1),
                jnp.concatenate([jnp.where(left_target, nothing, first), nothing], axis=1),
                jnp.concatenate([nothing, jnp.where(left_target, second, nothing)], axis=1),
                jnp.concatenate([nothing, jnp.where(left_target, nothing, second)], axis=1),
            ],
            axis=0,
        )
        totals = [jnp.zeros((2 * V_ROWS, 128), F32) for _ in range(2)]
        for chunk in range(8):
            sources = []
            for j in (2 * chunk, 2 * chunk + 1):
                rows = [rows_ref[ll_ref[4 * quad + group, j]] for group in range(4)]
                low = jnp.where(owner == 0, rows[0], rows[1])
                high = jnp.where(owner == 2, rows[2], rows[3])
                sources.append(jnp.where(owner < 2, low, high))
            dist_sq = jnp.dot(jnp.concatenate(sources, axis=0), targets, preferred_element_type=F32)
            inv = lax.rsqrt(dist_sq)
            weights = stacked(inv * inv * inv)
            moments = [slot_ref[group, pl.ds(chunk, V_ROWS, stride=8), :].astype(BF16) for group in range(4)]
            for side in range(2):
                rows = jnp.concatenate(moments[2 * side : 2 * side + 2], axis=0)
                rows = jnp.concatenate([rows, rows], axis=1)
                totals[side] += jnp.dot(rows, weights[:, 128 * side : 128 * side + 128], preferred_element_type=F32)
        for side in range(2):
            pair = 2 * quad + side
            sums = jnp.where(left, totals[side][0:V_ROWS], totals[side][V_ROWS:])
            lanes = pair_lanes(pair)
            out_ref[:, lanes] = cell_ref[:, lanes] + point_sums(sums, pair_place(tg_ref, pair))

    quads = LEAF_DEV // 4
    features(0, 0, even_ref)

    def two_quads(step, carry):
        quad = 2 * step
        features(quad + 1, 4, odd_ref)
        pull(quad, even_ref)
        features(jnp.minimum(quad + 2, quads - 1), 0, even_ref)
        pull(quad + 1, odd_ref)
        return carry

    lax.fori_loop(0, quads // 2, two_quads, 0)


def on_device(n_dom, n_sub, positions, masses, cell_mass, cell_center, cell_quad, cell_list, leaf_list, send_list, send_count):
    vmem = pl.BlockSpec(memory_space=pltpu.VMEM)
    smem = pl.BlockSpec(memory_space=pltpu.SMEM)
    params = pltpu.CompilerParams(vmem_limit_bytes=48 * 1024 * 1024)
    packed = pl.pallas_call(
        pack_kernel,
        out_shape=jax.ShapeDtypeStruct((OWN_ROWS, 128), F32),
        in_specs=[vmem] * 5,
        out_specs=vmem,
        compiler_params=params,
        name="pack_own",
    )(positions, masses.reshape(1, -1), cell_mass.reshape(1, -1), cell_center, cell_quad)
    nearby = lax.all_gather(packed, "sub", axis=0, tiled=True)
    outgoing = pl.pallas_call(
        functools.partial(outgoing_kernel, n_dom, n_sub),
        out_shape=jax.ShapeDtypeStruct((n_dom, OUT_ROWS + CELL_PAD * n_sub, 128), F32),
        in_specs=[vmem, vmem, smem, smem],
        out_specs=vmem,
        compiler_params=params,
        name="pack_outgoing",
    )(packed, nearby, send_list.reshape(2 * RANGE, CAP), send_count.reshape(1, 2 * RANGE))
    received = lax.all_to_all(outgoing, "dom", split_axis=0, concat_axis=0, tiled=True)
    cell_part, places, centres = pl.pallas_call(
        functools.partial(cell_kernel, n_dom, n_sub),
        out_shape=(
            jax.ShapeDtypeStruct((3, LEAF_DEV * LEAF), F32),
            jax.ShapeDtypeStruct((4 * PAIRS, 128), F32),
            jax.ShapeDtypeStruct((3, LEAF_DEV, 128), F32),
        ),
        in_specs=[vmem] * 3,
        out_specs=[vmem] * 3,
        scratch_shapes=[
            pltpu.VMEM((8 * (H_ROWS + Q_ROWS), 128), F32),
            pltpu.VMEM((PAIRS, 128, H_ROWS), BF16),
            pltpu.VMEM((PAIRS, 128, Q_ROWS), BF16),
            pltpu.VMEM((8 * CELL_ROWS, 128), F32),
            pltpu.VMEM((8 * CELL_ROWS, 128), F32),
            pltpu.VMEM((2, 8, 128), F32),
        ],
        compiler_params=params,
        name="cells",
    )(nearby, received, cell_list)
    n_blocks = n_sub * LEAF_DEV + 2 * RANGE * CAP
    return pl.pallas_call(
        functools.partial(direct_kernel, n_dom, n_sub),
        out_shape=jax.ShapeDtypeStruct((3, LEAF_DEV * LEAF), F32),
        in_specs=[vmem, vmem, smem] + [vmem] * 3,
        out_specs=vmem,
        scratch_shapes=[
            pltpu.VMEM((n_blocks, 4, 128), F32),
            pltpu.VMEM((n_blocks, LEAF, 128), BF16),
            pltpu.VMEM((8 * H_ROWS, 128), F32),
            pltpu.VMEM((PAIRS, H_ROWS, 128), BF16),
            pltpu.VMEM((8, 32, 128), F32),
            pltpu.VMEM((4, 8 * V_ROWS, 128), F32),
            pltpu.VMEM((4, 8 * V_ROWS, 128), F32),
        ],
        compiler_params=params,
        name="direct",
    )(nearby, received, leaf_list, places, centres, cell_part)


def solution(mesh):
    sharded = P(("dom", "sub"))
    return jax.shard_map(
        functools.partial(on_device, mesh.shape["dom"], mesh.shape["sub"]),
        mesh=mesh,
        in_specs=(
            P(None, ("dom", "sub")),
            sharded,
            sharded,
            P(None, ("dom", "sub")),
            P(None, ("dom", "sub")),
            P(("dom", "sub"), None),
            P(("dom", "sub"), None),
            P("dom", "sub", None, None),
            P("dom", "sub", None),
        ),
        out_specs=P(None, ("dom", "sub")),
        check_vma=False,
    )
```

```python
import functools

import jax
import jax.numpy as jnp
from jax import lax
from jax.experimental import pallas as pl
from jax.experimental.pallas import tpu as pltpu
from jax.sharding import PartitionSpec as P

LEAF = 64
LEAF_DEV = 128
NCELL = 128
NLEAF = 16
RANGE = 4
CAP = 8
PAIRS = LEAF_DEV // 2
OUT_UNITS = CAP // 2
OWN_ROWS = 4 * PAIRS + 16
OUT_ROWS = 4 * OUT_UNITS
CELL_AT = 4 * PAIRS
CELL_COMPS = 10
CELL_PAD = 12
OFFSETS = list(range(-RANGE, 0)) + list(range(1, RANGE + 1))

softening_sq = 0.0025
GRID_ROUND = 49152.0
F32 = jnp.float32
BF16 = jnp.bfloat16

H_ROWS = 32
Q_ROWS = 64
V_ROWS = 16
U_ROWS = 48
Q_AT = H_ROWS
V_AT = Q_AT + Q_ROWS
U_AT = V_AT + V_ROWS
CELL_ROWS = U_AT + U_ROWS
SOURCE_ROWS = H_ROWS + V_ROWS


def rounded(value):
    return value.astype(BF16).astype(F32)


def three_parts(value):
    first = rounded(value)
    rest = value - first
    second = rounded(rest)
    return first, second, rest - second


def two_parts(value):
    first = value.astype(BF16)
    return first, (value - first.astype(F32)).astype(BF16)


def grid_parts(value):
    high = (value + GRID_ROUND) - GRID_ROUND
    low = value - high
    first = rounded(low)
    return high, low, first, low - first


def norm_parts(parts, extra=None):
    big = sum(high * high for high, _, _, _ in parts)
    small = sum(low * (2.0 * high + low) for high, low, _, _ in parts)
    if extra is not None:
        small = small + extra
    return three_parts(big), three_parts(small)


def pack_kernel(n_dom, *refs):
    ins, out_ref, sent_ref, scratch, sems = refs[:7], refs[7], refs[8], refs[9:16], refs[16]
    copies = [pltpu.make_async_copy(src, dst, sems.at[at]) for at, (src, dst) in enumerate(zip(ins, scratch))]
    for copy in copies:
        copy.start()
    pos_ref, mass_ref, cmass_ref, center_ref, quad_ref, list_ref, count_ref = scratch
    me = lax.axis_index("dom")
    left = lax.broadcasted_iota(jnp.int32, (4, 128), 1) < LEAF
    sent_ref[...] = jnp.zeros((n_dom, OUT_ROWS, 128), F32)
    out_ref[CELL_AT + 10 : OWN_ROWS, :] = jnp.zeros((OWN_ROWS - CELL_AT - 10, 128), F32)
    for copy in copies:
        copy.wait()
    for pair in range(PAIRS):
        lanes = pl.ds(128 * pair, 128)
        out_ref[4 * pair : 4 * pair + 3, :] = pos_ref[:, lanes]
        out_ref[4 * pair + 3 : 4 * pair + 4, :] = mass_ref[:, lanes]
    out_ref[CELL_AT : CELL_AT + 1, :] = cmass_ref[...]
    out_ref[CELL_AT + 1 : CELL_AT + 4, :] = center_ref[...]
    out_ref[CELL_AT + 4 : CELL_AT + 10, :] = quad_ref[...]

    def half(slot, j, right):
        block = list_ref[slot, j]
        value = out_ref[pl.ds(pl.multiple_of(4 * (block // 2), 4), 4), :]
        value = jnp.where(j < count_ref[0, slot], value, 0.0)
        return jnp.where((block & 1) == right, value, pltpu.roll(value, LEAF, 1))

    for slot in range(2 * RANGE):
        target = me + OFFSETS[slot]

        @pl.when((target >= 0) & (target < n_dom))
        def _():
            for unit in range(OUT_UNITS):
                sent_ref[target, 4 * unit : 4 * unit + 4, :] = jnp.where(left, half(slot, 2 * unit, 0), half(slot, 2 * unit + 1, 1))


def outgoing_kernel(n_dom, n_sub, sent_ref, all_ref, out_ref, sem):
    copy = pltpu.make_async_copy(sent_ref, out_ref.at[:, 0:OUT_ROWS, :], sem)
    copy.start()

    def one_target(target, carry):
        for seg in range(n_sub):
            at = OUT_ROWS + CELL_PAD * seg
            first = seg * OWN_ROWS + CELL_AT
            out_ref[target, at : at + CELL_PAD, :] = all_ref[first : first + CELL_PAD, :]
        return carry

    lax.fori_loop(0, n_dom, one_target, 0)
    copy.wait()


def target_h_rows(parts, one, zero):
    big, small = norm_parts(parts, softening_sq)
    minus_high = [-2.0 * part[0] for part in parts]
    minus_one = [-2.0 * part[2] for part in parts]
    minus_two = [-2.0 * part[3] for part in parts]
    rows = minus_high + [one] * 3 + list(big) + minus_high + minus_one + minus_high
    return rows + minus_two + minus_one + [one] * 3 + list(small) + [zero] * 2


def target_features(all_ref, tg_ref, ce_ref, feat_ref, ah_ref, aq_ref):
    me = lax.axis_index("sub")
    left = lax.broadcasted_iota(jnp.int32, (8, 128), 1) < LEAF
    one = jnp.ones((8, 128), F32)
    zero = jnp.zeros((8, 128), F32)
    raw_ref = tg_ref

    raw_ref[...] = all_ref[pl.ds(pl.multiple_of(me * OWN_ROWS, 8), 4 * PAIRS), :]

    def one_octet(octet, carry):
        parts, centred = [], []
        for comp in range(3):
            rows = pl.ds(octet * 32 + comp, 8, stride=4)
            value = raw_ref[rows, :]
            first = jnp.broadcast_to(value[:, 0:1], (8, 128))
            second = jnp.broadcast_to(value[:, LEAF : LEAF + 1], (8, 128))
            ce_ref[comp, pl.ds(octet * 16, 8, stride=2), :] = first
            ce_ref[comp, pl.ds(octet * 16 + 1, 8, stride=2), :] = second
            value = value - jnp.where(left, first, second)
            raw_ref[rows, :] = value
            centred.append(value)
            parts.append(grid_parts(value))
        rows = target_h_rows(parts, one, zero)
        x, y, z = centred
        split = [three_parts(v) for v in (x, y, z, x * x, y * y, z * z, x * y, x * z, y * z)]
        for which in (0, 0, 1, 0, 1, 2):
            rows += [part[which] for part in split]
        rows += [one] * 3 + [zero] * 7
        for at, value in enumerate(rows):
            feat_ref[8 * at : 8 * at + 8, :] = value
        for sub in range(8):
            pair = octet * 8 + sub
            ah_ref[pair] = feat_ref[pl.ds(sub, H_ROWS, stride=8), :].T.astype(BF16)
            aq_ref[pair] = feat_ref[pl.ds(8 * H_ROWS + sub, Q_ROWS, stride=8), :].T.astype(BF16)
        return carry

    lax.fori_loop(0, PAIRS // 8, one_octet, 0)


def source_h_rows(parts):
    (p1, p2, p3), (s1, s2, s3) = norm_parts(parts)
    high = [part[0] for part in parts]
    one = [part[2] for part in parts]
    two = [part[3] for part in parts]
    rows = dict(enumerate(high + [p1, p2, p3]))
    rows.update(enumerate(one + high + two + high + one + [s1, s2, s3], 9))
    return rows


def put_rows(ref, rows):
    for at, value in rows.items():
        ref[8 * at : 8 * at + 8, :] = value


def fill_constant_rows(ref, count):
    one = jnp.ones((8, 128), F32)
    zero = jnp.zeros((8, 128), F32)
    for at in range(count):
        ones = at in (6, 7, 8, 27, 28, 29) or at == V_AT + 3
        ref[8 * at : 8 * at + 8, :] = one if ones else zero


def cell_features(n_dom, n_sub, octet, cl_ref, recv_ref, ce_ref, cf_ref, cm_ref):
    ids = cl_ref[pl.ds(pl.multiple_of(8 * octet, 8), 8), :]
    lane = ids & 127
    owner = ids >> 7

    def one_domain(dom, found):
        for seg in range(n_sub):
            here = owner == dom * n_sub + seg
            new = []
            for comp in range(CELL_COMPS):
                at = OUT_ROWS + CELL_PAD * seg + comp
                row = jnp.broadcast_to(recv_ref[dom, at : at + 1, :], (8, 128))
                value = jnp.take_along_axis(row, lane, axis=1, mode="promise_in_bounds")
                new.append(jnp.where(here, value, found[comp]))
            found = tuple(new)
        return found

    found = tuple(jnp.zeros((8, 128), F32) for _ in range(CELL_COMPS))
    if n_dom <= 8:
        for dom in range(n_dom):
            found = one_domain(dom, found)
    else:
        found = lax.fori_loop(0, n_dom, one_domain, found)
    mass, cx, cy, cz, xx, yy, zz, xy, xz, yz = found
    cm_ref[...] = mass
    rows8 = pl.ds(pl.multiple_of(8 * octet, 8), 8)
    cx, cy, cz = [value - ce_ref[comp, rows8, :] for comp, value in enumerate((cx, cy, cz))]
    put_rows(cf_ref, source_h_rows([grid_parts(value) for value in (cx, cy, cz)]))
    qx = xx * cx + xy * cy + xz * cz
    qy = xy * cx + yy * cy + yz * cz
    qz = xz * cx + yz * cy + zz * cz
    const = three_parts(2.5 * (qx * cx + qy * cy + qz * cz))
    linear = [-5.0 * qx, -5.0 * qy, -5.0 * qz]
    square = [2.5 * xx, 2.5 * yy, 2.5 * zz, 5.0 * xy, 5.0 * xz, 5.0 * yz]
    split = [three_parts(value) for value in linear + square]
    rows = []
    for which in (0, 1, 0, 2, 1, 0):
        rows += [part[which] for part in split]
    rows += list(const)
    put_rows(cf_ref, dict(enumerate(rows, Q_AT)))
    for comp, value in enumerate((cx, cy, cz)):
        for which, part in enumerate(three_parts(value)):
            cf_ref[8 * (V_AT + 4 * which + comp) : 8 * (V_AT + 4 * which + comp) + 8, :] = part
    columns = {name: three_parts(value) for name, value in dict(xx=xx, yy=yy, zz=zz, xy=xy, xz=xz, yz=yz, cx=qx, cy=qy, cz=qz).items()}
    order = (("xx", "xy", "xz"), ("xy", "yy", "yz"), ("xz", "yz", "zz"), ("cx", "cy", "cz"))
    for which in range(3):
        for column, names in enumerate(order):
            for row, name in enumerate(names):
                at = U_AT + 16 * which + 4 * column + row
                cf_ref[8 * at : 8 * at + 8, :] = columns[name][which]


def source_moments(group, ll_ref, tab_ref, ce_ref, raw_ref, sf_ref):
    left = lax.broadcasted_iota(jnp.int32, (4, 128), 1) < LEAF
    for pair in range(NLEAF // 2):
        first = tab_ref[ll_ref[group, 2 * pair]]
        second = tab_ref[ll_ref[group, 2 * pair + 1]]
        raw_ref[4 * pair : 4 * pair + 4, :] = jnp.where(left, first, second)
    value = [raw_ref[pl.ds(comp, 8, stride=4), :] for comp in range(4)]
    mass = value[3]
    centred = [value[comp] - ce_ref[comp, pl.ds(group, 1), :] for comp in range(3)]
    for comp, v in enumerate([mass * v for v in centred] + [mass]):
        for which, part in enumerate(three_parts(v)):
            at = 4 * which + comp
            sf_ref[8 * at : 8 * at + 8, :] = part


def transposed_dot(rows, weights):
    return lax.dot_general(rows, weights, (((1,), (1,)), ((), ())), preferred_element_type=F32)


def stacked(value):
    return jnp.concatenate(two_parts(value), axis=0)


def cell_group(sub, target_h, target_q, cf_ref, cm_ref):
    def cell_rows(at, count):
        return cf_ref[pl.ds(8 * at + sub, count, stride=8), :].astype(BF16)

    dist_sq = jnp.dot(target_h, cell_rows(0, H_ROWS), preferred_element_type=F32)
    quad_form = jnp.dot(target_q, cell_rows(Q_AT, Q_ROWS), preferred_element_type=F32)
    inv = lax.rsqrt(dist_sq)
    inv_two = inv * inv
    inv_three = inv * inv_two
    pull = inv_three * (cm_ref[pl.ds(sub, 1), :] + quad_form * (inv_two * inv_two))
    moments = jnp.concatenate(
        [
            jnp.concatenate([cell_rows(V_AT, V_ROWS), jnp.zeros((V_ROWS, 128), BF16)], axis=1),
            jnp.concatenate([jnp.zeros((U_ROWS, 128), BF16), cell_rows(U_AT, U_ROWS)], axis=1),
        ],
        axis=0,
    )
    both = jnp.concatenate([stacked(pull), stacked(inv_three * inv_two)], axis=1)
    sums = transposed_dot(both, moments)
    return sums[0:LEAF] + sums[LEAF:]


def pair_lanes(pair):
    return pl.ds(pl.multiple_of(128 * pair, 128), 128)


def pair_place(tg_ref, pair):
    return tg_ref[pl.ds(pl.multiple_of(4 * pair, 4), 4), :]


def point_sums(sums, place):
    sums = sums[0:8] + sums[8:16]
    sums = sums + pltpu.roll(sums, 4, 0)
    return sums[0:3] - place[0:3] * sums[3:4]


def cell_kernel(n_dom, n_sub, recv_ref, cl_ref, tg_ref, ce_ref, ah_ref, aq_ref, out_ref, even_ref, odd_ref, cm_ref):
    fill_constant_rows(even_ref, CELL_ROWS)
    fill_constant_rows(odd_ref, CELL_ROWS)
    upper = lax.broadcasted_iota(jnp.int32, (8, 128), 0) < 4

    def build(octet, slot, slot_ref):
        cell_features(n_dom, n_sub, octet, cl_ref, recv_ref, ce_ref, slot_ref, cm_ref.at[slot])

    def pull(octet, slot, slot_ref):
        for inner in range(4):
            pair = octet * 4 + inner
            sums = []
            for half in range(2):
                rows = pl.ds(LEAF * half, LEAF)
                sums.append(cell_group(2 * inner + half, ah_ref[pair, rows, :], aq_ref[pair, rows, :], slot_ref, cm_ref.at[slot]))
            sums = jnp.concatenate(sums, axis=0).T
            place = pair_place(tg_ref, pair)
            x, y, z = [place[comp : comp + 1, :] for comp in range(3)]
            quads = sums[16:32] + sums[32:48] + sums[48:64]
            turned = quads[0:8] * jnp.where(upper, x, y) + quads[8:16] * jnp.where(upper, z, -1.0)
            turned = turned + pltpu.roll(turned, 4, 0)
            out_ref[:, pair_lanes(pair)] = point_sums(sums[0:16], place) + turned[0:3]

    octets = LEAF_DEV // 8
    build(0, 0, even_ref)

    def two_octets(step, carry):
        octet = 2 * step
        build(octet + 1, 1, odd_ref)
        pull(octet, 0, even_ref)
        build(jnp.minimum(octet + 2, octets - 1), 0, even_ref)
        pull(octet + 1, 1, odd_ref)
        return carry

    lax.fori_loop(0, octets // 2, two_octets, 0)


def put_block_pair(tab_ref, block, value):
    left = lax.broadcasted_iota(jnp.int32, (4, 128), 1) < LEAF
    turned = pltpu.roll(value, LEAF, 1)
    tab_ref[block] = jnp.where(left, value, turned)
    tab_ref[block + 1] = jnp.where(left, turned, value)


def put_eight_pairs(rows_ref, block, coords, feat_ref):
    copies = lax.broadcasted_iota(jnp.int32, (H_ROWS, 128), 1) % H_ROWS
    copies = jnp.where(copies == lax.broadcasted_iota(jnp.int32, (H_ROWS, 128), 0), 1.0, 0.0).astype(BF16)
    put_rows(feat_ref, source_h_rows([grid_parts(value) for value in coords]))
    for pair in range(8):
        spread = feat_ref[pl.ds(pair, H_ROWS, stride=8), :].T.astype(BF16)
        spread = jnp.dot(spread, copies, preferred_element_type=F32).astype(BF16)
        rows_ref[block + 2 * pair] = spread[0:LEAF]
        rows_ref[block + 2 * pair + 1] = spread[LEAF:]


def prepare_kernel(n_sub, all_ref, tab_ref, rows_ref, at_ref, tg_ref, ce_ref, ah_ref, aq_ref, feat_ref, four_ref):
    target_features(all_ref, tg_ref, ce_ref, feat_ref, ah_ref, aq_ref)
    target_rows(all_ref, four_ref.at[0], at_ref)
    for at in range(4):
        fill_constant_rows(four_ref.at[at], H_ROWS)

    def near(step, carry):
        seg, part = step // (PAIRS // 32), step % (PAIRS // 32)
        for at in range(4):
            octet = 4 * part + at
            block = seg * LEAF_DEV + 16 * octet
            first = pl.multiple_of(seg * OWN_ROWS + 32 * octet, 8)
            for pair in range(8):
                put_block_pair(tab_ref, block + 2 * pair, all_ref[pl.ds(pl.multiple_of(first + 4 * pair, 4), 4), :])
            coords = [all_ref[pl.ds(first + comp, 8, stride=4), :] for comp in range(3)]
            put_eight_pairs(rows_ref, block, coords, four_ref.at[at])
        return carry

    lax.fori_loop(0, n_sub * PAIRS // 32, near, 0)


def far_tables(n_dom, first_block, recv_ref, tab_ref, rows_ref, four_ref):
    for at in range(4):
        fill_constant_rows(four_ref.at[at], H_ROWS)
    me = lax.axis_index("dom")
    for two in range(RANGE):
        halves = []
        for slot in (2 * two, 2 * two + 1):
            source = me - OFFSETS[slot]
            inside = (source >= 0) & (source < n_dom)
            source = jnp.clip(source, 0, n_dom - 1)
            for unit in range(OUT_UNITS):
                value = jnp.where(inside, recv_ref[source, 4 * unit : 4 * unit + 4, :], 0.0)
                put_block_pair(tab_ref, first_block + slot * CAP + 2 * unit, value)
            halves.append([jnp.where(inside, recv_ref[source, pl.ds(comp, OUT_UNITS, stride=4), :], 0.0) for comp in range(3)])
        coords = [jnp.concatenate([one, other], axis=0) for one, other in zip(*halves)]
        put_eight_pairs(rows_ref, first_block + 2 * two * CAP, coords, four_ref.at[two])


def target_rows(all_ref, feat_ref, at_ref):
    first = lax.axis_index("sub") * OWN_ROWS
    one = jnp.ones((8, 128), F32)
    zero = jnp.zeros((8, 128), F32)

    def one_octet(octet, carry):
        parts = [grid_parts(all_ref[pl.ds(first + octet * 32 + comp, 8, stride=4), :]) for comp in range(3)]
        for at, value in enumerate(target_h_rows(parts, one, zero)):
            feat_ref[8 * at : 8 * at + 8, :] = value
        for pair in range(8):
            at_ref[octet * 8 + pair] = feat_ref[pl.ds(pair, H_ROWS, stride=8), :].astype(BF16)
        return carry

    lax.fori_loop(0, PAIRS // 8, one_octet, 0)


def direct_kernel(n_dom, n_sub, near_tab, near_rows, at_ref, recv_ref, ll_ref, tg_ref, ce_ref, cell_ref, out_ref, tab_ref, rows_ref, four_ref, raw_ref, even_ref, odd_ref, sems):
    n_near = n_sub * LEAF_DEV
    copies = [
        pltpu.make_async_copy(near_tab, tab_ref.at[0:n_near], sems.at[0]),
        pltpu.make_async_copy(near_rows, rows_ref.at[0:n_near], sems.at[1]),
    ]
    for copy in copies:
        copy.start()
    far_tables(n_dom, n_near, recv_ref, tab_ref, rows_ref, four_ref)
    for copy in copies:
        copy.wait()
    nothing = jnp.zeros((8, 128), F32)
    for group in range(4):
        for at in range(12, V_ROWS):
            even_ref[group, 8 * at : 8 * at + 8, :] = nothing
            odd_ref[group, 8 * at : 8 * at + 8, :] = nothing
    left = lax.broadcasted_iota(jnp.int32, (V_ROWS, 128), 1) < LEAF
    left_target = lax.broadcasted_iota(jnp.int32, (H_ROWS, 128), 1) < LEAF
    owner = lax.broadcasted_iota(jnp.int32, (LEAF, 128), 1) // H_ROWS

    def features(quad, raw_at, slot_ref):
        for group in range(4):
            source_moments(4 * quad + group, ll_ref, tab_ref, ce_ref, raw_ref.at[raw_at + group], slot_ref.at[group])

    def pull(quad, slot_ref):
        nothing = jnp.zeros((H_ROWS, 128), BF16)
        first, second = at_ref[2 * quad], at_ref[2 * quad + 1]
        targets = jnp.concatenate(
            [
                jnp.concatenate([jnp.where(left_target, first, nothing), nothing], axis=1),
                jnp.concatenate([jnp.where(left_target, nothing, first), nothing], axis=1),
                jnp.concatenate([nothing, jnp.where(left_target, second, nothing)], axis=1),
                jnp.concatenate([nothing, jnp.where(left_target, nothing, second)], axis=1),
            ],
            axis=0,
        )
        totals = [jnp.zeros((2 * V_ROWS, 128), F32) for _ in range(2)]
        for chunk in range(8):
            sources = []
            for j in (2 * chunk, 2 * chunk + 1):
                rows = [rows_ref[ll_ref[4 * quad + group, j]] for group in range(4)]
                low = jnp.where(owner == 0, rows[0], rows[1])
                high = jnp.where(owner == 2, rows[2], rows[3])
                sources.append(jnp.where(owner < 2, low, high))
            dist_sq = jnp.dot(jnp.concatenate(sources, axis=0), targets, preferred_element_type=F32)
            inv = lax.rsqrt(dist_sq)
            weights = stacked(inv * inv * inv)
            moments = [slot_ref[group, pl.ds(chunk, V_ROWS, stride=8), :].astype(BF16) for group in range(4)]
            for side in range(2):
                rows = jnp.concatenate(moments[2 * side : 2 * side + 2], axis=0)
                rows = jnp.concatenate([rows, rows], axis=1)
                totals[side] += jnp.dot(rows, weights[:, 128 * side : 128 * side + 128], preferred_element_type=F32)
        for side in range(2):
            pair = 2 * quad + side
            sums = jnp.where(left, totals[side][0:V_ROWS], totals[side][V_ROWS:])
            lanes = pair_lanes(pair)
            out_ref[:, lanes] = cell_ref[:, lanes] + point_sums(sums, pair_place(tg_ref, pair))

    quads = LEAF_DEV // 4
    features(0, 0, even_ref)

    def two_quads(step, carry):
        quad = 2 * step
        features(quad + 1, 4, odd_ref)
        pull(quad, even_ref)
        features(jnp.minimum(quad + 2, quads - 1), 0, even_ref)
        pull(quad + 1, odd_ref)
        return carry

    lax.fori_loop(0, quads // 2, two_quads, 0)


def on_device(n_dom, n_sub, positions, masses, cell_mass, cell_center, cell_quad, cell_list, leaf_list, send_list, send_count):
    vmem = pl.BlockSpec(memory_space=pltpu.VMEM)
    smem = pl.BlockSpec(memory_space=pltpu.SMEM)
    anywhere = pl.BlockSpec(memory_space=pl.ANY)

    def limit(mib):
        return pltpu.CompilerParams(vmem_limit_bytes=mib * 1024 * 1024)

    ins = (
        positions,
        masses.reshape(1, -1),
        cell_mass.reshape(1, -1),
        cell_center,
        cell_quad,
        send_list.reshape(2 * RANGE, CAP),
        send_count.reshape(1, 2 * RANGE),
    )
    packed, sent = pl.pallas_call(
        functools.partial(pack_kernel, n_dom),
        out_shape=(
            jax.ShapeDtypeStruct((OWN_ROWS, 128), F32),
            jax.ShapeDtypeStruct((n_dom, OUT_ROWS, 128), F32),
        ),
        in_specs=[pl.BlockSpec(memory_space=pltpu.HBM)] * 7,
        out_specs=[vmem] * 2,
        scratch_shapes=[pltpu.VMEM(array.shape, F32) for array in ins[:5]]
        + [pltpu.SMEM(array.shape, jnp.int32) for array in ins[5:]]
        + [pltpu.SemaphoreType.DMA((7,))],
        compiler_params=limit(63),
        name="pack_own",
    )(*ins)
    nearby = lax.all_gather(packed, "sub", axis=0, tiled=True)
    outgoing = pl.pallas_call(
        functools.partial(outgoing_kernel, n_dom, n_sub),
        out_shape=jax.ShapeDtypeStruct((n_dom, OUT_ROWS + CELL_PAD * n_sub, 128), F32),
        in_specs=[anywhere, vmem],
        out_specs=vmem,
        scratch_shapes=[pltpu.SemaphoreType.DMA(())],
        compiler_params=limit(16),
        name="pack_outgoing",
    )(sent, nearby)
    received = lax.all_to_all(outgoing, "dom", split_axis=0, concat_axis=0, tiled=True)
    n_near = n_sub * LEAF_DEV
    n_blocks = n_near + 2 * RANGE * CAP
    near_tab, near_rows, targets, places, centres, cell_targets, quad_targets = pl.pallas_call(
        functools.partial(prepare_kernel, n_sub),
        out_shape=(
            jax.ShapeDtypeStruct((n_near, 4, 128), F32),
            jax.ShapeDtypeStruct((n_near, LEAF, 128), BF16),
            jax.ShapeDtypeStruct((PAIRS, H_ROWS, 128), BF16),
            jax.ShapeDtypeStruct((4 * PAIRS, 128), F32),
            jax.ShapeDtypeStruct((3, LEAF_DEV, 128), F32),
            jax.ShapeDtypeStruct((PAIRS, 128, H_ROWS), BF16),
            jax.ShapeDtypeStruct((PAIRS, 128, Q_ROWS), BF16),
        ),
        in_specs=[vmem],
        out_specs=[vmem] * 7,
        scratch_shapes=[
            pltpu.VMEM((8 * (H_ROWS + Q_ROWS), 128), F32),
            pltpu.VMEM((4, 8 * H_ROWS, 128), F32),
        ],
        compiler_params=limit(24),
        cost_estimate=pl.CostEstimate(flops=50_000_000, bytes_accessed=16_000_000, transcendentals=0),
        name="prepare",
    )(nearby)
    cell_part = pl.pallas_call(
        functools.partial(cell_kernel, n_dom, n_sub),
        out_shape=jax.ShapeDtypeStruct((3, LEAF_DEV * LEAF), F32),
        in_specs=[vmem] * 6,
        out_specs=vmem,
        scratch_shapes=[
            pltpu.VMEM((8 * CELL_ROWS, 128), F32),
            pltpu.VMEM((8 * CELL_ROWS, 128), F32),
            pltpu.VMEM((2, 8, 128), F32),
        ],
        compiler_params=limit(24),
        name="cells",
    )(received, cell_list, places, centres, cell_targets, quad_targets)
    return pl.pallas_call(
        functools.partial(direct_kernel, n_dom, n_sub),
        out_shape=jax.ShapeDtypeStruct((3, LEAF_DEV * LEAF), F32),
        in_specs=[anywhere, anywhere, vmem, vmem, smem, vmem, vmem, vmem],
        out_specs=vmem,
        scratch_shapes=[
            pltpu.VMEM((n_blocks, 4, 128), F32),
            pltpu.VMEM((n_blocks, LEAF, 128), BF16),
            pltpu.VMEM((4, 8 * H_ROWS, 128), F32),
            pltpu.VMEM((8, 32, 128), F32),
            pltpu.VMEM((4, 8 * V_ROWS, 128), F32),
            pltpu.VMEM((4, 8 * V_ROWS, 128), F32),
            pltpu.SemaphoreType.DMA((2,)),
        ],
        compiler_params=limit(32),
        name="direct",
    )(near_tab, near_rows, targets, received, leaf_list, places, centres, cell_part)


def solution(mesh):
    sharded = P(("dom", "sub"))
    return jax.shard_map(
        functools.partial(on_device, mesh.shape["dom"], mesh.shape["sub"]),
        mesh=mesh,
        in_specs=(
            P(None, ("dom", "sub")),
            sharded,
            sharded,
            P(None, ("dom", "sub")),
            P(None, ("dom", "sub")),
            P(("dom", "sub"), None),
            P(("dom", "sub"), None),
            P("dom", "sub", None, None),
            P("dom", "sub", None),
        ),
        out_specs=P(None, ("dom", "sub")),
        check_vma=False,
    )
```

```python
import functools

import jax
import jax.numpy as jnp
from jax import lax
from jax.experimental import pallas as pl
from jax.experimental.pallas import tpu as pltpu
from jax.sharding import PartitionSpec as P

LEAF = 64
LEAF_DEV = 128
NCELL = 128
NLEAF = 16
RANGE = 4
CAP = 8
PAIRS = LEAF_DEV // 2
OUT_UNITS = CAP // 2
OWN_ROWS = 4 * PAIRS + 16
OUT_ROWS = 4 * OUT_UNITS
CELL_AT = 4 * PAIRS
CELL_COMPS = 10
CELL_PAD = 12
OFFSETS = list(range(-RANGE, 0)) + list(range(1, RANGE + 1))

softening_sq = 0.0025
GRID_ROUND = 49152.0
F32 = jnp.float32
BF16 = jnp.bfloat16

H_ROWS = 32
Q_ROWS = 64
V_ROWS = 16
U_ROWS = 48
Q_AT = H_ROWS
V_AT = Q_AT + Q_ROWS
U_AT = V_AT + V_ROWS
CELL_ROWS = U_AT + U_ROWS
SOURCE_ROWS = H_ROWS + V_ROWS


def rounded(value):
    return value.astype(BF16).astype(F32)


def three_parts(value):
    first = rounded(value)
    rest = value - first
    second = rounded(rest)
    return first, second, rest - second


def two_parts(value):
    first = value.astype(BF16)
    return first, (value - first.astype(F32)).astype(BF16)


def grid_parts(value):
    high = (value + GRID_ROUND) - GRID_ROUND
    low = value - high
    first = rounded(low)
    return high, low, first, low - first


def norm_parts(parts, extra=None):
    big = sum(high * high for high, _, _, _ in parts)
    small = sum(low * (2.0 * high + low) for high, low, _, _ in parts)
    if extra is not None:
        small = small + extra
    return three_parts(big), three_parts(small)


def pack_kernel(n_dom, *refs):
    ins, out_ref, sent_ref, scratch, sems = refs[:7], refs[7], refs[8], refs[9:16], refs[16]
    copies = [pltpu.make_async_copy(src, dst, sems.at[at]) for at, (src, dst) in enumerate(zip(ins, scratch))]
    for copy in copies:
        copy.start()
    pos_ref, mass_ref, cmass_ref, center_ref, quad_ref, list_ref, count_ref = scratch
    me = lax.axis_index("dom")
    left = lax.broadcasted_iota(jnp.int32, (4, 128), 1) < LEAF
    sent_ref[...] = jnp.zeros((n_dom, OUT_ROWS, 128), F32)
    out_ref[CELL_AT + 10 : OWN_ROWS, :] = jnp.zeros((OWN_ROWS - CELL_AT - 10, 128), F32)
    for copy in copies:
        copy.wait()
    for pair in range(PAIRS):
        lanes = pl.ds(128 * pair, 128)
        out_ref[4 * pair : 4 * pair + 3, :] = pos_ref[:, lanes]
        out_ref[4 * pair + 3 : 4 * pair + 4, :] = mass_ref[:, lanes]
    out_ref[CELL_AT : CELL_AT + 1, :] = cmass_ref[...]
    out_ref[CELL_AT + 1 : CELL_AT + 4, :] = center_ref[...]
    out_ref[CELL_AT + 4 : CELL_AT + 10, :] = quad_ref[...]

    def half(slot, j, right):
        block = list_ref[slot, j]
        value = out_ref[pl.ds(pl.multiple_of(4 * (block // 2), 4), 4), :]
        value = jnp.where(j < count_ref[0, slot], value, 0.0)
        return jnp.where((block & 1) == right, value, pltpu.roll(value, LEAF, 1))

    for slot in range(2 * RANGE):
        target = me + OFFSETS[slot]

        @pl.when((target >= 0) & (target < n_dom))
        def _():
            for unit in range(OUT_UNITS):
                sent_ref[target, 4 * unit : 4 * unit + 4, :] = jnp.where(left, half(slot, 2 * unit, 0), half(slot, 2 * unit + 1, 1))


def outgoing_kernel(n_dom, n_sub, sent_ref, all_ref, out_ref, sem):
    copy = pltpu.make_async_copy(sent_ref, out_ref.at[:, 0:OUT_ROWS, :], sem)
    copy.start()

    def one_target(target, carry):
        for seg in range(n_sub):
            at = OUT_ROWS + CELL_PAD * seg
            first = seg * OWN_ROWS + CELL_AT
            out_ref[target, at : at + CELL_PAD, :] = all_ref[first : first + CELL_PAD, :]
        return carry

    lax.fori_loop(0, n_dom, one_target, 0)
    copy.wait()


def target_h_rows(parts, one, zero):
    big, small = norm_parts(parts, softening_sq)
    minus_high = [-2.0 * part[0] for part in parts]
    minus_one = [-2.0 * part[2] for part in parts]
    minus_two = [-2.0 * part[3] for part in parts]
    rows = minus_high + [one] * 3 + list(big) + minus_high + minus_one + minus_high
    return rows + minus_two + minus_one + [one] * 3 + list(small) + [zero] * 2


def target_features(all_ref, tg_ref, ce_ref, feat_ref, ah_ref, aq_ref):
    me = lax.axis_index("sub")
    left = lax.broadcasted_iota(jnp.int32, (8, 128), 1) < LEAF
    one = jnp.ones((8, 128), F32)
    zero = jnp.zeros((8, 128), F32)
    raw_ref = tg_ref

    raw_ref[...] = all_ref[pl.ds(pl.multiple_of(me * OWN_ROWS, 8), 4 * PAIRS), :]

    def one_octet(octet, carry):
        parts, centred = [], []
        for comp in range(3):
            rows = pl.ds(octet * 32 + comp, 8, stride=4)
            value = raw_ref[rows, :]
            first = jnp.broadcast_to(value[:, 0:1], (8, 128))
            second = jnp.broadcast_to(value[:, LEAF : LEAF + 1], (8, 128))
            ce_ref[comp, pl.ds(octet * 16, 8, stride=2), :] = first
            ce_ref[comp, pl.ds(octet * 16 + 1, 8, stride=2), :] = second
            value = value - jnp.where(left, first, second)
            raw_ref[rows, :] = value
            centred.append(value)
            parts.append(grid_parts(value))
        rows = target_h_rows(parts, one, zero)
        x, y, z = centred
        split = [three_parts(v) for v in (x, y, z, x * x, y * y, z * z, x * y, x * z, y * z)]
        for which in (0, 0, 1, 0, 1, 2):
            rows += [part[which] for part in split]
        rows += [one] * 3 + [zero] * 7
        for at, value in enumerate(rows):
            feat_ref[8 * at : 8 * at + 8, :] = value
        for sub in range(8):
            pair = octet * 8 + sub
            ah_ref[pair] = feat_ref[pl.ds(sub, H_ROWS, stride=8), :].T.astype(BF16)
            aq_ref[pair] = feat_ref[pl.ds(8 * H_ROWS + sub, Q_ROWS, stride=8), :].T.astype(BF16)
        return carry

    lax.fori_loop(0, PAIRS // 8, one_octet, 0)


def source_h_rows(parts):
    (p1, p2, p3), (s1, s2, s3) = norm_parts(parts)
    high = [part[0] for part in parts]
    one = [part[2] for part in parts]
    two = [part[3] for part in parts]
    rows = dict(enumerate(high + [p1, p2, p3]))
    rows.update(enumerate(one + high + two + high + one + [s1, s2, s3], 9))
    return rows


def put_rows(ref, rows):
    for at, value in rows.items():
        ref[8 * at : 8 * at + 8, :] = value


def fill_constant_rows(ref, count):
    one = jnp.ones((8, 128), F32)
    zero = jnp.zeros((8, 128), F32)
    for at in range(count):
        ones = at in (6, 7, 8, 27, 28, 29) or at == V_AT + 3
        ref[8 * at : 8 * at + 8, :] = one if ones else zero


def cell_features(n_dom, n_sub, octet, cl_ref, recv_ref, ce_ref, cf_ref, cm_ref):
    ids = cl_ref[pl.ds(pl.multiple_of(8 * octet, 8), 8), :]
    lane = ids & 127
    owner = ids >> 7

    def one_domain(dom, found):
        for seg in range(n_sub):
            here = owner == dom * n_sub + seg
            new = []
            for comp in range(CELL_COMPS):
                at = OUT_ROWS + CELL_PAD * seg + comp
                row = jnp.broadcast_to(recv_ref[dom, at : at + 1, :], (8, 128))
                value = jnp.take_along_axis(row, lane, axis=1, mode="promise_in_bounds")
                new.append(jnp.where(here, value, found[comp]))
            found = tuple(new)
        return found

    found = tuple(jnp.zeros((8, 128), F32) for _ in range(CELL_COMPS))
    if n_dom <= 8:
        for dom in range(n_dom):
            found = one_domain(dom, found)
    else:
        found = lax.fori_loop(0, n_dom, one_domain, found)
    mass, cx, cy, cz, xx, yy, zz, xy, xz, yz = found
    cm_ref[...] = mass
    rows8 = pl.ds(pl.multiple_of(8 * octet, 8), 8)
    cx, cy, cz = [value - ce_ref[comp, rows8, :] for comp, value in enumerate((cx, cy, cz))]
    put_rows(cf_ref, source_h_rows([grid_parts(value) for value in (cx, cy, cz)]))
    qx = xx * cx + xy * cy + xz * cz
    qy = xy * cx + yy * cy + yz * cz
    qz = xz * cx + yz * cy + zz * cz
    const = three_parts(2.5 * (qx * cx + qy * cy + qz * cz))
    linear = [-5.0 * qx, -5.0 * qy, -5.0 * qz]
    square = [2.5 * xx, 2.5 * yy, 2.5 * zz, 5.0 * xy, 5.0 * xz, 5.0 * yz]
    split = [three_parts(value) for value in linear + square]
    rows = []
    for which in (0, 1, 0, 2, 1, 0):
        rows += [part[which] for part in split]
    rows += list(const)
    put_rows(cf_ref, dict(enumerate(rows, Q_AT)))
    for comp, value in enumerate((cx, cy, cz)):
        for which, part in enumerate(three_parts(value)):
            cf_ref[8 * (V_AT + 4 * which + comp) : 8 * (V_AT + 4 * which + comp) + 8, :] = part
    columns = {name: three_parts(value) for name, value in dict(xx=xx, yy=yy, zz=zz, xy=xy, xz=xz, yz=yz, cx=qx, cy=qy, cz=qz).items()}
    order = (("xx", "xy", "xz"), ("xy", "yy", "yz"), ("xz", "yz", "zz"), ("cx", "cy", "cz"))
    for which in range(3):
        for column, names in enumerate(order):
            for row, name in enumerate(names):
                at = U_AT + 16 * which + 4 * column + row
                cf_ref[8 * at : 8 * at + 8, :] = columns[name][which]


def source_moments(group, ll_ref, tab_ref, ce_ref, raw_ref, sf_ref):
    left = lax.broadcasted_iota(jnp.int32, (4, 128), 1) < LEAF
    for pair in range(NLEAF // 2):
        first = tab_ref[ll_ref[group, 2 * pair]]
        second = tab_ref[ll_ref[group, 2 * pair + 1]]
        raw_ref[4 * pair : 4 * pair + 4, :] = jnp.where(left, first, second)
    value = [raw_ref[pl.ds(comp, 8, stride=4), :] for comp in range(4)]
    mass = value[3]
    centred = [value[comp] - ce_ref[comp, pl.ds(group, 1), :] for comp in range(3)]
    for comp, v in enumerate([mass * v for v in centred] + [mass]):
        for which, part in enumerate(three_parts(v)):
            at = 4 * which + comp
            sf_ref[8 * at : 8 * at + 8, :] = part


def transposed_dot(rows, weights):
    return lax.dot_general(rows, weights, (((1,), (1,)), ((), ())), preferred_element_type=F32)


def stacked(value):
    return jnp.concatenate(two_parts(value), axis=0)


def cell_group(sub, target_h, target_q, cf_ref, cm_ref):
    def cell_rows(at, count):
        return cf_ref[pl.ds(8 * at + sub, count, stride=8), :].astype(BF16)

    dist_sq = jnp.dot(target_h, cell_rows(0, H_ROWS), preferred_element_type=F32)
    quad_form = jnp.dot(target_q, cell_rows(Q_AT, Q_ROWS), preferred_element_type=F32)
    inv = lax.rsqrt(dist_sq)
    inv_two = inv * inv
    inv_three = inv * inv_two
    pull = inv_three * (cm_ref[pl.ds(sub, 1), :] + quad_form * (inv_two * inv_two))
    moments = jnp.concatenate(
        [
            jnp.concatenate([cell_rows(V_AT, V_ROWS), jnp.zeros((V_ROWS, 128), BF16)], axis=1),
            jnp.concatenate([jnp.zeros((U_ROWS, 128), BF16), cell_rows(U_AT, U_ROWS)], axis=1),
        ],
        axis=0,
    )
    both = jnp.concatenate([stacked(pull), stacked(inv_three * inv_two)], axis=1)
    sums = transposed_dot(both, moments)
    return sums[0:LEAF] + sums[LEAF:]


def pair_lanes(pair):
    return pl.ds(pl.multiple_of(128 * pair, 128), 128)


def pair_place(tg_ref, pair):
    return tg_ref[pl.ds(pl.multiple_of(4 * pair, 4), 4), :]


def point_sums(sums, place):
    sums = sums[0:8] + sums[8:16]
    sums = sums + pltpu.roll(sums, 4, 0)
    return sums[0:3] - place[0:3] * sums[3:4]


def cell_kernel(
    n_dom, n_sub, tab_in, rows_in, recv_ref, cl_ref, tg_ref, ce_ref, ah_ref, aq_ref,
    tab_out, rows_out, out_ref, far_tab, far_rows, four_ref, even_ref, odd_ref, cm_ref, sems,
):
    del tab_in, rows_in
    far_tables(n_dom, recv_ref, far_tab, far_rows, four_ref)
    far = pl.ds(n_sub * LEAF_DEV, 2 * RANGE * CAP)
    copies = [
        pltpu.make_async_copy(far_tab, tab_out.at[far], sems.at[0]),
        pltpu.make_async_copy(far_rows, rows_out.at[far], sems.at[1]),
    ]
    for copy in copies:
        copy.start()
    fill_constant_rows(even_ref, CELL_ROWS)
    fill_constant_rows(odd_ref, CELL_ROWS)
    upper = lax.broadcasted_iota(jnp.int32, (8, 128), 0) < 4

    def build(octet, slot, slot_ref):
        cell_features(n_dom, n_sub, octet, cl_ref, recv_ref, ce_ref, slot_ref, cm_ref.at[slot])

    def pull(octet, slot, slot_ref):
        for inner in range(4):
            pair = octet * 4 + inner
            sums = []
            for half in range(2):
                rows = pl.ds(LEAF * half, LEAF)
                sums.append(cell_group(2 * inner + half, ah_ref[pair, rows, :], aq_ref[pair, rows, :], slot_ref, cm_ref.at[slot]))
            sums = jnp.concatenate(sums, axis=0).T
            place = pair_place(tg_ref, pair)
            x, y, z = [place[comp : comp + 1, :] for comp in range(3)]
            quads = sums[16:32] + sums[32:48] + sums[48:64]
            turned = quads[0:8] * jnp.where(upper, x, y) + quads[8:16] * jnp.where(upper, z, -1.0)
            turned = turned + pltpu.roll(turned, 4, 0)
            out_ref[:, pair_lanes(pair)] = point_sums(sums[0:16], place) + turned[0:3]

    octets = LEAF_DEV // 8
    build(0, 0, even_ref)

    def two_octets(step, carry):
        octet = 2 * step
        build(octet + 1, 1, odd_ref)
        pull(octet, 0, even_ref)
        build(jnp.minimum(octet + 2, octets - 1), 0, even_ref)
        pull(octet + 1, 1, odd_ref)
        return carry

    lax.fori_loop(0, octets // 2, two_octets, 0)
    for copy in copies:
        copy.wait()


def put_block_pair(tab_ref, block, value):
    left = lax.broadcasted_iota(jnp.int32, (4, 128), 1) < LEAF
    turned = pltpu.roll(value, LEAF, 1)
    tab_ref[block] = jnp.where(left, value, turned)
    tab_ref[block + 1] = jnp.where(left, turned, value)


def put_eight_pairs(rows_ref, block, coords, feat_ref):
    copies = lax.broadcasted_iota(jnp.int32, (H_ROWS, 128), 1) % H_ROWS
    copies = jnp.where(copies == lax.broadcasted_iota(jnp.int32, (H_ROWS, 128), 0), 1.0, 0.0).astype(BF16)
    put_rows(feat_ref, source_h_rows([grid_parts(value) for value in coords]))
    for pair in range(8):
        spread = feat_ref[pl.ds(pair, H_ROWS, stride=8), :].T.astype(BF16)
        spread = jnp.dot(spread, copies, preferred_element_type=F32).astype(BF16)
        rows_ref[block + 2 * pair] = spread[0:LEAF]
        rows_ref[block + 2 * pair + 1] = spread[LEAF:]


def prepare_kernel(n_sub, all_ref, tab_ref, rows_ref, at_ref, tg_ref, ce_ref, ah_ref, aq_ref, feat_ref, four_ref):
    target_features(all_ref, tg_ref, ce_ref, feat_ref, ah_ref, aq_ref)
    target_rows(all_ref, four_ref.at[0], at_ref)
    for at in range(4):
        fill_constant_rows(four_ref.at[at], H_ROWS)

    def near(step, carry):
        seg, part = step // (PAIRS // 32), step % (PAIRS // 32)
        for at in range(4):
            octet = 4 * part + at
            block = seg * LEAF_DEV + 16 * octet
            first = pl.multiple_of(seg * OWN_ROWS + 32 * octet, 8)
            for pair in range(8):
                put_block_pair(tab_ref, block + 2 * pair, all_ref[pl.ds(pl.multiple_of(first + 4 * pair, 4), 4), :])
            coords = [all_ref[pl.ds(first + comp, 8, stride=4), :] for comp in range(3)]
            put_eight_pairs(rows_ref, block, coords, four_ref.at[at])
        return carry

    lax.fori_loop(0, n_sub * PAIRS // 32, near, 0)


def far_tables(n_dom, recv_ref, tab_ref, rows_ref, four_ref):
    for at in range(4):
        fill_constant_rows(four_ref.at[at], H_ROWS)
    me = lax.axis_index("dom")
    for two in range(RANGE):
        halves = []
        for slot in (2 * two, 2 * two + 1):
            source = me - OFFSETS[slot]
            inside = (source >= 0) & (source < n_dom)
            source = jnp.clip(source, 0, n_dom - 1)
            for unit in range(OUT_UNITS):
                value = jnp.where(inside, recv_ref[source, 4 * unit : 4 * unit + 4, :], 0.0)
                put_block_pair(tab_ref, slot * CAP + 2 * unit, value)
            halves.append([jnp.where(inside, recv_ref[source, pl.ds(comp, OUT_UNITS, stride=4), :], 0.0) for comp in range(3)])
        coords = [jnp.concatenate([one, other], axis=0) for one, other in zip(*halves)]
        put_eight_pairs(rows_ref, 2 * two * CAP, coords, four_ref.at[two])


def target_rows(all_ref, feat_ref, at_ref):
    first = lax.axis_index("sub") * OWN_ROWS
    one = jnp.ones((8, 128), F32)
    zero = jnp.zeros((8, 128), F32)

    def one_octet(octet, carry):
        parts = [grid_parts(all_ref[pl.ds(first + octet * 32 + comp, 8, stride=4), :]) for comp in range(3)]
        for at, value in enumerate(target_h_rows(parts, one, zero)):
            feat_ref[8 * at : 8 * at + 8, :] = value
        for pair in range(8):
            at_ref[octet * 8 + pair] = feat_ref[pl.ds(pair, H_ROWS, stride=8), :].astype(BF16)
        return carry

    lax.fori_loop(0, PAIRS // 8, one_octet, 0)


def direct_kernel(tab_ref, rows_ref, at_ref, ll_ref, tg_ref, ce_ref, cell_ref, out_ref, raw_ref, even_ref, odd_ref):
    nothing = jnp.zeros((8, 128), F32)
    for group in range(4):
        for at in range(12, V_ROWS):
            even_ref[group, 8 * at : 8 * at + 8, :] = nothing
            odd_ref[group, 8 * at : 8 * at + 8, :] = nothing
    left = lax.broadcasted_iota(jnp.int32, (V_ROWS, 128), 1) < LEAF
    left_target = lax.broadcasted_iota(jnp.int32, (H_ROWS, 128), 1) < LEAF
    owner = (lax.broadcasted_iota(jnp.int32, (LEAF, 128), 1) // H_ROWS).astype(BF16)
    lower_half, first_own, third_own = owner < 2.0, owner == 0.0, owner == 2.0

    def features(quad, raw_at, slot_ref):
        for group in range(4):
            source_moments(4 * quad + group, ll_ref, tab_ref, ce_ref, raw_ref.at[raw_at + group], slot_ref.at[group])

    def pull(quad, slot_ref):
        nothing = jnp.zeros((H_ROWS, 128), BF16)
        first, second = at_ref[2 * quad], at_ref[2 * quad + 1]
        targets = jnp.concatenate(
            [
                jnp.concatenate([jnp.where(left_target, first, nothing), nothing], axis=1),
                jnp.concatenate([jnp.where(left_target, nothing, first), nothing], axis=1),
                jnp.concatenate([nothing, jnp.where(left_target, second, nothing)], axis=1),
                jnp.concatenate([nothing, jnp.where(left_target, nothing, second)], axis=1),
            ],
            axis=0,
        )
        totals = [jnp.zeros((2 * V_ROWS, 128), F32) for _ in range(2)]

        def distances(chunk):
            sources = []
            for j in (2 * chunk, 2 * chunk + 1):
                rows = [rows_ref[ll_ref[4 * quad + group, j]] for group in range(4)]
                low = jnp.where(first_own, rows[0], rows[1])
                high = jnp.where(third_own, rows[2], rows[3])
                sources.append(jnp.where(lower_half, low, high))
            return jnp.dot(jnp.concatenate(sources, axis=0), targets, preferred_element_type=F32)

        def add_chunk(chunk, weights):
            moments = [slot_ref[group, pl.ds(chunk, V_ROWS, stride=8), :].astype(BF16) for group in range(4)]
            for side in range(2):
                rows = jnp.concatenate(moments[2 * side : 2 * side + 2], axis=0)
                rows = jnp.concatenate([rows, rows], axis=1)
                totals[side] += jnp.dot(rows, weights[:, 128 * side : 128 * side + 128], preferred_element_type=F32)

        dist_sq, before = distances(0), None
        for chunk in range(8):
            ahead = distances(chunk + 1) if chunk < 7 else None
            inv = lax.rsqrt(dist_sq)
            weights = stacked(inv * inv * inv)
            if before is not None:
                add_chunk(chunk - 1, before)
            dist_sq, before = ahead, weights
        add_chunk(7, before)
        for side in range(2):
            pair = 2 * quad + side
            sums = jnp.where(left, totals[side][0:V_ROWS], totals[side][V_ROWS:])
            lanes = pair_lanes(pair)
            out_ref[:, lanes] = cell_ref[:, lanes] + point_sums(sums, pair_place(tg_ref, pair))

    quads = LEAF_DEV // 4
    features(0, 0, even_ref)

    def two_quads(step, carry):
        quad = 2 * step
        features(quad + 1, 4, odd_ref)
        pull(quad, even_ref)
        features(jnp.minimum(quad + 2, quads - 1), 0, even_ref)
        pull(quad + 1, odd_ref)
        return carry

    lax.fori_loop(0, quads // 2, two_quads, 0)


def on_device(n_dom, n_sub, positions, masses, cell_mass, cell_center, cell_quad, cell_list, leaf_list, send_list, send_count):
    vmem = pl.BlockSpec(memory_space=pltpu.VMEM)
    smem = pl.BlockSpec(memory_space=pltpu.SMEM)
    anywhere = pl.BlockSpec(memory_space=pl.ANY)

    def limit(mib):
        return pltpu.CompilerParams(vmem_limit_bytes=mib * 1024 * 1024)

    ins = (
        positions,
        masses.reshape(1, -1),
        cell_mass.reshape(1, -1),
        cell_center,
        cell_quad,
        send_list.reshape(2 * RANGE, CAP),
        send_count.reshape(1, 2 * RANGE),
    )
    packed, sent = pl.pallas_call(
        functools.partial(pack_kernel, n_dom),
        out_shape=(
            jax.ShapeDtypeStruct((OWN_ROWS, 128), F32),
            jax.ShapeDtypeStruct((n_dom, OUT_ROWS, 128), F32),
        ),
        in_specs=[pl.BlockSpec(memory_space=pltpu.HBM)] * 7,
        out_specs=[vmem] * 2,
        scratch_shapes=[pltpu.VMEM(array.shape, F32) for array in ins[:5]]
        + [pltpu.SMEM(array.shape, jnp.int32) for array in ins[5:]]
        + [pltpu.SemaphoreType.DMA((7,))],
        compiler_params=limit(63),
        name="pack_own",
    )(*ins)
    nearby = lax.all_gather(packed, "sub", axis=0, tiled=True)
    outgoing = pl.pallas_call(
        functools.partial(outgoing_kernel, n_dom, n_sub),
        out_shape=jax.ShapeDtypeStruct((n_dom, OUT_ROWS + CELL_PAD * n_sub, 128), F32),
        in_specs=[anywhere, vmem],
        out_specs=vmem,
        scratch_shapes=[pltpu.SemaphoreType.DMA(())],
        compiler_params=limit(16),
        name="pack_outgoing",
    )(sent, nearby)
    received = lax.all_to_all(outgoing, "dom", split_axis=0, concat_axis=0, tiled=True)
    n_blocks = n_sub * LEAF_DEV + 2 * RANGE * CAP
    near_tab, near_rows, targets, places, centres, cell_targets, quad_targets = pl.pallas_call(
        functools.partial(prepare_kernel, n_sub),
        out_shape=(
            jax.ShapeDtypeStruct((n_blocks, 4, 128), F32),
            jax.ShapeDtypeStruct((n_blocks, LEAF, 128), BF16),
            jax.ShapeDtypeStruct((PAIRS, H_ROWS, 128), BF16),
            jax.ShapeDtypeStruct((4 * PAIRS, 128), F32),
            jax.ShapeDtypeStruct((3, LEAF_DEV, 128), F32),
            jax.ShapeDtypeStruct((PAIRS, 128, H_ROWS), BF16),
            jax.ShapeDtypeStruct((PAIRS, 128, Q_ROWS), BF16),
        ),
        in_specs=[vmem],
        out_specs=[vmem] * 7,
        scratch_shapes=[
            pltpu.VMEM((8 * (H_ROWS + Q_ROWS), 128), F32),
            pltpu.VMEM((4, 8 * H_ROWS, 128), F32),
        ],
        compiler_params=limit(24),
        cost_estimate=pl.CostEstimate(flops=50_000_000, bytes_accessed=16_000_000, transcendentals=0),
        name="prepare",
    )(nearby)
    table, rows, cell_part = pl.pallas_call(
        functools.partial(cell_kernel, n_dom, n_sub),
        out_shape=(
            jax.ShapeDtypeStruct(near_tab.shape, F32),
            jax.ShapeDtypeStruct(near_rows.shape, BF16),
            jax.ShapeDtypeStruct((3, LEAF_DEV * LEAF), F32),
        ),
        in_specs=[anywhere] * 2 + [vmem] * 6,
        out_specs=[anywhere, anywhere, vmem],
        input_output_aliases={0: 0, 1: 1},
        scratch_shapes=[
            pltpu.VMEM((2 * RANGE * CAP, 4, 128), F32),
            pltpu.VMEM((2 * RANGE * CAP, LEAF, 128), BF16),
            pltpu.VMEM((4, 8 * H_ROWS, 128), F32),
            pltpu.VMEM((8 * CELL_ROWS, 128), F32),
            pltpu.VMEM((8 * CELL_ROWS, 128), F32),
            pltpu.VMEM((2, 8, 128), F32),
            pltpu.SemaphoreType.DMA((2,)),
        ],
        compiler_params=limit(16),
        name="cells",
    )(near_tab, near_rows, received, cell_list, places, centres, cell_targets, quad_targets)
    return pl.pallas_call(
        direct_kernel,
        out_shape=jax.ShapeDtypeStruct((3, LEAF_DEV * LEAF), F32),
        in_specs=[vmem] * 3 + [smem] + [vmem] * 3,
        out_specs=vmem,
        scratch_shapes=[
            pltpu.VMEM((8, 32, 128), F32),
            pltpu.VMEM((4, 8 * V_ROWS, 128), F32),
            pltpu.VMEM((4, 8 * V_ROWS, 128), F32),
        ],
        compiler_params=limit(16),
        name="direct",
    )(table, rows, targets, leaf_list, places, centres, cell_part)


def solution(mesh):
    sharded = P(("dom", "sub"))
    return jax.shard_map(
        functools.partial(on_device, mesh.shape["dom"], mesh.shape["sub"]),
        mesh=mesh,
        in_specs=(
            P(None, ("dom", "sub")),
            sharded,
            sharded,
            P(None, ("dom", "sub")),
            P(None, ("dom", "sub")),
            P(("dom", "sub"), None),
            P(("dom", "sub"), None),
            P("dom", "sub", None, None),
            P("dom", "sub", None),
        ),
        out_specs=P(None, ("dom", "sub")),
        check_vma=False,
    )
```

```python
import functools

import jax
import jax.numpy as jnp
from jax import lax
from jax.experimental import pallas as pl
from jax.experimental.pallas import tpu as pltpu
from jax.sharding import PartitionSpec as P

LEAF = 64
LEAF_DEV = 128
NCELL = 128
NLEAF = 16
RANGE = 4
CAP = 8
PAIRS = LEAF_DEV // 2
OUT_UNITS = CAP // 2
OWN_ROWS = 4 * PAIRS + 16
OUT_ROWS = 4 * OUT_UNITS
CELL_AT = 4 * PAIRS
CELL_COMPS = 10
CELL_PAD = 12
OFFSETS = list(range(-RANGE, 0)) + list(range(1, RANGE + 1))

softening_sq = 0.0025
GRID_ROUND = 49152.0
F32 = jnp.float32
BF16 = jnp.bfloat16

H_ROWS = 32
Q_ROWS = 64
V_ROWS = 16
U_ROWS = 48
Q_AT = H_ROWS
V_AT = Q_AT + Q_ROWS
U_AT = V_AT + V_ROWS
CELL_ROWS = U_AT + U_ROWS
SOURCE_ROWS = H_ROWS + V_ROWS


def rounded(value):
    return value.astype(BF16).astype(F32)


def three_parts(value):
    first = rounded(value)
    rest = value - first
    second = rounded(rest)
    return first, second, rest - second


def two_parts(value):
    first = value.astype(BF16)
    return first, (value - first.astype(F32)).astype(BF16)


def grid_parts(value):
    high = (value + GRID_ROUND) - GRID_ROUND
    low = value - high
    first = rounded(low)
    return high, low, first, low - first


def norm_parts(parts, extra=None):
    big = sum(high * high for high, _, _, _ in parts)
    small = sum(low * (2.0 * high + low) for high, low, _, _ in parts)
    if extra is not None:
        small = small + extra
    return three_parts(big), three_parts(small)


def pack_kernel(n_dom, *refs):
    ins, out_ref, sent_ref, scratch, sems = refs[:7], refs[7], refs[8], refs[9:16], refs[16]
    copies = [pltpu.make_async_copy(src, dst, sems.at[at]) for at, (src, dst) in enumerate(zip(ins, scratch))]
    for copy in copies:
        copy.start()
    pos_ref, mass_ref, cmass_ref, center_ref, quad_ref, list_ref, count_ref = scratch
    me = lax.axis_index("dom")
    left = lax.broadcasted_iota(jnp.int32, (4, 128), 1) < LEAF
    sent_ref[...] = jnp.zeros((n_dom, OUT_ROWS, 128), F32)
    out_ref[CELL_AT + 10 : OWN_ROWS, :] = jnp.zeros((OWN_ROWS - CELL_AT - 10, 128), F32)
    for copy in copies:
        copy.wait()
    for pair in range(PAIRS):
        lanes = pl.ds(128 * pair, 128)
        out_ref[4 * pair : 4 * pair + 3, :] = pos_ref[:, lanes]
        out_ref[4 * pair + 3 : 4 * pair + 4, :] = mass_ref[:, lanes]
    out_ref[CELL_AT : CELL_AT + 1, :] = cmass_ref[...]
    out_ref[CELL_AT + 1 : CELL_AT + 4, :] = center_ref[...]
    out_ref[CELL_AT + 4 : CELL_AT + 10, :] = quad_ref[...]

    def half(slot, j, right):
        block = list_ref[slot, j]
        value = out_ref[pl.ds(pl.multiple_of(4 * (block // 2), 4), 4), :]
        value = jnp.where(j < count_ref[0, slot], value, 0.0)
        return jnp.where((block & 1) == right, value, pltpu.roll(value, LEAF, 1))

    for slot in range(2 * RANGE):
        target = me + OFFSETS[slot]

        @pl.when((target >= 0) & (target < n_dom))
        def _():
            for unit in range(OUT_UNITS):
                sent_ref[target, 4 * unit : 4 * unit + 4, :] = jnp.where(left, half(slot, 2 * unit, 0), half(slot, 2 * unit + 1, 1))


def outgoing_kernel(n_dom, n_sub, sent_ref, all_ref, out_ref, sem):
    copy = pltpu.make_async_copy(sent_ref, out_ref.at[:, 0:OUT_ROWS, :], sem)
    copy.start()

    def one_target(target, carry):
        for seg in range(n_sub):
            at = OUT_ROWS + CELL_PAD * seg
            first = seg * OWN_ROWS + CELL_AT
            out_ref[target, at : at + CELL_PAD, :] = all_ref[first : first + CELL_PAD, :]
        return carry

    lax.fori_loop(0, n_dom, one_target, 0)
    copy.wait()


def target_h_rows(parts, one, zero):
    big, small = norm_parts(parts, softening_sq)
    minus_high = [-2.0 * part[0] for part in parts]
    minus_one = [-2.0 * part[2] for part in parts]
    minus_two = [-2.0 * part[3] for part in parts]
    rows = minus_high + [one] * 3 + list(big) + minus_high + minus_one + minus_high
    return rows + minus_two + minus_one + [one] * 3 + list(small) + [zero] * 2


def target_features(all_ref, tg_ref, ce_ref, feat_ref, ah_ref):
    me = lax.axis_index("sub")
    left = lax.broadcasted_iota(jnp.int32, (8, 128), 1) < LEAF
    one = jnp.ones((8, 128), F32)
    zero = jnp.zeros((8, 128), F32)
    raw_ref = tg_ref

    raw_ref[...] = all_ref[pl.ds(pl.multiple_of(me * OWN_ROWS, 8), 4 * PAIRS), :]

    def one_octet(octet, carry):
        parts, centred = [], []
        for comp in range(3):
            rows = pl.ds(octet * 32 + comp, 8, stride=4)
            value = raw_ref[rows, :]
            first = jnp.broadcast_to(value[:, 0:1], (8, 128))
            second = jnp.broadcast_to(value[:, LEAF : LEAF + 1], (8, 128))
            ce_ref[comp, pl.ds(octet * 16, 8, stride=2), :] = first
            ce_ref[comp, pl.ds(octet * 16 + 1, 8, stride=2), :] = second
            value = value - jnp.where(left, first, second)
            raw_ref[rows, :] = value
            centred.append(value)
            parts.append(grid_parts(value))
        rows = target_h_rows(parts, one, zero)
        x, y, z = centred
        split = [three_parts(v) for v in (x, y, z, x * x, y * y, z * z, x * y, x * z, y * z)]
        for which in (0, 0, 1, 0, 1, 2):
            rows += [part[which] for part in split]
        rows += [one] * 3 + [zero] * 7
        for at, value in enumerate(rows):
            feat_ref[8 * at : 8 * at + 8, :] = value
        for sub in range(8):
            pair = octet * 8 + sub
            ah_ref[pair, :, 0 : H_ROWS + Q_ROWS] = feat_ref[pl.ds(sub, H_ROWS + Q_ROWS, stride=8), :].T.astype(BF16)
        return carry

    lax.fori_loop(0, PAIRS // 8, one_octet, 0)


def source_h_rows(parts):
    (p1, p2, p3), (s1, s2, s3) = norm_parts(parts)
    high = [part[0] for part in parts]
    one = [part[2] for part in parts]
    two = [part[3] for part in parts]
    rows = dict(enumerate(high + [p1, p2, p3]))
    rows.update(enumerate(one + high + two + high + one + [s1, s2, s3], 9))
    return rows


def put_rows(ref, rows):
    for at, value in rows.items():
        ref[8 * at : 8 * at + 8, :] = value


def fill_constant_rows(ref, count):
    one = jnp.ones((8, 128), F32)
    zero = jnp.zeros((8, 128), F32)
    for at in range(count):
        ones = at in (6, 7, 8, 27, 28, 29) or at == V_AT + 3
        ref[8 * at : 8 * at + 8, :] = one if ones else zero


def cell_features(n_dom, n_sub, octet, cl_ref, recv_ref, ce_ref, cf_ref, cm_ref):
    ids = cl_ref[pl.ds(pl.multiple_of(8 * octet, 8), 8), :]
    lane = ids & 127
    owner = ids >> 7

    def one_domain(dom, found):
        for seg in range(n_sub):
            here = owner == dom * n_sub + seg
            new = []
            for comp in range(CELL_COMPS):
                at = OUT_ROWS + CELL_PAD * seg + comp
                row = jnp.broadcast_to(recv_ref[dom, at : at + 1, :], (8, 128))
                value = jnp.take_along_axis(row, lane, axis=1, mode="promise_in_bounds")
                new.append(jnp.where(here, value, found[comp]))
            found = tuple(new)
        return found

    found = tuple(jnp.zeros((8, 128), F32) for _ in range(CELL_COMPS))
    if n_dom <= 8:
        for dom in range(n_dom):
            found = one_domain(dom, found)
    else:
        found = lax.fori_loop(0, n_dom, one_domain, found)
    mass, cx, cy, cz, xx, yy, zz, xy, xz, yz = found
    cm_ref[...] = mass
    rows8 = pl.ds(pl.multiple_of(8 * octet, 8), 8)
    cx, cy, cz = [value - ce_ref[comp, rows8, :] for comp, value in enumerate((cx, cy, cz))]
    put_rows(cf_ref, source_h_rows([grid_parts(value) for value in (cx, cy, cz)]))
    qx = xx * cx + xy * cy + xz * cz
    qy = xy * cx + yy * cy + yz * cz
    qz = xz * cx + yz * cy + zz * cz
    const = three_parts(2.5 * (qx * cx + qy * cy + qz * cz))
    linear = [-5.0 * qx, -5.0 * qy, -5.0 * qz]
    square = [2.5 * xx, 2.5 * yy, 2.5 * zz, 5.0 * xy, 5.0 * xz, 5.0 * yz]
    split = [three_parts(value) for value in linear + square]
    rows = []
    for which in (0, 1, 0, 2, 1, 0):
        rows += [part[which] for part in split]
    rows += list(const)
    put_rows(cf_ref, dict(enumerate(rows, Q_AT)))
    for comp, value in enumerate((cx, cy, cz)):
        for which, part in enumerate(three_parts(value)):
            cf_ref[8 * (V_AT + 4 * which + comp) : 8 * (V_AT + 4 * which + comp) + 8, :] = part
    columns = {name: three_parts(value) for name, value in dict(xx=xx, yy=yy, zz=zz, xy=xy, xz=xz, yz=yz, cx=qx, cy=qy, cz=qz).items()}
    order = (("xx", "xy", "xz"), ("xy", "yy", "yz"), ("xz", "yz", "zz"), ("cx", "cy", "cz"))
    for which in range(3):
        for column, names in enumerate(order):
            for row, name in enumerate(names):
                at = U_AT + 16 * which + 4 * column + row
                cf_ref[8 * at : 8 * at + 8, :] = columns[name][which]


def source_moments(group, ll_ref, tab_ref, ce_ref, raw_ref, sf_ref):
    left = lax.broadcasted_iota(jnp.int32, (4, 128), 1) < LEAF
    for pair in range(NLEAF // 2):
        first = tab_ref[ll_ref[group, 2 * pair]]
        second = tab_ref[ll_ref[group, 2 * pair + 1]]
        raw_ref[4 * pair : 4 * pair + 4, :] = jnp.where(left, first, second)
    value = [raw_ref[pl.ds(comp, 8, stride=4), :] for comp in range(4)]
    mass = value[3]
    centred = [value[comp] - ce_ref[comp, pl.ds(group, 1), :] for comp in range(3)]
    for comp, v in enumerate([mass * v for v in centred] + [mass]):
        for which, part in enumerate(three_parts(v)):
            at = 4 * which + comp
            sf_ref[8 * at : 8 * at + 8, :] = part


def transposed_dot(rows, weights):
    return lax.dot_general(rows, weights, (((1,), (1,)), ((), ())), preferred_element_type=F32)


def stacked(value):
    return jnp.concatenate(two_parts(value), axis=0)


def cell_group(sub, target, cf_ref, cm_ref):
    def cell_rows(at, count):
        return cf_ref[pl.ds(8 * at + sub, count, stride=8), :].astype(BF16)

    forms = jnp.concatenate(
        [
            jnp.concatenate([cell_rows(0, H_ROWS), jnp.zeros((H_ROWS, 128), BF16)], axis=1),
            jnp.concatenate([jnp.zeros((Q_ROWS, 128), BF16), cell_rows(Q_AT, Q_ROWS)], axis=1),
        ],
        axis=0,
    )
    forms = jnp.dot(target[:, 0 : H_ROWS + Q_ROWS], forms, preferred_element_type=F32)
    dist_sq, quad_form = forms[:, 0:128], forms[:, 128:256]
    inv = lax.rsqrt(dist_sq)
    inv_two = inv * inv
    inv_three = inv * inv_two
    pull = inv_three * (cm_ref[pl.ds(sub, 1), :] + quad_form * (inv_two * inv_two))
    moments = jnp.concatenate(
        [
            jnp.concatenate([cell_rows(V_AT, V_ROWS), jnp.zeros((V_ROWS, 128), BF16)], axis=1),
            jnp.concatenate([jnp.zeros((U_ROWS, 128), BF16), cell_rows(U_AT, U_ROWS)], axis=1),
        ],
        axis=0,
    )
    both = jnp.concatenate([stacked(pull), stacked(inv_three * inv_two)], axis=1)
    sums = transposed_dot(both, moments)
    return sums[0:LEAF] + sums[LEAF:]


def pair_lanes(pair):
    return pl.ds(pl.multiple_of(128 * pair, 128), 128)


def pair_place(tg_ref, pair):
    return tg_ref[pl.ds(pl.multiple_of(4 * pair, 4), 4), :]


def point_sums(sums, place):
    sums = sums[0:8] + sums[8:16]
    sums = sums + pltpu.roll(sums, 4, 0)
    return sums[0:3] - place[0:3] * sums[3:4]


def cell_pull(octet, tg_ref, ah_ref, cf_ref, cm_ref, out_ref):
    upper = lax.broadcasted_iota(jnp.int32, (8, 128), 0) < 4
    for inner in range(4):
        pair = octet * 4 + inner
        sums = [cell_group(2 * inner + half, ah_ref[pair, pl.ds(LEAF * half, LEAF), :], cf_ref, cm_ref) for half in range(2)]
        sums = jnp.concatenate(sums, axis=0).T
        place = pair_place(tg_ref, pair)
        x, y, z = [place[comp : comp + 1, :] for comp in range(3)]
        quads = sums[16:32] + sums[32:48] + sums[48:64]
        turned = quads[0:8] * jnp.where(upper, x, y) + quads[8:16] * jnp.where(upper, z, -1.0)
        turned = turned + pltpu.roll(turned, 4, 0)
        out_ref[:, pair_lanes(pair)] = point_sums(sums[0:16], place) + turned[0:3]


def put_block_pair(tab_ref, block, value):
    left = lax.broadcasted_iota(jnp.int32, (4, 128), 1) < LEAF
    turned = pltpu.roll(value, LEAF, 1)
    tab_ref[block] = jnp.where(left, value, turned)
    tab_ref[block + 1] = jnp.where(left, turned, value)


def put_eight_pairs(rows_ref, block, coords, feat_ref):
    copies = lax.broadcasted_iota(jnp.int32, (H_ROWS, 128), 1) % H_ROWS
    copies = jnp.where(copies == lax.broadcasted_iota(jnp.int32, (H_ROWS, 128), 0), 1.0, 0.0).astype(BF16)
    put_rows(feat_ref, source_h_rows([grid_parts(value) for value in coords]))
    for pair in range(8):
        spread = feat_ref[pl.ds(pair, H_ROWS, stride=8), :].T.astype(BF16)
        spread = jnp.dot(spread, copies, preferred_element_type=F32).astype(BF16)
        rows_ref[block + 2 * pair] = spread[0:LEAF]
        rows_ref[block + 2 * pair + 1] = spread[LEAF:]


def prepare_kernel(n_sub, all_ref, tab_out, rows_out, at_out, tg_out, ce_out, ah_out, tab_ref, rows_ref, at_ref, tg_ref, ce_ref, ah_ref, feat_ref, four_ref, sems):
    for at in range(4):
        fill_constant_rows(four_ref.at[at], H_ROWS)
    near_blocks = pl.ds(0, n_sub * LEAF_DEV)

    def near(step, carry):
        seg, part = step // (PAIRS // 32), step % (PAIRS // 32)
        for at in range(4):
            octet = 4 * part + at
            block = seg * LEAF_DEV + 16 * octet
            first = pl.multiple_of(seg * OWN_ROWS + 32 * octet, 8)
            for pair in range(8):
                put_block_pair(tab_ref, block + 2 * pair, all_ref[pl.ds(pl.multiple_of(first + 4 * pair, 4), 4), :])
            coords = [all_ref[pl.ds(first + comp, 8, stride=4), :] for comp in range(3)]
            put_eight_pairs(rows_ref, block, coords, four_ref.at[at])
        done = pl.ds(64 * step, 64)
        pltpu.make_async_copy(rows_ref.at[done], rows_out.at[done], sems.at[0]).start()
        return carry

    lax.fori_loop(0, n_sub * PAIRS // 32, near, 0)
    copies = [pltpu.make_async_copy(tab_ref, tab_out.at[near_blocks], sems.at[1])]
    copies[0].start()
    target_features(all_ref, tg_ref, ce_ref, feat_ref, ah_ref)
    target_rows(all_ref, four_ref.at[0], at_ref)
    for src, dst, at in ((at_ref, at_out, 2), (tg_ref, tg_out, 3), (ce_ref, ce_out, 4), (ah_ref, ah_out, 5)):
        copies.append(pltpu.make_async_copy(src, dst, sems.at[at]))
        copies[-1].start()
    pltpu.make_async_copy(rows_ref, rows_out.at[near_blocks], sems.at[0]).wait()
    for copy in copies:
        copy.wait()


def far_tables(n_dom, first_block, recv_ref, tab_ref, rows_ref, four_ref):
    for at in range(4):
        fill_constant_rows(four_ref.at[at], H_ROWS)
    me = lax.axis_index("dom")
    for two in range(RANGE):
        halves = []
        for slot in (2 * two, 2 * two + 1):
            source = me - OFFSETS[slot]
            inside = (source >= 0) & (source < n_dom)
            source = jnp.clip(source, 0, n_dom - 1)
            for unit in range(OUT_UNITS):
                value = jnp.where(inside, recv_ref[source, 4 * unit : 4 * unit + 4, :], 0.0)
                put_block_pair(tab_ref, first_block + slot * CAP + 2 * unit, value)
            halves.append([jnp.where(inside, recv_ref[source, pl.ds(comp, OUT_UNITS, stride=4), :], 0.0) for comp in range(3)])
        coords = [jnp.concatenate([one, other], axis=0) for one, other in zip(*halves)]
        put_eight_pairs(rows_ref, first_block + 2 * two * CAP, coords, four_ref.at[two])


def target_rows(all_ref, feat_ref, at_ref):
    first = lax.axis_index("sub") * OWN_ROWS
    one = jnp.ones((8, 128), F32)
    zero = jnp.zeros((8, 128), F32)

    def one_octet(octet, carry):
        parts = [grid_parts(all_ref[pl.ds(first + octet * 32 + comp, 8, stride=4), :]) for comp in range(3)]
        for at, value in enumerate(target_h_rows(parts, one, zero)):
            feat_ref[8 * at : 8 * at + 8, :] = value
        for pair in range(8):
            at_ref[octet * 8 + pair] = feat_ref[pl.ds(pair, H_ROWS, stride=8), :].astype(BF16)
        return carry

    lax.fori_loop(0, PAIRS // 8, one_octet, 0)


def pull_kernel(n_dom, n_sub, *refs):
    ins, ll_ref, out_ref, scratch, rest = refs[:8], refs[8], refs[9], refs[10:18], refs[18:]
    four_ref, cf_ref, cm_ref, raw_ref, even_ref, odd_ref, sems = rest
    recv_ref, cl_ref, ce_ref, tg_ref, ah_ref, at_ref, tab_ref, rows_ref = scratch
    n_near = n_sub * LEAF_DEV
    copies = []
    for at, (src, dst) in enumerate(zip(ins, scratch)):
        if at >= 6:
            src, dst = src.at[pl.ds(0, n_near)], dst.at[pl.ds(0, n_near)]
        copies.append(pltpu.make_async_copy(src, dst, sems.at[at]))
        copies[-1].start()
    fill_constant_rows(cf_ref, CELL_ROWS)
    copies[0].wait()
    far_tables(n_dom, n_near, recv_ref, tab_ref, rows_ref, four_ref)
    copies[1].wait()
    copies[2].wait()

    def build(octet):
        cell_features(n_dom, n_sub, octet, cl_ref, recv_ref, ce_ref, cf_ref, cm_ref)

    build(0)
    for copy in copies[3:]:
        copy.wait()
    nothing = jnp.zeros((8, 128), F32)
    for group in range(4):
        for at in range(12, V_ROWS):
            even_ref[group, 8 * at : 8 * at + 8, :] = nothing
            odd_ref[group, 8 * at : 8 * at + 8, :] = nothing
    left = lax.broadcasted_iota(jnp.int32, (V_ROWS, 128), 1) < LEAF
    left_target = lax.broadcasted_iota(jnp.int32, (H_ROWS, 128), 1) < LEAF
    owner = (lax.broadcasted_iota(jnp.int32, (LEAF, 128), 1) // H_ROWS).astype(BF16)
    lower_half, first_own, third_own = owner < 2.0, owner == 0.0, owner == 2.0

    def features(quad, raw_at, slot_ref):
        for group in range(4):
            source_moments(4 * quad + group, ll_ref, tab_ref, ce_ref, raw_ref.at[raw_at + group], slot_ref.at[group])

    def pull(quad, slot_ref):
        nothing = jnp.zeros((H_ROWS, 128), BF16)
        first, second = at_ref[2 * quad], at_ref[2 * quad + 1]
        targets = jnp.concatenate(
            [
                jnp.concatenate([jnp.where(left_target, first, nothing), nothing], axis=1),
                jnp.concatenate([jnp.where(left_target, nothing, first), nothing], axis=1),
                jnp.concatenate([nothing, jnp.where(left_target, second, nothing)], axis=1),
                jnp.concatenate([nothing, jnp.where(left_target, nothing, second)], axis=1),
            ],
            axis=0,
        )
        totals = [jnp.zeros((2 * V_ROWS, 128), F32) for _ in range(2)]

        def distances(chunk):
            sources = []
            for j in (2 * chunk, 2 * chunk + 1):
                rows = [rows_ref[ll_ref[4 * quad + group, j]] for group in range(4)]
                low = jnp.where(first_own, rows[0], rows[1])
                high = jnp.where(third_own, rows[2], rows[3])
                sources.append(jnp.where(lower_half, low, high))
            return jnp.dot(jnp.concatenate(sources, axis=0), targets, preferred_element_type=F32)

        def add_chunk(chunk, weights):
            moments = [slot_ref[group, pl.ds(chunk, V_ROWS, stride=8), :].astype(BF16) for group in range(4)]
            for side in range(2):
                rows = jnp.concatenate(moments[2 * side : 2 * side + 2], axis=0)
                rows = jnp.concatenate([rows, rows], axis=1)
                totals[side] += jnp.dot(rows, weights[:, 128 * side : 128 * side + 128], preferred_element_type=F32)

        dist_sq, before = distances(0), None
        for chunk in range(8):
            ahead = distances(chunk + 1) if chunk < 7 else None
            inv = lax.rsqrt(dist_sq)
            weights = stacked(inv * inv * inv)
            if before is not None:
                add_chunk(chunk - 1, before)
            dist_sq, before = ahead, weights
        add_chunk(7, before)
        for side in range(2):
            pair = 2 * quad + side
            sums = jnp.where(left, totals[side][0:V_ROWS], totals[side][V_ROWS:])
            lanes = pair_lanes(pair)
            out_ref[:, lanes] = out_ref[:, lanes] + point_sums(sums, pair_place(tg_ref, pair))

    quads, octets = LEAF_DEV // 4, LEAF_DEV // 8
    features(0, 0, even_ref)

    def one_octet(octet, carry):
        quad = 2 * octet
        cell_pull(octet, tg_ref, ah_ref, cf_ref, cm_ref, out_ref)
        features(quad + 1, 4, odd_ref)
        pull(quad, even_ref)
        build(jnp.minimum(octet + 1, octets - 1))
        features(jnp.minimum(quad + 2, quads - 1), 0, even_ref)
        pull(quad + 1, odd_ref)
        return carry

    lax.fori_loop(0, octets, one_octet, 0)


def on_device(n_dom, n_sub, positions, masses, cell_mass, cell_center, cell_quad, cell_list, leaf_list, send_list, send_count):
    vmem = pl.BlockSpec(memory_space=pltpu.VMEM)
    smem = pl.BlockSpec(memory_space=pltpu.SMEM)
    anywhere = pl.BlockSpec(memory_space=pl.ANY)

    def limit(mib):
        return pltpu.CompilerParams(vmem_limit_bytes=mib * 1024 * 1024)

    ins = (
        positions,
        masses.reshape(1, -1),
        cell_mass.reshape(1, -1),
        cell_center,
        cell_quad,
        send_list.reshape(2 * RANGE, CAP),
        send_count.reshape(1, 2 * RANGE),
    )
    packed, sent = pl.pallas_call(
        functools.partial(pack_kernel, n_dom),
        out_shape=(
            jax.ShapeDtypeStruct((OWN_ROWS, 128), F32),
            jax.ShapeDtypeStruct((n_dom, OUT_ROWS, 128), F32),
        ),
        in_specs=[pl.BlockSpec(memory_space=pltpu.HBM)] * 7,
        out_specs=[vmem] * 2,
        scratch_shapes=[pltpu.VMEM(array.shape, F32) for array in ins[:5]]
        + [pltpu.SMEM(array.shape, jnp.int32) for array in ins[5:]]
        + [pltpu.SemaphoreType.DMA((7,))],
        compiler_params=limit(63),
        name="pack_own",
    )(*ins)
    nearby = lax.all_gather(packed, "sub", axis=0, tiled=True)
    outgoing = pl.pallas_call(
        functools.partial(outgoing_kernel, n_dom, n_sub),
        out_shape=jax.ShapeDtypeStruct((n_dom, OUT_ROWS + CELL_PAD * n_sub, 128), F32),
        in_specs=[anywhere, vmem],
        out_specs=vmem,
        scratch_shapes=[pltpu.SemaphoreType.DMA(())],
        compiler_params=limit(16),
        name="pack_outgoing",
    )(sent, nearby)
    received = lax.all_to_all(outgoing, "dom", split_axis=0, concat_axis=0, tiled=True)
    n_blocks = n_sub * LEAF_DEV + 2 * RANGE * CAP
    prepared = (
        jax.ShapeDtypeStruct((n_blocks, 4, 128), F32),
        jax.ShapeDtypeStruct((n_blocks, LEAF, 128), BF16),
        jax.ShapeDtypeStruct((PAIRS, H_ROWS, 128), BF16),
        jax.ShapeDtypeStruct((4 * PAIRS, 128), F32),
        jax.ShapeDtypeStruct((3, LEAF_DEV, 128), F32),
        jax.ShapeDtypeStruct((PAIRS, 128, 128), BF16),
    )
    n_near = n_sub * LEAF_DEV
    table, rows, targets, places, centres, cell_targets = pl.pallas_call(
        functools.partial(prepare_kernel, n_sub),
        out_shape=prepared,
        in_specs=[vmem],
        out_specs=[anywhere] * 6,
        scratch_shapes=[pltpu.VMEM((n_near,) + kind.shape[1:], kind.dtype) for kind in prepared[:2]]
        + [pltpu.VMEM(kind.shape, kind.dtype) for kind in prepared[2:]]
        + [
            pltpu.VMEM((8 * (H_ROWS + Q_ROWS), 128), F32),
            pltpu.VMEM((4, 8 * H_ROWS, 128), F32),
            pltpu.SemaphoreType.DMA((6,)),
        ],
        compiler_params=limit(62),
        cost_estimate=pl.CostEstimate(flops=50_000_000, bytes_accessed=16_000_000, transcendentals=0),
        name="prepare",
    )(nearby)
    ins = (received, cell_list, centres, places, cell_targets, targets, table, rows)
    return pl.pallas_call(
        functools.partial(pull_kernel, n_dom, n_sub),
        out_shape=jax.ShapeDtypeStruct((3, LEAF_DEV * LEAF), F32),
        in_specs=[anywhere] * 8 + [smem],
        out_specs=vmem,
        scratch_shapes=[pltpu.VMEM(array.shape, array.dtype) for array in ins]
        + [
            pltpu.VMEM((4, 8 * H_ROWS, 128), F32),
            pltpu.VMEM((8 * CELL_ROWS, 128), F32),
            pltpu.VMEM((8, 128), F32),
            pltpu.VMEM((8, 32, 128), F32),
            pltpu.VMEM((4, 8 * V_ROWS, 128), F32),
            pltpu.VMEM((4, 8 * V_ROWS, 128), F32),
            pltpu.SemaphoreType.DMA((8,)),
        ],
        compiler_params=limit(62),
        name="pull",
    )(*ins, leaf_list)


def solution(mesh):
    sharded = P(("dom", "sub"))
    return jax.shard_map(
        functools.partial(on_device, mesh.shape["dom"], mesh.shape["sub"]),
        mesh=mesh,
        in_specs=(
            P(None, ("dom", "sub")),
            sharded,
            sharded,
            P(None, ("dom", "sub")),
            P(None, ("dom", "sub")),
            P(("dom", "sub"), None),
            P(("dom", "sub"), None),
            P("dom", "sub", None, None),
            P("dom", "sub", None),
        ),
        out_specs=P(None, ("dom", "sub")),
        check_vma=False,
    )
```

```python
import functools

import jax
import jax.numpy as jnp
from jax import lax
from jax.experimental import pallas as pl
from jax.experimental.pallas import tpu as pltpu
from jax.sharding import PartitionSpec as P

LEAF = 64
LEAF_DEV = 128
NCELL = 128
NLEAF = 16
RANGE = 4
CAP = 8
PAIRS = LEAF_DEV // 2
OUT_UNITS = CAP // 2
OWN_ROWS = 4 * PAIRS + 16
OUT_ROWS = 4 * OUT_UNITS
CELL_AT = 4 * PAIRS
CELL_COMPS = 10
CELL_PAD = 12
OFFSETS = list(range(-RANGE, 0)) + list(range(1, RANGE + 1))

softening_sq = 0.0025
GRID_ROUND = 49152.0
F32 = jnp.float32
BF16 = jnp.bfloat16

H_ROWS = 32
Q_ROWS = 64
V_ROWS = 16
U_ROWS = 48
Q_AT = H_ROWS
V_AT = Q_AT + Q_ROWS
U_AT = V_AT + V_ROWS
CELL_ROWS = U_AT + U_ROWS
SOURCE_ROWS = H_ROWS + V_ROWS


def rounded(value):
    return value.astype(BF16).astype(F32)


def three_parts(value):
    first = rounded(value)
    rest = value - first
    second = rounded(rest)
    return first, second, rest - second


def two_parts(value):
    first = value.astype(BF16)
    return first, (value - first.astype(F32)).astype(BF16)


def grid_parts(value):
    high = (value + GRID_ROUND) - GRID_ROUND
    low = value - high
    first = rounded(low)
    return high, low, first, low - first


def norm_parts(parts, extra=None):
    big = sum(high * high for high, _, _, _ in parts)
    small = sum(low * (2.0 * high + low) for high, low, _, _ in parts)
    if extra is not None:
        small = small + extra
    return three_parts(big), three_parts(small)


def pack_kernel(n_dom, *refs):
    ins, out_ref, sent_ref, scratch, sems = refs[:7], refs[7], refs[8], refs[9:16], refs[16]
    copies = [pltpu.make_async_copy(src, dst, sems.at[at]) for at, (src, dst) in enumerate(zip(ins, scratch))]
    for copy in copies:
        copy.start()
    pos_ref, mass_ref, cmass_ref, center_ref, quad_ref, list_ref, count_ref = scratch
    me = lax.axis_index("dom")
    left = lax.broadcasted_iota(jnp.int32, (4, 128), 1) < LEAF
    sent_ref[...] = jnp.zeros((n_dom, OUT_ROWS, 128), F32)
    out_ref[CELL_AT + 10 : OWN_ROWS, :] = jnp.zeros((OWN_ROWS - CELL_AT - 10, 128), F32)
    for copy in copies:
        copy.wait()
    for pair in range(PAIRS):
        lanes = pl.ds(128 * pair, 128)
        out_ref[4 * pair : 4 * pair + 3, :] = pos_ref[:, lanes]
        out_ref[4 * pair + 3 : 4 * pair + 4, :] = mass_ref[:, lanes]
    out_ref[CELL_AT : CELL_AT + 1, :] = cmass_ref[...]
    out_ref[CELL_AT + 1 : CELL_AT + 4, :] = center_ref[...]
    out_ref[CELL_AT + 4 : CELL_AT + 10, :] = quad_ref[...]

    def half(slot, j, right):
        block = list_ref[slot, j]
        value = out_ref[pl.ds(pl.multiple_of(4 * (block // 2), 4), 4), :]
        value = jnp.where(j < count_ref[0, slot], value, 0.0)
        return jnp.where((block & 1) == right, value, pltpu.roll(value, LEAF, 1))

    for slot in range(2 * RANGE):
        target = me + OFFSETS[slot]

        @pl.when((target >= 0) & (target < n_dom))
        def _():
            for unit in range(OUT_UNITS):
                sent_ref[target, 4 * unit : 4 * unit + 4, :] = jnp.where(left, half(slot, 2 * unit, 0), half(slot, 2 * unit + 1, 1))


def outgoing_kernel(n_dom, n_sub, sent_ref, all_ref, out_ref, sem):
    copy = pltpu.make_async_copy(sent_ref, out_ref.at[:, 0:OUT_ROWS, :], sem)
    copy.start()

    def one_target(target, carry):
        for seg in range(n_sub):
            at = OUT_ROWS + CELL_PAD * seg
            first = seg * OWN_ROWS + CELL_AT
            out_ref[target, at : at + CELL_PAD, :] = all_ref[first : first + CELL_PAD, :]
        return carry

    lax.fori_loop(0, n_dom, one_target, 0)
    copy.wait()


def target_h_rows(parts, one, zero):
    big, small = norm_parts(parts, softening_sq)
    minus_high = [-2.0 * part[0] for part in parts]
    minus_one = [-2.0 * part[2] for part in parts]
    minus_two = [-2.0 * part[3] for part in parts]
    rows = minus_high + [one] * 3 + list(big) + minus_high + minus_one + minus_high
    return rows + minus_two + minus_one + [one] * 3 + list(small) + [zero] * 2


def target_features(all_ref, tg_ref, ce_ref, feat_ref, ah_ref):
    me = lax.axis_index("sub")
    left = lax.broadcasted_iota(jnp.int32, (8, 128), 1) < LEAF
    one = jnp.ones((8, 128), F32)
    zero = jnp.zeros((8, 128), F32)
    raw_ref = tg_ref

    raw_ref[...] = all_ref[pl.ds(pl.multiple_of(me * OWN_ROWS, 8), 4 * PAIRS), :]

    def one_octet(octet, carry):
        parts, centred = [], []
        for comp in range(3):
            rows = pl.ds(octet * 32 + comp, 8, stride=4)
            value = raw_ref[rows, :]
            first = jnp.broadcast_to(value[:, 0:1], (8, 128))
            second = jnp.broadcast_to(value[:, LEAF : LEAF + 1], (8, 128))
            ce_ref[comp, pl.ds(octet * 16, 8, stride=2), :] = first
            ce_ref[comp, pl.ds(octet * 16 + 1, 8, stride=2), :] = second
            value = value - jnp.where(left, first, second)
            raw_ref[rows, :] = value
            centred.append(value)
            parts.append(grid_parts(value))
        rows = target_h_rows(parts, one, zero)
        x, y, z = centred
        split = [three_parts(v) for v in (x, y, z, x * x, y * y, z * z, x * y, x * z, y * z)]
        for which in (0, 0, 1, 0, 1, 2):
            rows += [part[which] for part in split]
        rows += [one] * 3 + [zero] * 7
        for at, value in enumerate(rows):
            feat_ref[8 * at : 8 * at + 8, :] = value
        for sub in range(8):
            pair = octet * 8 + sub
            ah_ref[pair, :, 0 : H_ROWS + Q_ROWS] = feat_ref[pl.ds(sub, H_ROWS + Q_ROWS, stride=8), :].T.astype(BF16)
        return carry

    lax.fori_loop(0, PAIRS // 8, one_octet, 0)


def source_h_rows(parts):
    (p1, p2, p3), (s1, s2, s3) = norm_parts(parts)
    high = [part[0] for part in parts]
    one = [part[2] for part in parts]
    two = [part[3] for part in parts]
    rows = dict(enumerate(high + [p1, p2, p3]))
    rows.update(enumerate(one + high + two + high + one + [s1, s2, s3], 9))
    return rows


def put_rows(ref, rows):
    for at, value in rows.items():
        ref[8 * at : 8 * at + 8, :] = value


def fill_constant_rows(ref, count):
    one = jnp.ones((8, 128), F32)
    zero = jnp.zeros((8, 128), F32)
    for at in range(count):
        ones = at in (6, 7, 8, 27, 28, 29) or at == V_AT + 3
        ref[8 * at : 8 * at + 8, :] = one if ones else zero


def cell_features(n_dom, n_sub, octet, cl_ref, recv_ref, ce_ref, cf_ref, cm_ref):
    ids = cl_ref[pl.ds(pl.multiple_of(8 * octet, 8), 8), :]
    lane = ids & 127
    owner = ids >> 7

    def one_domain(dom, found):
        for seg in range(n_sub):
            here = owner == dom * n_sub + seg
            new = []
            for comp in range(CELL_COMPS):
                at = OUT_ROWS + CELL_PAD * seg + comp
                row = jnp.broadcast_to(recv_ref[dom, at : at + 1, :], (8, 128))
                value = jnp.take_along_axis(row, lane, axis=1, mode="promise_in_bounds")
                new.append(jnp.where(here, value, found[comp]))
            found = tuple(new)
        return found

    found = tuple(jnp.zeros((8, 128), F32) for _ in range(CELL_COMPS))
    if n_dom <= 8:
        for dom in range(n_dom):
            found = one_domain(dom, found)
    else:
        found = lax.fori_loop(0, n_dom, one_domain, found)
    mass, cx, cy, cz, xx, yy, zz, xy, xz, yz = found
    cm_ref[...] = mass
    rows8 = pl.ds(pl.multiple_of(8 * octet, 8), 8)
    cx, cy, cz = [value - ce_ref[comp, rows8, :] for comp, value in enumerate((cx, cy, cz))]
    put_rows(cf_ref, source_h_rows([grid_parts(value) for value in (cx, cy, cz)]))
    qx = xx * cx + xy * cy + xz * cz
    qy = xy * cx + yy * cy + yz * cz
    qz = xz * cx + yz * cy + zz * cz
    const = three_parts(2.5 * (qx * cx + qy * cy + qz * cz))
    linear = [-5.0 * qx, -5.0 * qy, -5.0 * qz]
    square = [2.5 * xx, 2.5 * yy, 2.5 * zz, 5.0 * xy, 5.0 * xz, 5.0 * yz]
    split = [three_parts(value) for value in linear + square]
    rows = []
    for which in (0, 1, 0, 2, 1, 0):
        rows += [part[which] for part in split]
    rows += list(const)
    put_rows(cf_ref, dict(enumerate(rows, Q_AT)))
    for comp, value in enumerate((cx, cy, cz)):
        for which, part in enumerate(three_parts(value)):
            cf_ref[8 * (V_AT + 4 * which + comp) : 8 * (V_AT + 4 * which + comp) + 8, :] = part
    columns = {name: three_parts(value) for name, value in dict(xx=xx, yy=yy, zz=zz, xy=xy, xz=xz, yz=yz, cx=qx, cy=qy, cz=qz).items()}
    order = (("xx", "xy", "xz"), ("xy", "yy", "yz"), ("xz", "yz", "zz"), ("cx", "cy", "cz"))
    for which in range(3):
        for column, names in enumerate(order):
            for row, name in enumerate(names):
                at = U_AT + 16 * which + 4 * column + row
                cf_ref[8 * at : 8 * at + 8, :] = columns[name][which]


def source_moments(group, ll_ref, tab_ref, ce_ref, raw_ref, sf_ref):
    left = lax.broadcasted_iota(jnp.int32, (4, 128), 1) < LEAF
    for pair in range(NLEAF // 2):
        first = tab_ref[ll_ref[group, 2 * pair]]
        second = tab_ref[ll_ref[group, 2 * pair + 1]]
        raw_ref[4 * pair : 4 * pair + 4, :] = jnp.where(left, first, second)
    value = [raw_ref[pl.ds(comp, 8, stride=4), :] for comp in range(4)]
    mass = value[3]
    centred = [value[comp] - ce_ref[comp, pl.ds(group, 1), :] for comp in range(3)]
    for comp, v in enumerate([mass * v for v in centred] + [mass]):
        for which, part in enumerate(three_parts(v)):
            at = 4 * which + comp
            sf_ref[8 * at : 8 * at + 8, :] = part


def transposed_dot(rows, weights):
    return lax.dot_general(rows, weights, (((1,), (1,)), ((), ())), preferred_element_type=F32)


def stacked(value):
    return jnp.concatenate(two_parts(value), axis=0)


def cell_group(sub, target, cf_ref, cm_ref):
    def cell_rows(at, count):
        return cf_ref[pl.ds(8 * at + sub, count, stride=8), :].astype(BF16)

    forms = jnp.concatenate(
        [
            jnp.concatenate([cell_rows(0, H_ROWS), jnp.zeros((H_ROWS, 128), BF16)], axis=1),
            jnp.concatenate([jnp.zeros((Q_ROWS, 128), BF16), cell_rows(Q_AT, Q_ROWS)], axis=1),
        ],
        axis=0,
    )
    forms = jnp.dot(target[:, 0 : H_ROWS + Q_ROWS], forms, preferred_element_type=F32)
    dist_sq, quad_form = forms[:, 0:128], forms[:, 128:256]
    inv = lax.rsqrt(dist_sq)
    inv_two = inv * inv
    inv_three = inv * inv_two
    pull = inv_three * (cm_ref[pl.ds(sub, 1), :] + quad_form * (inv_two * inv_two))
    moments = jnp.concatenate(
        [
            jnp.concatenate([cell_rows(V_AT, V_ROWS), jnp.zeros((V_ROWS, 128), BF16)], axis=1),
            jnp.concatenate([jnp.zeros((U_ROWS, 128), BF16), cell_rows(U_AT, U_ROWS)], axis=1),
        ],
        axis=0,
    )
    both = jnp.concatenate([stacked(pull), stacked(inv_three * inv_two)], axis=1)
    sums = transposed_dot(both, moments)
    return sums[0:LEAF] + sums[LEAF:]


def pair_lanes(pair):
    return pl.ds(pl.multiple_of(128 * pair, 128), 128)


def pair_place(tg_ref, pair):
    return tg_ref[pl.ds(pl.multiple_of(4 * pair, 4), 4), :]


def point_sums(sums, place):
    sums = sums[0:8] + sums[8:16]
    sums = sums + pltpu.roll(sums, 4, 0)
    return sums[0:3] - place[0:3] * sums[3:4]


def cell_pull(octet, tg_ref, ah_ref, cf_ref, cm_ref, out_ref):
    upper = lax.broadcasted_iota(jnp.int32, (8, 128), 0) < 4
    for inner in range(4):
        pair = octet * 4 + inner
        sums = [cell_group(2 * inner + half, ah_ref[pair, pl.ds(LEAF * half, LEAF), :], cf_ref, cm_ref) for half in range(2)]
        sums = jnp.concatenate(sums, axis=0).T
        place = pair_place(tg_ref, pair)
        x, y, z = [place[comp : comp + 1, :] for comp in range(3)]
        quads = sums[16:32] + sums[32:48] + sums[48:64]
        turned = quads[0:8] * jnp.where(upper, x, y) + quads[8:16] * jnp.where(upper, z, -1.0)
        turned = turned + pltpu.roll(turned, 4, 0)
        out_ref[:, pair_lanes(pair)] = point_sums(sums[0:16], place) + turned[0:3]


def put_block_pair(tab_ref, block, value):
    left = lax.broadcasted_iota(jnp.int32, (4, 128), 1) < LEAF
    turned = pltpu.roll(value, LEAF, 1)
    tab_ref[block] = jnp.where(left, value, turned)
    tab_ref[block + 1] = jnp.where(left, turned, value)


def put_eight_pairs(rows_ref, block, coords, feat_ref):
    copies = lax.broadcasted_iota(jnp.int32, (H_ROWS, 128), 1) % H_ROWS
    copies = jnp.where(copies == lax.broadcasted_iota(jnp.int32, (H_ROWS, 128), 0), 1.0, 0.0).astype(BF16)
    put_rows(feat_ref, source_h_rows([grid_parts(value) for value in coords]))
    for pair in range(8):
        spread = feat_ref[pl.ds(pair, H_ROWS, stride=8), :].T.astype(BF16)
        spread = jnp.dot(spread, copies, preferred_element_type=F32).astype(BF16)
        rows_ref[block + 2 * pair] = spread[0:LEAF]
        rows_ref[block + 2 * pair + 1] = spread[LEAF:]


def prepare_kernel(n_sub, all_ref, tab_out, rows_out, at_out, tg_out, ce_out, ah_out, tab_ref, rows_ref, at_ref, tg_ref, ce_ref, ah_ref, feat_ref, four_ref, sems):
    for at in range(4):
        fill_constant_rows(four_ref.at[at], H_ROWS)
    near_blocks = pl.ds(0, n_sub * LEAF_DEV)

    def near(step, carry):
        seg, part = step // (PAIRS // 32), step % (PAIRS // 32)
        for at in range(4):
            octet = 4 * part + at
            block = seg * LEAF_DEV + 16 * octet
            first = pl.multiple_of(seg * OWN_ROWS + 32 * octet, 8)
            for pair in range(8):
                put_block_pair(tab_ref, block + 2 * pair, all_ref[pl.ds(pl.multiple_of(first + 4 * pair, 4), 4), :])
            coords = [all_ref[pl.ds(first + comp, 8, stride=4), :] for comp in range(3)]
            put_eight_pairs(rows_ref, block, coords, four_ref.at[at])
        done = pl.ds(64 * step, 64)
        pltpu.make_async_copy(rows_ref.at[done], rows_out.at[done], sems.at[0]).start()
        return carry

    lax.fori_loop(0, n_sub * PAIRS // 32, near, 0)
    copies = [pltpu.make_async_copy(tab_ref, tab_out.at[near_blocks], sems.at[1])]
    copies[0].start()
    target_features(all_ref, tg_ref, ce_ref, feat_ref, ah_ref)
    target_rows(all_ref, four_ref.at[0], at_ref)
    for src, dst, at in ((at_ref, at_out, 2), (tg_ref, tg_out, 3), (ce_ref, ce_out, 4), (ah_ref, ah_out, 5)):
        copies.append(pltpu.make_async_copy(src, dst, sems.at[at]))
        copies[-1].start()
    pltpu.make_async_copy(rows_ref, rows_out.at[near_blocks], sems.at[0]).wait()
    for copy in copies:
        copy.wait()


def far_tables(n_dom, first_block, recv_ref, tab_ref, rows_ref, four_ref):
    for at in range(4):
        fill_constant_rows(four_ref.at[at], H_ROWS)
    me = lax.axis_index("dom")
    for two in range(RANGE):
        halves = []
        for slot in (2 * two, 2 * two + 1):
            source = me - OFFSETS[slot]
            inside = (source >= 0) & (source < n_dom)
            source = jnp.clip(source, 0, n_dom - 1)
            for unit in range(OUT_UNITS):
                value = jnp.where(inside, recv_ref[source, 4 * unit : 4 * unit + 4, :], 0.0)
                put_block_pair(tab_ref, first_block + slot * CAP + 2 * unit, value)
            halves.append([jnp.where(inside, recv_ref[source, pl.ds(comp, OUT_UNITS, stride=4), :], 0.0) for comp in range(3)])
        coords = [jnp.concatenate([one, other], axis=0) for one, other in zip(*halves)]
        put_eight_pairs(rows_ref, first_block + 2 * two * CAP, coords, four_ref.at[two])


def target_rows(all_ref, feat_ref, at_ref):
    first = lax.axis_index("sub") * OWN_ROWS
    one = jnp.ones((8, 128), F32)
    zero = jnp.zeros((8, 128), F32)

    def one_octet(octet, carry):
        parts = [grid_parts(all_ref[pl.ds(first + octet * 32 + comp, 8, stride=4), :]) for comp in range(3)]
        for at, value in enumerate(target_h_rows(parts, one, zero)):
            feat_ref[8 * at : 8 * at + 8, :] = value
        for pair in range(8):
            at_ref[octet * 8 + pair] = feat_ref[pl.ds(pair, H_ROWS, stride=8), :].astype(BF16)
        return carry

    lax.fori_loop(0, PAIRS // 8, one_octet, 0)


def pull_kernel(n_dom, n_sub, *refs):
    ins, ll_ref, out_ref, scratch, rest = refs[:8], refs[8], refs[9], refs[10:18], refs[18:]
    four_ref, cf_ref, cm_ref, raw_ref, even_ref, odd_ref, dist_even, dist_odd, sems = rest
    recv_ref, cl_ref, ce_ref, tg_ref, ah_ref, at_ref, tab_ref, rows_ref = scratch
    n_near = n_sub * LEAF_DEV
    copies = []
    for at, (src, dst) in enumerate(zip(ins, scratch)):
        if at >= 6:
            src, dst = src.at[pl.ds(0, n_near)], dst.at[pl.ds(0, n_near)]
        copies.append(pltpu.make_async_copy(src, dst, sems.at[at]))
        copies[-1].start()
    fill_constant_rows(cf_ref, CELL_ROWS)
    copies[0].wait()
    far_tables(n_dom, n_near, recv_ref, tab_ref, rows_ref, four_ref)
    copies[1].wait()
    copies[2].wait()

    def build(octet):
        cell_features(n_dom, n_sub, octet, cl_ref, recv_ref, ce_ref, cf_ref, cm_ref)

    build(0)
    for copy in copies[3:]:
        copy.wait()
    nothing = jnp.zeros((8, 128), F32)
    for group in range(4):
        for at in range(12, V_ROWS):
            even_ref[group, 8 * at : 8 * at + 8, :] = nothing
            odd_ref[group, 8 * at : 8 * at + 8, :] = nothing
    left = lax.broadcasted_iota(jnp.int32, (V_ROWS, 128), 1) < LEAF
    left_target = lax.broadcasted_iota(jnp.int32, (H_ROWS, 128), 1) < LEAF
    owner = (lax.broadcasted_iota(jnp.int32, (LEAF, 128), 1) // H_ROWS).astype(BF16)
    lower_half, first_own, third_own = owner < 2.0, owner == 0.0, owner == 2.0

    def features(quad, raw_at, slot_ref):
        for group in range(4):
            source_moments(4 * quad + group, ll_ref, tab_ref, ce_ref, raw_ref.at[raw_at + group], slot_ref.at[group])

    def distances(quad, dist_ref):
        nothing = jnp.zeros((H_ROWS, 128), BF16)
        first, second = at_ref[2 * quad], at_ref[2 * quad + 1]
        targets = jnp.concatenate(
            [
                jnp.concatenate([jnp.where(left_target, first, nothing), nothing], axis=1),
                jnp.concatenate([jnp.where(left_target, nothing, first), nothing], axis=1),
                jnp.concatenate([nothing, jnp.where(left_target, second, nothing)], axis=1),
                jnp.concatenate([nothing, jnp.where(left_target, nothing, second)], axis=1),
            ],
            axis=0,
        )
        sources = []
        for j in range(NLEAF):
            rows = [rows_ref[ll_ref[4 * quad + group, j]] for group in range(4)]
            low = jnp.where(first_own, rows[0], rows[1])
            high = jnp.where(third_own, rows[2], rows[3])
            sources.append(jnp.where(lower_half, low, high))
        dist_ref[...] = jnp.dot(jnp.concatenate(sources, axis=0), targets, preferred_element_type=F32)

    def pull(quad, slot_ref, dist_ref):
        total = jnp.zeros((4 * V_ROWS, 256), F32)
        for chunk in range(8):
            inv = lax.rsqrt(dist_ref[128 * chunk : 128 * chunk + 128, :])
            weights = stacked(inv * inv * inv)
            rows = [slot_ref[group, pl.ds(chunk, V_ROWS, stride=8), :].astype(BF16) for group in range(4)]
            rows = jnp.concatenate(rows, axis=0)
            total += jnp.dot(jnp.concatenate([rows, rows], axis=1), weights, preferred_element_type=F32)
        for side in range(2):
            pair = 2 * quad + side
            at, columns = 2 * V_ROWS * side, slice(128 * side, 128 * side + 128)
            sums = jnp.where(left, total[at : at + V_ROWS, columns], total[at + V_ROWS : at + 2 * V_ROWS, columns])
            lanes = pair_lanes(pair)
            out_ref[:, lanes] = out_ref[:, lanes] + point_sums(sums, pair_place(tg_ref, pair))

    quads, octets = LEAF_DEV // 4, LEAF_DEV // 8
    features(0, 0, even_ref)
    distances(0, dist_even)

    def one_octet(octet, carry):
        quad = 2 * octet
        after = jnp.minimum(quad + 2, quads - 1)
        cell_pull(octet, tg_ref, ah_ref, cf_ref, cm_ref, out_ref)
        features(quad + 1, 4, odd_ref)
        distances(quad + 1, dist_odd)
        pull(quad, even_ref, dist_even)
        build(jnp.minimum(octet + 1, octets - 1))
        features(after, 0, even_ref)
        distances(after, dist_even)
        pull(quad + 1, odd_ref, dist_odd)
        return carry

    lax.fori_loop(0, octets, one_octet, 0)


def on_device(n_dom, n_sub, positions, masses, cell_mass, cell_center, cell_quad, cell_list, leaf_list, send_list, send_count):
    vmem = pl.BlockSpec(memory_space=pltpu.VMEM)
    smem = pl.BlockSpec(memory_space=pltpu.SMEM)
    anywhere = pl.BlockSpec(memory_space=pl.ANY)

    def limit(mib):
        return pltpu.CompilerParams(vmem_limit_bytes=mib * 1024 * 1024)

    ins = (
        positions,
        masses.reshape(1, -1),
        cell_mass.reshape(1, -1),
        cell_center,
        cell_quad,
        send_list.reshape(2 * RANGE, CAP),
        send_count.reshape(1, 2 * RANGE),
    )
    packed, sent = pl.pallas_call(
        functools.partial(pack_kernel, n_dom),
        out_shape=(
            jax.ShapeDtypeStruct((OWN_ROWS, 128), F32),
            jax.ShapeDtypeStruct((n_dom, OUT_ROWS, 128), F32),
        ),
        in_specs=[pl.BlockSpec(memory_space=pltpu.HBM)] * 7,
        out_specs=[vmem] * 2,
        scratch_shapes=[pltpu.VMEM(array.shape, F32) for array in ins[:5]]
        + [pltpu.SMEM(array.shape, jnp.int32) for array in ins[5:]]
        + [pltpu.SemaphoreType.DMA((7,))],
        compiler_params=limit(63),
        name="pack_own",
    )(*ins)
    nearby = lax.all_gather(packed, "sub", axis=0, tiled=True)
    outgoing = pl.pallas_call(
        functools.partial(outgoing_kernel, n_dom, n_sub),
        out_shape=jax.ShapeDtypeStruct((n_dom, OUT_ROWS + CELL_PAD * n_sub, 128), F32),
        in_specs=[anywhere, vmem],
        out_specs=vmem,
        scratch_shapes=[pltpu.SemaphoreType.DMA(())],
        compiler_params=limit(16),
        name="pack_outgoing",
    )(sent, nearby)
    received = lax.all_to_all(outgoing, "dom", split_axis=0, concat_axis=0, tiled=True)
    n_blocks = n_sub * LEAF_DEV + 2 * RANGE * CAP
    prepared = (
        jax.ShapeDtypeStruct((n_blocks, 4, 128), F32),
        jax.ShapeDtypeStruct((n_blocks, LEAF, 128), BF16),
        jax.ShapeDtypeStruct((PAIRS, H_ROWS, 128), BF16),
        jax.ShapeDtypeStruct((4 * PAIRS, 128), F32),
        jax.ShapeDtypeStruct((3, LEAF_DEV, 128), F32),
        jax.ShapeDtypeStruct((PAIRS, 128, 128), BF16),
    )
    n_near = n_sub * LEAF_DEV
    table, rows, targets, places, centres, cell_targets = pl.pallas_call(
        functools.partial(prepare_kernel, n_sub),
        out_shape=prepared,
        in_specs=[vmem],
        out_specs=[anywhere] * 6,
        scratch_shapes=[pltpu.VMEM((n_near,) + kind.shape[1:], kind.dtype) for kind in prepared[:2]]
        + [pltpu.VMEM(kind.shape, kind.dtype) for kind in prepared[2:]]
        + [
            pltpu.VMEM((8 * (H_ROWS + Q_ROWS), 128), F32),
            pltpu.VMEM((4, 8 * H_ROWS, 128), F32),
            pltpu.SemaphoreType.DMA((6,)),
        ],
        compiler_params=limit(62),
        cost_estimate=pl.CostEstimate(flops=50_000_000, bytes_accessed=16_000_000, transcendentals=0),
        name="prepare",
    )(nearby)
    ins = (received, cell_list, centres, places, cell_targets, targets, table, rows)
    return pl.pallas_call(
        functools.partial(pull_kernel, n_dom, n_sub),
        out_shape=jax.ShapeDtypeStruct((3, LEAF_DEV * LEAF), F32),
        in_specs=[anywhere] * 8 + [smem],
        out_specs=vmem,
        scratch_shapes=[pltpu.VMEM(array.shape, array.dtype) for array in ins]
        + [
            pltpu.VMEM((4, 8 * H_ROWS, 128), F32),
            pltpu.VMEM((8 * CELL_ROWS, 128), F32),
            pltpu.VMEM((8, 128), F32),
            pltpu.VMEM((8, 32, 128), F32),
            pltpu.VMEM((4, 8 * V_ROWS, 128), F32),
            pltpu.VMEM((4, 8 * V_ROWS, 128), F32),
            pltpu.VMEM((NLEAF * LEAF, 256), F32),
            pltpu.VMEM((NLEAF * LEAF, 256), F32),
            pltpu.SemaphoreType.DMA((8,)),
        ],
        compiler_params=limit(62),
        name="pull",
    )(*ins, leaf_list)


def solution(mesh):
    sharded = P(("dom", "sub"))
    return jax.shard_map(
        functools.partial(on_device, mesh.shape["dom"], mesh.shape["sub"]),
        mesh=mesh,
        in_specs=(
            P(None, ("dom", "sub")),
            sharded,
            sharded,
            P(None, ("dom", "sub")),
            P(None, ("dom", "sub")),
            P(("dom", "sub"), None),
            P(("dom", "sub"), None),
            P("dom", "sub", None, None),
            P("dom", "sub", None),
        ),
        out_specs=P(None, ("dom", "sub")),
        check_vma=False,
    )
```

```python
import functools

import jax
import jax.numpy as jnp
from jax import lax
from jax.experimental import pallas as pl
from jax.experimental.pallas import tpu as pltpu
from jax.sharding import PartitionSpec as P

LEAF = 64
LEAF_DEV = 128
NCELL = 128
NLEAF = 16
RANGE = 4
CAP = 8
PAIRS = LEAF_DEV // 2
OUT_UNITS = CAP // 2
OWN_ROWS = 4 * PAIRS
OUT_ROWS = 4 * OUT_UNITS
CELL_COMPS = 10
CELL_PAD = 16
SENT_ROWS = OUT_ROWS + CELL_PAD
OFFSETS = list(range(-RANGE, 0)) + list(range(1, RANGE + 1))

softening_sq = 0.0025
GRID_ROUND = 49152.0
F32 = jnp.float32
BF16 = jnp.bfloat16

H_ROWS = 32
Q_ROWS = 64
V_ROWS = 16
U_ROWS = 48
Q_AT = H_ROWS
V_AT = Q_AT + Q_ROWS
U_AT = V_AT + V_ROWS
CELL_ROWS = U_AT + U_ROWS
SOURCE_ROWS = H_ROWS + V_ROWS


def rounded(value):
    return value.astype(BF16).astype(F32)


def three_parts(value):
    first = rounded(value)
    rest = value - first
    second = rounded(rest)
    return first, second, rest - second


def two_parts(value):
    first = value.astype(BF16)
    return first, (value - first.astype(F32)).astype(BF16)


def grid_parts(value):
    high = (value + GRID_ROUND) - GRID_ROUND
    low = value - high
    first = rounded(low)
    return high, low, first, low - first


def norm_parts(parts, extra=None):
    big = sum(high * high for high, _, _, _ in parts)
    small = sum(low * (2.0 * high + low) for high, low, _, _ in parts)
    if extra is not None:
        small = small + extra
    return three_parts(big), three_parts(small)


def pack_kernel(n_dom, *refs):
    ins, out_ref, sent_ref, scratch, sems = refs[:7], refs[7], refs[8], refs[9:16], refs[16]
    copies = [pltpu.make_async_copy(src, dst, sems.at[at]) for at, (src, dst) in enumerate(zip(ins, scratch))]
    for copy in copies:
        copy.start()
    pos_ref, mass_ref, cmass_ref, center_ref, quad_ref, list_ref, count_ref = scratch
    me = lax.axis_index("dom")
    left = lax.broadcasted_iota(jnp.int32, (4, 128), 1) < LEAF
    sent_ref[...] = jnp.zeros((n_dom, SENT_ROWS, 128), F32)
    for copy in copies:
        copy.wait()
    for pair in range(PAIRS):
        lanes = pl.ds(128 * pair, 128)
        out_ref[4 * pair : 4 * pair + 3, :] = pos_ref[:, lanes]
        out_ref[4 * pair + 3 : 4 * pair + 4, :] = mass_ref[:, lanes]

    def put_cells(target, carry):
        sent_ref[target, OUT_ROWS : OUT_ROWS + 1, :] = cmass_ref[...]
        sent_ref[target, OUT_ROWS + 1 : OUT_ROWS + 4, :] = center_ref[...]
        sent_ref[target, OUT_ROWS + 4 : OUT_ROWS + 10, :] = quad_ref[...]
        return carry

    lax.fori_loop(0, n_dom, put_cells, 0)

    def half(slot, j, right):
        block = list_ref[slot, j]
        value = out_ref[pl.ds(pl.multiple_of(4 * (block // 2), 4), 4), :]
        value = jnp.where(j < count_ref[0, slot], value, 0.0)
        return jnp.where((block & 1) == right, value, pltpu.roll(value, LEAF, 1))

    for slot in range(2 * RANGE):
        target = me + OFFSETS[slot]

        @pl.when((target >= 0) & (target < n_dom))
        def _():
            for unit in range(OUT_UNITS):
                sent_ref[target, 4 * unit : 4 * unit + 4, :] = jnp.where(left, half(slot, 2 * unit, 0), half(slot, 2 * unit + 1, 1))


def target_h_rows(parts, one, zero):
    big, small = norm_parts(parts, softening_sq)
    minus_high = [-2.0 * part[0] for part in parts]
    minus_one = [-2.0 * part[2] for part in parts]
    minus_two = [-2.0 * part[3] for part in parts]
    rows = minus_high + [one] * 3 + list(big) + minus_high + minus_one + minus_high
    return rows + minus_two + minus_one + [one] * 3 + list(small) + [zero] * 2


def target_features(all_ref, tg_ref, ce_ref, feat_ref, ah_ref):
    me = lax.axis_index("sub")
    left = lax.broadcasted_iota(jnp.int32, (8, 128), 1) < LEAF
    one = jnp.ones((8, 128), F32)
    zero = jnp.zeros((8, 128), F32)
    raw_ref = tg_ref

    raw_ref[...] = all_ref[pl.ds(pl.multiple_of(me * OWN_ROWS, 8), OWN_ROWS), :]

    def one_octet(octet, carry):
        parts, centred = [], []
        for comp in range(3):
            rows = pl.ds(octet * 32 + comp, 8, stride=4)
            value = raw_ref[rows, :]
            first = jnp.broadcast_to(value[:, 0:1], (8, 128))
            second = jnp.broadcast_to(value[:, LEAF : LEAF + 1], (8, 128))
            ce_ref[comp, pl.ds(octet * 16, 8, stride=2), :] = first
            ce_ref[comp, pl.ds(octet * 16 + 1, 8, stride=2), :] = second
            value = value - jnp.where(left, first, second)
            raw_ref[rows, :] = value
            centred.append(value)
            parts.append(grid_parts(value))
        rows = target_h_rows(parts, one, zero)
        x, y, z = centred
        split = [three_parts(v) for v in (x, y, z, x * x, y * y, z * z, x * y, x * z, y * z)]
        for which in (0, 0, 1, 0, 1, 2):
            rows += [part[which] for part in split]
        rows += [one] * 3 + [zero] * 7
        for at, value in enumerate(rows):
            feat_ref[8 * at : 8 * at + 8, :] = value
        for sub in range(8):
            pair = octet * 8 + sub
            ah_ref[pair, :, 0 : H_ROWS + Q_ROWS] = feat_ref[pl.ds(sub, H_ROWS + Q_ROWS, stride=8), :].T.astype(BF16)
        return carry

    lax.fori_loop(0, PAIRS // 8, one_octet, 0)


def source_h_rows(parts):
    (p1, p2, p3), (s1, s2, s3) = norm_parts(parts)
    high = [part[0] for part in parts]
    one = [part[2] for part in parts]
    two = [part[3] for part in parts]
    rows = dict(enumerate(high + [p1, p2, p3]))
    rows.update(enumerate(one + high + two + high + one + [s1, s2, s3], 9))
    return rows


def put_rows(ref, rows):
    for at, value in rows.items():
        ref[8 * at : 8 * at + 8, :] = value


def fill_constant_rows(ref, count):
    one = jnp.ones((8, 128), F32)
    zero = jnp.zeros((8, 128), F32)
    for at in range(count):
        ones = at in (6, 7, 8, 27, 28, 29) or at == V_AT + 3
        ref[8 * at : 8 * at + 8, :] = one if ones else zero


def cell_features(n_dom, n_sub, octet, cl_ref, all_ref, ce_ref, cf_ref, cm_ref):
    ids = cl_ref[pl.ds(pl.multiple_of(8 * octet, 8), 8), :]
    lane = ids & 127
    owner = ids >> 7

    def one_domain(dom, found):
        for seg in range(n_sub):
            here = owner == dom * n_sub + seg
            new = []
            for comp in range(CELL_COMPS):
                row = jnp.broadcast_to(all_ref[seg, dom, comp : comp + 1, :], (8, 128))
                value = jnp.take_along_axis(row, lane, axis=1, mode="promise_in_bounds")
                new.append(jnp.where(here, value, found[comp]))
            found = tuple(new)
        return found

    found = tuple(jnp.zeros((8, 128), F32) for _ in range(CELL_COMPS))
    if n_dom <= 8:
        for dom in range(n_dom):
            found = one_domain(dom, found)
    else:
        found = lax.fori_loop(0, n_dom, one_domain, found)
    mass, cx, cy, cz, xx, yy, zz, xy, xz, yz = found
    cm_ref[...] = mass
    rows8 = pl.ds(pl.multiple_of(8 * octet, 8), 8)
    cx, cy, cz = [value - ce_ref[comp, rows8, :] for comp, value in enumerate((cx, cy, cz))]
    put_rows(cf_ref, source_h_rows([grid_parts(value) for value in (cx, cy, cz)]))
    qx = xx * cx + xy * cy + xz * cz
    qy = xy * cx + yy * cy + yz * cz
    qz = xz * cx + yz * cy + zz * cz
    const = three_parts(2.5 * (qx * cx + qy * cy + qz * cz))
    linear = [-5.0 * qx, -5.0 * qy, -5.0 * qz]
    square = [2.5 * xx, 2.5 * yy, 2.5 * zz, 5.0 * xy, 5.0 * xz, 5.0 * yz]
    split = [three_parts(value) for value in linear + square]
    rows = []
    for which in (0, 1, 0, 2, 1, 0):
        rows += [part[which] for part in split]
    rows += list(const)
    put_rows(cf_ref, dict(enumerate(rows, Q_AT)))
    for comp, value in enumerate((cx, cy, cz)):
        for which, part in enumerate(three_parts(value)):
            cf_ref[8 * (V_AT + 4 * which + comp) : 8 * (V_AT + 4 * which + comp) + 8, :] = part
    columns = {name: three_parts(value) for name, value in dict(xx=xx, yy=yy, zz=zz, xy=xy, xz=xz, yz=yz, cx=qx, cy=qy, cz=qz).items()}
    order = (("xx", "xy", "xz"), ("xy", "yy", "yz"), ("xz", "yz", "zz"), ("cx", "cy", "cz"))
    for which in range(3):
        for column, names in enumerate(order):
            for row, name in enumerate(names):
                at = U_AT + 16 * which + 4 * column + row
                cf_ref[8 * at : 8 * at + 8, :] = columns[name][which]


def source_moments(group, ll_ref, tab_ref, ce_ref, raw_ref, sf_ref):
    left = lax.broadcasted_iota(jnp.int32, (4, 128), 1) < LEAF
    for pair in range(NLEAF // 2):
        first = tab_ref[ll_ref[2 * pair, group]]
        second = tab_ref[ll_ref[2 * pair + 1, group]]
        raw_ref[4 * pair : 4 * pair + 4, :] = jnp.where(left, first, second)
    value = [raw_ref[pl.ds(comp, 8, stride=4), :] for comp in range(4)]
    mass = value[3]
    centred = [value[comp] - ce_ref[comp, pl.ds(group, 1), :] for comp in range(3)]
    for comp, v in enumerate([mass * v for v in centred] + [mass]):
        for which, part in enumerate(three_parts(v)):
            at = 4 * which + comp
            sf_ref[8 * at : 8 * at + 8, :] = part


def transposed_dot(rows, weights):
    return lax.dot_general(rows, weights, (((1,), (1,)), ((), ())), preferred_element_type=F32)


def stacked(value):
    return jnp.concatenate(two_parts(value), axis=0)


def cell_group(sub, target, cf_ref, cm_ref):
    def cell_rows(at, count):
        return cf_ref[pl.ds(8 * at + sub, count, stride=8), :].astype(BF16)

    forms = jnp.concatenate(
        [
            jnp.concatenate([cell_rows(0, H_ROWS), jnp.zeros((H_ROWS, 128), BF16)], axis=1),
            jnp.concatenate([jnp.zeros((Q_ROWS, 128), BF16), cell_rows(Q_AT, Q_ROWS)], axis=1),
        ],
        axis=0,
    )
    forms = jnp.dot(target[:, 0 : H_ROWS + Q_ROWS], forms, preferred_element_type=F32)
    dist_sq, quad_form = forms[:, 0:128], forms[:, 128:256]
    inv = lax.rsqrt(dist_sq)
    inv_two = inv * inv
    inv_three = inv * inv_two
    pull = inv_three * (cm_ref[pl.ds(sub, 1), :] + quad_form * (inv_two * inv_two))
    moments = jnp.concatenate(
        [
            jnp.concatenate([cell_rows(V_AT, V_ROWS), jnp.zeros((V_ROWS, 128), BF16)], axis=1),
            jnp.concatenate([jnp.zeros((U_ROWS, 128), BF16), cell_rows(U_AT, U_ROWS)], axis=1),
        ],
        axis=0,
    )
    both = jnp.concatenate([stacked(pull), stacked(inv_three * inv_two)], axis=1)
    sums = transposed_dot(both, moments)
    return sums[0:LEAF] + sums[LEAF:]


def pair_lanes(pair):
    return pl.ds(pl.multiple_of(128 * pair, 128), 128)


def pair_place(tg_ref, pair):
    return tg_ref[pl.ds(pl.multiple_of(4 * pair, 4), 4), :]


def point_sums(sums, place):
    sums = sums[0:8] + sums[8:16]
    sums = sums + pltpu.roll(sums, 4, 0)
    return sums[0:3] - place[0:3] * sums[3:4]


def cell_pull(octet, tg_ref, ah_ref, cf_ref, cm_ref, out_ref):
    upper = lax.broadcasted_iota(jnp.int32, (8, 128), 0) < 4
    for inner in range(4):
        pair = octet * 4 + inner
        sums = [cell_group(2 * inner + half, ah_ref[pair, pl.ds(LEAF * half, LEAF), :], cf_ref, cm_ref) for half in range(2)]
        sums = jnp.concatenate(sums, axis=0).T
        place = pair_place(tg_ref, pair)
        x, y, z = [place[comp : comp + 1, :] for comp in range(3)]
        quads = sums[16:32] + sums[32:48] + sums[48:64]
        turned = quads[0:8] * jnp.where(upper, x, y) + quads[8:16] * jnp.where(upper, z, -1.0)
        turned = turned + pltpu.roll(turned, 4, 0)
        out_ref[:, pair_lanes(pair)] = point_sums(sums[0:16], place) + turned[0:3]


def put_block_pair(tab_ref, block, value):
    left = lax.broadcasted_iota(jnp.int32, (4, 128), 1) < LEAF
    turned = pltpu.roll(value, LEAF, 1)
    tab_ref[block] = jnp.where(left, value, turned)
    tab_ref[block + 1] = jnp.where(left, turned, value)


def put_eight_pairs(rows_ref, block, coords, feat_ref):
    put_rows(feat_ref, source_h_rows([grid_parts(value) for value in coords]))
    for pair in range(8):
        columns = feat_ref[pl.ds(pair, H_ROWS, stride=8), :].astype(BF16)
        spread = jnp.concatenate([columns] * 4, axis=0).T
        rows_ref[block + 2 * pair] = spread[0:LEAF]
        rows_ref[block + 2 * pair + 1] = spread[LEAF:]


def prepare_kernel(n_dom, n_sub, all_ref, recv_ref, tab_ref, rows_ref, at_ref, tg_ref, ce_ref, ah_ref, feat_ref, four_ref):
    target_features(all_ref, tg_ref, ce_ref, feat_ref, ah_ref)
    target_rows(all_ref, four_ref.at[0], at_ref)
    for at in range(4):
        fill_constant_rows(four_ref.at[at], H_ROWS)

    def near(step, carry):
        seg, part = step // (PAIRS // 32), step % (PAIRS // 32)
        for at in range(4):
            octet = 4 * part + at
            block = seg * LEAF_DEV + 16 * octet
            first = pl.multiple_of(seg * OWN_ROWS + 32 * octet, 8)
            for pair in range(8):
                put_block_pair(tab_ref, block + 2 * pair, all_ref[pl.ds(pl.multiple_of(first + 4 * pair, 4), 4), :])
            coords = [all_ref[pl.ds(first + comp, 8, stride=4), :] for comp in range(3)]
            put_eight_pairs(rows_ref, block, coords, four_ref.at[at])
        return carry

    lax.fori_loop(0, n_sub * PAIRS // 32, near, 0)
    far_tables(n_dom, n_sub * LEAF_DEV, recv_ref, tab_ref, rows_ref, four_ref)


def far_tables(n_dom, first_block, recv_ref, tab_ref, rows_ref, four_ref):
    me = lax.axis_index("dom")
    for two in range(RANGE):
        halves = []
        for slot in (2 * two, 2 * two + 1):
            source = me - OFFSETS[slot]
            inside = (source >= 0) & (source < n_dom)
            source = jnp.clip(source, 0, n_dom - 1)
            for unit in range(OUT_UNITS):
                value = jnp.where(inside, recv_ref[source, 4 * unit : 4 * unit + 4, :], 0.0)
                put_block_pair(tab_ref, first_block + slot * CAP + 2 * unit, value)
            halves.append([jnp.where(inside, recv_ref[source, pl.ds(comp, OUT_UNITS, stride=4), :], 0.0) for comp in range(3)])
        coords = [jnp.concatenate([one, other], axis=0) for one, other in zip(*halves)]
        put_eight_pairs(rows_ref, first_block + 2 * two * CAP, coords, four_ref.at[two])


def target_rows(all_ref, feat_ref, at_ref):
    first = lax.axis_index("sub") * OWN_ROWS
    one = jnp.ones((8, 128), F32)
    zero = jnp.zeros((8, 128), F32)

    def one_octet(octet, carry):
        parts = [grid_parts(all_ref[pl.ds(first + octet * 32 + comp, 8, stride=4), :]) for comp in range(3)]
        for at, value in enumerate(target_h_rows(parts, one, zero)):
            feat_ref[8 * at : 8 * at + 8, :] = value
        for pair in range(8):
            at_ref[octet * 8 + pair] = feat_ref[pl.ds(pair, H_ROWS, stride=8), :].astype(BF16)
        return carry

    lax.fori_loop(0, PAIRS // 8, one_octet, 0)


def pull_kernel(
    n_dom, n_sub, cells_ref, cl_ref, ll_hbm, tab_ref, rows_ref, at_ref, tg_ref, ce_ref, ah_ref, out_ref,
    ll_ref, cf_ref, cm_ref, raw_ref, even_ref, odd_ref, dist_even, dist_odd, sem,
):
    copy = pltpu.make_async_copy(ll_hbm, ll_ref, sem)
    copy.start()
    fill_constant_rows(cf_ref, CELL_ROWS)

    def build(octet):
        cell_features(n_dom, n_sub, octet, cl_ref, cells_ref, ce_ref, cf_ref, cm_ref)

    build(0)
    copy.wait()
    nothing = jnp.zeros((8, 128), F32)
    for group in range(4):
        for at in range(12, V_ROWS):
            even_ref[group, 8 * at : 8 * at + 8, :] = nothing
            odd_ref[group, 8 * at : 8 * at + 8, :] = nothing
    left = lax.broadcasted_iota(jnp.int32, (V_ROWS, 128), 1) < LEAF
    left_target = lax.broadcasted_iota(jnp.int32, (H_ROWS, 128), 1) < LEAF
    owner = (lax.broadcasted_iota(jnp.int32, (LEAF, 128), 1) // H_ROWS).astype(BF16)
    lower_half, first_own, third_own = owner < 2.0, owner == 0.0, owner == 2.0

    def features(quad, raw_at, slot_ref):
        for group in range(4):
            source_moments(4 * quad + group, ll_ref, tab_ref, ce_ref, raw_ref.at[raw_at + group], slot_ref.at[group])

    def distances(quad, dist_ref):
        nothing = jnp.zeros((H_ROWS, 128), BF16)
        first, second = at_ref[2 * quad], at_ref[2 * quad + 1]
        targets = jnp.concatenate(
            [
                jnp.concatenate([jnp.where(left_target, first, nothing), nothing], axis=1),
                jnp.concatenate([jnp.where(left_target, nothing, first), nothing], axis=1),
                jnp.concatenate([nothing, jnp.where(left_target, second, nothing)], axis=1),
                jnp.concatenate([nothing, jnp.where(left_target, nothing, second)], axis=1),
            ],
            axis=0,
        )
        sources = []
        for j in range(NLEAF):
            rows = [rows_ref[ll_ref[j, 4 * quad + group]] for group in range(4)]
            low = jnp.where(first_own, rows[0], rows[1])
            high = jnp.where(third_own, rows[2], rows[3])
            sources.append(jnp.where(lower_half, low, high))
        dist_ref[...] = jnp.dot(jnp.concatenate(sources, axis=0), targets, preferred_element_type=F32)

    def pull(quad, slot_ref, dist_ref):
        total = jnp.zeros((4 * V_ROWS, 256), F32)
        for chunk in range(8):
            inv = lax.rsqrt(dist_ref[128 * chunk : 128 * chunk + 128, :])
            weights = stacked(inv * inv * inv)
            rows = [slot_ref[group, pl.ds(chunk, V_ROWS, stride=8), :].astype(BF16) for group in range(4)]
            rows = jnp.concatenate(rows, axis=0)
            total += jnp.dot(jnp.concatenate([rows, rows], axis=1), weights, preferred_element_type=F32)
        for side in range(2):
            pair = 2 * quad + side
            at, columns = 2 * V_ROWS * side, slice(128 * side, 128 * side + 128)
            sums = jnp.where(left, total[at : at + V_ROWS, columns], total[at + V_ROWS : at + 2 * V_ROWS, columns])
            lanes = pair_lanes(pair)
            out_ref[:, lanes] = out_ref[:, lanes] + point_sums(sums, pair_place(tg_ref, pair))

    quads, octets = LEAF_DEV // 4, LEAF_DEV // 8
    features(0, 0, even_ref)
    distances(0, dist_even)

    def one_octet(octet, carry):
        quad = 2 * octet
        after = jnp.minimum(quad + 2, quads - 1)
        cell_pull(octet, tg_ref, ah_ref, cf_ref, cm_ref, out_ref)
        features(quad + 1, 4, odd_ref)
        distances(quad + 1, dist_odd)
        pull(quad, even_ref, dist_even)
        build(jnp.minimum(octet + 1, octets - 1))
        features(after, 0, even_ref)
        distances(after, dist_even)
        pull(quad + 1, odd_ref, dist_odd)
        return carry

    lax.fori_loop(0, octets, one_octet, 0)


def on_device(n_dom, n_sub, positions, masses, cell_mass, cell_center, cell_quad, cell_list, leaf_list, send_list, send_count):
    vmem = pl.BlockSpec(memory_space=pltpu.VMEM)
    smem = pl.BlockSpec(memory_space=pltpu.SMEM)
    anywhere = pl.BlockSpec(memory_space=pl.ANY)

    def limit(mib):
        return pltpu.CompilerParams(vmem_limit_bytes=mib * 1024 * 1024)

    ins = (
        positions,
        masses.reshape(1, -1),
        cell_mass.reshape(1, -1),
        cell_center,
        cell_quad,
        send_list.reshape(2 * RANGE, CAP),
        send_count.reshape(1, 2 * RANGE),
    )
    packed, sent = pl.pallas_call(
        functools.partial(pack_kernel, n_dom),
        out_shape=(
            jax.ShapeDtypeStruct((OWN_ROWS, 128), F32),
            jax.ShapeDtypeStruct((n_dom, SENT_ROWS, 128), F32),
        ),
        in_specs=[pl.BlockSpec(memory_space=pltpu.HBM)] * 7,
        out_specs=[vmem] * 2,
        scratch_shapes=[pltpu.VMEM(array.shape, F32) for array in ins[:5]]
        + [pltpu.SMEM(array.shape, jnp.int32) for array in ins[5:]]
        + [pltpu.SemaphoreType.DMA((7,))],
        compiler_params=limit(63),
        name="pack_own",
    )(*ins)
    received = lax.all_to_all(sent, "dom", split_axis=0, concat_axis=0, tiled=True)
    nearby = lax.all_gather(packed, "sub", axis=0, tiled=True)
    cells = lax.all_gather(received[:, OUT_ROWS:], "sub", axis=0, tiled=False)
    n_blocks = n_sub * LEAF_DEV + 2 * RANGE * CAP
    prepared = pl.pallas_call(
        functools.partial(prepare_kernel, n_dom, n_sub),
        out_shape=(
            jax.ShapeDtypeStruct((n_blocks, 4, 128), F32),
            jax.ShapeDtypeStruct((n_blocks, LEAF, 128), BF16),
            jax.ShapeDtypeStruct((PAIRS, H_ROWS, 128), BF16),
            jax.ShapeDtypeStruct((OWN_ROWS, 128), F32),
            jax.ShapeDtypeStruct((3, LEAF_DEV, 128), F32),
            jax.ShapeDtypeStruct((PAIRS, 128, 128), BF16),
        ),
        in_specs=[vmem] * 2,
        out_specs=[vmem] * 6,
        scratch_shapes=[
            pltpu.VMEM((8 * (H_ROWS + Q_ROWS), 128), F32),
            pltpu.VMEM((4, 8 * H_ROWS, 128), F32),
        ],
        compiler_params=limit(24),
        name="prepare",
    )(nearby, received)
    return pl.pallas_call(
        functools.partial(pull_kernel, n_dom, n_sub),
        out_shape=jax.ShapeDtypeStruct((3, LEAF_DEV * LEAF), F32),
        in_specs=[vmem, vmem, anywhere] + [vmem] * 6,
        out_specs=vmem,
        scratch_shapes=[
            pltpu.SMEM((NLEAF, LEAF_DEV), jnp.int32),
            pltpu.VMEM((8 * CELL_ROWS, 128), F32),
            pltpu.VMEM((8, 128), F32),
            pltpu.VMEM((8, 32, 128), F32),
            pltpu.VMEM((4, 8 * V_ROWS, 128), F32),
            pltpu.VMEM((4, 8 * V_ROWS, 128), F32),
            pltpu.VMEM((NLEAF * LEAF, 256), F32),
            pltpu.VMEM((NLEAF * LEAF, 256), F32),
            pltpu.SemaphoreType.DMA(()),
        ],
        compiler_params=limit(24),
        name="pull",
    )(cells, cell_list, leaf_list.T, *prepared)


def solution(mesh):
    sharded = P(("dom", "sub"))
    return jax.shard_map(
        functools.partial(on_device, mesh.shape["dom"], mesh.shape["sub"]),
        mesh=mesh,
        in_specs=(
            P(None, ("dom", "sub")),
            sharded,
            sharded,
            P(None, ("dom", "sub")),
            P(None, ("dom", "sub")),
            P(("dom", "sub"), None),
            P(("dom", "sub"), None),
            P("dom", "sub", None, None),
            P("dom", "sub", None),
        ),
        out_specs=P(None, ("dom", "sub")),
        check_vma=False,
    )
```

```python
import functools

import jax
import jax.numpy as jnp
from jax import lax
from jax.experimental import pallas as pl
from jax.experimental.pallas import tpu as pltpu
from jax.sharding import PartitionSpec as P

LEAF = 64
LEAF_DEV = 128
NCELL = 128
NLEAF = 16
RANGE = 4
CAP = 8
PAIRS = LEAF_DEV // 2
OUT_UNITS = CAP // 2
OWN_ROWS = 4 * PAIRS
OUT_ROWS = 4 * OUT_UNITS
CELL_COMPS = 10
CELL_PAD = 16
SENT_ROWS = OUT_ROWS + CELL_PAD
OFFSETS = list(range(-RANGE, 0)) + list(range(1, RANGE + 1))

softening_sq = 0.0025
GRID_ROUND = 49152.0
F32 = jnp.float32
BF16 = jnp.bfloat16

H_ROWS = 32
Q_ROWS = 64
V_ROWS = 16
U_ROWS = 48
Q_AT = H_ROWS
V_AT = Q_AT + Q_ROWS
U_AT = V_AT + V_ROWS
CELL_ROWS = U_AT + U_ROWS
SOURCE_ROWS = H_ROWS + V_ROWS


def rounded(value):
    return value.astype(BF16).astype(F32)


def three_parts(value):
    first = rounded(value)
    rest = value - first
    second = rounded(rest)
    return first, second, rest - second


def two_parts(value):
    first = value.astype(BF16)
    return first, (value - first.astype(F32)).astype(BF16)


def grid_parts(value):
    high = (value + GRID_ROUND) - GRID_ROUND
    low = value - high
    first = rounded(low)
    return high, low, first, low - first


def norm_parts(parts, extra=None):
    big = sum(high * high for high, _, _, _ in parts)
    small = sum(low * (2.0 * high + low) for high, low, _, _ in parts)
    if extra is not None:
        small = small + extra
    return three_parts(big), three_parts(small)


def pack_kernel(n_dom, *refs):
    ins, out_ref, sent_ref, scratch, sems = refs[:7], refs[7], refs[8], refs[9:16], refs[16]
    copies = [pltpu.make_async_copy(src, dst, sems.at[at]) for at, (src, dst) in enumerate(zip(ins, scratch))]
    for copy in copies:
        copy.start()
    pos_ref, mass_ref, cmass_ref, center_ref, quad_ref, list_ref, count_ref = scratch
    me = lax.axis_index("dom")
    left = lax.broadcasted_iota(jnp.int32, (4, 128), 1) < LEAF
    sent_ref[...] = jnp.zeros((n_dom, SENT_ROWS, 128), F32)
    for copy in copies:
        copy.wait()
    for pair in range(PAIRS):
        lanes = pl.ds(128 * pair, 128)
        out_ref[4 * pair : 4 * pair + 3, :] = pos_ref[:, lanes]
        out_ref[4 * pair + 3 : 4 * pair + 4, :] = mass_ref[:, lanes]

    def put_cells(target, carry):
        sent_ref[target, OUT_ROWS : OUT_ROWS + 1, :] = cmass_ref[...]
        sent_ref[target, OUT_ROWS + 1 : OUT_ROWS + 4, :] = center_ref[...]
        sent_ref[target, OUT_ROWS + 4 : OUT_ROWS + 10, :] = quad_ref[...]
        return carry

    lax.fori_loop(0, n_dom, put_cells, 0)

    def half(slot, j, right):
        block = list_ref[slot, j]
        value = out_ref[pl.ds(pl.multiple_of(4 * (block // 2), 4), 4), :]
        value = jnp.where(j < count_ref[0, slot], value, 0.0)
        return jnp.where((block & 1) == right, value, pltpu.roll(value, LEAF, 1))

    for slot in range(2 * RANGE):
        target = me + OFFSETS[slot]

        @pl.when((target >= 0) & (target < n_dom))
        def _():
            for unit in range(OUT_UNITS):
                sent_ref[target, 4 * unit : 4 * unit + 4, :] = jnp.where(left, half(slot, 2 * unit, 0), half(slot, 2 * unit + 1, 1))


def target_h_rows(parts, one, zero):
    big, small = norm_parts(parts, softening_sq)
    minus_high = [-2.0 * part[0] for part in parts]
    minus_one = [-2.0 * part[2] for part in parts]
    minus_two = [-2.0 * part[3] for part in parts]
    rows = minus_high + [one] * 3 + list(big) + minus_high + minus_one + minus_high
    return rows + minus_two + minus_one + [one] * 3 + list(small) + [zero] * 2


def target_features(own_ref, tg_ref, ce_ref, feat_ref, ah_ref):
    left = lax.broadcasted_iota(jnp.int32, (8, 128), 1) < LEAF
    one = jnp.ones((8, 128), F32)
    zero = jnp.zeros((8, 128), F32)
    raw_ref = tg_ref

    raw_ref[...] = own_ref[...]

    def one_octet(octet, carry):
        parts, centred = [], []
        for comp in range(3):
            rows = pl.ds(octet * 32 + comp, 8, stride=4)
            value = raw_ref[rows, :]
            first = jnp.broadcast_to(value[:, 0:1], (8, 128))
            second = jnp.broadcast_to(value[:, LEAF : LEAF + 1], (8, 128))
            ce_ref[comp, pl.ds(octet * 16, 8, stride=2), :] = first
            ce_ref[comp, pl.ds(octet * 16 + 1, 8, stride=2), :] = second
            value = value - jnp.where(left, first, second)
            raw_ref[rows, :] = value
            centred.append(value)
            parts.append(grid_parts(value))
        rows = target_h_rows(parts, one, zero)
        x, y, z = centred
        split = [three_parts(v) for v in (x, y, z, x * x, y * y, z * z, x * y, x * z, y * z)]
        for which in (0, 0, 1, 0, 1, 2):
            rows += [part[which] for part in split]
        rows += [one] * 3 + [zero] * 7
        for at, value in enumerate(rows):
            feat_ref[8 * at : 8 * at + 8, :] = value
        for sub in range(8):
            pair = octet * 8 + sub
            ah_ref[pair, :, 0 : H_ROWS + Q_ROWS] = feat_ref[pl.ds(sub, H_ROWS + Q_ROWS, stride=8), :].T.astype(BF16)
        return carry

    lax.fori_loop(0, PAIRS // 8, one_octet, 0)


def source_h_rows(parts):
    (p1, p2, p3), (s1, s2, s3) = norm_parts(parts)
    high = [part[0] for part in parts]
    one = [part[2] for part in parts]
    two = [part[3] for part in parts]
    rows = dict(enumerate(high + [p1, p2, p3]))
    rows.update(enumerate(one + high + two + high + one + [s1, s2, s3], 9))
    return rows


def put_rows(ref, rows):
    for at, value in rows.items():
        ref[8 * at : 8 * at + 8, :] = value


def fill_constant_rows(ref, count):
    one = jnp.ones((8, 128), F32)
    zero = jnp.zeros((8, 128), F32)
    for at in range(count):
        ones = at in (6, 7, 8, 27, 28, 29) or at == V_AT + 3
        ref[8 * at : 8 * at + 8, :] = one if ones else zero


def cell_features(n_dom, n_sub, octet, cl_ref, cell_refs, ce_ref, cf_ref, cm_ref):
    ids = cl_ref[pl.ds(pl.multiple_of(8 * octet, 8), 8), :]
    lane = ids & 127
    owner = ids >> 7
    me = lax.axis_index("sub")

    def look_up(dom, shift, found):
        here = owner == dom * n_sub + lax.rem(me + n_sub - shift, n_sub)
        new = []
        for comp in range(CELL_COMPS):
            row = jnp.broadcast_to(cell_refs[shift][dom, comp : comp + 1, :], (8, 128))
            value = jnp.take_along_axis(row, lane, axis=1, mode="promise_in_bounds")
            new.append(jnp.where(here, value, found[comp]))
        return tuple(new)

    found = tuple(jnp.zeros((8, 128), F32) for _ in range(CELL_COMPS))
    if n_dom <= 8:
        for dom in range(n_dom):
            for shift in range(n_sub):
                found = look_up(dom, shift, found)
                yield
    else:

        def one_domain(dom, found):
            for shift in range(n_sub):
                found = look_up(dom, shift, found)
            return found

        found = lax.fori_loop(0, n_dom, one_domain, found)
    mass, cx, cy, cz, xx, yy, zz, xy, xz, yz = found
    yield "found"
    cm_ref[...] = mass
    rows8 = pl.ds(pl.multiple_of(8 * octet, 8), 8)
    cx, cy, cz = [value - ce_ref[comp, rows8, :] for comp, value in enumerate((cx, cy, cz))]
    put_rows(cf_ref, source_h_rows([grid_parts(value) for value in (cx, cy, cz)]))
    yield
    qx = xx * cx + xy * cy + xz * cz
    qy = xy * cx + yy * cy + yz * cz
    qz = xz * cx + yz * cy + zz * cz
    const = three_parts(2.5 * (qx * cx + qy * cy + qz * cz))
    linear = [-5.0 * qx, -5.0 * qy, -5.0 * qz]
    square = [2.5 * xx, 2.5 * yy, 2.5 * zz, 5.0 * xy, 5.0 * xz, 5.0 * yz]
    split = [three_parts(value) for value in linear + square]
    rows = []
    for which in (0, 1, 0, 2, 1, 0):
        rows += [part[which] for part in split]
    rows += list(const)
    put_rows(cf_ref, dict(enumerate(rows, Q_AT)))
    yield
    for comp, value in enumerate((cx, cy, cz)):
        for which, part in enumerate(three_parts(value)):
            cf_ref[8 * (V_AT + 4 * which + comp) : 8 * (V_AT + 4 * which + comp) + 8, :] = part
    yield
    columns = {name: three_parts(value) for name, value in dict(xx=xx, yy=yy, zz=zz, xy=xy, xz=xz, yz=yz, cx=qx, cy=qy, cz=qz).items()}
    order = (("xx", "xy", "xz"), ("xy", "yy", "yz"), ("xz", "yz", "zz"), ("cx", "cy", "cz"))
    for which in range(3):
        for column, names in enumerate(order):
            for row, name in enumerate(names):
                at = U_AT + 16 * which + 4 * column + row
                cf_ref[8 * at : 8 * at + 8, :] = columns[name][which]


def source_moments(group, ll_ref, tab_ref, ce_ref, raw_ref, sf_ref):
    left = lax.broadcasted_iota(jnp.int32, (4, 128), 1) < LEAF
    for pair in range(NLEAF // 2):
        first = tab_ref[ll_ref[2 * pair, group]]
        second = tab_ref[ll_ref[2 * pair + 1, group]]
        raw_ref[4 * pair : 4 * pair + 4, :] = jnp.where(left, first, second)
    value = [raw_ref[pl.ds(comp, 8, stride=4), :] for comp in range(4)]
    mass = value[3]
    centred = [value[comp] - ce_ref[comp, pl.ds(group, 1), :] for comp in range(3)]
    for comp, v in enumerate([mass * v for v in centred] + [mass]):
        for which, part in enumerate(three_parts(v)):
            at = 4 * which + comp
            sf_ref[8 * at : 8 * at + 8, :] = part


def transposed_dot(rows, weights):
    return lax.dot_general(rows, weights, (((1,), (1,)), ((), ())), preferred_element_type=F32)


def stacked(value):
    return jnp.concatenate(two_parts(value), axis=0)


def cell_group(sub, target, cf_ref, cm_ref):
    def cell_rows(at, count):
        return cf_ref[pl.ds(8 * at + sub, count, stride=8), :].astype(BF16)

    forms = jnp.concatenate(
        [
            jnp.concatenate([cell_rows(0, H_ROWS), jnp.zeros((H_ROWS, 128), BF16)], axis=1),
            jnp.concatenate([jnp.zeros((Q_ROWS, 128), BF16), cell_rows(Q_AT, Q_ROWS)], axis=1),
        ],
        axis=0,
    )
    forms = jnp.dot(target[:, 0 : H_ROWS + Q_ROWS], forms, preferred_element_type=F32)
    dist_sq, quad_form = forms[:, 0:128], forms[:, 128:256]
    inv = lax.rsqrt(dist_sq)
    inv_two = inv * inv
    inv_three = inv * inv_two
    pull = inv_three * (cm_ref[pl.ds(sub, 1), :] + quad_form * (inv_two * inv_two))
    moments = jnp.concatenate(
        [
            jnp.concatenate([cell_rows(V_AT, V_ROWS), jnp.zeros((V_ROWS, 128), BF16)], axis=1),
            jnp.concatenate([jnp.zeros((U_ROWS, 128), BF16), cell_rows(U_AT, U_ROWS)], axis=1),
        ],
        axis=0,
    )
    both = jnp.concatenate([stacked(pull), stacked(inv_three * inv_two)], axis=1)
    sums = transposed_dot(both, moments)
    return sums[0:LEAF] + sums[LEAF:]


def pair_lanes(pair):
    return pl.ds(pl.multiple_of(128 * pair, 128), 128)


def pair_place(tg_ref, pair):
    return tg_ref[pl.ds(pl.multiple_of(4 * pair, 4), 4), :]


def point_sums(sums, place):
    sums = sums[0:8] + sums[8:16]
    sums = sums + pltpu.roll(sums, 4, 0)
    return sums[0:3] - place[0:3] * sums[3:4]


def cell_pull(octet, tg_ref, ah_ref, cf_ref, cm_ref, out_ref):
    upper = lax.broadcasted_iota(jnp.int32, (8, 128), 0) < 4
    for inner in range(4):
        pair = octet * 4 + inner
        sums = []
        for half in range(2):
            sums.append(cell_group(2 * inner + half, ah_ref[pair, pl.ds(LEAF * half, LEAF), :], cf_ref, cm_ref))
            yield
        sums = jnp.concatenate(sums, axis=0).T
        place = pair_place(tg_ref, pair)
        x, y, z = [place[comp : comp + 1, :] for comp in range(3)]
        quads = sums[16:32] + sums[32:48] + sums[48:64]
        turned = quads[0:8] * jnp.where(upper, x, y) + quads[8:16] * jnp.where(upper, z, -1.0)
        turned = turned + pltpu.roll(turned, 4, 0)
        out_ref[:, pair_lanes(pair)] = point_sums(sums[0:16], place) + turned[0:3]


def put_block_pair(tab_ref, block, value):
    left = lax.broadcasted_iota(jnp.int32, (4, 128), 1) < LEAF
    turned = pltpu.roll(value, LEAF, 1)
    tab_ref[block] = jnp.where(left, value, turned)
    tab_ref[block + 1] = jnp.where(left, turned, value)


def put_eight_pairs(rows_ref, block, coords, feat_ref):
    put_rows(feat_ref, source_h_rows([grid_parts(value) for value in coords]))
    for pair in range(8):
        columns = feat_ref[pl.ds(pair, H_ROWS, stride=8), :].astype(BF16)
        spread = jnp.concatenate([columns] * 4, axis=0).T
        rows_ref[block + 2 * pair] = spread[0:LEAF]
        rows_ref[block + 2 * pair + 1] = spread[LEAF:]


def prepare_kernel(n_dom, n_sub, *refs):
    near_refs, recv_ref = refs[:n_sub], refs[n_sub]
    tab_ref, rows_ref, at_ref, tg_ref, ce_ref, ah_ref, feat_ref, four_ref = refs[n_sub + 1 :]
    target_features(near_refs[0], tg_ref, ce_ref, feat_ref, ah_ref)
    target_rows(near_refs[0], four_ref.at[0], at_ref)
    for at in range(4):
        fill_constant_rows(four_ref.at[at], H_ROWS)
    me = lax.axis_index("sub")
    for shift, near_ref in enumerate(near_refs):
        seg = lax.rem(me + n_sub - shift, n_sub)

        def near(step, carry):
            for at in range(4):
                octet = 4 * step + at
                block = seg * LEAF_DEV + 16 * octet
                first = pl.multiple_of(32 * octet, 32)
                for pair in range(8):
                    put_block_pair(tab_ref, block + 2 * pair, near_ref[pl.ds(pl.multiple_of(first + 4 * pair, 4), 4), :])
                coords = [near_ref[pl.ds(first + comp, 8, stride=4), :] for comp in range(3)]
                put_eight_pairs(rows_ref, block, coords, four_ref.at[at])
            return carry

        lax.fori_loop(0, PAIRS // 32, near, 0)
    far_tables(n_dom, n_sub * LEAF_DEV, recv_ref, tab_ref, rows_ref, four_ref)


def far_tables(n_dom, first_block, recv_ref, tab_ref, rows_ref, four_ref):
    me = lax.axis_index("dom")
    for two in range(RANGE):
        halves = []
        for slot in (2 * two, 2 * two + 1):
            source = me - OFFSETS[slot]
            inside = (source >= 0) & (source < n_dom)
            source = jnp.clip(source, 0, n_dom - 1)
            for unit in range(OUT_UNITS):
                value = jnp.where(inside, recv_ref[source, 4 * unit : 4 * unit + 4, :], 0.0)
                put_block_pair(tab_ref, first_block + slot * CAP + 2 * unit, value)
            halves.append([jnp.where(inside, recv_ref[source, pl.ds(comp, OUT_UNITS, stride=4), :], 0.0) for comp in range(3)])
        coords = [jnp.concatenate([one, other], axis=0) for one, other in zip(*halves)]
        put_eight_pairs(rows_ref, first_block + 2 * two * CAP, coords, four_ref.at[two])


def target_rows(own_ref, feat_ref, at_ref):
    one = jnp.ones((8, 128), F32)
    zero = jnp.zeros((8, 128), F32)

    def one_octet(octet, carry):
        parts = [grid_parts(own_ref[pl.ds(octet * 32 + comp, 8, stride=4), :]) for comp in range(3)]
        for at, value in enumerate(target_h_rows(parts, one, zero)):
            feat_ref[8 * at : 8 * at + 8, :] = value
        for pair in range(8):
            at_ref[octet * 8 + pair] = feat_ref[pl.ds(pair, H_ROWS, stride=8), :].astype(BF16)
        return carry

    lax.fori_loop(0, PAIRS // 8, one_octet, 0)


def run(strand, steps=None):
    taken = 0
    while steps is None or taken < steps:
        taken += 1
        if next(strand, "end") == "end":
            return


def pull_kernel(n_dom, n_sub, *refs):
    cell_refs, cl_ref, ll_hbm = refs[:n_sub], refs[n_sub], refs[n_sub + 1]
    tab_ref, rows_ref, at_ref, tg_ref, ce_ref, ah_ref, out_ref = refs[n_sub + 2 : n_sub + 9]
    ll_ref, cf_ref, cm_ref, raw_ref, even_ref, odd_ref, dist_even, dist_odd, sem = refs[n_sub + 9 :]
    copy = pltpu.make_async_copy(ll_hbm, ll_ref, sem)
    copy.start()
    fill_constant_rows(cf_ref, CELL_ROWS)

    def build(octet):
        return cell_features(n_dom, n_sub, octet, cl_ref, cell_refs, ce_ref, cf_ref, cm_ref)

    run(build(0))
    copy.wait()
    nothing = jnp.zeros((8, 128), F32)
    for group in range(4):
        for at in range(12, V_ROWS):
            even_ref[group, 8 * at : 8 * at + 8, :] = nothing
            odd_ref[group, 8 * at : 8 * at + 8, :] = nothing
    left = lax.broadcasted_iota(jnp.int32, (V_ROWS, 128), 1) < LEAF
    left_target = lax.broadcasted_iota(jnp.int32, (H_ROWS, 128), 1) < LEAF
    owner = (lax.broadcasted_iota(jnp.int32, (LEAF, 128), 1) // H_ROWS).astype(BF16)
    lower_half, first_own, third_own = owner < 2.0, owner == 0.0, owner == 2.0

    def features(quad, raw_at, slot_ref):
        for group in range(4):
            source_moments(4 * quad + group, ll_ref, tab_ref, ce_ref, raw_ref.at[raw_at + group], slot_ref.at[group])
            yield

    def distances(quad, dist_ref):
        nothing = jnp.zeros((H_ROWS, 128), BF16)
        first, second = at_ref[2 * quad], at_ref[2 * quad + 1]
        targets = jnp.concatenate(
            [
                jnp.concatenate([jnp.where(left_target, first, nothing), nothing], axis=1),
                jnp.concatenate([jnp.where(left_target, nothing, first), nothing], axis=1),
                jnp.concatenate([nothing, jnp.where(left_target, second, nothing)], axis=1),
                jnp.concatenate([nothing, jnp.where(left_target, nothing, second)], axis=1),
            ],
            axis=0,
        )
        sources = []
        for j in range(NLEAF):
            rows = [rows_ref[ll_ref[j, 4 * quad + group]] for group in range(4)]
            low = jnp.where(first_own, rows[0], rows[1])
            high = jnp.where(third_own, rows[2], rows[3])
            sources.append(jnp.where(lower_half, low, high))
            if j % 8 == 7:
                rows = pl.ds(LEAF * (j - 7), 8 * LEAF)
                dist_ref[rows, :] = jnp.dot(jnp.concatenate(sources, axis=0), targets, preferred_element_type=F32)
                sources = []
                yield

    def pull(quad, slot_ref, dist_ref):
        total = jnp.zeros((4 * V_ROWS, 256), F32)
        for chunk in range(8):
            inv = lax.rsqrt(dist_ref[128 * chunk : 128 * chunk + 128, :])
            weights = stacked(inv * inv * inv)
            rows = [slot_ref[group, pl.ds(chunk, V_ROWS, stride=8), :].astype(BF16) for group in range(4)]
            rows = jnp.concatenate(rows, axis=0)
            total += jnp.dot(jnp.concatenate([rows, rows], axis=1), weights, preferred_element_type=F32)
            yield
        for side in range(2):
            pair = 2 * quad + side
            at, columns = 2 * V_ROWS * side, slice(128 * side, 128 * side + 128)
            sums = jnp.where(left, total[at : at + V_ROWS, columns], total[at + V_ROWS : at + 2 * V_ROWS, columns])
            lanes = pair_lanes(pair)
            out_ref[:, lanes] = out_ref[:, lanes] + point_sums(sums, pair_place(tg_ref, pair))

    quads, octets = LEAF_DEV // 4, LEAF_DEV // 8
    run(features(0, 0, even_ref))
    run(distances(0, dist_even))

    def one_octet(octet, carry):
        quad = 2 * octet
        after = jnp.minimum(quad + 2, quads - 1)
        cells = cell_pull(octet, tg_ref, ah_ref, cf_ref, cm_ref, out_ref)
        coming = build(jnp.minimum(octet + 1, octets - 1))
        for half, (now, slot_ref, dist_ref, ahead, ahead_slot, ahead_dist, raw_at) in enumerate(
            (
                (quad, even_ref, dist_even, quad + 1, odd_ref, dist_odd, 4),
                (quad + 1, odd_ref, dist_odd, after, even_ref, dist_even, 0),
            )
        ):
            direct = pull(now, slot_ref, dist_ref)
            moments, distance = features(ahead, raw_at, ahead_slot), distances(ahead, ahead_dist)
            for step in range(8):
                if step in (1, 4):
                    run(distance, 1)
                run(direct, 1)
                if step % 2 == 0:
                    run(moments, 1)
                if half == 0 or step < 4:
                    run(coming, 3)
                    if step % 4 != 3:
                        run(cells, 1)
                elif step == 4:
                    run(cells)
                else:
                    run(coming, 1)
            run(moments)
            run(distance)
            run(direct)
        run(coming)
        return carry

    lax.fori_loop(0, octets, one_octet, 0)


def on_device(n_dom, n_sub, positions, masses, cell_mass, cell_center, cell_quad, cell_list, leaf_list, send_list, send_count):
    vmem = pl.BlockSpec(memory_space=pltpu.VMEM)
    smem = pl.BlockSpec(memory_space=pltpu.SMEM)
    anywhere = pl.BlockSpec(memory_space=pl.ANY)

    def limit(mib):
        return pltpu.CompilerParams(vmem_limit_bytes=mib * 1024 * 1024)

    ins = (
        positions,
        masses.reshape(1, -1),
        cell_mass.reshape(1, -1),
        cell_center,
        cell_quad,
        send_list.reshape(2 * RANGE, CAP),
        send_count.reshape(1, 2 * RANGE),
    )
    packed, sent = pl.pallas_call(
        functools.partial(pack_kernel, n_dom),
        out_shape=(
            jax.ShapeDtypeStruct((OWN_ROWS, 128), F32),
            jax.ShapeDtypeStruct((n_dom, SENT_ROWS, 128), F32),
        ),
        in_specs=[pl.BlockSpec(memory_space=pltpu.HBM)] * 7,
        out_specs=[vmem] * 2,
        scratch_shapes=[pltpu.VMEM(array.shape, F32) for array in ins[:5]]
        + [pltpu.SMEM(array.shape, jnp.int32) for array in ins[5:]]
        + [pltpu.SemaphoreType.DMA((7,))],
        compiler_params=limit(63),
        name="pack_own",
    )(*ins)
    received = lax.all_to_all(sent, "dom", split_axis=0, concat_axis=0, tiled=True)

    def around(value):
        pieces = [value]
        for shift in range(1, n_sub):
            pieces.append(lax.ppermute(value, "sub", [(seg, (seg + shift) % n_sub) for seg in range(n_sub)]))
        return pieces

    nearby = around(packed)
    cells = around(received[:, OUT_ROWS:])
    n_blocks = n_sub * LEAF_DEV + 2 * RANGE * CAP
    prepared = pl.pallas_call(
        functools.partial(prepare_kernel, n_dom, n_sub),
        out_shape=(
            jax.ShapeDtypeStruct((n_blocks, 4, 128), F32),
            jax.ShapeDtypeStruct((n_blocks, LEAF, 128), BF16),
            jax.ShapeDtypeStruct((PAIRS, H_ROWS, 128), BF16),
            jax.ShapeDtypeStruct((OWN_ROWS, 128), F32),
            jax.ShapeDtypeStruct((3, LEAF_DEV, 128), F32),
            jax.ShapeDtypeStruct((PAIRS, 128, 128), BF16),
        ),
        in_specs=[vmem] * (n_sub + 1),
        out_specs=[vmem] * 6,
        scratch_shapes=[
            pltpu.VMEM((8 * (H_ROWS + Q_ROWS), 128), F32),
            pltpu.VMEM((4, 8 * H_ROWS, 128), F32),
        ],
        compiler_params=limit(24),
        name="prepare",
    )(*nearby, received)
    return pl.pallas_call(
        functools.partial(pull_kernel, n_dom, n_sub),
        out_shape=jax.ShapeDtypeStruct((3, LEAF_DEV * LEAF), F32),
        in_specs=[vmem] * (n_sub + 1) + [anywhere] + [vmem] * 6,
        out_specs=vmem,
        scratch_shapes=[
            pltpu.SMEM((NLEAF, LEAF_DEV), jnp.int32),
            pltpu.VMEM((8 * CELL_ROWS, 128), F32),
            pltpu.VMEM((8, 128), F32),
            pltpu.VMEM((8, 32, 128), F32),
            pltpu.VMEM((4, 8 * V_ROWS, 128), F32),
            pltpu.VMEM((4, 8 * V_ROWS, 128), F32),
            pltpu.VMEM((NLEAF * LEAF, 256), F32),
            pltpu.VMEM((NLEAF * LEAF, 256), F32),
            pltpu.SemaphoreType.DMA(()),
        ],
        compiler_params=limit(24),
        name="pull",
    )(*cells, cell_list, leaf_list.T, *prepared)


def solution(mesh):
    sharded = P(("dom", "sub"))
    return jax.shard_map(
        functools.partial(on_device, mesh.shape["dom"], mesh.shape["sub"]),
        mesh=mesh,
        in_specs=(
            P(None, ("dom", "sub")),
            sharded,
            sharded,
            P(None, ("dom", "sub")),
            P(None, ("dom", "sub")),
            P(("dom", "sub"), None),
            P(("dom", "sub"), None),
            P("dom", "sub", None, None),
            P("dom", "sub", None),
        ),
        out_specs=P(None, ("dom", "sub")),
        check_vma=False,
    )
```

```python
import functools

import jax
import jax.numpy as jnp
from jax import lax
from jax.experimental import pallas as pl
from jax.experimental.pallas import tpu as pltpu
from jax.sharding import PartitionSpec as P

LEAF = 64
LEAF_DEV = 128
NCELL = 128
NLEAF = 16
RANGE = 4
CAP = 8
PAIRS = LEAF_DEV // 2
OUT_UNITS = CAP // 2
OWN_ROWS = 4 * PAIRS
OUT_ROWS = 4 * OUT_UNITS
CELL_COMPS = 10
CELL_PAD = 16
SENT_ROWS = OUT_ROWS + CELL_PAD
OFFSETS = list(range(-RANGE, 0)) + list(range(1, RANGE + 1))

softening_sq = 0.0025
GRID_ROUND = 49152.0
F32 = jnp.float32
BF16 = jnp.bfloat16

H_ROWS = 32
Q_ROWS = 64
V_ROWS = 16
U_ROWS = 48
Q_AT = H_ROWS
V_AT = Q_AT + Q_ROWS
U_AT = V_AT + V_ROWS
CELL_ROWS = U_AT + U_ROWS
SOURCE_ROWS = H_ROWS + V_ROWS


def rounded(value):
    return value.astype(BF16).astype(F32)


def three_parts(value):
    first = rounded(value)
    rest = value - first
    second = rounded(rest)
    return first, second, rest - second


def two_parts(value):
    first = value.astype(BF16)
    return first, (value - first.astype(F32)).astype(BF16)


def grid_parts(value):
    high = (value + GRID_ROUND) - GRID_ROUND
    low = value - high
    first = rounded(low)
    return high, low, first, low - first


def norm_parts(parts, extra=None):
    big = sum(high * high for high, _, _, _ in parts)
    small = sum(low * (2.0 * high + low) for high, low, _, _ in parts)
    if extra is not None:
        small = small + extra
    return three_parts(big), three_parts(small)


def put_own(pos_ref, mass_ref, own_ref):
    for pair in range(PAIRS):
        lanes = pl.ds(128 * pair, 128)
        own_ref[4 * pair : 4 * pair + 3, :] = pos_ref[:, lanes]
        own_ref[4 * pair + 3 : 4 * pair + 4, :] = mass_ref[:, lanes]


def pack_kernel(n_dom, *refs):
    ins, outs, scratch, (out_ref, sent_ref, sems) = refs[:9], refs[9:12], refs[12:21], refs[21:]
    results = [
        pltpu.make_async_copy(out_ref.at[pl.ds(0, OWN_ROWS)], outs[0], sems.at[9]),
        pltpu.make_async_copy(sent_ref.at[pl.ds(0, n_dom)], outs[1], sems.at[10]),
        pltpu.make_async_copy(out_ref, outs[2], sems.at[11]),
    ]
    copies = [pltpu.make_async_copy(src, dst, sems.at[at]) for at, (src, dst) in enumerate(zip(ins, scratch))]
    for copy in copies:
        copy.start()
    pos_ref, mass_ref, cmass_ref, center_ref, quad_ref, cl_ref, ll_ref, list_ref, count_ref = scratch
    me = lax.axis_index("dom")
    left = lax.broadcasted_iota(jnp.int32, (4, 128), 1) < LEAF
    sent_ref[...] = jnp.zeros((n_dom + 1, SENT_ROWS, 128), F32)
    for copy in copies:
        copy.wait()
    put_own(pos_ref, mass_ref, out_ref)
    out_ref[OWN_ROWS : OWN_ROWS + LEAF_DEV, :] = cl_ref[...].astype(F32)
    out_ref[OWN_ROWS + LEAF_DEV :, :] = ll_ref[...].astype(F32)

    def put_cells(target, carry):
        sent_ref[target, OUT_ROWS : OUT_ROWS + 1, :] = cmass_ref[...]
        sent_ref[target, OUT_ROWS + 1 : OUT_ROWS + 4, :] = center_ref[...]
        sent_ref[target, OUT_ROWS + 4 : OUT_ROWS + 10, :] = quad_ref[...]
        return carry

    lax.fori_loop(0, n_dom, put_cells, 0)

    def half(slot, j, right):
        block = list_ref[slot, j]
        value = out_ref[pl.ds(pl.multiple_of(4 * (block // 2), 4), 4), :]
        value = jnp.where(j < count_ref[0, slot], value, 0.0)
        return jnp.where((block & 1) == right, value, pltpu.roll(value, LEAF, 1))

    for slot in range(2 * RANGE):
        target = me + OFFSETS[slot]
        target = jnp.where((target >= 0) & (target < n_dom), target, n_dom)
        for unit in range(OUT_UNITS):
            sent_ref[target, 4 * unit : 4 * unit + 4, :] = jnp.where(left, half(slot, 2 * unit, 0), half(slot, 2 * unit + 1, 1))
    for copy in results:
        copy.start()
    for copy in results:
        copy.wait()


def target_h_rows(parts, one, zero):
    big, small = norm_parts(parts, softening_sq)
    minus_high = [-2.0 * part[0] for part in parts]
    minus_one = [-2.0 * part[2] for part in parts]
    minus_two = [-2.0 * part[3] for part in parts]
    rows = minus_high + [one] * 3 + list(big) + minus_high + minus_one + minus_high
    return rows + minus_two + minus_one + [one] * 3 + list(small) + [zero] * 2


def target_features(own_ref, tg_ref, ce_ref, feat_ref, ah_ref):
    left = lax.broadcasted_iota(jnp.int32, (8, 128), 1) < LEAF
    one = jnp.ones((8, 128), F32)
    zero = jnp.zeros((8, 128), F32)
    raw_ref = tg_ref

    raw_ref[...] = own_ref[...]

    def one_octet(octet, carry):
        parts, centred = [], []
        for comp in range(3):
            rows = pl.ds(octet * 32 + comp, 8, stride=4)
            value = raw_ref[rows, :]
            first = jnp.broadcast_to(value[:, 0:1], (8, 128))
            second = jnp.broadcast_to(value[:, LEAF : LEAF + 1], (8, 128))
            ce_ref[comp, pl.ds(octet * 16, 8, stride=2), :] = first
            ce_ref[comp, pl.ds(octet * 16 + 1, 8, stride=2), :] = second
            value = value - jnp.where(left, first, second)
            raw_ref[rows, :] = value
            centred.append(value)
            parts.append(grid_parts(value))
        rows = target_h_rows(parts, one, zero)
        x, y, z = centred
        split = [three_parts(v) for v in (x, y, z, x * x, y * y, z * z, x * y, x * z, y * z)]
        for which in (0, 0, 1, 0, 1, 2):
            rows += [part[which] for part in split]
        rows += [one] * 3 + [zero] * 7
        for at, value in enumerate(rows):
            feat_ref[8 * at : 8 * at + 8, :] = value
        for sub in range(8):
            pair = octet * 8 + sub
            ah_ref[pair, :, 0 : H_ROWS + Q_ROWS] = feat_ref[pl.ds(sub, H_ROWS + Q_ROWS, stride=8), :].T.astype(BF16)
        return carry

    lax.fori_loop(0, PAIRS // 8, one_octet, 0)


def source_h_rows(parts):
    (p1, p2, p3), (s1, s2, s3) = norm_parts(parts)
    high = [part[0] for part in parts]
    one = [part[2] for part in parts]
    two = [part[3] for part in parts]
    rows = dict(enumerate(high + [p1, p2, p3]))
    rows.update(enumerate(one + high + two + high + one + [s1, s2, s3], 9))
    return rows


def put_rows(ref, rows):
    for at, value in rows.items():
        ref[8 * at : 8 * at + 8, :] = value


def fill_constant_rows(ref, count):
    one = jnp.ones((8, 128), F32)
    zero = jnp.zeros((8, 128), F32)
    for at in range(count):
        ones = at in (6, 7, 8, 27, 28, 29) or at == V_AT + 3
        ref[8 * at : 8 * at + 8, :] = one if ones else zero


def cell_features(n_dom, n_sub, octet, cl_ref, cell_refs, ce_ref, cf_ref, cm_ref):
    ids = cl_ref[pl.ds(pl.multiple_of(8 * octet, 8), 8), :]
    lane = ids & 127
    owner = ids >> 7
    me = lax.axis_index("sub")

    def look_up(dom, shift, found):
        here = owner == dom * n_sub + lax.rem(me + n_sub - shift, n_sub)
        new = []
        for comp in range(CELL_COMPS):
            row = jnp.broadcast_to(cell_refs[shift][dom, comp : comp + 1, :], (8, 128))
            value = jnp.take_along_axis(row, lane, axis=1, mode="promise_in_bounds")
            new.append(jnp.where(here, value, found[comp]))
        return tuple(new)

    found = tuple(jnp.zeros((8, 128), F32) for _ in range(CELL_COMPS))
    if n_dom <= 8:
        for dom in range(n_dom):
            for shift in range(n_sub):
                found = look_up(dom, shift, found)
                yield
    else:

        def one_domain(dom, found):
            for shift in range(n_sub):
                found = look_up(dom, shift, found)
            return found

        found = lax.fori_loop(0, n_dom, one_domain, found)
    mass, cx, cy, cz, xx, yy, zz, xy, xz, yz = found
    yield "found"
    cm_ref[...] = mass
    rows8 = pl.ds(pl.multiple_of(8 * octet, 8), 8)
    cx, cy, cz = [value - ce_ref[comp, rows8, :] for comp, value in enumerate((cx, cy, cz))]
    put_rows(cf_ref, source_h_rows([grid_parts(value) for value in (cx, cy, cz)]))
    yield
    qx = xx * cx + xy * cy + xz * cz
    qy = xy * cx + yy * cy + yz * cz
    qz = xz * cx + yz * cy + zz * cz
    const = three_parts(2.5 * (qx * cx + qy * cy + qz * cz))
    linear = [-5.0 * qx, -5.0 * qy, -5.0 * qz]
    square = [2.5 * xx, 2.5 * yy, 2.5 * zz, 5.0 * xy, 5.0 * xz, 5.0 * yz]
    split = [three_parts(value) for value in linear + square]
    rows = []
    for which in (0, 1, 0, 2, 1, 0):
        rows += [part[which] for part in split]
    rows += list(const)
    put_rows(cf_ref, dict(enumerate(rows, Q_AT)))
    yield
    for comp, value in enumerate((cx, cy, cz)):
        for which, part in enumerate(three_parts(value)):
            cf_ref[8 * (V_AT + 4 * which + comp) : 8 * (V_AT + 4 * which + comp) + 8, :] = part
    yield
    columns = {name: three_parts(value) for name, value in dict(xx=xx, yy=yy, zz=zz, xy=xy, xz=xz, yz=yz, cx=qx, cy=qy, cz=qz).items()}
    order = (("xx", "xy", "xz"), ("xy", "yy", "yz"), ("xz", "yz", "zz"), ("cx", "cy", "cz"))
    for which in range(3):
        for column, names in enumerate(order):
            for row, name in enumerate(names):
                at = U_AT + 16 * which + 4 * column + row
                cf_ref[8 * at : 8 * at + 8, :] = columns[name][which]


def source_moments(group, ll_ref, tab_ref, ce_ref, raw_ref, sf_ref):
    left = lax.broadcasted_iota(jnp.int32, (4, 128), 1) < LEAF
    for pair in range(NLEAF // 2):
        first = tab_ref[ll_ref[2 * pair, group]]
        second = tab_ref[ll_ref[2 * pair + 1, group]]
        raw_ref[4 * pair : 4 * pair + 4, :] = jnp.where(left, first, second)
    value = [raw_ref[pl.ds(comp, 8, stride=4), :] for comp in range(4)]
    mass = value[3]
    centred = [value[comp] - ce_ref[comp, pl.ds(group, 1), :] for comp in range(3)]
    for comp, v in enumerate([mass * v for v in centred] + [mass]):
        for which, part in enumerate(three_parts(v)):
            at = 4 * which + comp
            sf_ref[8 * at : 8 * at + 8, :] = part


def transposed_dot(rows, weights):
    return lax.dot_general(rows, weights, (((1,), (1,)), ((), ())), preferred_element_type=F32)


def stacked(value):
    return jnp.concatenate(two_parts(value), axis=0)


def cell_group(sub, target, cf_ref, cm_ref):
    def cell_rows(at, count):
        return cf_ref[pl.ds(8 * at + sub, count, stride=8), :].astype(BF16)

    forms = jnp.concatenate(
        [
            jnp.concatenate([cell_rows(0, H_ROWS), jnp.zeros((H_ROWS, 128), BF16)], axis=1),
            jnp.concatenate([jnp.zeros((Q_ROWS, 128), BF16), cell_rows(Q_AT, Q_ROWS)], axis=1),
        ],
        axis=0,
    )
    forms = jnp.dot(target[:, 0 : H_ROWS + Q_ROWS], forms, preferred_element_type=F32)
    dist_sq, quad_form = forms[:, 0:128], forms[:, 128:256]
    inv = lax.rsqrt(dist_sq)
    inv_two = inv * inv
    inv_three = inv * inv_two
    pull = inv_three * (cm_ref[pl.ds(sub, 1), :] + quad_form * (inv_two * inv_two))
    moments = jnp.concatenate(
        [
            jnp.concatenate([cell_rows(V_AT, V_ROWS), jnp.zeros((V_ROWS, 128), BF16)], axis=1),
            jnp.concatenate([jnp.zeros((U_ROWS, 128), BF16), cell_rows(U_AT, U_ROWS)], axis=1),
        ],
        axis=0,
    )
    both = jnp.concatenate([stacked(pull), stacked(inv_three * inv_two)], axis=1)
    sums = transposed_dot(both, moments)
    return sums[0:LEAF] + sums[LEAF:]


def pair_lanes(pair):
    return pl.ds(pl.multiple_of(128 * pair, 128), 128)


def pair_place(tg_ref, pair):
    return tg_ref[pl.ds(pl.multiple_of(4 * pair, 4), 4), :]


def point_sums(sums, place):
    sums = sums[0:8] + sums[8:16]
    sums = sums + pltpu.roll(sums, 4, 0)
    return sums[0:3] - place[0:3] * sums[3:4]


def cell_pull(octet, tg_ref, ah_ref, cf_ref, cm_ref, out_ref):
    upper = lax.broadcasted_iota(jnp.int32, (8, 128), 0) < 4
    for inner in range(4):
        pair = octet * 4 + inner
        sums = []
        for half in range(2):
            sums.append(cell_group(2 * inner + half, ah_ref[pair, pl.ds(LEAF * half, LEAF), :], cf_ref, cm_ref))
            yield
        sums = jnp.concatenate(sums, axis=0).T
        place = pair_place(tg_ref, pair)
        x, y, z = [place[comp : comp + 1, :] for comp in range(3)]
        quads = sums[16:32] + sums[32:48] + sums[48:64]
        turned = quads[0:8] * jnp.where(upper, x, y) + quads[8:16] * jnp.where(upper, z, -1.0)
        turned = turned + pltpu.roll(turned, 4, 0)
        out_ref[:, pair_lanes(pair)] = point_sums(sums[0:16], place) + turned[0:3]


def put_block_pair(tab_ref, block, value):
    left = lax.broadcasted_iota(jnp.int32, (4, 128), 1) < LEAF
    turned = pltpu.roll(value, LEAF, 1)
    tab_ref[block] = jnp.where(left, value, turned)
    tab_ref[block + 1] = jnp.where(left, turned, value)


def put_eight_pairs(rows_ref, block, coords, feat_ref):
    put_rows(feat_ref, source_h_rows([grid_parts(value) for value in coords]))
    for pair in range(8):
        columns = feat_ref[pl.ds(pair, H_ROWS, stride=8), :].astype(BF16)
        spread = jnp.concatenate([columns] * 4, axis=0).T
        rows_ref[block + 2 * pair] = spread[0:LEAF]
        rows_ref[block + 2 * pair + 1] = spread[LEAF:]


def prepare_kernel(n_dom, n_sub, *refs):
    bundle_ref, near_refs, recv_ref = refs[0], refs[1:n_sub], refs[n_sub]
    tab_ref, rows_ref, at_ref, tg_ref, ce_ref, ah_ref, cl_ref, ll_ref, feat_ref, four_ref = refs[n_sub + 1 :]
    own_ref = bundle_ref.at[0:OWN_ROWS]
    cl_ref[...] = bundle_ref[OWN_ROWS : OWN_ROWS + LEAF_DEV, :].astype(jnp.int32)
    ll_ref[...] = bundle_ref[OWN_ROWS + LEAF_DEV :, :].astype(jnp.int32)
    for at in range(4):
        fill_constant_rows(four_ref.at[at], H_ROWS)
    me = lax.axis_index("sub")

    def near_blocks(shift, near_ref):
        seg = lax.rem(me + n_sub - shift, n_sub)

        def near(step, carry):
            for at in range(4):
                octet = 4 * step + at
                block = seg * LEAF_DEV + 16 * octet
                first = pl.multiple_of(32 * octet, 32)
                for pair in range(8):
                    put_block_pair(tab_ref, block + 2 * pair, near_ref[pl.ds(pl.multiple_of(first + 4 * pair, 4), 4), :])
                coords = [near_ref[pl.ds(first + comp, 8, stride=4), :] for comp in range(3)]
                put_eight_pairs(rows_ref, block, coords, four_ref.at[at])
            return carry

        lax.fori_loop(0, PAIRS // 32, near, 0)

    for shift in range(1, n_sub):
        near_blocks(shift, near_refs[shift - 1])
    far_tables(n_dom, n_sub * LEAF_DEV, recv_ref, tab_ref, rows_ref, four_ref)
    near_blocks(0, own_ref)
    target_features(own_ref, tg_ref, ce_ref, feat_ref, ah_ref)
    target_rows(own_ref, four_ref.at[0], at_ref)


def far_tables(n_dom, first_block, recv_ref, tab_ref, rows_ref, four_ref):
    me = lax.axis_index("dom")
    for two in range(RANGE):
        halves = []
        for slot in (2 * two, 2 * two + 1):
            source = me - OFFSETS[slot]
            inside = (source >= 0) & (source < n_dom)
            source = jnp.clip(source, 0, n_dom - 1)
            for unit in range(OUT_UNITS):
                value = jnp.where(inside, recv_ref[source, 4 * unit : 4 * unit + 4, :], 0.0)
                put_block_pair(tab_ref, first_block + slot * CAP + 2 * unit, value)
            halves.append([jnp.where(inside, recv_ref[source, pl.ds(comp, OUT_UNITS, stride=4), :], 0.0) for comp in range(3)])
        coords = [jnp.concatenate([one, other], axis=0) for one, other in zip(*halves)]
        put_eight_pairs(rows_ref, first_block + 2 * two * CAP, coords, four_ref.at[two])


def target_rows(own_ref, feat_ref, at_ref):
    one = jnp.ones((8, 128), F32)
    zero = jnp.zeros((8, 128), F32)

    def one_octet(octet, carry):
        parts = [grid_parts(own_ref[pl.ds(octet * 32 + comp, 8, stride=4), :]) for comp in range(3)]
        for at, value in enumerate(target_h_rows(parts, one, zero)):
            feat_ref[8 * at : 8 * at + 8, :] = value
        for pair in range(8):
            at_ref[octet * 8 + pair] = feat_ref[pl.ds(pair, H_ROWS, stride=8), :].astype(BF16)
        return carry

    lax.fori_loop(0, PAIRS // 8, one_octet, 0)


def run(strand, steps=None):
    taken = 0
    while steps is None or taken < steps:
        taken += 1
        if next(strand, "end") == "end":
            return


def pull_kernel(n_dom, n_sub, *refs):
    cell_refs = refs[:n_sub]
    tab_ref, rows_ref, at_ref, tg_ref, ce_ref, ah_ref, cl_ref, ll_in, out_ref = refs[n_sub : n_sub + 9]
    ll_ref, cf_ref, cm_ref, raw_ref, even_ref, odd_ref, dist_even, dist_odd, sem = refs[n_sub + 9 :]
    copy = pltpu.make_async_copy(ll_in, ll_ref, sem)
    copy.start()
    fill_constant_rows(cf_ref, CELL_ROWS)

    def build(octet):
        return cell_features(n_dom, n_sub, octet, cl_ref, cell_refs, ce_ref, cf_ref, cm_ref)

    run(build(0))
    copy.wait()
    nothing = jnp.zeros((8, 128), F32)
    for group in range(4):
        for at in range(12, V_ROWS):
            even_ref[group, 8 * at : 8 * at + 8, :] = nothing
            odd_ref[group, 8 * at : 8 * at + 8, :] = nothing
    left = lax.broadcasted_iota(jnp.int32, (V_ROWS, 128), 1) < LEAF
    left_target = lax.broadcasted_iota(jnp.int32, (H_ROWS, 128), 1) < LEAF
    owner = (lax.broadcasted_iota(jnp.int32, (LEAF, 128), 1) // H_ROWS).astype(BF16)
    lower_half, first_own, third_own = owner < 2.0, owner == 0.0, owner == 2.0

    def features(quad, raw_at, slot_ref):
        for group in range(4):
            source_moments(4 * quad + group, ll_ref, tab_ref, ce_ref, raw_ref.at[raw_at + group], slot_ref.at[group])
            yield

    def distances(quad, dist_ref):
        nothing = jnp.zeros((H_ROWS, 128), BF16)
        first, second = at_ref[2 * quad], at_ref[2 * quad + 1]
        targets = jnp.concatenate(
            [
                jnp.concatenate([jnp.where(left_target, first, nothing), nothing], axis=1),
                jnp.concatenate([jnp.where(left_target, nothing, first), nothing], axis=1),
                jnp.concatenate([nothing, jnp.where(left_target, second, nothing)], axis=1),
                jnp.concatenate([nothing, jnp.where(left_target, nothing, second)], axis=1),
            ],
            axis=0,
        )
        sources = []
        for j in range(NLEAF):
            rows = [rows_ref[ll_ref[j, 4 * quad + group]] for group in range(4)]
            low = jnp.where(first_own, rows[0], rows[1])
            high = jnp.where(third_own, rows[2], rows[3])
            sources.append(jnp.where(lower_half, low, high))
            if j % 8 == 7:
                rows = pl.ds(LEAF * (j - 7), 8 * LEAF)
                dist_ref[rows, :] = jnp.dot(jnp.concatenate(sources, axis=0), targets, preferred_element_type=F32)
                sources = []
                yield

    def pull(quad, slot_ref, dist_ref):
        total = jnp.zeros((4 * V_ROWS, 256), F32)
        for chunk in range(8):
            weights = stacked(jnp.exp2(-1.5 * jnp.log2(dist_ref[128 * chunk : 128 * chunk + 128, :])))
            rows = [slot_ref[group, pl.ds(chunk, V_ROWS, stride=8), :].astype(BF16) for group in range(4)]
            rows = jnp.concatenate(rows, axis=0)
            total += jnp.dot(jnp.concatenate([rows, rows], axis=1), weights, preferred_element_type=F32)
            yield
        for side in range(2):
            pair = 2 * quad + side
            at, columns = 2 * V_ROWS * side, slice(128 * side, 128 * side + 128)
            sums = jnp.where(left, total[at : at + V_ROWS, columns], total[at + V_ROWS : at + 2 * V_ROWS, columns])
            lanes = pair_lanes(pair)
            out_ref[:, lanes] = out_ref[:, lanes] + point_sums(sums, pair_place(tg_ref, pair))

    quads, octets = LEAF_DEV // 4, LEAF_DEV // 8
    run(features(0, 0, even_ref))
    run(distances(0, dist_even))

    def one_octet(octet, carry):
        quad = 2 * octet
        after = jnp.minimum(quad + 2, quads - 1)
        cells = cell_pull(octet, tg_ref, ah_ref, cf_ref, cm_ref, out_ref)
        coming = build(jnp.minimum(octet + 1, octets - 1))
        for half, (now, slot_ref, dist_ref, ahead, ahead_slot, ahead_dist, raw_at) in enumerate(
            (
                (quad, even_ref, dist_even, quad + 1, odd_ref, dist_odd, 4),
                (quad + 1, odd_ref, dist_odd, after, even_ref, dist_even, 0),
            )
        ):
            direct = pull(now, slot_ref, dist_ref)
            moments, distance = features(ahead, raw_at, ahead_slot), distances(ahead, ahead_dist)
            for step in range(8):
                if step in (1, 4):
                    run(distance, 1)
                run(direct, 1)
                if step % 2 == 0:
                    run(moments, 1)
                if half == 0 or step < 4:
                    run(coming, 3)
                    if step % 4 != 3:
                        run(cells, 1)
                elif step == 4:
                    run(cells)
                else:
                    run(coming, 1)
            run(moments)
            run(distance)
            run(direct)
        run(coming)
        return carry

    lax.fori_loop(0, octets, one_octet, 0)


def on_device(n_dom, n_sub, positions, masses, cell_mass, cell_center, cell_quad, cell_list, leaf_list, send_list, send_count):
    vmem = pl.BlockSpec(memory_space=pltpu.VMEM)
    smem = pl.BlockSpec(memory_space=pltpu.SMEM)
    anywhere = pl.BlockSpec(memory_space=pl.ANY)

    def limit(mib):
        return pltpu.CompilerParams(vmem_limit_bytes=mib * 1024 * 1024)

    ins = (
        positions,
        masses.reshape(1, -1),
        cell_mass.reshape(1, -1),
        cell_center,
        cell_quad,
        cell_list,
        leaf_list.T,
        send_list.reshape(2 * RANGE, CAP),
        send_count.reshape(1, 2 * RANGE),
    )
    bundle_rows = OWN_ROWS + LEAF_DEV + NLEAF
    packed, sent, bundle = pl.pallas_call(
        functools.partial(pack_kernel, n_dom),
        out_shape=(
            jax.ShapeDtypeStruct((OWN_ROWS, 128), F32),
            jax.ShapeDtypeStruct((n_dom, SENT_ROWS, 128), F32),
            jax.ShapeDtypeStruct((bundle_rows, 128), F32),
        ),
        in_specs=[pl.BlockSpec(memory_space=pltpu.HBM)] * 9,
        out_specs=[anywhere] * 3,
        scratch_shapes=[pltpu.VMEM(array.shape, array.dtype) for array in ins[:7]]
        + [pltpu.SMEM(array.shape, jnp.int32) for array in ins[7:]]
        + [
            pltpu.VMEM((bundle_rows, 128), F32),
            pltpu.VMEM((n_dom + 1, SENT_ROWS, 128), F32),
            pltpu.SemaphoreType.DMA((12,)),
        ],
        compiler_params=limit(63),
        name="pack_own",
    )(*ins)
    received = lax.all_to_all(sent, "dom", split_axis=0, concat_axis=0, tiled=True)

    def around(value):
        pieces = [value]
        for shift in range(1, n_sub):
            pieces.append(lax.ppermute(value, "sub", [(seg, (seg + shift) % n_sub) for seg in range(n_sub)]))
        return pieces

    nearby = around(packed)
    cells = around(received[:, OUT_ROWS:])
    n_blocks = n_sub * LEAF_DEV + 2 * RANGE * CAP
    prepared = pl.pallas_call(
        functools.partial(prepare_kernel, n_dom, n_sub),
        out_shape=(
            jax.ShapeDtypeStruct((n_blocks, 4, 128), F32),
            jax.ShapeDtypeStruct((n_blocks, LEAF, 128), BF16),
            jax.ShapeDtypeStruct((PAIRS, H_ROWS, 128), BF16),
            jax.ShapeDtypeStruct((OWN_ROWS, 128), F32),
            jax.ShapeDtypeStruct((3, LEAF_DEV, 128), F32),
            jax.ShapeDtypeStruct((PAIRS, 128, 128), BF16),
            jax.ShapeDtypeStruct((LEAF_DEV, NCELL), jnp.int32),
            jax.ShapeDtypeStruct((NLEAF, LEAF_DEV), jnp.int32),
        ),
        in_specs=[vmem] * (n_sub + 1),
        out_specs=[vmem] * 8,
        scratch_shapes=[
            pltpu.VMEM((8 * (H_ROWS + Q_ROWS), 128), F32),
            pltpu.VMEM((4, 8 * H_ROWS, 128), F32),
        ],
        compiler_params=limit(24),
        cost_estimate=pl.CostEstimate(flops=0, bytes_accessed=20_000_000, transcendentals=0),
        name="prepare",
    )(bundle, *nearby[1:], received)
    return pl.pallas_call(
        functools.partial(pull_kernel, n_dom, n_sub),
        out_shape=jax.ShapeDtypeStruct((3, LEAF_DEV * LEAF), F32),
        in_specs=[vmem] * (n_sub + 8),
        out_specs=vmem,
        scratch_shapes=[
            pltpu.SMEM((NLEAF, LEAF_DEV), jnp.int32),
            pltpu.VMEM((8 * CELL_ROWS, 128), F32),
            pltpu.VMEM((8, 128), F32),
            pltpu.VMEM((8, 32, 128), F32),
            pltpu.VMEM((4, 8 * V_ROWS, 128), F32),
            pltpu.VMEM((4, 8 * V_ROWS, 128), F32),
            pltpu.VMEM((NLEAF * LEAF, 256), F32),
            pltpu.VMEM((NLEAF * LEAF, 256), F32),
            pltpu.SemaphoreType.DMA(()),
        ],
        compiler_params=limit(24),
        name="pull",
    )(*cells, *prepared)


def solution(mesh):
    sharded = P(("dom", "sub"))
    return jax.shard_map(
        functools.partial(on_device, mesh.shape["dom"], mesh.shape["sub"]),
        mesh=mesh,
        in_specs=(
            P(None, ("dom", "sub")),
            sharded,
            sharded,
            P(None, ("dom", "sub")),
            P(None, ("dom", "sub")),
            P(("dom", "sub"), None),
            P(("dom", "sub"), None),
            P("dom", "sub", None, None),
            P("dom", "sub", None),
        ),
        out_specs=P(None, ("dom", "sub")),
        check_vma=False,
    )
```

```python
import functools

import jax
import jax.numpy as jnp
from jax import lax
from jax.experimental import pallas as pl
from jax.experimental.pallas import tpu as pltpu
from jax.sharding import PartitionSpec as P

LEAF = 64
LEAF_DEV = 128
NCELL = 128
NLEAF = 16
RANGE = 4
CAP = 8
PAIRS = LEAF_DEV // 2
OUT_UNITS = CAP // 2
OWN_ROWS = 4 * PAIRS
OUT_ROWS = 4 * OUT_UNITS
CELL_COMPS = 10
CELL_PAD = 16
SENT_ROWS = OUT_ROWS + CELL_PAD
OFFSETS = list(range(-RANGE, 0)) + list(range(1, RANGE + 1))

softening_sq = 0.0025
GRID_ROUND = 49152.0
F32 = jnp.float32
BF16 = jnp.bfloat16

H_ROWS = 32
Q_ROWS = 64
V_ROWS = 16
U_ROWS = 48
Q_AT = H_ROWS
V_AT = Q_AT + Q_ROWS
U_AT = V_AT + V_ROWS
CELL_ROWS = U_AT + U_ROWS
SOURCE_ROWS = H_ROWS + V_ROWS


def rounded(value):
    return value.astype(BF16).astype(F32)


def three_parts(value):
    first = rounded(value)
    rest = value - first
    second = rounded(rest)
    return first, second, rest - second


def two_parts(value):
    first = value.astype(BF16)
    return first, (value - first.astype(F32)).astype(BF16)


def grid_parts(value):
    high = (value + GRID_ROUND) - GRID_ROUND
    low = value - high
    first = rounded(low)
    return high, low, first, low - first


def norm_parts(parts, extra=None):
    big = sum(high * high for high, _, _, _ in parts)
    small = sum(low * (2.0 * high + low) for high, low, _, _ in parts)
    if extra is not None:
        small = small + extra
    return three_parts(big), three_parts(small)


def put_own(pos_ref, mass_ref, own_ref):
    for pair in range(PAIRS):
        lanes = pl.ds(128 * pair, 128)
        own_ref[4 * pair : 4 * pair + 3, :] = pos_ref[:, lanes]
        own_ref[4 * pair + 3 : 4 * pair + 4, :] = mass_ref[:, lanes]


def pack_kernel(n_dom, *refs):
    ins, outs, scratch, (out_ref, sent_ref, sems) = refs[:9], refs[9:12], refs[12:21], refs[21:]
    results = [
        pltpu.make_async_copy(out_ref.at[pl.ds(0, OWN_ROWS)], outs[0], sems.at[9]),
        pltpu.make_async_copy(sent_ref.at[pl.ds(0, n_dom)], outs[1], sems.at[10]),
        pltpu.make_async_copy(out_ref, outs[2], sems.at[11]),
    ]
    copies = [pltpu.make_async_copy(src, dst, sems.at[at]) for at, (src, dst) in enumerate(zip(ins, scratch))]
    for copy in copies:
        copy.start()
    pos_ref, mass_ref, cmass_ref, center_ref, quad_ref, cl_ref, ll_ref, list_ref, count_ref = scratch
    me = lax.axis_index("dom")
    left = lax.broadcasted_iota(jnp.int32, (4, 128), 1) < LEAF
    sent_ref[...] = jnp.zeros((n_dom + 1, SENT_ROWS, 128), F32)
    for copy in copies:
        copy.wait()
    put_own(pos_ref, mass_ref, out_ref)
    out_ref[OWN_ROWS : OWN_ROWS + LEAF_DEV, :] = cl_ref[...].astype(F32)
    out_ref[OWN_ROWS + LEAF_DEV :, :] = ll_ref[...].astype(F32)

    def put_cells(target, carry):
        sent_ref[target, OUT_ROWS : OUT_ROWS + 1, :] = cmass_ref[...]
        sent_ref[target, OUT_ROWS + 1 : OUT_ROWS + 4, :] = center_ref[...]
        sent_ref[target, OUT_ROWS + 4 : OUT_ROWS + 10, :] = quad_ref[...]
        return carry

    lax.fori_loop(0, n_dom, put_cells, 0)

    def half(slot, j, right):
        block = list_ref[slot, j]
        value = out_ref[pl.ds(pl.multiple_of(4 * (block // 2), 4), 4), :]
        value = jnp.where(j < count_ref[0, slot], value, 0.0)
        return jnp.where((block & 1) == right, value, pltpu.roll(value, LEAF, 1))

    for slot in range(2 * RANGE):
        target = me + OFFSETS[slot]
        target = jnp.where((target >= 0) & (target < n_dom), target, n_dom)
        for unit in range(OUT_UNITS):
            sent_ref[target, 4 * unit : 4 * unit + 4, :] = jnp.where(left, half(slot, 2 * unit, 0), half(slot, 2 * unit + 1, 1))
    for copy in results:
        copy.start()
    for copy in results:
        copy.wait()


def target_h_rows(parts, one, zero):
    big, small = norm_parts(parts, softening_sq)
    minus_high = [-2.0 * part[0] for part in parts]
    minus_one = [-2.0 * part[2] for part in parts]
    minus_two = [-2.0 * part[3] for part in parts]
    rows = minus_high + [one] * 3 + list(big) + minus_high + minus_one + minus_high
    return rows + minus_two + minus_one + [one] * 3 + list(small) + [zero] * 2


def target_features(own_ref, tg_ref, ce_ref, feat_ref, ah_ref):
    left = lax.broadcasted_iota(jnp.int32, (8, 128), 1) < LEAF
    one = jnp.ones((8, 128), F32)
    zero = jnp.zeros((8, 128), F32)
    raw_ref = tg_ref

    raw_ref[...] = own_ref[...]

    def one_octet(octet, carry):
        parts, centred = [], []
        for comp in range(3):
            rows = pl.ds(octet * 32 + comp, 8, stride=4)
            value = raw_ref[rows, :]
            first = jnp.broadcast_to(value[:, 0:1], (8, 128))
            second = jnp.broadcast_to(value[:, LEAF : LEAF + 1], (8, 128))
            ce_ref[comp, pl.ds(octet * 16, 8, stride=2), :] = first
            ce_ref[comp, pl.ds(octet * 16 + 1, 8, stride=2), :] = second
            value = value - jnp.where(left, first, second)
            raw_ref[rows, :] = value
            centred.append(value)
            parts.append(grid_parts(value))
        rows = target_h_rows(parts, one, zero)
        x, y, z = centred
        split = [three_parts(v) for v in (x, y, z, x * x, y * y, z * z, x * y, x * z, y * z)]
        for which in (0, 0, 1, 0, 1, 2):
            rows += [part[which] for part in split]
        rows += [one] * 3 + [zero] * 7
        for at, value in enumerate(rows):
            feat_ref[8 * at : 8 * at + 8, :] = value
        for sub in range(8):
            pair = octet * 8 + sub
            ah_ref[pair, :, 0 : H_ROWS + Q_ROWS] = feat_ref[pl.ds(sub, H_ROWS + Q_ROWS, stride=8), :].T.astype(BF16)
        return carry

    lax.fori_loop(0, PAIRS // 8, one_octet, 0)


def source_h_rows(parts):
    (p1, p2, p3), (s1, s2, s3) = norm_parts(parts)
    high = [part[0] for part in parts]
    one = [part[2] for part in parts]
    two = [part[3] for part in parts]
    rows = dict(enumerate(high + [p1, p2, p3]))
    rows.update(enumerate(one + high + two + high + one + [s1, s2, s3], 9))
    return rows


def put_rows(ref, rows):
    for at, value in rows.items():
        ref[8 * at : 8 * at + 8, :] = value


def fill_constant_rows(ref, count):
    one = jnp.ones((8, 128), F32)
    zero = jnp.zeros((8, 128), F32)
    for at in range(count):
        ones = at in (6, 7, 8, 27, 28, 29) or at == V_AT + 3
        ref[8 * at : 8 * at + 8, :] = one if ones else zero


def cell_features(n_dom, n_sub, octet, cl_ref, spread_ref, ce_ref, cf_ref, cm_ref):
    ids = cl_ref[pl.ds(pl.multiple_of(8 * octet, 8), 8), :]
    lane = ids & 127
    owner = ids >> 7
    me = lax.axis_index("sub")

    def look_up(dom, shift, found):
        here = owner == dom * n_sub + lax.rem(me + n_sub - shift, n_sub)
        new = []
        for comp in range(CELL_COMPS):
            value = jnp.take_along_axis(spread_ref[dom, shift, comp], lane, axis=1, mode="promise_in_bounds")
            new.append(jnp.where(here, value, found[comp]))
        return tuple(new)

    found = tuple(jnp.zeros((8, 128), F32) for _ in range(CELL_COMPS))
    if n_dom <= 8:
        for dom in range(n_dom):
            for shift in range(n_sub):
                found = look_up(dom, shift, found)
                yield
    else:

        def one_domain(dom, found):
            for shift in range(n_sub):
                found = look_up(dom, shift, found)
            return found

        found = lax.fori_loop(0, n_dom, one_domain, found)
    mass, cx, cy, cz, xx, yy, zz, xy, xz, yz = found
    yield "found"
    cm_ref[...] = mass
    rows8 = pl.ds(pl.multiple_of(8 * octet, 8), 8)
    cx, cy, cz = [value - ce_ref[comp, rows8, :] for comp, value in enumerate((cx, cy, cz))]
    put_rows(cf_ref, source_h_rows([grid_parts(value) for value in (cx, cy, cz)]))
    yield
    qx = xx * cx + xy * cy + xz * cz
    qy = xy * cx + yy * cy + yz * cz
    qz = xz * cx + yz * cy + zz * cz
    const = three_parts(2.5 * (qx * cx + qy * cy + qz * cz))
    linear = [-5.0 * qx, -5.0 * qy, -5.0 * qz]
    square = [2.5 * xx, 2.5 * yy, 2.5 * zz, 5.0 * xy, 5.0 * xz, 5.0 * yz]
    split = [three_parts(value) for value in linear + square]
    rows = []
    for which in (0, 1, 0, 2, 1, 0):
        rows += [part[which] for part in split]
    rows += list(const)
    put_rows(cf_ref, dict(enumerate(rows, Q_AT)))
    yield
    for comp, value in enumerate((cx, cy, cz)):
        for which, part in enumerate(three_parts(value)):
            cf_ref[8 * (V_AT + 4 * which + comp) : 8 * (V_AT + 4 * which + comp) + 8, :] = part
    yield
    columns = {name: three_parts(value) for name, value in dict(xx=xx, yy=yy, zz=zz, xy=xy, xz=xz, yz=yz, cx=qx, cy=qy, cz=qz).items()}
    order = (("xx", "xy", "xz"), ("xy", "yy", "yz"), ("xz", "yz", "zz"), ("cx", "cy", "cz"))
    for which in range(3):
        for column, names in enumerate(order):
            for row, name in enumerate(names):
                at = U_AT + 16 * which + 4 * column + row
                cf_ref[8 * at : 8 * at + 8, :] = columns[name][which]


def source_moments(group, ll_ref, tab_ref, ce_ref, raw_ref, sf_ref):
    left = lax.broadcasted_iota(jnp.int32, (4, 128), 1) < LEAF
    for pair in range(NLEAF // 2):
        first = tab_ref[ll_ref[2 * pair, group]]
        second = tab_ref[ll_ref[2 * pair + 1, group]]
        raw_ref[4 * pair : 4 * pair + 4, :] = jnp.where(left, first, second)
    value = [raw_ref[pl.ds(comp, 8, stride=4), :] for comp in range(4)]
    mass = value[3]
    centred = [value[comp] - ce_ref[comp, pl.ds(group, 1), :] for comp in range(3)]
    for comp, v in enumerate([mass * v for v in centred] + [mass]):
        for which, part in enumerate(three_parts(v)):
            at = 4 * which + comp
            sf_ref[8 * at : 8 * at + 8, :] = part


def transposed_dot(rows, weights):
    return lax.dot_general(rows, weights, (((1,), (1,)), ((), ())), preferred_element_type=F32)


def stacked(value):
    return jnp.concatenate(two_parts(value), axis=0)


def cell_group(sub, target, cf_ref, cm_ref):
    def cell_rows(at, count):
        return cf_ref[pl.ds(8 * at + sub, count, stride=8), :].astype(BF16)

    forms = jnp.concatenate(
        [
            jnp.concatenate([cell_rows(0, H_ROWS), jnp.zeros((H_ROWS, 128), BF16)], axis=1),
            jnp.concatenate([jnp.zeros((Q_ROWS, 128), BF16), cell_rows(Q_AT, Q_ROWS)], axis=1),
        ],
        axis=0,
    )
    forms = jnp.dot(target[:, 0 : H_ROWS + Q_ROWS], forms, preferred_element_type=F32)
    dist_sq, quad_form = forms[:, 0:128], forms[:, 128:256]
    inv = lax.rsqrt(dist_sq)
    inv_two = inv * inv
    inv_three = inv * inv_two
    pull = inv_three * (cm_ref[pl.ds(sub, 1), :] + quad_form * (inv_two * inv_two))
    moments = jnp.concatenate(
        [
            jnp.concatenate([cell_rows(V_AT, V_ROWS), jnp.zeros((V_ROWS, 128), BF16)], axis=1),
            jnp.concatenate([jnp.zeros((U_ROWS, 128), BF16), cell_rows(U_AT, U_ROWS)], axis=1),
        ],
        axis=0,
    )
    both = jnp.concatenate([stacked(pull), stacked(inv_three * inv_two)], axis=1)
    return both, moments


def pair_lanes(pair):
    return pl.ds(pl.multiple_of(128 * pair, 128), 128)


def pair_place(tg_ref, pair):
    return tg_ref[pl.ds(pl.multiple_of(4 * pair, 4), 4), :]


def point_sums(sums, place):
    sums = sums[0:8] + sums[8:16]
    sums = sums + pltpu.roll(sums, 4, 0)
    return sums[0:3] - place[0:3] * sums[3:4]


def cell_pull(octet, tg_ref, ah_ref, cf_ref, cm_ref, out_ref):
    upper = lax.broadcasted_iota(jnp.int32, (8, 128), 0) < 4
    left = lax.broadcasted_iota(jnp.int32, (LEAF, 128), 1) < LEAF
    for inner in range(4):
        pair = octet * 4 + inner
        first, first_moments = cell_group(2 * inner, ah_ref[pair, 0:LEAF, :], cf_ref, cm_ref)
        yield
        second, second_moments = cell_group(2 * inner + 1, ah_ref[pair, LEAF:, :], cf_ref, cm_ref)
        moments = jnp.concatenate([first_moments, second_moments], axis=0)
        sums = transposed_dot(jnp.concatenate([first, second], axis=0), moments)
        yield
        sums = jnp.where(left, sums[0:64] + sums[64:128], sums[128:192] + sums[192:256]).T
        sums = jnp.concatenate([sums[0:64], sums[64:128]], axis=1)
        place = pair_place(tg_ref, pair)
        x, y, z = [place[comp : comp + 1, :] for comp in range(3)]
        quads = sums[16:32] + sums[32:48] + sums[48:64]
        turned = quads[0:8] * jnp.where(upper, x, y) + quads[8:16] * jnp.where(upper, z, -1.0)
        turned = turned + pltpu.roll(turned, 4, 0)
        out_ref[:, pair_lanes(pair)] = point_sums(sums[0:16], place) + turned[0:3]


def put_block_pair(tab_ref, block, value):
    left = lax.broadcasted_iota(jnp.int32, (4, 128), 1) < LEAF
    turned = pltpu.roll(value, LEAF, 1)
    tab_ref[block] = jnp.where(left, value, turned)
    tab_ref[block + 1] = jnp.where(left, turned, value)


def put_eight_pairs(rows_ref, block, coords, feat_ref):
    put_rows(feat_ref, source_h_rows([grid_parts(value) for value in coords]))
    for pair in range(8):
        columns = feat_ref[pl.ds(pair, H_ROWS, stride=8), :].astype(BF16)
        spread = jnp.concatenate([columns] * 4, axis=0).T
        rows_ref[block + 2 * pair] = spread[0:LEAF]
        rows_ref[block + 2 * pair + 1] = spread[LEAF:]


def prepare_kernel(n_dom, n_sub, *refs):
    bundle_ref, near_refs, recv_ref = refs[0], refs[1:n_sub], refs[n_sub]
    tab_ref, rows_ref, at_ref, tg_ref, ce_ref, ah_ref, cl_ref, ll_ref, feat_ref, four_ref = refs[n_sub + 1 :]
    own_ref = bundle_ref.at[0:OWN_ROWS]
    cl_ref[...] = bundle_ref[OWN_ROWS : OWN_ROWS + LEAF_DEV, :].astype(jnp.int32)
    ll_ref[...] = bundle_ref[OWN_ROWS + LEAF_DEV :, :].astype(jnp.int32)
    for at in range(4):
        fill_constant_rows(four_ref.at[at], H_ROWS)
    me = lax.axis_index("sub")

    def near_blocks(shift, near_ref):
        seg = lax.rem(me + n_sub - shift, n_sub)

        def near(step, carry):
            for at in range(4):
                octet = 4 * step + at
                block = seg * LEAF_DEV + 16 * octet
                first = pl.multiple_of(32 * octet, 32)
                for pair in range(8):
                    put_block_pair(tab_ref, block + 2 * pair, near_ref[pl.ds(pl.multiple_of(first + 4 * pair, 4), 4), :])
                coords = [near_ref[pl.ds(first + comp, 8, stride=4), :] for comp in range(3)]
                put_eight_pairs(rows_ref, block, coords, four_ref.at[at])
            return carry

        lax.fori_loop(0, PAIRS // 32, near, 0)

    for shift in range(1, n_sub):
        near_blocks(shift, near_refs[shift - 1])
    far_tables(n_dom, n_sub * LEAF_DEV, recv_ref, tab_ref, rows_ref, four_ref)
    near_blocks(0, own_ref)
    target_features(own_ref, tg_ref, ce_ref, feat_ref, ah_ref)
    target_rows(own_ref, four_ref.at[0], at_ref)


def far_tables(n_dom, first_block, recv_ref, tab_ref, rows_ref, four_ref):
    me = lax.axis_index("dom")
    for two in range(RANGE):
        halves = []
        for slot in (2 * two, 2 * two + 1):
            source = me - OFFSETS[slot]
            inside = (source >= 0) & (source < n_dom)
            source = jnp.clip(source, 0, n_dom - 1)
            for unit in range(OUT_UNITS):
                value = jnp.where(inside, recv_ref[source, 4 * unit : 4 * unit + 4, :], 0.0)
                put_block_pair(tab_ref, first_block + slot * CAP + 2 * unit, value)
            halves.append([jnp.where(inside, recv_ref[source, pl.ds(comp, OUT_UNITS, stride=4), :], 0.0) for comp in range(3)])
        coords = [jnp.concatenate([one, other], axis=0) for one, other in zip(*halves)]
        put_eight_pairs(rows_ref, first_block + 2 * two * CAP, coords, four_ref.at[two])


def target_rows(own_ref, feat_ref, at_ref):
    one = jnp.ones((8, 128), F32)
    zero = jnp.zeros((8, 128), F32)

    def one_octet(octet, carry):
        parts = [grid_parts(own_ref[pl.ds(octet * 32 + comp, 8, stride=4), :]) for comp in range(3)]
        for at, value in enumerate(target_h_rows(parts, one, zero)):
            feat_ref[8 * at : 8 * at + 8, :] = value
        for pair in range(8):
            at_ref[octet * 8 + pair] = feat_ref[pl.ds(pair, H_ROWS, stride=8), :].astype(BF16)
        return carry

    lax.fori_loop(0, PAIRS // 8, one_octet, 0)


def run(strand, steps=None):
    taken = 0
    while steps is None or taken < steps:
        taken += 1
        if next(strand, "end") == "end":
            return


def pull_kernel(n_dom, n_sub, *refs):
    cell_refs = refs[:n_sub]
    tab_ref, rows_ref, at_ref, tg_ref, ce_ref, ah_ref, cl_ref, ll_in, out_ref = refs[n_sub : n_sub + 9]
    ll_ref, spread_ref, cf_ref, cm_ref, raw_ref, even_ref, odd_ref, dist_even, dist_odd, sem = refs[n_sub + 9 :]
    copy = pltpu.make_async_copy(ll_in, ll_ref, sem)
    copy.start()
    fill_constant_rows(cf_ref, CELL_ROWS)

    def build(octet):
        return cell_features(n_dom, n_sub, octet, cl_ref, spread_ref, ce_ref, cf_ref, cm_ref)

    def spread(dom, carry):
        for shift in range(n_sub):
            for comp in range(CELL_COMPS):
                row = cell_refs[shift][dom, comp : comp + 1, :]
                spread_ref[dom, shift, comp] = jnp.broadcast_to(row, (8, 128))
        return carry

    lax.fori_loop(0, n_dom, spread, 0)

    run(build(0))
    copy.wait()
    nothing = jnp.zeros((8, 128), F32)
    for group in range(4):
        for at in range(12, V_ROWS):
            even_ref[group, 8 * at : 8 * at + 8, :] = nothing
            odd_ref[group, 8 * at : 8 * at + 8, :] = nothing
    left = lax.broadcasted_iota(jnp.int32, (V_ROWS, 128), 1) < LEAF
    left_target = lax.broadcasted_iota(jnp.int32, (H_ROWS, 128), 1) < LEAF
    owner = (lax.broadcasted_iota(jnp.int32, (LEAF, 128), 1) // H_ROWS).astype(BF16)
    lower_half, first_own, third_own = owner < 2.0, owner == 0.0, owner == 2.0

    def features(quad, raw_at, slot_ref):
        for group in range(4):
            source_moments(4 * quad + group, ll_ref, tab_ref, ce_ref, raw_ref.at[raw_at + group], slot_ref.at[group])
            yield

    def distances(quad, dist_ref):
        nothing = jnp.zeros((H_ROWS, 128), BF16)
        first, second = at_ref[2 * quad], at_ref[2 * quad + 1]
        targets = jnp.concatenate(
            [
                jnp.concatenate([jnp.where(left_target, first, nothing), nothing], axis=1),
                jnp.concatenate([jnp.where(left_target, nothing, first), nothing], axis=1),
                jnp.concatenate([nothing, jnp.where(left_target, second, nothing)], axis=1),
                jnp.concatenate([nothing, jnp.where(left_target, nothing, second)], axis=1),
            ],
            axis=0,
        )
        sources = []
        for j in range(NLEAF):
            rows = [rows_ref[ll_ref[j, 4 * quad + group]] for group in range(4)]
            low = jnp.where(first_own, rows[0], rows[1])
            high = jnp.where(third_own, rows[2], rows[3])
            sources.append(jnp.where(lower_half, low, high))
            if j % 8 == 7:
                rows = pl.ds(LEAF * (j - 7), 8 * LEAF)
                dist_ref[rows, :] = jnp.dot(jnp.concatenate(sources, axis=0), targets, preferred_element_type=F32)
                sources = []
                yield

    def pull(quad, slot_ref, dist_ref):
        total = jnp.zeros((4 * V_ROWS, 256), F32)
        for chunk in range(8):
            inv = lax.rsqrt(dist_ref[128 * chunk : 128 * chunk + 128, :])
            weights = stacked(inv * inv * inv)
            rows = [slot_ref[group, pl.ds(chunk, V_ROWS, stride=8), :].astype(BF16) for group in range(4)]
            rows = jnp.concatenate(rows, axis=0)
            total += jnp.dot(jnp.concatenate([rows, rows], axis=1), weights, preferred_element_type=F32)
            yield
        for side in range(2):
            pair = 2 * quad + side
            at, columns = 2 * V_ROWS * side, slice(128 * side, 128 * side + 128)
            sums = jnp.where(left, total[at : at + V_ROWS, columns], total[at + V_ROWS : at + 2 * V_ROWS, columns])
            lanes = pair_lanes(pair)
            out_ref[:, lanes] = out_ref[:, lanes] + point_sums(sums, pair_place(tg_ref, pair))

    quads, octets = LEAF_DEV // 4, LEAF_DEV // 8
    run(features(0, 0, even_ref))
    run(distances(0, dist_even))

    def one_octet(octet, carry):
        quad = 2 * octet
        after = jnp.minimum(quad + 2, quads - 1)
        cells = cell_pull(octet, tg_ref, ah_ref, cf_ref, cm_ref, out_ref)
        coming = build(jnp.minimum(octet + 1, octets - 1))
        for half, (now, slot_ref, dist_ref, ahead, ahead_slot, ahead_dist, raw_at) in enumerate(
            (
                (quad, even_ref, dist_even, quad + 1, odd_ref, dist_odd, 4),
                (quad + 1, odd_ref, dist_odd, after, even_ref, dist_even, 0),
            )
        ):
            direct = pull(now, slot_ref, dist_ref)
            moments, distance = features(ahead, raw_at, ahead_slot), distances(ahead, ahead_dist)
            for step in range(8):
                if step in (1, 4):
                    run(distance, 1)
                run(direct, 1)
                if step % 2 == 0:
                    run(moments, 1)
                if half == 0 or step < 4:
                    run(coming, 3)
                    if step % 4 != 3:
                        run(cells, 1)
                elif step == 4:
                    run(cells)
                else:
                    run(coming, 1)
            run(moments)
            run(distance)
            run(direct)
        run(coming)
        return carry

    lax.fori_loop(0, octets, one_octet, 0)


def on_device(n_dom, n_sub, positions, masses, cell_mass, cell_center, cell_quad, cell_list, leaf_list, send_list, send_count):
    vmem = pl.BlockSpec(memory_space=pltpu.VMEM)
    smem = pl.BlockSpec(memory_space=pltpu.SMEM)
    anywhere = pl.BlockSpec(memory_space=pl.ANY)

    def limit(mib):
        return pltpu.CompilerParams(vmem_limit_bytes=mib * 1024 * 1024)

    ins = (
        positions,
        masses.reshape(1, -1),
        cell_mass.reshape(1, -1),
        cell_center,
        cell_quad,
        cell_list,
        leaf_list.T,
        send_list.reshape(2 * RANGE, CAP),
        send_count.reshape(1, 2 * RANGE),
    )
    bundle_rows = OWN_ROWS + LEAF_DEV + NLEAF
    packed, sent, bundle = pl.pallas_call(
        functools.partial(pack_kernel, n_dom),
        out_shape=(
            jax.ShapeDtypeStruct((OWN_ROWS, 128), F32),
            jax.ShapeDtypeStruct((n_dom, SENT_ROWS, 128), F32),
            jax.ShapeDtypeStruct((bundle_rows, 128), F32),
        ),
        in_specs=[pl.BlockSpec(memory_space=pltpu.HBM)] * 9,
        out_specs=[anywhere] * 3,
        scratch_shapes=[pltpu.VMEM(array.shape, array.dtype) for array in ins[:7]]
        + [pltpu.SMEM(array.shape, jnp.int32) for array in ins[7:]]
        + [
            pltpu.VMEM((bundle_rows, 128), F32),
            pltpu.VMEM((n_dom + 1, SENT_ROWS, 128), F32),
            pltpu.SemaphoreType.DMA((12,)),
        ],
        compiler_params=limit(63),
        name="pack_own",
    )(*ins)
    received = lax.all_to_all(sent, "dom", split_axis=0, concat_axis=0, tiled=True)

    def around(value):
        pieces = [value]
        for shift in range(1, n_sub):
            pieces.append(lax.ppermute(value, "sub", [(seg, (seg + shift) % n_sub) for seg in range(n_sub)]))
        return pieces

    nearby = around(packed)
    cells = around(received[:, OUT_ROWS:])
    n_blocks = n_sub * LEAF_DEV + 2 * RANGE * CAP
    prepared = pl.pallas_call(
        functools.partial(prepare_kernel, n_dom, n_sub),
        out_shape=(
            jax.ShapeDtypeStruct((n_blocks, 4, 128), F32),
            jax.ShapeDtypeStruct((n_blocks, LEAF, 128), BF16),
            jax.ShapeDtypeStruct((PAIRS, H_ROWS, 128), BF16),
            jax.ShapeDtypeStruct((OWN_ROWS, 128), F32),
            jax.ShapeDtypeStruct((3, LEAF_DEV, 128), F32),
            jax.ShapeDtypeStruct((PAIRS, 128, 128), BF16),
            jax.ShapeDtypeStruct((LEAF_DEV, NCELL), jnp.int32),
            jax.ShapeDtypeStruct((NLEAF, LEAF_DEV), jnp.int32),
        ),
        in_specs=[vmem] * (n_sub + 1),
        out_specs=[vmem] * 8,
        scratch_shapes=[
            pltpu.VMEM((8 * (H_ROWS + Q_ROWS), 128), F32),
            pltpu.VMEM((4, 8 * H_ROWS, 128), F32),
        ],
        compiler_params=limit(24),
        cost_estimate=pl.CostEstimate(flops=0, bytes_accessed=20_000_000, transcendentals=0),
        name="prepare",
    )(bundle, *nearby[1:], received)
    return pl.pallas_call(
        functools.partial(pull_kernel, n_dom, n_sub),
        out_shape=jax.ShapeDtypeStruct((3, LEAF_DEV * LEAF), F32),
        in_specs=[vmem] * (n_sub + 8),
        out_specs=vmem,
        scratch_shapes=[
            pltpu.SMEM((NLEAF, LEAF_DEV), jnp.int32),
            pltpu.VMEM((n_dom, n_sub, CELL_COMPS, 8, 128), F32),
            pltpu.VMEM((8 * CELL_ROWS, 128), F32),
            pltpu.VMEM((8, 128), F32),
            pltpu.VMEM((8, 32, 128), F32),
            pltpu.VMEM((4, 8 * V_ROWS, 128), F32),
            pltpu.VMEM((4, 8 * V_ROWS, 128), F32),
            pltpu.VMEM((NLEAF * LEAF, 256), F32),
            pltpu.VMEM((NLEAF * LEAF, 256), F32),
            pltpu.SemaphoreType.DMA(()),
        ],
        compiler_params=limit(24),
        name="pull",
    )(*cells, *prepared)


def solution(mesh):
    sharded = P(("dom", "sub"))
    return jax.shard_map(
        functools.partial(on_device, mesh.shape["dom"], mesh.shape["sub"]),
        mesh=mesh,
        in_specs=(
            P(None, ("dom", "sub")),
            sharded,
            sharded,
            P(None, ("dom", "sub")),
            P(None, ("dom", "sub")),
            P(("dom", "sub"), None),
            P(("dom", "sub"), None),
            P("dom", "sub", None, None),
            P("dom", "sub", None),
        ),
        out_specs=P(None, ("dom", "sub")),
        check_vma=False,
    )
```

```python
import functools

import jax
import jax.numpy as jnp
from jax import lax
from jax.experimental import pallas as pl
from jax.experimental.pallas import tpu as pltpu
from jax.sharding import PartitionSpec as P

LEAF = 64
LEAF_DEV = 128
NCELL = 128
NLEAF = 16
RANGE = 4
CAP = 8
PAIRS = LEAF_DEV // 2
OUT_UNITS = CAP // 2
OWN_ROWS = 4 * PAIRS
OUT_ROWS = 4 * OUT_UNITS
CELL_COMPS = 10
CELL_PAD = 16
SENT_ROWS = OUT_ROWS + CELL_PAD
OFFSETS = list(range(-RANGE, 0)) + list(range(1, RANGE + 1))

softening_sq = 0.0025
GRID_ROUND = 49152.0
F32 = jnp.float32
BF16 = jnp.bfloat16

H_ROWS = 32
Q_ROWS = 64
V_ROWS = 16
U_ROWS = 48
Q_AT = H_ROWS
V_AT = Q_AT + Q_ROWS
U_AT = V_AT + V_ROWS
CELL_ROWS = U_AT + U_ROWS
M_ROWS = 8


def rounded(value):
    return value.astype(BF16).astype(F32)


def three_parts(value):
    first = rounded(value)
    rest = value - first
    second = rounded(rest)
    return first, second, rest - second


def two_parts(value):
    first = value.astype(BF16)
    return first, (value - first.astype(F32)).astype(BF16)


def grid_parts(value):
    high = (value + GRID_ROUND) - GRID_ROUND
    low = value - high
    first = rounded(low)
    return high, low, first, low - first


def norm_parts(parts, extra=None):
    big = sum(high * high for high, _, _, _ in parts)
    small = sum(low * (2.0 * high + low) for high, low, _, _ in parts)
    if extra is not None:
        small = small + extra
    return three_parts(big), three_parts(small)


def put_own(pos_ref, mass_ref, own_ref):
    for pair in range(PAIRS):
        lanes = pl.ds(128 * pair, 128)
        own_ref[4 * pair : 4 * pair + 3, :] = pos_ref[:, lanes]
        own_ref[4 * pair + 3 : 4 * pair + 4, :] = mass_ref[:, lanes]


def pack_kernel(n_dom, *refs):
    ins, outs, scratch, (out_ref, sent_ref, sems) = refs[:9], refs[9:12], refs[12:21], refs[21:]
    results = [
        pltpu.make_async_copy(out_ref.at[pl.ds(0, OWN_ROWS)], outs[0], sems.at[9]),
        pltpu.make_async_copy(sent_ref.at[pl.ds(0, n_dom)], outs[1], sems.at[10]),
        pltpu.make_async_copy(out_ref, outs[2], sems.at[11]),
    ]
    copies = [pltpu.make_async_copy(src, dst, sems.at[at]) for at, (src, dst) in enumerate(zip(ins, scratch))]
    for copy in copies:
        copy.start()
    pos_ref, mass_ref, cmass_ref, center_ref, quad_ref, cl_ref, ll_ref, list_ref, count_ref = scratch
    me = lax.axis_index("dom")
    left = lax.broadcasted_iota(jnp.int32, (4, 128), 1) < LEAF
    sent_ref[...] = jnp.zeros((n_dom + 1, SENT_ROWS, 128), F32)
    for copy in copies:
        copy.wait()
    put_own(pos_ref, mass_ref, out_ref)
    out_ref[OWN_ROWS : OWN_ROWS + LEAF_DEV, :] = cl_ref[...].astype(F32)
    out_ref[OWN_ROWS + LEAF_DEV :, :] = ll_ref[...].astype(F32)

    def put_cells(target, carry):
        sent_ref[target, OUT_ROWS : OUT_ROWS + 1, :] = cmass_ref[...]
        sent_ref[target, OUT_ROWS + 1 : OUT_ROWS + 4, :] = center_ref[...]
        sent_ref[target, OUT_ROWS + 4 : OUT_ROWS + 10, :] = quad_ref[...]
        return carry

    lax.fori_loop(0, n_dom, put_cells, 0)

    def half(slot, j, right):
        block = list_ref[slot, j]
        value = out_ref[pl.ds(pl.multiple_of(4 * (block // 2), 4), 4), :]
        value = jnp.where(j < count_ref[0, slot], value, 0.0)
        return jnp.where((block & 1) == right, value, pltpu.roll(value, LEAF, 1))

    for slot in range(2 * RANGE):
        target = me + OFFSETS[slot]
        target = jnp.where((target >= 0) & (target < n_dom), target, n_dom)
        for unit in range(OUT_UNITS):
            sent_ref[target, 4 * unit : 4 * unit + 4, :] = jnp.where(left, half(slot, 2 * unit, 0), half(slot, 2 * unit + 1, 1))
    for copy in results:
        copy.start()
    for copy in results:
        copy.wait()


def target_h_rows(parts, one, zero):
    big, small = norm_parts(parts, softening_sq)
    minus_high = [-2.0 * part[0] for part in parts]
    minus_one = [-2.0 * part[2] for part in parts]
    minus_two = [-2.0 * part[3] for part in parts]
    rows = minus_high + [one] * 3 + list(big) + minus_high + minus_one + minus_high
    return rows + minus_two + minus_one + [one] * 3 + list(small) + [zero] * 2


def target_features(octet, tg_ref, ce_ref, feat_ref, ah_ref):
    left = lax.broadcasted_iota(jnp.int32, (8, 128), 1) < LEAF
    one = jnp.ones((8, 128), F32)
    zero = jnp.zeros((8, 128), F32)
    parts, centred = [], []
    for comp in range(3):
        rows = pl.ds(octet * 32 + comp, 8, stride=4)
        value = tg_ref[rows, :]
        first = jnp.broadcast_to(value[:, 0:1], (8, 128))
        second = jnp.broadcast_to(value[:, LEAF : LEAF + 1], (8, 128))
        ce_ref[comp, pl.ds(octet * 16, 8, stride=2), :] = first
        ce_ref[comp, pl.ds(octet * 16 + 1, 8, stride=2), :] = second
        value = value - jnp.where(left, first, second)
        tg_ref[rows, :] = value
        centred.append(value)
        parts.append(grid_parts(value))
    rows = target_h_rows(parts, one, zero)
    x, y, z = centred
    split = [three_parts(v) for v in (x, y, z, x * x, y * y, z * z, x * y, x * z, y * z)]
    for which in (0, 0, 1, 0, 1, 2):
        rows += [part[which] for part in split]
    rows += [one] * 3 + [zero] * 7
    for at, value in enumerate(rows):
        feat_ref[8 * at : 8 * at + 8, :] = value
    for sub in range(8):
        features = feat_ref[pl.ds(sub, H_ROWS + Q_ROWS, stride=8), :].T.astype(BF16)
        ah_ref[octet * 8 + sub, :, 0 : H_ROWS + Q_ROWS] = features


def source_h_rows(parts):
    (p1, p2, p3), (s1, s2, s3) = norm_parts(parts)
    high = [part[0] for part in parts]
    one = [part[2] for part in parts]
    two = [part[3] for part in parts]
    rows = dict(enumerate(high + [p1, p2, p3]))
    rows.update(enumerate(one + high + two + high + one + [s1, s2, s3], 9))
    return rows


def put_rows(ref, rows):
    for at, value in rows.items():
        ref[8 * at : 8 * at + 8, :] = value


def fill_constant_rows(ref, count):
    one = jnp.ones((8, 128), F32)
    zero = jnp.zeros((8, 128), F32)
    for at in range(count):
        ones = at in (6, 7, 8, 27, 28, 29) or at == V_AT + 3
        ref[8 * at : 8 * at + 8, :] = one if ones else zero


def cell_features(n_dom, n_sub, octet, cl_ref, spread_ref, ce_ref, cf_ref, cm_ref):
    ids = cl_ref[pl.ds(pl.multiple_of(8 * octet, 8), 8), :]
    lane = ids & 127
    owner = ids >> 7
    me = lax.axis_index("sub")

    def look_up(dom, shift, found):
        here = owner == dom * n_sub + lax.rem(me + n_sub - shift, n_sub)
        new = []
        for comp in range(CELL_COMPS):
            value = jnp.take_along_axis(spread_ref[dom, shift, comp], lane, axis=1, mode="promise_in_bounds")
            new.append(jnp.where(here, value, found[comp]))
        return tuple(new)

    found = tuple(jnp.zeros((8, 128), F32) for _ in range(CELL_COMPS))
    if n_dom <= 8:
        for dom in range(n_dom):
            for shift in range(n_sub):
                found = look_up(dom, shift, found)
                yield
    else:

        def one_domain(dom, found):
            for shift in range(n_sub):
                found = look_up(dom, shift, found)
            return found

        found = lax.fori_loop(0, n_dom, one_domain, found)
    mass, cx, cy, cz, xx, yy, zz, xy, xz, yz = found
    yield "found"
    cm_ref[...] = mass
    rows8 = pl.ds(pl.multiple_of(8 * octet, 8), 8)
    cx, cy, cz = [value - ce_ref[comp, rows8, :] for comp, value in enumerate((cx, cy, cz))]
    put_rows(cf_ref, source_h_rows([grid_parts(value) for value in (cx, cy, cz)]))
    yield
    qx = xx * cx + xy * cy + xz * cz
    qy = xy * cx + yy * cy + yz * cz
    qz = xz * cx + yz * cy + zz * cz
    const = three_parts(2.5 * (qx * cx + qy * cy + qz * cz))
    linear = [-5.0 * qx, -5.0 * qy, -5.0 * qz]
    square = [2.5 * xx, 2.5 * yy, 2.5 * zz, 5.0 * xy, 5.0 * xz, 5.0 * yz]
    split = [three_parts(value) for value in linear + square]
    rows = []
    for which in (0, 1, 0, 2, 1, 0):
        rows += [part[which] for part in split]
    rows += list(const)
    put_rows(cf_ref, dict(enumerate(rows, Q_AT)))
    yield
    for comp, value in enumerate((cx, cy, cz)):
        for which, part in enumerate(three_parts(value)):
            cf_ref[8 * (V_AT + 4 * which + comp) : 8 * (V_AT + 4 * which + comp) + 8, :] = part
    yield
    columns = {name: three_parts(value) for name, value in dict(xx=xx, yy=yy, zz=zz, xy=xy, xz=xz, yz=yz, cx=qx, cy=qy, cz=qz).items()}
    order = (("xx", "xy", "xz"), ("xy", "yy", "yz"), ("xz", "yz", "zz"), ("cx", "cy", "cz"))
    for which in range(3):
        for column, names in enumerate(order):
            for row, name in enumerate(names):
                at = U_AT + 16 * which + 4 * column + row
                cf_ref[8 * at : 8 * at + 8, :] = columns[name][which]


def source_moments(group, ll_ref, tab_ref, ce_ref, raw_ref, sf_ref):
    left = lax.broadcasted_iota(jnp.int32, (4, 128), 1) < LEAF
    for pair in range(NLEAF // 2):
        first = tab_ref[ll_ref[2 * pair, group]]
        second = tab_ref[ll_ref[2 * pair + 1, group]]
        raw_ref[4 * pair : 4 * pair + 4, :] = jnp.where(left, first, second)
    value = [raw_ref[pl.ds(comp, 8, stride=4), :] for comp in range(4)]
    mass = value[3]
    centred = [value[comp] - ce_ref[comp, pl.ds(group, 1), :] for comp in range(3)]
    for comp, v in enumerate([mass * v for v in centred] + [mass]):
        high = rounded(v)
        for which, part in enumerate((high, v - high)):
            at = 4 * which + comp
            sf_ref[8 * at : 8 * at + 8, :] = part


def transposed_dot(rows, weights):
    return lax.dot_general(rows, weights, (((1,), (1,)), ((), ())), preferred_element_type=F32)


def stacked(value):
    return jnp.concatenate(two_parts(value), axis=0)


def cell_group(sub, target, cf_ref, cm_ref):
    def cell_rows(at, count):
        return cf_ref[pl.ds(8 * at + sub, count, stride=8), :].astype(BF16)

    forms = jnp.concatenate(
        [
            jnp.concatenate([cell_rows(0, H_ROWS), jnp.zeros((H_ROWS, 128), BF16)], axis=1),
            jnp.concatenate([jnp.zeros((Q_ROWS, 128), BF16), cell_rows(Q_AT, Q_ROWS)], axis=1),
        ],
        axis=0,
    )
    forms = jnp.dot(target[:, 0 : H_ROWS + Q_ROWS], forms, preferred_element_type=F32)
    dist_sq, quad_form = forms[:, 0:128], forms[:, 128:256]
    inv = lax.rsqrt(dist_sq)
    inv_two = inv * inv
    inv_three = inv * inv_two
    pull = inv_three * (cm_ref[pl.ds(sub, 1), :] + quad_form * (inv_two * inv_two))
    moments = jnp.concatenate(
        [
            jnp.concatenate([cell_rows(V_AT, V_ROWS), jnp.zeros((V_ROWS, 128), BF16)], axis=1),
            jnp.concatenate([jnp.zeros((U_ROWS, 128), BF16), cell_rows(U_AT, U_ROWS)], axis=1),
        ],
        axis=0,
    )
    both = jnp.concatenate([stacked(pull), stacked(inv_three * inv_two)], axis=1)
    return both, moments


def pair_lanes(pair):
    return pl.ds(pl.multiple_of(128 * pair, 128), 128)


def pair_place(tg_ref, pair):
    return tg_ref[pl.ds(pl.multiple_of(4 * pair, 4), 4), :]


def point_sums(sums, place):
    sums = sums + pltpu.roll(sums, 4, 0)
    return sums[0:3] - place[0:3] * sums[3:4]


def cell_pull(octet, tg_ref, ah_ref, cf_ref, cm_ref, out_ref):
    upper = lax.broadcasted_iota(jnp.int32, (8, 128), 0) < 4
    left = lax.broadcasted_iota(jnp.int32, (LEAF, 128), 1) < LEAF
    for inner in range(4):
        pair = octet * 4 + inner
        first, first_moments = cell_group(2 * inner, ah_ref[pair, 0:LEAF, :], cf_ref, cm_ref)
        yield
        second, second_moments = cell_group(2 * inner + 1, ah_ref[pair, LEAF:, :], cf_ref, cm_ref)
        moments = jnp.concatenate([first_moments, second_moments], axis=0)
        sums = transposed_dot(jnp.concatenate([first, second], axis=0), moments)
        yield
        sums = jnp.where(left, sums[0:64] + sums[64:128], sums[128:192] + sums[192:256]).T
        sums = jnp.concatenate([sums[0:64], sums[64:128]], axis=1)
        place = pair_place(tg_ref, pair)
        x, y, z = [place[comp : comp + 1, :] for comp in range(3)]
        quads = sums[16:32] + sums[32:48] + sums[48:64]
        turned = quads[0:8] * jnp.where(upper, x, y) + quads[8:16] * jnp.where(upper, z, -1.0)
        turned = turned + pltpu.roll(turned, 4, 0)
        out_ref[:, pair_lanes(pair)] = point_sums(sums[0:8] + sums[8:16], place) + turned[0:3]


def put_block_pair(tab_ref, block, value):
    left = lax.broadcasted_iota(jnp.int32, (4, 128), 1) < LEAF
    turned = pltpu.roll(value, LEAF, 1)
    tab_ref[block] = jnp.where(left, value, turned)
    tab_ref[block + 1] = jnp.where(left, turned, value)


def put_eight_pairs(rows_ref, block, coords, feat_ref):
    put_rows(feat_ref, source_h_rows([grid_parts(value) for value in coords]))
    for pair in range(8):
        columns = feat_ref[pl.ds(pair, H_ROWS, stride=8), :].astype(BF16)
        spread = jnp.concatenate([columns] * 4, axis=0).T
        rows_ref[block + 2 * pair] = spread[0:LEAF]
        rows_ref[block + 2 * pair + 1] = spread[LEAF:]


def prepare_kernel(n_dom, n_sub, *refs):
    bundle_ref, near_refs, recv_ref = refs[0], refs[1:n_sub], refs[n_sub]
    tab_ref, rows_ref, at_ref, tg_ref, ce_ref, ah_ref, cl_ref, ll_ref, feat_ref, four_ref = refs[n_sub + 1 :]
    own_ref = bundle_ref.at[0:OWN_ROWS]
    cl_ref[...] = bundle_ref[OWN_ROWS : OWN_ROWS + LEAF_DEV, :].astype(jnp.int32)
    ll_ref[...] = bundle_ref[OWN_ROWS + LEAF_DEV :, :].astype(jnp.int32)
    for at in range(8):
        fill_constant_rows(four_ref.at[at], H_ROWS)
    me = lax.axis_index("sub")

    def near_blocks(shift, near_ref):
        seg = lax.rem(me + n_sub - shift, n_sub)

        def near(step, carry):
            for at in range(8):
                octet = 8 * step + at
                block = seg * LEAF_DEV + 16 * octet
                first = pl.multiple_of(32 * octet, 32)
                for pair in range(8):
                    put_block_pair(tab_ref, block + 2 * pair, near_ref[pl.ds(pl.multiple_of(first + 4 * pair, 4), 4), :])
                coords = [near_ref[pl.ds(first + comp, 8, stride=4), :] for comp in range(3)]
                put_eight_pairs(rows_ref, block, coords, four_ref.at[at])
            return carry

        lax.fori_loop(0, PAIRS // 64, near, 0)

    for shift in range(1, n_sub):
        near_blocks(shift, near_refs[shift - 1])
    far_tables(n_dom, n_sub * LEAF_DEV, recv_ref, tab_ref, rows_ref, four_ref)
    near_blocks(0, own_ref)
    tg_ref[...] = own_ref[...]

    def targets(step, carry):
        for at in range(2):
            octet = 2 * step + at
            target_features(octet, tg_ref, ce_ref, feat_ref.at[at], ah_ref)
            target_rows(octet, own_ref, four_ref.at[at], at_ref)
        return carry

    lax.fori_loop(0, PAIRS // 16, targets, 0)


def far_tables(n_dom, first_block, recv_ref, tab_ref, rows_ref, four_ref):
    me = lax.axis_index("dom")
    for two in range(RANGE):
        halves = []
        for slot in (2 * two, 2 * two + 1):
            source = me - OFFSETS[slot]
            inside = (source >= 0) & (source < n_dom)
            source = jnp.clip(source, 0, n_dom - 1)
            for unit in range(OUT_UNITS):
                value = jnp.where(inside, recv_ref[source, 4 * unit : 4 * unit + 4, :], 0.0)
                put_block_pair(tab_ref, first_block + slot * CAP + 2 * unit, value)
            halves.append([jnp.where(inside, recv_ref[source, pl.ds(comp, OUT_UNITS, stride=4), :], 0.0) for comp in range(3)])
        coords = [jnp.concatenate([one, other], axis=0) for one, other in zip(*halves)]
        put_eight_pairs(rows_ref, first_block + 2 * two * CAP, coords, four_ref.at[two])


def target_rows(octet, own_ref, feat_ref, at_ref):
    one = jnp.ones((8, 128), F32)
    zero = jnp.zeros((8, 128), F32)
    parts = [grid_parts(own_ref[pl.ds(octet * 32 + comp, 8, stride=4), :]) for comp in range(3)]
    for at, value in enumerate(target_h_rows(parts, one, zero)):
        feat_ref[8 * at : 8 * at + 8, :] = value
    for pair in range(8):
        at_ref[octet * 8 + pair] = feat_ref[pl.ds(pair, H_ROWS, stride=8), :].astype(BF16)


def run(strand, steps=None):
    taken = 0
    while steps is None or taken < steps:
        taken += 1
        if next(strand, "end") == "end":
            return


def pull_kernel(n_dom, n_sub, *refs):
    cell_refs = refs[:n_sub]
    tab_ref, rows_ref, at_ref, tg_ref, ce_ref, ah_ref, cl_ref, ll_in, out_ref = refs[n_sub : n_sub + 9]
    ll_ref, spread_ref, cf_ref, cm_ref, raw_ref, even_ref, odd_ref, dist_even, dist_odd, sem = refs[n_sub + 9 :]
    copy = pltpu.make_async_copy(ll_in, ll_ref, sem)
    copy.start()
    fill_constant_rows(cf_ref, CELL_ROWS)

    def build(octet):
        return cell_features(n_dom, n_sub, octet, cl_ref, spread_ref, ce_ref, cf_ref, cm_ref)

    def spread(dom, carry):
        for shift in range(n_sub):
            for comp in range(CELL_COMPS):
                row = cell_refs[shift][dom, comp : comp + 1, :]
                spread_ref[dom, shift, comp] = jnp.broadcast_to(row, (8, 128))
        return carry

    lax.fori_loop(0, n_dom, spread, 0)

    run(build(0))
    copy.wait()
    left = lax.broadcasted_iota(jnp.int32, (M_ROWS, 128), 1) < LEAF
    left_target = lax.broadcasted_iota(jnp.int32, (H_ROWS, 128), 1) < LEAF
    owner = (lax.broadcasted_iota(jnp.int32, (LEAF, 128), 1) // H_ROWS).astype(BF16)
    lower_half, first_own, third_own = owner < 2.0, owner == 0.0, owner == 2.0

    def features(quad, raw_at, slot_ref):
        for group in range(4):
            source_moments(4 * quad + group, ll_ref, tab_ref, ce_ref, raw_ref.at[raw_at + group], slot_ref.at[group])
            yield

    def distances(quad, dist_ref):
        nothing = jnp.zeros((H_ROWS, 128), BF16)
        first, second = at_ref[2 * quad], at_ref[2 * quad + 1]
        targets = jnp.concatenate(
            [
                jnp.concatenate([jnp.where(left_target, first, nothing), nothing], axis=1),
                jnp.concatenate([jnp.where(left_target, nothing, first), nothing], axis=1),
                jnp.concatenate([nothing, jnp.where(left_target, second, nothing)], axis=1),
                jnp.concatenate([nothing, jnp.where(left_target, nothing, second)], axis=1),
            ],
            axis=0,
        )
        sources = []
        for j in range(NLEAF):
            rows = [rows_ref[ll_ref[j, 4 * quad + group]] for group in range(4)]
            low = jnp.where(first_own, rows[0], rows[1])
            high = jnp.where(third_own, rows[2], rows[3])
            sources.append(jnp.where(lower_half, low, high))
            if j % 8 == 7:
                rows = pl.ds(LEAF * (j - 7), 8 * LEAF)
                dist_ref[rows, :] = jnp.dot(jnp.concatenate(sources, axis=0), targets, preferred_element_type=F32)
                sources = []
                yield

    def pull(quad, slot_ref, dist_ref):
        total = jnp.zeros((4 * M_ROWS, 256), F32)
        for chunk in range(8):
            inv = lax.rsqrt(dist_ref[128 * chunk : 128 * chunk + 128, :])
            weights = stacked(inv * inv * inv)
            rows = [slot_ref[group, pl.ds(chunk, M_ROWS, stride=8), :] for group in range(4)]
            rows = jnp.concatenate(rows, axis=0).astype(BF16)
            total += jnp.dot(jnp.concatenate([rows, rows], axis=1), weights, preferred_element_type=F32)
            yield
        for side in range(2):
            pair = 2 * quad + side
            at, columns = 2 * M_ROWS * side, slice(128 * side, 128 * side + 128)
            sums = jnp.where(left, total[at : at + M_ROWS, columns], total[at + M_ROWS : at + 2 * M_ROWS, columns])
            lanes = pair_lanes(pair)
            out_ref[:, lanes] = out_ref[:, lanes] + point_sums(sums, pair_place(tg_ref, pair))

    quads, octets = LEAF_DEV // 4, LEAF_DEV // 8
    run(features(0, 0, even_ref))
    run(distances(0, dist_even))

    def one_octet(octet, carry):
        quad = 2 * octet
        after = jnp.minimum(quad + 2, quads - 1)
        cells = cell_pull(octet, tg_ref, ah_ref, cf_ref, cm_ref, out_ref)
        coming = build(jnp.minimum(octet + 1, octets - 1))
        for half, (now, slot_ref, dist_ref, ahead, ahead_slot, ahead_dist, raw_at) in enumerate(
            (
                (quad, even_ref, dist_even, quad + 1, odd_ref, dist_odd, 4),
                (quad + 1, odd_ref, dist_odd, after, even_ref, dist_even, 0),
            )
        ):
            direct = pull(now, slot_ref, dist_ref)
            moments, distance = features(ahead, raw_at, ahead_slot), distances(ahead, ahead_dist)
            for step in range(8):
                if step in (1, 4):
                    run(distance, 1)
                run(direct, 1)
                if step % 2 == 0:
                    run(moments, 1)
                if half == 0 or step < 4:
                    run(coming, 3)
                    if step % 4 != 3:
                        run(cells, 1)
                elif step == 4:
                    run(cells)
                else:
                    run(coming, 1)
            run(moments)
            run(distance)
            run(direct)
        run(coming)
        return carry

    lax.fori_loop(0, octets, one_octet, 0)


def on_device(n_dom, n_sub, positions, masses, cell_mass, cell_center, cell_quad, cell_list, leaf_list, send_list, send_count):
    vmem = pl.BlockSpec(memory_space=pltpu.VMEM)
    smem = pl.BlockSpec(memory_space=pltpu.SMEM)
    anywhere = pl.BlockSpec(memory_space=pl.ANY)

    def limit(mib):
        return pltpu.CompilerParams(vmem_limit_bytes=mib * 1024 * 1024)

    ins = (
        positions,
        masses.reshape(1, -1),
        cell_mass.reshape(1, -1),
        cell_center,
        cell_quad,
        cell_list,
        leaf_list.T,
        send_list.reshape(2 * RANGE, CAP),
        send_count.reshape(1, 2 * RANGE),
    )
    bundle_rows = OWN_ROWS + LEAF_DEV + NLEAF
    packed, sent, bundle = pl.pallas_call(
        functools.partial(pack_kernel, n_dom),
        out_shape=(
            jax.ShapeDtypeStruct((OWN_ROWS, 128), F32),
            jax.ShapeDtypeStruct((n_dom, SENT_ROWS, 128), F32),
            jax.ShapeDtypeStruct((bundle_rows, 128), F32),
        ),
        in_specs=[pl.BlockSpec(memory_space=pltpu.HBM)] * 9,
        out_specs=[anywhere] * 3,
        scratch_shapes=[pltpu.VMEM(array.shape, array.dtype) for array in ins[:7]]
        + [pltpu.SMEM(array.shape, jnp.int32) for array in ins[7:]]
        + [
            pltpu.VMEM((bundle_rows, 128), F32),
            pltpu.VMEM((n_dom + 1, SENT_ROWS, 128), F32),
            pltpu.SemaphoreType.DMA((12,)),
        ],
        compiler_params=limit(63),
        name="pack_own",
    )(*ins)
    received = lax.all_to_all(sent, "dom", split_axis=0, concat_axis=0, tiled=True)

    def around(value):
        pieces = [value]
        for shift in range(1, n_sub):
            pieces.append(lax.ppermute(value, "sub", [(seg, (seg + shift) % n_sub) for seg in range(n_sub)]))
        return pieces

    nearby = around(packed)
    cells = around(received[:, OUT_ROWS:])
    n_blocks = n_sub * LEAF_DEV + 2 * RANGE * CAP
    prepared = pl.pallas_call(
        functools.partial(prepare_kernel, n_dom, n_sub),
        out_shape=(
            jax.ShapeDtypeStruct((n_blocks, 4, 128), F32),
            jax.ShapeDtypeStruct((n_blocks, LEAF, 128), BF16),
            jax.ShapeDtypeStruct((PAIRS, H_ROWS, 128), BF16),
            jax.ShapeDtypeStruct((OWN_ROWS, 128), F32),
            jax.ShapeDtypeStruct((3, LEAF_DEV, 128), F32),
            jax.ShapeDtypeStruct((PAIRS, 128, 128), BF16),
            jax.ShapeDtypeStruct((LEAF_DEV, NCELL), jnp.int32),
            jax.ShapeDtypeStruct((NLEAF, LEAF_DEV), jnp.int32),
        ),
        in_specs=[vmem] * (n_sub + 1),
        out_specs=[vmem] * 8,
        scratch_shapes=[
            pltpu.VMEM((2, 8 * (H_ROWS + Q_ROWS), 128), F32),
            pltpu.VMEM((8, 8 * H_ROWS, 128), F32),
        ],
        compiler_params=limit(24),
        cost_estimate=pl.CostEstimate(flops=0, bytes_accessed=20_000_000, transcendentals=0),
        name="prepare",
    )(bundle, *nearby[1:], received)
    return pl.pallas_call(
        functools.partial(pull_kernel, n_dom, n_sub),
        out_shape=jax.ShapeDtypeStruct((3, LEAF_DEV * LEAF), F32),
        in_specs=[vmem] * (n_sub + 8),
        out_specs=vmem,
        scratch_shapes=[
            pltpu.SMEM((NLEAF, LEAF_DEV), jnp.int32),
            pltpu.VMEM((n_dom, n_sub, CELL_COMPS, 8, 128), F32),
            pltpu.VMEM((8 * CELL_ROWS, 128), F32),
            pltpu.VMEM((8, 128), F32),
            pltpu.VMEM((8, 32, 128), F32),
            pltpu.VMEM((4, 8 * M_ROWS, 128), F32),
            pltpu.VMEM((4, 8 * M_ROWS, 128), F32),
            pltpu.VMEM((NLEAF * LEAF, 256), F32),
            pltpu.VMEM((NLEAF * LEAF, 256), F32),
            pltpu.SemaphoreType.DMA(()),
        ],
        compiler_params=limit(24),
        name="pull",
    )(*cells, *prepared)


def solution(mesh):
    sharded = P(("dom", "sub"))
    return jax.shard_map(
        functools.partial(on_device, mesh.shape["dom"], mesh.shape["sub"]),
        mesh=mesh,
        in_specs=(
            P(None, ("dom", "sub")),
            sharded,
            sharded,
            P(None, ("dom", "sub")),
            P(None, ("dom", "sub")),
            P(("dom", "sub"), None),
            P(("dom", "sub"), None),
            P("dom", "sub", None, None),
            P("dom", "sub", None),
        ),
        out_specs=P(None, ("dom", "sub")),
        check_vma=False,
    )
```

```python
import functools

import jax
import jax.numpy as jnp
from jax import lax
from jax.experimental import pallas as pl
from jax.experimental.pallas import tpu as pltpu
from jax.sharding import PartitionSpec as P

LEAF = 64
LEAF_DEV = 128
NCELL = 128
NLEAF = 16
RANGE = 4
CAP = 8
PAIRS = LEAF_DEV // 2
OUT_UNITS = CAP // 2
OWN_ROWS = 4 * PAIRS
OUT_ROWS = 4 * OUT_UNITS
CELL_COMPS = 10
CELL_PAD = 16
SENT_ROWS = OUT_ROWS + CELL_PAD
OFFSETS = list(range(-RANGE, 0)) + list(range(1, RANGE + 1))

softening_sq = 0.0025
GRID_ROUND = 49152.0
F32 = jnp.float32
BF16 = jnp.bfloat16

H_ROWS = 32
Q_ROWS = 64
V_ROWS = 8
U_ROWS = 32
Q_AT = H_ROWS
V_AT = Q_AT + Q_ROWS
U_AT = V_AT + V_ROWS
CELL_ROWS = U_AT + U_ROWS
M_ROWS = 8
MOMENTS = V_ROWS + U_ROWS


def rounded(value):
    return value.astype(BF16).astype(F32)


def three_parts(value):
    first = rounded(value)
    rest = value - first
    second = rounded(rest)
    return first, second, rest - second


def high_low(value):
    high = rounded(value)
    return high, value - high


def two_parts(value):
    first = value.astype(BF16)
    return first, (value - first.astype(F32)).astype(BF16)


def grid_parts(value):
    high = (value + GRID_ROUND) - GRID_ROUND
    low = value - high
    first = rounded(low)
    return high, low, first, low - first


def norm_parts(parts, extra=None):
    big = sum(high * high for high, _, _, _ in parts)
    small = sum(low * (2.0 * high + low) for high, low, _, _ in parts)
    if extra is not None:
        small = small + extra
    return three_parts(big), three_parts(small)


def put_own(pos_ref, mass_ref, own_ref):
    for pair in range(PAIRS):
        lanes = pl.ds(128 * pair, 128)
        own_ref[4 * pair : 4 * pair + 3, :] = pos_ref[:, lanes]
        own_ref[4 * pair + 3 : 4 * pair + 4, :] = mass_ref[:, lanes]


def pack_kernel(n_dom, *refs):
    ins, outs, scratch, (out_ref, sent_ref, sems) = refs[:9], refs[9:12], refs[12:21], refs[21:]
    results = [
        pltpu.make_async_copy(out_ref.at[pl.ds(0, OWN_ROWS)], outs[0], sems.at[9]),
        pltpu.make_async_copy(sent_ref.at[pl.ds(0, n_dom)], outs[1], sems.at[10]),
        pltpu.make_async_copy(out_ref, outs[2], sems.at[11]),
    ]
    copies = [pltpu.make_async_copy(src, dst, sems.at[at]) for at, (src, dst) in enumerate(zip(ins, scratch))]
    for copy in copies:
        copy.start()
    pos_ref, mass_ref, cmass_ref, center_ref, quad_ref, cl_ref, ll_ref, list_ref, count_ref = scratch
    me = lax.axis_index("dom")
    left = lax.broadcasted_iota(jnp.int32, (4, 128), 1) < LEAF
    sent_ref[...] = jnp.zeros((n_dom + 1, SENT_ROWS, 128), F32)
    for copy in copies:
        copy.wait()
    put_own(pos_ref, mass_ref, out_ref)
    results[0].start()
    out_ref[OWN_ROWS : OWN_ROWS + LEAF_DEV, :] = cl_ref[...].astype(F32)
    out_ref[OWN_ROWS + LEAF_DEV :, :] = ll_ref[...].astype(F32)
    results[2].start()

    def put_cells(target, carry):
        sent_ref[target, OUT_ROWS : OUT_ROWS + 1, :] = cmass_ref[...]
        sent_ref[target, OUT_ROWS + 1 : OUT_ROWS + 4, :] = center_ref[...]
        sent_ref[target, OUT_ROWS + 4 : OUT_ROWS + 10, :] = quad_ref[...]
        return carry

    lax.fori_loop(0, n_dom, put_cells, 0)

    def half(slot, j, right):
        block = list_ref[slot, j]
        value = out_ref[pl.ds(pl.multiple_of(4 * (block // 2), 4), 4), :]
        value = jnp.where(j < count_ref[0, slot], value, 0.0)
        return jnp.where((block & 1) == right, value, pltpu.roll(value, LEAF, 1))

    for slot in range(2 * RANGE):
        target = me + OFFSETS[slot]
        target = jnp.where((target >= 0) & (target < n_dom), target, n_dom)
        for unit in range(OUT_UNITS):
            sent_ref[target, 4 * unit : 4 * unit + 4, :] = jnp.where(left, half(slot, 2 * unit, 0), half(slot, 2 * unit + 1, 1))
    results[1].start()
    for copy in results:
        copy.wait()


def target_h_rows(parts, one, zero):
    big, small = norm_parts(parts, softening_sq)
    minus_high = [-2.0 * part[0] for part in parts]
    minus_one = [-2.0 * part[2] for part in parts]
    minus_two = [-2.0 * part[3] for part in parts]
    rows = minus_high + [one] * 3 + list(big) + minus_high + minus_one + minus_high
    return rows + minus_two + minus_one + [one] * 3 + list(small) + [zero] * 2


def target_features(octet, tg_ref, ce_ref, feat_ref, ah_ref):
    left = lax.broadcasted_iota(jnp.int32, (8, 128), 1) < LEAF
    one = jnp.ones((8, 128), F32)
    zero = jnp.zeros((8, 128), F32)
    parts, centred = [], []
    for comp in range(3):
        rows = pl.ds(octet * 32 + comp, 8, stride=4)
        value = tg_ref[rows, :]
        first = jnp.broadcast_to(value[:, 0:1], (8, 128))
        second = jnp.broadcast_to(value[:, LEAF : LEAF + 1], (8, 128))
        ce_ref[comp, pl.ds(octet * 16, 8, stride=2), :] = first
        ce_ref[comp, pl.ds(octet * 16 + 1, 8, stride=2), :] = second
        value = value - jnp.where(left, first, second)
        tg_ref[rows, :] = value
        centred.append(value)
        parts.append(grid_parts(value))
    rows = target_h_rows(parts, one, zero)
    x, y, z = centred
    split = [three_parts(v) for v in (x, y, z, x * x, y * y, z * z, x * y, x * z, y * z)]
    for which in (0, 0, 1, 0, 1, 2):
        rows += [part[which] for part in split]
    rows += [one] * 3 + [zero] * 7
    for at, value in enumerate(rows):
        feat_ref[8 * at : 8 * at + 8, :] = value
    for sub in range(8):
        features = feat_ref[pl.ds(sub, H_ROWS + Q_ROWS, stride=8), :].T.astype(BF16)
        ah_ref[octet * 8 + sub, :, 0 : H_ROWS + Q_ROWS] = features


def source_h_rows(parts):
    (p1, p2, p3), (s1, s2, s3) = norm_parts(parts)
    high = [part[0] for part in parts]
    one = [part[2] for part in parts]
    two = [part[3] for part in parts]
    rows = dict(enumerate(high + [p1, p2, p3]))
    rows.update(enumerate(one + high + two + high + one + [s1, s2, s3], 9))
    return rows


def put_rows(ref, rows):
    for at, value in rows.items():
        ref[8 * at : 8 * at + 8, :] = value


def fill_constant_rows(ref, count):
    one = jnp.ones((8, 128), F32)
    zero = jnp.zeros((8, 128), F32)
    for at in range(count):
        ones = at in (6, 7, 8, 27, 28, 29) or at == V_AT + 3
        ref[8 * at : 8 * at + 8, :] = one if ones else zero


def cell_features(n_dom, n_sub, octet, cl_ref, spread_ref, ce_ref, cf_ref, cm_ref):
    ids = cl_ref[pl.ds(pl.multiple_of(8 * octet, 8), 8), :]
    lane = ids & 127
    owner = ids >> 7
    me = lax.axis_index("sub")

    def look_up(dom, shift, found):
        here = owner == dom * n_sub + lax.bitwise_xor(me, shift)
        new = []
        for comp in range(CELL_COMPS):
            value = jnp.take_along_axis(spread_ref[dom, shift, comp], lane, axis=1, mode="promise_in_bounds")
            new.append(jnp.where(here, value, found[comp]))
        return tuple(new)

    found = tuple(jnp.zeros((8, 128), F32) for _ in range(CELL_COMPS))
    if n_dom <= 8:
        for dom in range(n_dom):
            for shift in range(n_sub):
                found = look_up(dom, shift, found)
                yield
    else:

        def one_domain(dom, found):
            for shift in range(n_sub):
                found = look_up(dom, shift, found)
            return found

        found = lax.fori_loop(0, n_dom, one_domain, found)
    mass, cx, cy, cz, xx, yy, zz, xy, xz, yz = found
    yield "found"
    cm_ref[...] = mass
    rows8 = pl.ds(pl.multiple_of(8 * octet, 8), 8)
    cx, cy, cz = [value - ce_ref[comp, rows8, :] for comp, value in enumerate((cx, cy, cz))]
    put_rows(cf_ref, source_h_rows([grid_parts(value) for value in (cx, cy, cz)]))
    yield
    qx = xx * cx + xy * cy + xz * cz
    qy = xy * cx + yy * cy + yz * cz
    qz = xz * cx + yz * cy + zz * cz
    const = three_parts(2.5 * (qx * cx + qy * cy + qz * cz))
    linear = [-5.0 * qx, -5.0 * qy, -5.0 * qz]
    square = [2.5 * xx, 2.5 * yy, 2.5 * zz, 5.0 * xy, 5.0 * xz, 5.0 * yz]
    split = [three_parts(value) for value in linear + square]
    rows = []
    for which in (0, 1, 0, 2, 1, 0):
        rows += [part[which] for part in split]
    rows += list(const)
    put_rows(cf_ref, dict(enumerate(rows, Q_AT)))
    yield
    for comp, value in enumerate((cx, cy, cz)):
        for which, part in enumerate(high_low(value)):
            cf_ref[8 * (V_AT + 4 * which + comp) : 8 * (V_AT + 4 * which + comp) + 8, :] = part
    yield
    columns = {name: high_low(value) for name, value in dict(xx=xx, yy=yy, zz=zz, xy=xy, xz=xz, yz=yz, cx=qx, cy=qy, cz=qz).items()}
    order = (("xx", "xy", "xz"), ("xy", "yy", "yz"), ("xz", "yz", "zz"), ("cx", "cy", "cz"))
    for which in range(2):
        for column, names in enumerate(order):
            for row, name in enumerate(names):
                at = U_AT + 16 * which + 4 * column + row
                cf_ref[8 * at : 8 * at + 8, :] = columns[name][which]


def source_moments(group, ll_ref, tab_ref, ce_ref, raw_ref, sf_ref):
    left = lax.broadcasted_iota(jnp.int32, (4, 128), 1) < LEAF
    for pair in range(NLEAF // 2):
        first = tab_ref[ll_ref[2 * pair, group]]
        second = tab_ref[ll_ref[2 * pair + 1, group]]
        raw_ref[4 * pair : 4 * pair + 4, :] = jnp.where(left, first, second)
    value = [raw_ref[pl.ds(comp, 8, stride=4), :] for comp in range(4)]
    mass = value[3]
    centred = [value[comp] - ce_ref[comp, pl.ds(group, 1), :] for comp in range(3)]
    for comp, v in enumerate([mass * v for v in centred] + [mass]):
        for which, part in enumerate(high_low(v)):
            at = 4 * which + comp
            sf_ref[8 * at : 8 * at + 8, :] = part


def transposed_dot(rows, weights):
    return lax.dot_general(rows, weights, (((1,), (1,)), ((), ())), preferred_element_type=F32)


def stacked(value):
    return jnp.concatenate(two_parts(value), axis=0)


def cell_group(sub, target, cf_ref, cm_ref):
    def cell_rows(at, count):
        return cf_ref[pl.ds(8 * at + sub, count, stride=8), :].astype(BF16)

    forms = jnp.concatenate(
        [
            jnp.concatenate([cell_rows(0, H_ROWS), jnp.zeros((H_ROWS, 128), BF16)], axis=1),
            jnp.concatenate([jnp.zeros((Q_ROWS, 128), BF16), cell_rows(Q_AT, Q_ROWS)], axis=1),
        ],
        axis=0,
    )
    forms = jnp.dot(target[:, 0 : H_ROWS + Q_ROWS], forms, preferred_element_type=F32)
    dist_sq, quad_form = forms[:, 0:128], forms[:, 128:256]
    inv = lax.rsqrt(dist_sq)
    inv_two = inv * inv
    inv_three = inv * inv_two
    pull = inv_three * (cm_ref[pl.ds(sub, 1), :] + quad_form * (inv_two * inv_two))
    moments = cf_ref[pl.ds(8 * V_AT + sub, MOMENTS, stride=8), :]
    kind = lax.broadcasted_iota(jnp.int32, (MOMENTS, 128), 0) < V_ROWS
    moments = jnp.concatenate([jnp.where(kind, moments, 0.0), jnp.where(kind, 0.0, moments)], axis=1)
    both = jnp.concatenate([stacked(pull), stacked(inv_three * inv_two)], axis=1)
    return both, moments


def pair_lanes(pair):
    return pl.ds(pl.multiple_of(128 * pair, 128), 128)


def pair_place(tg_ref, pair):
    return tg_ref[pl.ds(pl.multiple_of(4 * pair, 4), 4), :]


def point_sums(sums, place):
    sums = sums + pltpu.roll(sums, 4, 0)
    return sums[0:3] - place[0:3] * sums[3:4]


def cell_pull(octet, tg_ref, ah_ref, cf_ref, cm_ref, out_ref):
    upper = lax.broadcasted_iota(jnp.int32, (8, 128), 0) < 4
    first_lanes = lax.broadcasted_iota(jnp.int32, (LEAF, 128), 1) < MOMENTS
    padding = jnp.zeros((128 - 2 * MOMENTS, 256), F32)
    for half in range(2):
        both, moments = [], []
        for group in range(4):
            sub = 4 * half + group
            rows = pl.ds(LEAF * (group % 2), LEAF)
            weights, own_moments = cell_group(sub, ah_ref[octet * 4 + sub // 2, rows, :], cf_ref, cm_ref)
            both.append(weights)
            moments.append(own_moments)
            if group % 2 == 1:
                moments.append(padding)
            yield
        moments = jnp.concatenate(moments, axis=0).astype(BF16)
        totals = transposed_dot(jnp.concatenate(both, axis=0), moments)
        yield
        for side in range(2):
            pair = octet * 4 + 2 * half + side
            at, columns = 256 * side, slice(128 * side, 128 * side + 128)
            sums = [totals[row : row + LEAF, columns] + totals[row + LEAF : row + 128, columns] for row in (at, at + 128)]
            sums = jnp.where(first_lanes, sums[0], sums[1]).T
            sums = jnp.concatenate([sums[0:MOMENTS], sums[MOMENTS : 2 * MOMENTS]], axis=1)
            place = pair_place(tg_ref, pair)
            x, y, z = [place[comp : comp + 1, :] for comp in range(3)]
            quads = sums[V_ROWS : V_ROWS + 16] + sums[V_ROWS + 16 :]
            turned = quads[0:8] * jnp.where(upper, x, y) + quads[8:16] * jnp.where(upper, z, -1.0)
            turned = turned + pltpu.roll(turned, 4, 0)
            out_ref[:, pair_lanes(pair)] = point_sums(sums[0:V_ROWS], place) + turned[0:3]


def put_block_pair(tab_ref, block, value):
    left = lax.broadcasted_iota(jnp.int32, (4, 128), 1) < LEAF
    turned = pltpu.roll(value, LEAF, 1)
    tab_ref[block] = jnp.where(left, value, turned)
    tab_ref[block + 1] = jnp.where(left, turned, value)


def put_eight_pairs(rows_ref, block, coords, feat_ref):
    put_rows(feat_ref, source_h_rows([grid_parts(value) for value in coords]))
    for pair in range(8):
        columns = feat_ref[pl.ds(pair, H_ROWS, stride=8), :].astype(BF16)
        spread = jnp.concatenate([columns] * 4, axis=0).T
        rows_ref[block + 2 * pair] = spread[0:LEAF]
        rows_ref[block + 2 * pair + 1] = spread[LEAF:]


def prepare_kernel(n_dom, n_sub, *refs):
    bundle_ref, near_refs, recv_ref = refs[0], refs[1:n_sub], refs[n_sub]
    tab_ref, rows_ref, at_ref, tg_ref, ce_ref, ah_ref, cl_ref, ll_ref, feat_ref, four_ref = refs[n_sub + 1 :]
    own_ref = bundle_ref.at[0:OWN_ROWS]
    cl_ref[...] = bundle_ref[OWN_ROWS : OWN_ROWS + LEAF_DEV, :].astype(jnp.int32)
    ll_ref[...] = bundle_ref[OWN_ROWS + LEAF_DEV :, :].astype(jnp.int32)
    for at in range(8):
        fill_constant_rows(four_ref.at[at], H_ROWS)
    me = lax.axis_index("sub")

    def near_blocks(shift, near_ref):
        seg = lax.bitwise_xor(me, shift)

        def near(step, carry):
            for at in range(8):
                octet = 8 * step + at
                block = seg * LEAF_DEV + 16 * octet
                first = pl.multiple_of(32 * octet, 32)
                for pair in range(8):
                    put_block_pair(tab_ref, block + 2 * pair, near_ref[pl.ds(pl.multiple_of(first + 4 * pair, 4), 4), :])
                coords = [near_ref[pl.ds(first + comp, 8, stride=4), :] for comp in range(3)]
                put_eight_pairs(rows_ref, block, coords, four_ref.at[at])
            return carry

        lax.fori_loop(0, PAIRS // 64, near, 0)

    for shift in range(1, n_sub):
        near_blocks(shift, near_refs[shift - 1])
    far_tables(n_dom, n_sub * LEAF_DEV, recv_ref, tab_ref, rows_ref, four_ref)
    near_blocks(0, own_ref)
    tg_ref[...] = own_ref[...]

    def targets(step, carry):
        for at in range(2):
            octet = 2 * step + at
            target_features(octet, tg_ref, ce_ref, feat_ref.at[at], ah_ref)
            target_rows(octet, own_ref, four_ref.at[at], at_ref)
        return carry

    lax.fori_loop(0, PAIRS // 16, targets, 0)


def far_tables(n_dom, first_block, recv_ref, tab_ref, rows_ref, four_ref):
    me = lax.axis_index("dom")
    for two in range(RANGE):
        halves = []
        for slot in (2 * two, 2 * two + 1):
            source = me - OFFSETS[slot]
            inside = (source >= 0) & (source < n_dom)
            source = jnp.clip(source, 0, n_dom - 1)
            for unit in range(OUT_UNITS):
                value = jnp.where(inside, recv_ref[source, 4 * unit : 4 * unit + 4, :], 0.0)
                put_block_pair(tab_ref, first_block + slot * CAP + 2 * unit, value)
            halves.append([jnp.where(inside, recv_ref[source, pl.ds(comp, OUT_UNITS, stride=4), :], 0.0) for comp in range(3)])
        coords = [jnp.concatenate([one, other], axis=0) for one, other in zip(*halves)]
        put_eight_pairs(rows_ref, first_block + 2 * two * CAP, coords, four_ref.at[two])


def target_rows(octet, own_ref, feat_ref, at_ref):
    one = jnp.ones((8, 128), F32)
    zero = jnp.zeros((8, 128), F32)
    parts = [grid_parts(own_ref[pl.ds(octet * 32 + comp, 8, stride=4), :]) for comp in range(3)]
    for at, value in enumerate(target_h_rows(parts, one, zero)):
        feat_ref[8 * at : 8 * at + 8, :] = value
    for pair in range(8):
        at_ref[octet * 8 + pair] = feat_ref[pl.ds(pair, H_ROWS, stride=8), :].astype(BF16)


def run(strand, steps=None):
    taken = 0
    while steps is None or taken < steps:
        taken += 1
        if next(strand, "end") == "end":
            return


def pull_kernel(n_dom, n_sub, *refs):
    cell_refs = refs[:n_sub]
    tab_ref, rows_ref, at_ref, tg_ref, ce_ref, ah_ref, cl_ref, ll_in, out_ref = refs[n_sub : n_sub + 9]
    ll_ref, spread_ref, cf_ref, cm_ref, raw_ref, even_ref, odd_ref, dist_even, dist_odd, sem = refs[n_sub + 9 :]
    copy = pltpu.make_async_copy(ll_in, ll_ref, sem)
    copy.start()
    fill_constant_rows(cf_ref, CELL_ROWS)

    def build(octet):
        return cell_features(n_dom, n_sub, octet, cl_ref, spread_ref, ce_ref, cf_ref, cm_ref)

    def spread(dom, carry):
        for shift in range(n_sub):
            for comp in range(CELL_COMPS):
                row = cell_refs[shift][dom, comp : comp + 1, :]
                spread_ref[dom, shift, comp] = jnp.broadcast_to(row, (8, 128))
        return carry

    lax.fori_loop(0, n_dom, spread, 0)

    left = lax.broadcasted_iota(jnp.int32, (M_ROWS, 128), 1) < LEAF
    left_target = lax.broadcasted_iota(jnp.int32, (H_ROWS, 128), 1) < LEAF
    owner = (lax.broadcasted_iota(jnp.int32, (LEAF, 128), 1) // H_ROWS).astype(BF16)
    lower_half, first_own, third_own = owner < 2.0, owner == 0.0, owner == 2.0

    def features(quad, raw_at, slot_ref):
        for group in range(4):
            source_moments(4 * quad + group, ll_ref, tab_ref, ce_ref, raw_ref.at[raw_at + group], slot_ref.at[group])
            yield

    def distances(quad, dist_ref):
        nothing = jnp.zeros((H_ROWS, 128), BF16)
        first, second = at_ref[2 * quad], at_ref[2 * quad + 1]
        targets = jnp.concatenate(
            [
                jnp.concatenate([jnp.where(left_target, first, nothing), nothing], axis=1),
                jnp.concatenate([jnp.where(left_target, nothing, first), nothing], axis=1),
                jnp.concatenate([nothing, jnp.where(left_target, second, nothing)], axis=1),
                jnp.concatenate([nothing, jnp.where(left_target, nothing, second)], axis=1),
            ],
            axis=0,
        )
        sources = []
        for j in range(NLEAF):
            rows = [rows_ref[ll_ref[j, 4 * quad + group]] for group in range(4)]
            low = jnp.where(first_own, rows[0], rows[1])
            high = jnp.where(third_own, rows[2], rows[3])
            sources.append(jnp.where(lower_half, low, high))
            if j % 8 == 7:
                rows = pl.ds(LEAF * (j - 7), 8 * LEAF)
                dist_ref[rows, :] = jnp.dot(jnp.concatenate(sources, axis=0), targets, preferred_element_type=F32)
                sources = []
                yield

    def pull(quad, slot_ref, dist_ref):
        total = jnp.zeros((4 * M_ROWS, 256), F32)
        for chunk in range(8):
            inv = lax.rsqrt(dist_ref[128 * chunk : 128 * chunk + 128, :])
            weights = stacked(inv * inv * inv)
            rows = [slot_ref[group, pl.ds(chunk, M_ROWS, stride=8), :] for group in range(4)]
            rows = jnp.concatenate(rows, axis=0).astype(BF16)
            total += jnp.dot(jnp.concatenate([rows, rows], axis=1), weights, preferred_element_type=F32)
            yield
        for side in range(2):
            pair = 2 * quad + side
            at, columns = 2 * M_ROWS * side, slice(128 * side, 128 * side + 128)
            sums = jnp.where(left, total[at : at + M_ROWS, columns], total[at + M_ROWS : at + 2 * M_ROWS, columns])
            lanes = pair_lanes(pair)
            out_ref[:, lanes] = out_ref[:, lanes] + point_sums(sums, pair_place(tg_ref, pair))

    quads, octets = LEAF_DEV // 4, LEAF_DEV // 8
    copy.wait()
    first, moments, distance = build(0), features(0, 0, even_ref), distances(0, dist_even)
    for step in range(4):
        run(first, 8)
        run(moments, 1)
        if step % 2 == 0:
            run(distance, 1)
    run(first)
    run(moments)
    run(distance)

    def one_octet(octet, carry):
        quad = 2 * octet
        after = jnp.minimum(quad + 2, quads - 1)
        cells = cell_pull(octet, tg_ref, ah_ref, cf_ref, cm_ref, out_ref)
        coming = build(jnp.minimum(octet + 1, octets - 1))
        for half, (now, slot_ref, dist_ref, ahead, ahead_slot, ahead_dist, raw_at) in enumerate(
            (
                (quad, even_ref, dist_even, quad + 1, odd_ref, dist_odd, 4),
                (quad + 1, odd_ref, dist_odd, after, even_ref, dist_even, 0),
            )
        ):
            direct = pull(now, slot_ref, dist_ref)
            moments, distance = features(ahead, raw_at, ahead_slot), distances(ahead, ahead_dist)
            for step in range(8):
                if step in (1, 4):
                    run(distance, 1)
                run(direct, 1)
                if step % 2 == 0:
                    run(moments, 1)
                if half == 0 or step < 4:
                    run(coming, 3)
                    if step % 4 != 3:
                        run(cells, 1)
                elif step == 4:
                    run(cells)
                else:
                    run(coming, 1)
            run(moments)
            run(distance)
            run(direct)
        run(coming)
        return carry

    lax.fori_loop(0, octets, one_octet, 0)


def on_device(n_dom, n_sub, positions, masses, cell_mass, cell_center, cell_quad, cell_list, leaf_list, send_list, send_count):
    vmem = pl.BlockSpec(memory_space=pltpu.VMEM)
    smem = pl.BlockSpec(memory_space=pltpu.SMEM)
    anywhere = pl.BlockSpec(memory_space=pl.ANY)

    def limit(mib):
        return pltpu.CompilerParams(vmem_limit_bytes=mib * 1024 * 1024)

    ins = (
        positions,
        masses.reshape(1, -1),
        cell_mass.reshape(1, -1),
        cell_center,
        cell_quad,
        cell_list,
        leaf_list.T,
        send_list.reshape(2 * RANGE, CAP),
        send_count.reshape(1, 2 * RANGE),
    )
    bundle_rows = OWN_ROWS + LEAF_DEV + NLEAF
    packed, sent, bundle = pl.pallas_call(
        functools.partial(pack_kernel, n_dom),
        out_shape=(
            jax.ShapeDtypeStruct((OWN_ROWS, 128), F32),
            jax.ShapeDtypeStruct((n_dom, SENT_ROWS, 128), F32),
            jax.ShapeDtypeStruct((bundle_rows, 128), F32),
        ),
        in_specs=[pl.BlockSpec(memory_space=pltpu.HBM)] * 9,
        out_specs=[anywhere] * 3,
        scratch_shapes=[pltpu.VMEM(array.shape, array.dtype) for array in ins[:7]]
        + [pltpu.SMEM(array.shape, jnp.int32) for array in ins[7:]]
        + [
            pltpu.VMEM((bundle_rows, 128), F32),
            pltpu.VMEM((n_dom + 1, SENT_ROWS, 128), F32),
            pltpu.SemaphoreType.DMA((12,)),
        ],
        compiler_params=limit(63),
        name="pack_own",
    )(*ins)
    received = lax.all_to_all(sent, "dom", split_axis=0, concat_axis=0, tiled=True)

    def across(value, bits):
        return lax.ppermute(value, "sub", [(seg, seg ^ bits) for seg in range(n_sub)])

    nearby = {0: packed}
    bit = n_sub // 2
    while bit:
        nearby.update({at ^ bit: across(value, bit) for at, value in nearby.items()})
        bit //= 2
    nearby = [nearby[at] for at in range(n_sub)]
    own_cells = received[:, OUT_ROWS:]
    cells = [own_cells] + [across(own_cells, bits) for bits in range(1, n_sub)]
    n_blocks = n_sub * LEAF_DEV + 2 * RANGE * CAP
    prepared = pl.pallas_call(
        functools.partial(prepare_kernel, n_dom, n_sub),
        out_shape=(
            jax.ShapeDtypeStruct((n_blocks, 4, 128), F32),
            jax.ShapeDtypeStruct((n_blocks, LEAF, 128), BF16),
            jax.ShapeDtypeStruct((PAIRS, H_ROWS, 128), BF16),
            jax.ShapeDtypeStruct((OWN_ROWS, 128), F32),
            jax.ShapeDtypeStruct((3, LEAF_DEV, 128), F32),
            jax.ShapeDtypeStruct((PAIRS, 128, 128), BF16),
            jax.ShapeDtypeStruct((LEAF_DEV, NCELL), jnp.int32),
            jax.ShapeDtypeStruct((NLEAF, LEAF_DEV), jnp.int32),
        ),
        in_specs=[vmem] * (n_sub + 1),
        out_specs=[vmem] * 8,
        scratch_shapes=[
            pltpu.VMEM((2, 8 * (H_ROWS + Q_ROWS), 128), F32),
            pltpu.VMEM((8, 8 * H_ROWS, 128), F32),
        ],
        compiler_params=limit(24),
        cost_estimate=pl.CostEstimate(flops=0, bytes_accessed=20_000_000, transcendentals=0),
        name="prepare",
    )(bundle, *nearby[1:], received)
    return pl.pallas_call(
        functools.partial(pull_kernel, n_dom, n_sub),
        out_shape=jax.ShapeDtypeStruct((3, LEAF_DEV * LEAF), F32),
        in_specs=[vmem] * (n_sub + 8),
        out_specs=vmem,
        scratch_shapes=[
            pltpu.SMEM((NLEAF, LEAF_DEV), jnp.int32),
            pltpu.VMEM((n_dom, n_sub, CELL_COMPS, 8, 128), F32),
            pltpu.VMEM((8 * CELL_ROWS, 128), F32),
            pltpu.VMEM((8, 128), F32),
            pltpu.VMEM((8, 32, 128), F32),
            pltpu.VMEM((4, 8 * M_ROWS, 128), F32),
            pltpu.VMEM((4, 8 * M_ROWS, 128), F32),
            pltpu.VMEM((NLEAF * LEAF, 256), F32),
            pltpu.VMEM((NLEAF * LEAF, 256), F32),
            pltpu.SemaphoreType.DMA(()),
        ],
        compiler_params=limit(24),
        name="pull",
    )(*cells, *prepared)


def solution(mesh):
    sharded = P(("dom", "sub"))
    return jax.shard_map(
        functools.partial(on_device, mesh.shape["dom"], mesh.shape["sub"]),
        mesh=mesh,
        in_specs=(
            P(None, ("dom", "sub")),
            sharded,
            sharded,
            P(None, ("dom", "sub")),
            P(None, ("dom", "sub")),
            P(("dom", "sub"), None),
            P(("dom", "sub"), None),
            P("dom", "sub", None, None),
            P("dom", "sub", None),
        ),
        out_specs=P(None, ("dom", "sub")),
        check_vma=False,
    )
```

```python
import functools

import jax
import jax.numpy as jnp
from jax import lax
from jax.experimental import pallas as pl
from jax.experimental.pallas import tpu as pltpu
from jax.sharding import PartitionSpec as P

LEAF = 64
LEAF_DEV = 128
NCELL = 128
NLEAF = 16
RANGE = 4
CAP = 8
PAIRS = LEAF_DEV // 2
OUT_UNITS = CAP // 2
OWN_ROWS = 4 * PAIRS
OUT_ROWS = 4 * OUT_UNITS
CELL_COMPS = 10
CELL_PAD = 16
SENT_ROWS = OUT_ROWS + CELL_PAD
OFFSETS = list(range(-RANGE, 0)) + list(range(1, RANGE + 1))

softening_sq = 0.0025
GRID_ROUND = 49152.0
F32 = jnp.float32
BF16 = jnp.bfloat16

H_ROWS = 32
Q_ROWS = 64
V_ROWS = 16
U_ROWS = 48
Q_AT = H_ROWS
V_AT = Q_AT + Q_ROWS
U_AT = V_AT + V_ROWS
CELL_ROWS = U_AT + U_ROWS
M_ROWS = 8


def rounded(value):
    return value.astype(BF16).astype(F32)


def three_parts(value):
    first = rounded(value)
    rest = value - first
    second = rounded(rest)
    return first, second, rest - second


def high_low(value):
    high = rounded(value)
    return high, value - high


def two_parts(value):
    first = value.astype(BF16)
    return first, (value - first.astype(F32)).astype(BF16)


def grid_parts(value):
    high = (value + GRID_ROUND) - GRID_ROUND
    low = value - high
    first = rounded(low)
    return high, low, first, low - first


def norm_parts(parts, extra=None):
    big = sum(high * high for high, _, _, _ in parts)
    small = sum(low * (2.0 * high + low) for high, low, _, _ in parts)
    if extra is not None:
        small = small + extra
    return three_parts(big), three_parts(small)


def put_own(pos_ref, mass_ref, own_ref):
    for pair in range(PAIRS):
        lanes = pl.ds(128 * pair, 128)
        own_ref[4 * pair : 4 * pair + 3, :] = pos_ref[:, lanes]
        own_ref[4 * pair + 3 : 4 * pair + 4, :] = mass_ref[:, lanes]


def pack_kernel(n_dom, *refs):
    ins, outs, scratch, (out_ref, sent_ref, sems) = refs[:9], refs[9:12], refs[12:21], refs[21:]
    results = [
        pltpu.make_async_copy(out_ref.at[pl.ds(0, OWN_ROWS)], outs[0], sems.at[9]),
        pltpu.make_async_copy(sent_ref.at[pl.ds(0, n_dom)], outs[1], sems.at[10]),
        pltpu.make_async_copy(out_ref, outs[2], sems.at[11]),
    ]
    copies = [pltpu.make_async_copy(src, dst, sems.at[at]) for at, (src, dst) in enumerate(zip(ins, scratch))]
    for copy in copies:
        copy.start()
    pos_ref, mass_ref, cmass_ref, center_ref, quad_ref, cl_ref, ll_ref, list_ref, count_ref = scratch
    me = lax.axis_index("dom")
    left = lax.broadcasted_iota(jnp.int32, (4, 128), 1) < LEAF
    sent_ref[...] = jnp.zeros((n_dom + 1, SENT_ROWS, 128), F32)
    for copy in copies:
        copy.wait()
    put_own(pos_ref, mass_ref, out_ref)
    results[0].start()
    out_ref[OWN_ROWS : OWN_ROWS + LEAF_DEV, :] = cl_ref[...].astype(F32)
    out_ref[OWN_ROWS + LEAF_DEV :, :] = ll_ref[...].astype(F32)
    results[2].start()

    def put_cells(target, carry):
        sent_ref[target, OUT_ROWS : OUT_ROWS + 1, :] = cmass_ref[...]
        sent_ref[target, OUT_ROWS + 1 : OUT_ROWS + 4, :] = center_ref[...]
        sent_ref[target, OUT_ROWS + 4 : OUT_ROWS + 10, :] = quad_ref[...]
        return carry

    lax.fori_loop(0, n_dom, put_cells, 0)

    def half(slot, j, right):
        block = list_ref[slot, j]
        value = out_ref[pl.ds(pl.multiple_of(4 * (block // 2), 4), 4), :]
        value = jnp.where(j < count_ref[0, slot], value, 0.0)
        return jnp.where((block & 1) == right, value, pltpu.roll(value, LEAF, 1))

    for slot in range(2 * RANGE):
        target = me + OFFSETS[slot]
        target = jnp.where((target >= 0) & (target < n_dom), target, n_dom)
        for unit in range(OUT_UNITS):
            sent_ref[target, 4 * unit : 4 * unit + 4, :] = jnp.where(left, half(slot, 2 * unit, 0), half(slot, 2 * unit + 1, 1))
    results[1].start()
    for copy in results:
        copy.wait()


def target_h_rows(parts, one, zero):
    big, small = norm_parts(parts, softening_sq)
    minus_high = [-2.0 * part[0] for part in parts]
    minus_one = [-2.0 * part[2] for part in parts]
    minus_two = [-2.0 * part[3] for part in parts]
    rows = minus_high + [one] * 3 + list(big) + minus_high + minus_one + minus_high
    return rows + minus_two + minus_one + [one] * 3 + list(small) + [zero] * 2


def target_features(octet, tg_ref, ce_ref, feat_ref, ah_ref):
    left = lax.broadcasted_iota(jnp.int32, (8, 128), 1) < LEAF
    one = jnp.ones((8, 128), F32)
    zero = jnp.zeros((8, 128), F32)
    parts, centred = [], []
    for comp in range(3):
        rows = pl.ds(octet * 32 + comp, 8, stride=4)
        value = tg_ref[rows, :]
        first = jnp.broadcast_to(value[:, 0:1], (8, 128))
        second = jnp.broadcast_to(value[:, LEAF : LEAF + 1], (8, 128))
        ce_ref[comp, pl.ds(octet * 16, 8, stride=2), :] = first
        ce_ref[comp, pl.ds(octet * 16 + 1, 8, stride=2), :] = second
        value = value - jnp.where(left, first, second)
        tg_ref[rows, :] = value
        centred.append(value)
        parts.append(grid_parts(value))
    rows = target_h_rows(parts, one, zero)
    x, y, z = centred
    split = [three_parts(v) for v in (x, y, z, x * x, y * y, z * z, x * y, x * z, y * z)]
    for which in (0, 0, 1, 0, 1, 2):
        rows += [part[which] for part in split]
    rows += [one] * 3 + [zero] * 7
    for at, value in enumerate(rows):
        feat_ref[8 * at : 8 * at + 8, :] = value
    for sub in range(8):
        features = feat_ref[pl.ds(sub, H_ROWS + Q_ROWS, stride=8), :].T.astype(BF16)
        ah_ref[octet * 8 + sub, :, 0 : H_ROWS + Q_ROWS] = features


def source_h_rows(parts):
    (p1, p2, p3), (s1, s2, s3) = norm_parts(parts)
    high = [part[0] for part in parts]
    one = [part[2] for part in parts]
    two = [part[3] for part in parts]
    rows = dict(enumerate(high + [p1, p2, p3]))
    rows.update(enumerate(one + high + two + high + one + [s1, s2, s3], 9))
    return rows


def put_rows(ref, rows):
    for at, value in rows.items():
        ref[8 * at : 8 * at + 8, :] = value


def fill_constant_rows(ref, count):
    one = jnp.ones((8, 128), F32)
    zero = jnp.zeros((8, 128), F32)
    for at in range(count):
        ones = at in (6, 7, 8, 27, 28, 29) or at == V_AT + 3
        ref[8 * at : 8 * at + 8, :] = one if ones else zero


def cell_features(n_dom, n_sub, octet, cl_ref, spread_ref, ce_ref, cf_ref, cm_ref):
    ids = cl_ref[pl.ds(pl.multiple_of(8 * octet, 8), 8), :]
    lane = ids & 127
    owner = ids >> 7
    me = lax.axis_index("sub")

    def look_up(dom, shift, found):
        here = owner == dom * n_sub + lax.bitwise_xor(me, shift)
        new = []
        for comp in range(CELL_COMPS):
            value = jnp.take_along_axis(spread_ref[dom, shift, comp], lane, axis=1, mode="promise_in_bounds")
            new.append(jnp.where(here, value, found[comp]))
        return tuple(new)

    found = tuple(jnp.zeros((8, 128), F32) for _ in range(CELL_COMPS))
    if n_dom <= 8:
        for dom in range(n_dom):
            for shift in range(n_sub):
                found = look_up(dom, shift, found)
                yield
    else:

        def one_domain(dom, found):
            for shift in range(n_sub):
                found = look_up(dom, shift, found)
            return found

        found = lax.fori_loop(0, n_dom, one_domain, found)
    mass, cx, cy, cz, xx, yy, zz, xy, xz, yz = found
    yield "found"
    cm_ref[...] = mass
    rows8 = pl.ds(pl.multiple_of(8 * octet, 8), 8)
    cx, cy, cz = [value - ce_ref[comp, rows8, :] for comp, value in enumerate((cx, cy, cz))]
    put_rows(cf_ref, source_h_rows([grid_parts(value) for value in (cx, cy, cz)]))
    yield
    qx = xx * cx + xy * cy + xz * cz
    qy = xy * cx + yy * cy + yz * cz
    qz = xz * cx + yz * cy + zz * cz
    const = three_parts(2.5 * (qx * cx + qy * cy + qz * cz))
    linear = [-5.0 * qx, -5.0 * qy, -5.0 * qz]
    square = [2.5 * xx, 2.5 * yy, 2.5 * zz, 5.0 * xy, 5.0 * xz, 5.0 * yz]
    split = [three_parts(value) for value in linear + square]
    rows = []
    for which in (0, 1, 0, 2, 1, 0):
        rows += [part[which] for part in split]
    rows += list(const)
    put_rows(cf_ref, dict(enumerate(rows, Q_AT)))
    yield
    for comp, value in enumerate((cx, cy, cz)):
        for which, part in enumerate(three_parts(value)):
            cf_ref[8 * (V_AT + 4 * which + comp) : 8 * (V_AT + 4 * which + comp) + 8, :] = part
    yield
    columns = {name: three_parts(value) for name, value in dict(xx=xx, yy=yy, zz=zz, xy=xy, xz=xz, yz=yz, cx=qx, cy=qy, cz=qz).items()}
    order = (("xx", "xy", "xz"), ("xy", "yy", "yz"), ("xz", "yz", "zz"), ("cx", "cy", "cz"))
    for which in range(3):
        for column, names in enumerate(order):
            for row, name in enumerate(names):
                at = U_AT + 16 * which + 4 * column + row
                cf_ref[8 * at : 8 * at + 8, :] = columns[name][which]


def source_moments(group, ll_ref, tab_ref, ce_ref, raw_ref, sf_ref):
    left = lax.broadcasted_iota(jnp.int32, (4, 128), 1) < LEAF
    for pair in range(NLEAF // 2):
        first = tab_ref[ll_ref[2 * pair, group]]
        second = tab_ref[ll_ref[2 * pair + 1, group]]
        raw_ref[4 * pair : 4 * pair + 4, :] = jnp.where(left, first, second)
    value = [raw_ref[pl.ds(comp, 8, stride=4), :] for comp in range(4)]
    mass = value[3]
    centred = [value[comp] - ce_ref[comp, pl.ds(group, 1), :] for comp in range(3)]
    for comp, v in enumerate([mass * v for v in centred] + [mass]):
        for which, part in enumerate(high_low(v)):
            at = 4 * which + comp
            sf_ref[8 * at : 8 * at + 8, :] = part


def transposed_dot(rows, weights):
    return lax.dot_general(rows, weights, (((1,), (1,)), ((), ())), preferred_element_type=F32)


def stacked(value):
    return jnp.concatenate(two_parts(value), axis=0)


def cell_group(sub, target, cf_ref, cm_ref):
    def cell_rows(at, count):
        return cf_ref[pl.ds(8 * at + sub, count, stride=8), :].astype(BF16)

    forms = jnp.concatenate(
        [
            jnp.concatenate([cell_rows(0, H_ROWS), jnp.zeros((H_ROWS, 128), BF16)], axis=1),
            jnp.concatenate([jnp.zeros((Q_ROWS, 128), BF16), cell_rows(Q_AT, Q_ROWS)], axis=1),
        ],
        axis=0,
    )
    forms = jnp.dot(target[:, 0 : H_ROWS + Q_ROWS], forms, preferred_element_type=F32)
    dist_sq, quad_form = forms[:, 0:128], forms[:, 128:256]
    inv = lax.rsqrt(dist_sq)
    inv_two = inv * inv
    inv_three = inv * inv_two
    pull = inv_three * (cm_ref[pl.ds(sub, 1), :] + quad_form * (inv_two * inv_two))
    moments = jnp.concatenate(
        [
            jnp.concatenate([cell_rows(V_AT, V_ROWS), jnp.zeros((V_ROWS, 128), BF16)], axis=1),
            jnp.concatenate([jnp.zeros((U_ROWS, 128), BF16), cell_rows(U_AT, U_ROWS)], axis=1),
        ],
        axis=0,
    )
    both = jnp.concatenate([stacked(pull), stacked(inv_three * inv_two)], axis=1)
    return both, moments


def pair_lanes(pair):
    return pl.ds(pl.multiple_of(128 * pair, 128), 128)


def pair_place(tg_ref, pair):
    return tg_ref[pl.ds(pl.multiple_of(4 * pair, 4), 4), :]


def point_sums(sums, place):
    sums = sums + pltpu.roll(sums, 4, 0)
    return sums[0:3] - place[0:3] * sums[3:4]


def cell_pull(octet, tg_ref, ah_ref, cf_ref, cm_ref, out_ref):
    upper = lax.broadcasted_iota(jnp.int32, (8, 128), 0) < 4
    left = lax.broadcasted_iota(jnp.int32, (LEAF, 128), 1) < LEAF
    for inner in range(4):
        pair = octet * 4 + inner
        first, first_moments = cell_group(2 * inner, ah_ref[pair, 0:LEAF, :], cf_ref, cm_ref)
        yield
        second, second_moments = cell_group(2 * inner + 1, ah_ref[pair, LEAF:, :], cf_ref, cm_ref)
        moments = jnp.concatenate([first_moments, second_moments], axis=0)
        sums = transposed_dot(jnp.concatenate([first, second], axis=0), moments)
        yield
        sums = jnp.where(left, sums[0:64] + sums[64:128], sums[128:192] + sums[192:256]).T
        sums = jnp.concatenate([sums[0:64], sums[64:128]], axis=1)
        place = pair_place(tg_ref, pair)
        x, y, z = [place[comp : comp + 1, :] for comp in range(3)]
        quads = sums[16:32] + sums[32:48] + sums[48:64]
        turned = quads[0:8] * jnp.where(upper, x, y) + quads[8:16] * jnp.where(upper, z, -1.0)
        turned = turned + pltpu.roll(turned, 4, 0)
        out_ref[:, pair_lanes(pair)] = point_sums(sums[0:8] + sums[8:16], place) + turned[0:3]


def put_block_pair(tab_ref, block, value):
    left = lax.broadcasted_iota(jnp.int32, (4, 128), 1) < LEAF
    turned = pltpu.roll(value, LEAF, 1)
    tab_ref[block] = jnp.where(left, value, turned)
    tab_ref[block + 1] = jnp.where(left, turned, value)


def put_eight_pairs(rows_ref, block, coords, feat_ref):
    put_rows(feat_ref, source_h_rows([grid_parts(value) for value in coords]))
    for pair in range(8):
        columns = feat_ref[pl.ds(pair, H_ROWS, stride=8), :].astype(BF16)
        spread = jnp.concatenate([columns] * 4, axis=0).T
        rows_ref[block + 2 * pair] = spread[0:LEAF]
        rows_ref[block + 2 * pair + 1] = spread[LEAF:]


def prepare_kernel(n_dom, n_sub, *refs):
    bundle_ref, near_refs, recv_ref = refs[0], refs[1:n_sub], refs[n_sub]
    tab_ref, rows_ref, at_ref, tg_ref, ce_ref, ah_ref, cl_ref, ll_ref, feat_ref, four_ref = refs[n_sub + 1 :]
    own_ref = bundle_ref.at[0:OWN_ROWS]
    cl_ref[...] = bundle_ref[OWN_ROWS : OWN_ROWS + LEAF_DEV, :].astype(jnp.int32)
    ll_ref[...] = bundle_ref[OWN_ROWS + LEAF_DEV :, :].astype(jnp.int32)
    for at in range(8):
        fill_constant_rows(four_ref.at[at], H_ROWS)
    me = lax.axis_index("sub")

    def near_blocks(shift, near_ref):
        seg = lax.bitwise_xor(me, shift)

        def near(step, carry):
            for at in range(8):
                octet = 8 * step + at
                block = seg * LEAF_DEV + 16 * octet
                first = pl.multiple_of(32 * octet, 32)
                for pair in range(8):
                    put_block_pair(tab_ref, block + 2 * pair, near_ref[pl.ds(pl.multiple_of(first + 4 * pair, 4), 4), :])
                coords = [near_ref[pl.ds(first + comp, 8, stride=4), :] for comp in range(3)]
                put_eight_pairs(rows_ref, block, coords, four_ref.at[at])
            return carry

        lax.fori_loop(0, PAIRS // 64, near, 0)

    for shift in range(1, n_sub):
        near_blocks(shift, near_refs[shift - 1])
    far_tables(n_dom, n_sub * LEAF_DEV, recv_ref, tab_ref, rows_ref, four_ref)
    near_blocks(0, own_ref)
    tg_ref[...] = own_ref[...]

    def targets(step, carry):
        for at in range(2):
            octet = 2 * step + at
            target_features(octet, tg_ref, ce_ref, feat_ref.at[at], ah_ref)
            target_rows(octet, own_ref, four_ref.at[at], at_ref)
        return carry

    lax.fori_loop(0, PAIRS // 16, targets, 0)


def far_tables(n_dom, first_block, recv_ref, tab_ref, rows_ref, four_ref):
    me = lax.axis_index("dom")
    for two in range(RANGE):
        halves = []
        for slot in (2 * two, 2 * two + 1):
            source = me - OFFSETS[slot]
            inside = (source >= 0) & (source < n_dom)
            source = jnp.clip(source, 0, n_dom - 1)
            for unit in range(OUT_UNITS):
                value = jnp.where(inside, recv_ref[source, 4 * unit : 4 * unit + 4, :], 0.0)
                put_block_pair(tab_ref, first_block + slot * CAP + 2 * unit, value)
            halves.append([jnp.where(inside, recv_ref[source, pl.ds(comp, OUT_UNITS, stride=4), :], 0.0) for comp in range(3)])
        coords = [jnp.concatenate([one, other], axis=0) for one, other in zip(*halves)]
        put_eight_pairs(rows_ref, first_block + 2 * two * CAP, coords, four_ref.at[two])


def target_rows(octet, own_ref, feat_ref, at_ref):
    one = jnp.ones((8, 128), F32)
    zero = jnp.zeros((8, 128), F32)
    parts = [grid_parts(own_ref[pl.ds(octet * 32 + comp, 8, stride=4), :]) for comp in range(3)]
    for at, value in enumerate(target_h_rows(parts, one, zero)):
        feat_ref[8 * at : 8 * at + 8, :] = value
    for pair in range(8):
        at_ref[octet * 8 + pair] = feat_ref[pl.ds(pair, H_ROWS, stride=8), :].astype(BF16)


def run(strand, steps=None):
    taken = 0
    while steps is None or taken < steps:
        taken += 1
        if next(strand, "end") == "end":
            return


def pull_kernel(n_dom, n_sub, *refs):
    cell_refs = refs[:n_sub]
    tab_ref, rows_ref, at_ref, tg_ref, ce_ref, ah_ref, cl_ref, ll_in, out_ref = refs[n_sub : n_sub + 9]
    ll_ref, spread_ref, cf_ref, cm_ref, raw_ref, even_ref, odd_ref, dist_even, dist_odd, sem = refs[n_sub + 9 :]
    copy = pltpu.make_async_copy(ll_in, ll_ref, sem)
    copy.start()
    fill_constant_rows(cf_ref, CELL_ROWS)

    def build(octet):
        return cell_features(n_dom, n_sub, octet, cl_ref, spread_ref, ce_ref, cf_ref, cm_ref)

    def spread(dom, carry):
        for shift in range(n_sub):
            for comp in range(CELL_COMPS):
                row = cell_refs[shift][dom, comp : comp + 1, :]
                spread_ref[dom, shift, comp] = jnp.broadcast_to(row, (8, 128))
        return carry

    lax.fori_loop(0, n_dom, spread, 0)

    left = lax.broadcasted_iota(jnp.int32, (M_ROWS, 128), 1) < LEAF
    left_target = lax.broadcasted_iota(jnp.int32, (H_ROWS, 128), 1) < LEAF
    owner = (lax.broadcasted_iota(jnp.int32, (LEAF, 128), 1) // H_ROWS).astype(BF16)
    lower_half, first_own, third_own = owner < 2.0, owner == 0.0, owner == 2.0

    def features(quad, raw_at, slot_ref):
        for group in range(4):
            source_moments(4 * quad + group, ll_ref, tab_ref, ce_ref, raw_ref.at[raw_at + group], slot_ref.at[group])
            yield

    def distances(quad, dist_ref):
        nothing = jnp.zeros((H_ROWS, 128), BF16)
        first, second = at_ref[2 * quad], at_ref[2 * quad + 1]
        targets = jnp.concatenate(
            [
                jnp.concatenate([jnp.where(left_target, first, nothing), nothing], axis=1),
                jnp.concatenate([jnp.where(left_target, nothing, first), nothing], axis=1),
                jnp.concatenate([nothing, jnp.where(left_target, second, nothing)], axis=1),
                jnp.concatenate([nothing, jnp.where(left_target, nothing, second)], axis=1),
            ],
            axis=0,
        )
        sources = []
        for j in range(NLEAF):
            rows = [rows_ref[ll_ref[j, 4 * quad + group]] for group in range(4)]
            low = jnp.where(first_own, rows[0], rows[1])
            high = jnp.where(third_own, rows[2], rows[3])
            sources.append(jnp.where(lower_half, low, high))
        dist_ref[...] = jnp.dot(jnp.concatenate(sources, axis=0), targets, preferred_element_type=F32)
        yield

    def pull(quad, slot_ref, dist_ref):
        total = jnp.zeros((4 * M_ROWS, 256), F32)
        for chunk in range(8):
            inv = lax.rsqrt(dist_ref[128 * chunk : 128 * chunk + 128, :])
            weights = stacked(inv * inv * inv)
            rows = [slot_ref[group, pl.ds(chunk, M_ROWS, stride=8), :] for group in range(4)]
            rows = jnp.concatenate(rows, axis=0).astype(BF16)
            total += jnp.dot(jnp.concatenate([rows, rows], axis=1), weights, preferred_element_type=F32)
            yield
        for side in range(2):
            pair = 2 * quad + side
            at, columns = 2 * M_ROWS * side, slice(128 * side, 128 * side + 128)
            sums = jnp.where(left, total[at : at + M_ROWS, columns], total[at + M_ROWS : at + 2 * M_ROWS, columns])
            lanes = pair_lanes(pair)
            out_ref[:, lanes] = out_ref[:, lanes] + point_sums(sums, pair_place(tg_ref, pair))

    quads, octets = LEAF_DEV // 4, LEAF_DEV // 8
    copy.wait()
    first, moments, distance = build(0), features(0, 0, even_ref), distances(0, dist_even)
    for step in range(4):
        run(first, 8)
        run(moments, 1)
        if step % 2 == 0:
            run(distance, 1)
    run(first)
    run(moments)
    run(distance)

    def one_octet(octet, carry):
        quad = 2 * octet
        after = jnp.minimum(quad + 2, quads - 1)
        cells = cell_pull(octet, tg_ref, ah_ref, cf_ref, cm_ref, out_ref)
        coming = build(jnp.minimum(octet + 1, octets - 1))
        for half, (now, slot_ref, dist_ref, ahead, ahead_slot, ahead_dist, raw_at) in enumerate(
            (
                (quad, even_ref, dist_even, quad + 1, odd_ref, dist_odd, 4),
                (quad + 1, odd_ref, dist_odd, after, even_ref, dist_even, 0),
            )
        ):
            direct = pull(now, slot_ref, dist_ref)
            moments, distance = features(ahead, raw_at, ahead_slot), distances(ahead, ahead_dist)
            for step in range(8):
                if step == 1:
                    run(distance, 1)
                run(direct, 1)
                if step % 2 == 0:
                    run(moments, 1)
                if half == 0 or step < 4:
                    run(coming, 3)
                    if step % 4 != 3:
                        run(cells, 1)
                elif step == 4:
                    run(cells)
                else:
                    run(coming, 1)
            run(moments)
            run(distance)
            run(direct)
        run(coming)
        return carry

    lax.fori_loop(0, octets, one_octet, 0)


def on_device(n_dom, n_sub, positions, masses, cell_mass, cell_center, cell_quad, cell_list, leaf_list, send_list, send_count):
    vmem = pl.BlockSpec(memory_space=pltpu.VMEM)
    smem = pl.BlockSpec(memory_space=pltpu.SMEM)
    anywhere = pl.BlockSpec(memory_space=pl.ANY)

    def limit(mib):
        return pltpu.CompilerParams(vmem_limit_bytes=mib * 1024 * 1024)

    ins = (
        positions,
        masses.reshape(1, -1),
        cell_mass.reshape(1, -1),
        cell_center,
        cell_quad,
        cell_list,
        leaf_list.T,
        send_list.reshape(2 * RANGE, CAP),
        send_count.reshape(1, 2 * RANGE),
    )
    bundle_rows = OWN_ROWS + LEAF_DEV + NLEAF
    packed, sent, bundle = pl.pallas_call(
        functools.partial(pack_kernel, n_dom),
        out_shape=(
            jax.ShapeDtypeStruct((OWN_ROWS, 128), F32),
            jax.ShapeDtypeStruct((n_dom, SENT_ROWS, 128), F32),
            jax.ShapeDtypeStruct((bundle_rows, 128), F32),
        ),
        in_specs=[pl.BlockSpec(memory_space=pltpu.HBM)] * 9,
        out_specs=[anywhere] * 3,
        scratch_shapes=[pltpu.VMEM(array.shape, array.dtype) for array in ins[:7]]
        + [pltpu.SMEM(array.shape, jnp.int32) for array in ins[7:]]
        + [
            pltpu.VMEM((bundle_rows, 128), F32),
            pltpu.VMEM((n_dom + 1, SENT_ROWS, 128), F32),
            pltpu.SemaphoreType.DMA((12,)),
        ],
        compiler_params=limit(63),
        name="pack_own",
    )(*ins)
    received = lax.all_to_all(sent, "dom", split_axis=0, concat_axis=0, tiled=True)

    def across(value, bits):
        return lax.ppermute(value, "sub", [(seg, seg ^ bits) for seg in range(n_sub)])

    nearby = {0: packed}
    bit = n_sub // 2
    while bit:
        nearby.update({at ^ bit: across(value, bit) for at, value in nearby.items()})
        bit //= 2
    nearby = [nearby[at] for at in range(n_sub)]
    own_cells = received[:, OUT_ROWS:]
    cells = [own_cells] + [across(own_cells, bits) for bits in range(1, n_sub)]
    n_blocks = n_sub * LEAF_DEV + 2 * RANGE * CAP
    prepared = pl.pallas_call(
        functools.partial(prepare_kernel, n_dom, n_sub),
        out_shape=(
            jax.ShapeDtypeStruct((n_blocks, 4, 128), F32),
            jax.ShapeDtypeStruct((n_blocks, LEAF, 128), BF16),
            jax.ShapeDtypeStruct((PAIRS, H_ROWS, 128), BF16),
            jax.ShapeDtypeStruct((OWN_ROWS, 128), F32),
            jax.ShapeDtypeStruct((3, LEAF_DEV, 128), F32),
            jax.ShapeDtypeStruct((PAIRS, 128, 128), BF16),
            jax.ShapeDtypeStruct((LEAF_DEV, NCELL), jnp.int32),
            jax.ShapeDtypeStruct((NLEAF, LEAF_DEV), jnp.int32),
        ),
        in_specs=[vmem] * (n_sub + 1),
        out_specs=[vmem] * 8,
        scratch_shapes=[
            pltpu.VMEM((2, 8 * (H_ROWS + Q_ROWS), 128), F32),
            pltpu.VMEM((8, 8 * H_ROWS, 128), F32),
        ],
        compiler_params=limit(24),
        cost_estimate=pl.CostEstimate(flops=0, bytes_accessed=20_000_000, transcendentals=0),
        name="prepare",
    )(bundle, *nearby[1:], received)
    return pl.pallas_call(
        functools.partial(pull_kernel, n_dom, n_sub),
        out_shape=jax.ShapeDtypeStruct((3, LEAF_DEV * LEAF), F32),
        in_specs=[vmem] * (n_sub + 8),
        out_specs=vmem,
        scratch_shapes=[
            pltpu.SMEM((NLEAF, LEAF_DEV), jnp.int32),
            pltpu.VMEM((n_dom, n_sub, CELL_COMPS, 8, 128), F32),
            pltpu.VMEM((8 * CELL_ROWS, 128), F32),
            pltpu.VMEM((8, 128), F32),
            pltpu.VMEM((8, 32, 128), F32),
            pltpu.VMEM((4, 8 * M_ROWS, 128), F32),
            pltpu.VMEM((4, 8 * M_ROWS, 128), F32),
            pltpu.VMEM((NLEAF * LEAF, 256), F32),
            pltpu.VMEM((NLEAF * LEAF, 256), F32),
            pltpu.SemaphoreType.DMA(()),
        ],
        compiler_params=limit(24),
        name="pull",
    )(*cells, *prepared)


def solution(mesh):
    sharded = P(("dom", "sub"))
    return jax.shard_map(
        functools.partial(on_device, mesh.shape["dom"], mesh.shape["sub"]),
        mesh=mesh,
        in_specs=(
            P(None, ("dom", "sub")),
            sharded,
            sharded,
            P(None, ("dom", "sub")),
            P(None, ("dom", "sub")),
            P(("dom", "sub"), None),
            P(("dom", "sub"), None),
            P("dom", "sub", None, None),
            P("dom", "sub", None),
        ),
        out_specs=P(None, ("dom", "sub")),
        check_vma=False,
    )
```

```python
import functools

import jax
import jax.numpy as jnp
from jax import lax
from jax.experimental import pallas as pl
from jax.experimental.pallas import tpu as pltpu
from jax.sharding import PartitionSpec as P

LEAF = 64
LEAF_DEV = 128
NCELL = 128
NLEAF = 16
RANGE = 4
CAP = 8
PAIRS = LEAF_DEV // 2
OUT_UNITS = CAP // 2
OWN_ROWS = 4 * PAIRS
OUT_ROWS = 4 * OUT_UNITS
CELL_COMPS = 10
CELL_PAD = 16
SENT_ROWS = OUT_ROWS + CELL_PAD
OFFSETS = list(range(-RANGE, 0)) + list(range(1, RANGE + 1))

softening_sq = 0.0025
GRID_ROUND = 49152.0
F32 = jnp.float32
BF16 = jnp.bfloat16

H_ROWS = 32
Q_ROWS = 64
V_ROWS = 16
U_ROWS = 48
Q_AT = H_ROWS
V_AT = Q_AT + Q_ROWS
U_AT = V_AT + V_ROWS
CELL_ROWS = U_AT + U_ROWS
M_ROWS = 8


def rounded(value):
    return value.astype(BF16).astype(F32)


def three_parts(value):
    first = rounded(value)
    rest = value - first
    second = rounded(rest)
    return first, second, rest - second


def high_low(value):
    high = rounded(value)
    return high, value - high


def two_parts(value):
    first = value.astype(BF16)
    return first, (value - first.astype(F32)).astype(BF16)


def grid_parts(value):
    high = (value + GRID_ROUND) - GRID_ROUND
    low = value - high
    first = rounded(low)
    return high, low, first, low - first


def norm_parts(parts, extra=None):
    big = sum(high * high for high, _, _, _ in parts)
    small = sum(low * (2.0 * high + low) for high, low, _, _ in parts)
    if extra is not None:
        small = small + extra
    return three_parts(big), three_parts(small)


def put_own(pos_ref, mass_ref, own_ref):
    for pair in range(PAIRS):
        lanes = pl.ds(128 * pair, 128)
        own_ref[4 * pair : 4 * pair + 3, :] = pos_ref[:, lanes]
        own_ref[4 * pair + 3 : 4 * pair + 4, :] = mass_ref[:, lanes]


def pack_kernel(n_dom, *refs):
    ins, outs, scratch, (out_ref, sent_ref, sems) = refs[:9], refs[9:12], refs[12:21], refs[21:]
    results = [
        pltpu.make_async_copy(out_ref.at[pl.ds(0, OWN_ROWS)], outs[0], sems.at[9]),
        pltpu.make_async_copy(sent_ref.at[pl.ds(0, n_dom)], outs[1], sems.at[10]),
        pltpu.make_async_copy(out_ref, outs[2], sems.at[11]),
    ]
    copies = [pltpu.make_async_copy(src, dst, sems.at[at]) for at, (src, dst) in enumerate(zip(ins, scratch))]
    for copy in copies:
        copy.start()
    pos_ref, mass_ref, cmass_ref, center_ref, quad_ref, cl_ref, ll_ref, list_ref, count_ref = scratch
    me = lax.axis_index("dom")
    left = lax.broadcasted_iota(jnp.int32, (4, 128), 1) < LEAF
    sent_ref[...] = jnp.zeros((n_dom + 1, SENT_ROWS, 128), F32)
    for copy in copies:
        copy.wait()
    put_own(pos_ref, mass_ref, out_ref)
    results[0].start()
    out_ref[OWN_ROWS : OWN_ROWS + LEAF_DEV, :] = cl_ref[...].astype(F32)
    out_ref[OWN_ROWS + LEAF_DEV :, :] = ll_ref[...].astype(F32)
    results[2].start()

    def put_cells(target, carry):
        sent_ref[target, OUT_ROWS : OUT_ROWS + 1, :] = cmass_ref[...]
        sent_ref[target, OUT_ROWS + 1 : OUT_ROWS + 4, :] = center_ref[...]
        sent_ref[target, OUT_ROWS + 4 : OUT_ROWS + 10, :] = quad_ref[...]
        return carry

    lax.fori_loop(0, n_dom, put_cells, 0)

    def half(slot, j, right):
        block = list_ref[slot, j]
        value = out_ref[pl.ds(pl.multiple_of(4 * (block // 2), 4), 4), :]
        value = jnp.where(j < count_ref[0, slot], value, 0.0)
        return jnp.where((block & 1) == right, value, pltpu.roll(value, LEAF, 1))

    for slot in range(2 * RANGE):
        target = me + OFFSETS[slot]
        target = jnp.where((target >= 0) & (target < n_dom), target, n_dom)
        for unit in range(OUT_UNITS):
            sent_ref[target, 4 * unit : 4 * unit + 4, :] = jnp.where(left, half(slot, 2 * unit, 0), half(slot, 2 * unit + 1, 1))
    results[1].start()
    for copy in results:
        copy.wait()


def target_h_rows(parts, one, zero):
    big, small = norm_parts(parts, softening_sq)
    minus_high = [-2.0 * part[0] for part in parts]
    minus_one = [-2.0 * part[2] for part in parts]
    minus_two = [-2.0 * part[3] for part in parts]
    rows = minus_high + [one] * 3 + list(big) + minus_high + minus_one + minus_high
    return rows + minus_two + minus_one + [one] * 3 + list(small) + [zero] * 2


def target_features(octet, tg_ref, ce_ref, feat_ref, ah_ref):
    left = lax.broadcasted_iota(jnp.int32, (8, 128), 1) < LEAF
    one = jnp.ones((8, 128), F32)
    zero = jnp.zeros((8, 128), F32)
    parts, centred = [], []
    for comp in range(3):
        rows = pl.ds(octet * 32 + comp, 8, stride=4)
        value = tg_ref[rows, :]
        first = jnp.broadcast_to(value[:, 0:1], (8, 128))
        second = jnp.broadcast_to(value[:, LEAF : LEAF + 1], (8, 128))
        ce_ref[comp, pl.ds(octet * 16, 8, stride=2), :] = first
        ce_ref[comp, pl.ds(octet * 16 + 1, 8, stride=2), :] = second
        value = value - jnp.where(left, first, second)
        tg_ref[rows, :] = value
        centred.append(value)
        parts.append(grid_parts(value))
    rows = target_h_rows(parts, one, zero)
    x, y, z = centred
    split = [three_parts(v) for v in (x, y, z, x * x, y * y, z * z, x * y, x * z, y * z)]
    for which in (0, 0, 1, 0, 1, 2):
        rows += [part[which] for part in split]
    rows += [one] * 3 + [zero] * 7
    for at, value in enumerate(rows):
        feat_ref[8 * at : 8 * at + 8, :] = value
    for sub in range(8):
        features = feat_ref[pl.ds(sub, H_ROWS + Q_ROWS, stride=8), :].T.astype(BF16)
        ah_ref[octet * 8 + sub, :, 0 : H_ROWS + Q_ROWS] = features


def source_h_rows(parts):
    (p1, p2, p3), (s1, s2, s3) = norm_parts(parts)
    high = [part[0] for part in parts]
    one = [part[2] for part in parts]
    two = [part[3] for part in parts]
    rows = dict(enumerate(high + [p1, p2, p3]))
    rows.update(enumerate(one + high + two + high + one + [s1, s2, s3], 9))
    return rows


def put_rows(ref, rows):
    for at, value in rows.items():
        ref[8 * at : 8 * at + 8, :] = value


def fill_constant_rows(ref, count):
    one = jnp.ones((8, 128), F32)
    zero = jnp.zeros((8, 128), F32)
    for at in range(count):
        ones = at in (6, 7, 8, 27, 28, 29) or at == V_AT + 3
        ref[8 * at : 8 * at + 8, :] = one if ones else zero


def cell_features(n_dom, n_sub, octet, cl_ref, spread_ref, ce_ref, cf_ref, cm_ref):
    ids = cl_ref[pl.ds(pl.multiple_of(8 * octet, 8), 8), :]
    lane = ids & 127
    owner = ids >> 7
    me = lax.axis_index("sub")

    def look_up(dom, shift, found):
        here = owner == dom * n_sub + lax.bitwise_xor(me, shift)
        new = []
        for comp in range(CELL_COMPS):
            value = jnp.take_along_axis(spread_ref[dom, shift, comp], lane, axis=1, mode="promise_in_bounds")
            new.append(jnp.where(here, value, found[comp]))
        return tuple(new)

    found = tuple(jnp.zeros((8, 128), F32) for _ in range(CELL_COMPS))
    if n_dom <= 8:
        for dom in range(n_dom):
            for shift in range(n_sub):
                found = look_up(dom, shift, found)
                yield
    else:

        def one_domain(dom, found):
            for shift in range(n_sub):
                found = look_up(dom, shift, found)
            return found

        found = lax.fori_loop(0, n_dom, one_domain, found)
    mass, cx, cy, cz, xx, yy, zz, xy, xz, yz = found
    yield "found"
    cm_ref[...] = mass
    rows8 = pl.ds(pl.multiple_of(8 * octet, 8), 8)
    cx, cy, cz = [value - ce_ref[comp, rows8, :] for comp, value in enumerate((cx, cy, cz))]
    put_rows(cf_ref, source_h_rows([grid_parts(value) for value in (cx, cy, cz)]))
    yield
    qx = xx * cx + xy * cy + xz * cz
    qy = xy * cx + yy * cy + yz * cz
    qz = xz * cx + yz * cy + zz * cz
    const = three_parts(2.5 * (qx * cx + qy * cy + qz * cz))
    linear = [-5.0 * qx, -5.0 * qy, -5.0 * qz]
    square = [2.5 * xx, 2.5 * yy, 2.5 * zz, 5.0 * xy, 5.0 * xz, 5.0 * yz]
    split = [three_parts(value) for value in linear + square]
    rows = []
    for which in (0, 1, 0, 2, 1, 0):
        rows += [part[which] for part in split]
    rows += list(const)
    put_rows(cf_ref, dict(enumerate(rows, Q_AT)))
    yield
    for comp, value in enumerate((cx, cy, cz)):
        for which, part in enumerate(three_parts(value)):
            cf_ref[8 * (V_AT + 4 * which + comp) : 8 * (V_AT + 4 * which + comp) + 8, :] = part
    yield
    columns = {name: three_parts(value) for name, value in dict(xx=xx, yy=yy, zz=zz, xy=xy, xz=xz, yz=yz, cx=qx, cy=qy, cz=qz).items()}
    order = (("xx", "xy", "xz"), ("xy", "yy", "yz"), ("xz", "yz", "zz"), ("cx", "cy", "cz"))
    for which in range(3):
        for column, names in enumerate(order):
            for row, name in enumerate(names):
                at = U_AT + 16 * which + 4 * column + row
                cf_ref[8 * at : 8 * at + 8, :] = columns[name][which]


def source_moments(group, ll_ref, tab_ref, ce_ref, raw_ref, sf_ref):
    left = lax.broadcasted_iota(jnp.int32, (4, 128), 1) < LEAF
    for pair in range(NLEAF // 2):
        first = tab_ref[ll_ref[2 * pair, group]]
        second = tab_ref[ll_ref[2 * pair + 1, group]]
        raw_ref[4 * pair : 4 * pair + 4, :] = jnp.where(left, first, second)
    value = [raw_ref[pl.ds(comp, 8, stride=4), :] for comp in range(4)]
    mass = value[3]
    centred = [value[comp] - ce_ref[comp, pl.ds(group, 1), :] for comp in range(3)]
    for comp, v in enumerate([mass * v for v in centred] + [mass]):
        for which, part in enumerate(high_low(v)):
            at = 4 * which + comp
            sf_ref[8 * at : 8 * at + 8, :] = part


def transposed_dot(rows, weights):
    return lax.dot_general(rows, weights, (((1,), (1,)), ((), ())), preferred_element_type=F32)


def stacked(value):
    return jnp.concatenate(two_parts(value), axis=0)


def cell_group(sub, target, cf_ref, cm_ref):
    def cell_rows(at, count):
        return cf_ref[pl.ds(8 * at + sub, count, stride=8), :].astype(BF16)

    forms = jnp.concatenate(
        [
            jnp.concatenate([cell_rows(0, H_ROWS), jnp.zeros((H_ROWS, 128), BF16)], axis=1),
            jnp.concatenate([jnp.zeros((Q_ROWS, 128), BF16), cell_rows(Q_AT, Q_ROWS)], axis=1),
        ],
        axis=0,
    )
    forms = jnp.dot(target[:, 0 : H_ROWS + Q_ROWS], forms, preferred_element_type=F32)
    dist_sq, quad_form = forms[:, 0:128], forms[:, 128:256]
    inv = lax.rsqrt(dist_sq)
    inv_two = inv * inv
    inv_three = inv * inv_two
    pull = inv_three * (cm_ref[pl.ds(sub, 1), :] + quad_form * (inv_two * inv_two))
    moments = jnp.concatenate(
        [
            jnp.concatenate([cell_rows(V_AT, V_ROWS), jnp.zeros((V_ROWS, 128), BF16)], axis=1),
            jnp.concatenate([jnp.zeros((U_ROWS, 128), BF16), cell_rows(U_AT, U_ROWS)], axis=1),
        ],
        axis=0,
    )
    both = jnp.concatenate([stacked(pull), stacked(inv_three * inv_two)], axis=1)
    return both, moments


def pair_lanes(pair):
    return pl.ds(pl.multiple_of(128 * pair, 128), 128)


def pair_place(tg_ref, pair):
    return tg_ref[pl.ds(pl.multiple_of(4 * pair, 4), 4), :]


def point_sums(sums, place):
    sums = sums + pltpu.roll(sums, 4, 0)
    return sums[0:3] - place[0:3] * sums[3:4]


def cell_pull(octet, tg_ref, ah_ref, cf_ref, cm_ref, out_ref):
    upper = lax.broadcasted_iota(jnp.int32, (8, 128), 0) < 4
    left = lax.broadcasted_iota(jnp.int32, (LEAF, 128), 1) < LEAF
    for inner in range(4):
        pair = octet * 4 + inner
        first, first_moments = cell_group(2 * inner, ah_ref[pair, 0:LEAF, :], cf_ref, cm_ref)
        yield
        second, second_moments = cell_group(2 * inner + 1, ah_ref[pair, LEAF:, :], cf_ref, cm_ref)
        moments = jnp.concatenate([first_moments, second_moments], axis=0)
        sums = transposed_dot(jnp.concatenate([first, second], axis=0), moments)
        yield
        sums = jnp.where(left, sums[0:64] + sums[64:128], sums[128:192] + sums[192:256]).T
        sums = jnp.concatenate([sums[0:64], sums[64:128]], axis=1)
        place = pair_place(tg_ref, pair)
        x, y, z = [place[comp : comp + 1, :] for comp in range(3)]
        quads = sums[16:32] + sums[32:48] + sums[48:64]
        turned = quads[0:8] * jnp.where(upper, x, y) + quads[8:16] * jnp.where(upper, z, -1.0)
        turned = turned + pltpu.roll(turned, 4, 0)
        out_ref[:, pair_lanes(pair)] = point_sums(sums[0:8] + sums[8:16], place) + turned[0:3]


def put_block_pair(tab_ref, block, value):
    left = lax.broadcasted_iota(jnp.int32, (4, 128), 1) < LEAF
    turned = pltpu.roll(value, LEAF, 1)
    tab_ref[block] = jnp.where(left, value, turned)
    tab_ref[block + 1] = jnp.where(left, turned, value)


def put_eight_pairs(rows_ref, block, coords, feat_ref):
    put_rows(feat_ref, source_h_rows([grid_parts(value) for value in coords]))
    for pair in range(8):
        columns = feat_ref[pl.ds(pair, H_ROWS, stride=8), :].astype(BF16)
        spread = jnp.concatenate([columns] * 4, axis=0).T
        rows_ref[block + 2 * pair] = spread[0:LEAF]
        rows_ref[block + 2 * pair + 1] = spread[LEAF:]


def prepare_kernel(n_dom, n_sub, *refs):
    bundle_ref, near_refs, recv_ref = refs[0], refs[1:n_sub], refs[n_sub]
    tab_ref, rows_ref, at_ref, tg_ref, ce_ref, ah_ref, cl_ref, ll_ref, feat_ref, four_ref = refs[n_sub + 1 :]
    own_ref = bundle_ref.at[0:OWN_ROWS]
    cl_ref[...] = bundle_ref[OWN_ROWS : OWN_ROWS + LEAF_DEV, :].astype(jnp.int32)
    ll_ref[...] = bundle_ref[OWN_ROWS + LEAF_DEV :, :].astype(jnp.int32)
    for at in range(8):
        fill_constant_rows(four_ref.at[at], H_ROWS)
    me = lax.axis_index("sub")

    def near_blocks(shift, near_ref):
        seg = lax.bitwise_xor(me, shift)

        def near(step, carry):
            for at in range(8):
                octet = 8 * step + at
                block = seg * LEAF_DEV + 16 * octet
                first = pl.multiple_of(32 * octet, 32)
                for pair in range(8):
                    put_block_pair(tab_ref, block + 2 * pair, near_ref[pl.ds(pl.multiple_of(first + 4 * pair, 4), 4), :])
                coords = [near_ref[pl.ds(first + comp, 8, stride=4), :] for comp in range(3)]
                put_eight_pairs(rows_ref, block, coords, four_ref.at[at])
            return carry

        lax.fori_loop(0, PAIRS // 64, near, 0)

    for shift in range(1, n_sub):
        near_blocks(shift, near_refs[shift - 1])
    far_tables(n_dom, n_sub * LEAF_DEV, recv_ref, tab_ref, rows_ref, four_ref)
    near_blocks(0, own_ref)
    tg_ref[...] = own_ref[...]

    def targets(step, carry):
        for at in range(2):
            octet = 2 * step + at
            target_features(octet, tg_ref, ce_ref, feat_ref.at[at], ah_ref)
            target_rows(octet, own_ref, four_ref.at[at], at_ref)
        return carry

    lax.fori_loop(0, PAIRS // 16, targets, 0)


def far_tables(n_dom, first_block, recv_ref, tab_ref, rows_ref, four_ref):
    me = lax.axis_index("dom")
    for two in range(RANGE):
        halves = []
        for slot in (2 * two, 2 * two + 1):
            source = me - OFFSETS[slot]
            inside = (source >= 0) & (source < n_dom)
            source = jnp.clip(source, 0, n_dom - 1)
            for unit in range(OUT_UNITS):
                value = jnp.where(inside, recv_ref[source, 4 * unit : 4 * unit + 4, :], 0.0)
                put_block_pair(tab_ref, first_block + slot * CAP + 2 * unit, value)
            halves.append([jnp.where(inside, recv_ref[source, pl.ds(comp, OUT_UNITS, stride=4), :], 0.0) for comp in range(3)])
        coords = [jnp.concatenate([one, other], axis=0) for one, other in zip(*halves)]
        put_eight_pairs(rows_ref, first_block + 2 * two * CAP, coords, four_ref.at[two])


def target_rows(octet, own_ref, feat_ref, at_ref):
    one = jnp.ones((8, 128), F32)
    zero = jnp.zeros((8, 128), F32)
    parts = [grid_parts(own_ref[pl.ds(octet * 32 + comp, 8, stride=4), :]) for comp in range(3)]
    for at, value in enumerate(target_h_rows(parts, one, zero)):
        feat_ref[8 * at : 8 * at + 8, :] = value
    for pair in range(8):
        at_ref[octet * 8 + pair] = feat_ref[pl.ds(pair, H_ROWS, stride=8), :].astype(BF16)


def run(strand, steps=None):
    taken = 0
    while steps is None or taken < steps:
        taken += 1
        if next(strand, "end") == "end":
            return


def pull_kernel(n_dom, n_sub, *refs):
    cell_refs = refs[:n_sub]
    tab_ref, rows_ref, at_ref, tg_ref, ce_ref, ah_ref, cl_ref, ll_in, out_ref = refs[n_sub : n_sub + 9]
    ll_ref, spread_ref, cf_ref, cm_ref, raw_ref, even_ref, odd_ref, dist_even, dist_odd, sem = refs[n_sub + 9 :]
    copy = pltpu.make_async_copy(ll_in, ll_ref, sem)
    copy.start()
    fill_constant_rows(cf_ref, CELL_ROWS)

    def build(octet):
        return cell_features(n_dom, n_sub, octet, cl_ref, spread_ref, ce_ref, cf_ref, cm_ref)

    def spread(dom, carry):
        for shift in range(n_sub):
            for comp in range(CELL_COMPS):
                row = cell_refs[shift][dom, comp : comp + 1, :]
                spread_ref[dom, shift, comp] = jnp.broadcast_to(row, (8, 128))
        return carry

    lax.fori_loop(0, n_dom, spread, 0)

    left = lax.broadcasted_iota(jnp.int32, (M_ROWS, 128), 1) < LEAF
    left_target = lax.broadcasted_iota(jnp.int32, (H_ROWS, 128), 1) < LEAF
    owner = (lax.broadcasted_iota(jnp.int32, (LEAF, 128), 1) // H_ROWS).astype(BF16)
    lower_half, first_own, third_own = owner < 2.0, owner == 0.0, owner == 2.0

    def features(quad, raw_at, slot_ref):
        for group in range(4):
            source_moments(4 * quad + group, ll_ref, tab_ref, ce_ref, raw_ref.at[raw_at + group], slot_ref.at[group])
            yield

    def distances(quad, dist_ref):
        nothing = jnp.zeros((H_ROWS, 128), BF16)
        first, second = at_ref[2 * quad], at_ref[2 * quad + 1]
        targets = jnp.concatenate(
            [
                jnp.concatenate([jnp.where(left_target, first, nothing), nothing], axis=1),
                jnp.concatenate([jnp.where(left_target, nothing, first), nothing], axis=1),
                jnp.concatenate([nothing, jnp.where(left_target, second, nothing)], axis=1),
                jnp.concatenate([nothing, jnp.where(left_target, nothing, second)], axis=1),
            ],
            axis=0,
        )
        sources = []
        for j in range(NLEAF):
            rows = [rows_ref[ll_ref[j, 4 * quad + group]] for group in range(4)]
            low = jnp.where(first_own, rows[0], rows[1])
            high = jnp.where(third_own, rows[2], rows[3])
            sources.append(jnp.where(lower_half, low, high))
            if j % 4 == 3:
                rows = pl.ds(LEAF * (j - 3), 4 * LEAF)
                dist_ref[rows, :] = jnp.dot(jnp.concatenate(sources, axis=0), targets, preferred_element_type=F32)
                sources = []
                yield

    def pull(quad, slot_ref, dist_ref):
        total = jnp.zeros((4 * M_ROWS, 256), F32)
        for chunk in range(8):
            inv = lax.rsqrt(dist_ref[128 * chunk : 128 * chunk + 128, :])
            weights = stacked(inv * inv * inv)
            rows = [slot_ref[group, pl.ds(chunk, M_ROWS, stride=8), :] for group in range(4)]
            rows = jnp.concatenate(rows, axis=0).astype(BF16)
            total += jnp.dot(jnp.concatenate([rows, rows], axis=1), weights, preferred_element_type=F32)
            yield
        for side in range(2):
            pair = 2 * quad + side
            at, columns = 2 * M_ROWS * side, slice(128 * side, 128 * side + 128)
            sums = jnp.where(left, total[at : at + M_ROWS, columns], total[at + M_ROWS : at + 2 * M_ROWS, columns])
            lanes = pair_lanes(pair)
            out_ref[:, lanes] = out_ref[:, lanes] + point_sums(sums, pair_place(tg_ref, pair))

    quads, octets = LEAF_DEV // 4, LEAF_DEV // 8
    run(build(0))
    copy.wait()
    run(features(0, 0, even_ref))
    run(distances(0, dist_even))

    def one_octet(octet, carry):
        quad = 2 * octet
        after = jnp.minimum(quad + 2, quads - 1)
        cells = cell_pull(octet, tg_ref, ah_ref, cf_ref, cm_ref, out_ref)
        coming = build(jnp.minimum(octet + 1, octets - 1))
        for half, (now, slot_ref, dist_ref, ahead, ahead_slot, ahead_dist, raw_at) in enumerate(
            (
                (quad, even_ref, dist_even, quad + 1, odd_ref, dist_odd, 4),
                (quad + 1, odd_ref, dist_odd, after, even_ref, dist_even, 0),
            )
        ):
            direct = pull(now, slot_ref, dist_ref)
            moments, distance = features(ahead, raw_at, ahead_slot), distances(ahead, ahead_dist)
            for step in range(8):
                if step % 2 == 1:
                    run(distance, 1)
                run(direct, 1)
                if step % 2 == 0:
                    run(moments, 1)
                if half == 0 or step < 4:
                    run(coming, 3)
                    if step % 4 != 3:
                        run(cells, 1)
                elif step == 4:
                    run(cells)
                else:
                    run(coming, 1)
            run(moments)
            run(distance)
            run(direct)
        run(coming)
        return carry

    lax.fori_loop(0, octets, one_octet, 0)


def on_device(n_dom, n_sub, positions, masses, cell_mass, cell_center, cell_quad, cell_list, leaf_list, send_list, send_count):
    vmem = pl.BlockSpec(memory_space=pltpu.VMEM)
    smem = pl.BlockSpec(memory_space=pltpu.SMEM)
    anywhere = pl.BlockSpec(memory_space=pl.ANY)

    def limit(mib):
        return pltpu.CompilerParams(vmem_limit_bytes=mib * 1024 * 1024)

    ins = (
        positions,
        masses.reshape(1, -1),
        cell_mass.reshape(1, -1),
        cell_center,
        cell_quad,
        cell_list,
        leaf_list.T,
        send_list.reshape(2 * RANGE, CAP),
        send_count.reshape(1, 2 * RANGE),
    )
    bundle_rows = OWN_ROWS + LEAF_DEV + NLEAF
    packed, sent, bundle = pl.pallas_call(
        functools.partial(pack_kernel, n_dom),
        out_shape=(
            jax.ShapeDtypeStruct((OWN_ROWS, 128), F32),
            jax.ShapeDtypeStruct((n_dom, SENT_ROWS, 128), F32),
            jax.ShapeDtypeStruct((bundle_rows, 128), F32),
        ),
        in_specs=[pl.BlockSpec(memory_space=pltpu.HBM)] * 9,
        out_specs=[anywhere] * 3,
        scratch_shapes=[pltpu.VMEM(array.shape, array.dtype) for array in ins[:7]]
        + [pltpu.SMEM(array.shape, jnp.int32) for array in ins[7:]]
        + [
            pltpu.VMEM((bundle_rows, 128), F32),
            pltpu.VMEM((n_dom + 1, SENT_ROWS, 128), F32),
            pltpu.SemaphoreType.DMA((12,)),
        ],
        compiler_params=limit(63),
        name="pack_own",
    )(*ins)
    received = lax.all_to_all(sent, "dom", split_axis=0, concat_axis=0, tiled=True)

    def across(value, bits):
        return lax.ppermute(value, "sub", [(seg, seg ^ bits) for seg in range(n_sub)])

    nearby = {0: packed}
    bit = n_sub // 2
    while bit:
        nearby.update({at ^ bit: across(value, bit) for at, value in nearby.items()})
        bit //= 2
    nearby = [nearby[at] for at in range(n_sub)]
    own_cells = received[:, OUT_ROWS:]
    cells = [own_cells] + [across(own_cells, bits) for bits in range(1, n_sub)]
    n_blocks = n_sub * LEAF_DEV + 2 * RANGE * CAP
    prepared = pl.pallas_call(
        functools.partial(prepare_kernel, n_dom, n_sub),
        out_shape=(
            jax.ShapeDtypeStruct((n_blocks, 4, 128), F32),
            jax.ShapeDtypeStruct((n_blocks, LEAF, 128), BF16),
            jax.ShapeDtypeStruct((PAIRS, H_ROWS, 128), BF16),
            jax.ShapeDtypeStruct((OWN_ROWS, 128), F32),
            jax.ShapeDtypeStruct((3, LEAF_DEV, 128), F32),
            jax.ShapeDtypeStruct((PAIRS, 128, 128), BF16),
            jax.ShapeDtypeStruct((LEAF_DEV, NCELL), jnp.int32),
            jax.ShapeDtypeStruct((NLEAF, LEAF_DEV), jnp.int32),
        ),
        in_specs=[vmem] * (n_sub + 1),
        out_specs=[vmem] * 8,
        scratch_shapes=[
            pltpu.VMEM((2, 8 * (H_ROWS + Q_ROWS), 128), F32),
            pltpu.VMEM((8, 8 * H_ROWS, 128), F32),
        ],
        compiler_params=limit(24),
        cost_estimate=pl.CostEstimate(flops=0, bytes_accessed=20_000_000, transcendentals=0),
        name="prepare",
    )(bundle, *nearby[1:], received)
    return pl.pallas_call(
        functools.partial(pull_kernel, n_dom, n_sub),
        out_shape=jax.ShapeDtypeStruct((3, LEAF_DEV * LEAF), F32),
        in_specs=[vmem] * (n_sub + 8),
        out_specs=vmem,
        scratch_shapes=[
            pltpu.SMEM((NLEAF, LEAF_DEV), jnp.int32),
            pltpu.VMEM((n_dom, n_sub, CELL_COMPS, 8, 128), F32),
            pltpu.VMEM((8 * CELL_ROWS, 128), F32),
            pltpu.VMEM((8, 128), F32),
            pltpu.VMEM((8, 32, 128), F32),
            pltpu.VMEM((4, 8 * M_ROWS, 128), F32),
            pltpu.VMEM((4, 8 * M_ROWS, 128), F32),
            pltpu.VMEM((NLEAF * LEAF, 256), F32),
            pltpu.VMEM((NLEAF * LEAF, 256), F32),
            pltpu.SemaphoreType.DMA(()),
        ],
        compiler_params=limit(24),
        name="pull",
    )(*cells, *prepared)


def solution(mesh):
    sharded = P(("dom", "sub"))
    return jax.shard_map(
        functools.partial(on_device, mesh.shape["dom"], mesh.shape["sub"]),
        mesh=mesh,
        in_specs=(
            P(None, ("dom", "sub")),
            sharded,
            sharded,
            P(None, ("dom", "sub")),
            P(None, ("dom", "sub")),
            P(("dom", "sub"), None),
            P(("dom", "sub"), None),
            P("dom", "sub", None, None),
            P("dom", "sub", None),
        ),
        out_specs=P(None, ("dom", "sub")),
        check_vma=False,
    )
```

```python
import functools

import jax
import jax.numpy as jnp
from jax import lax
from jax.experimental import pallas as pl
from jax.experimental.pallas import tpu as pltpu
from jax.sharding import PartitionSpec as P

LEAF = 64
LEAF_DEV = 128
NCELL = 128
NLEAF = 16
RANGE = 4
CAP = 8
PAIRS = LEAF_DEV // 2
OUT_UNITS = CAP // 2
OWN_ROWS = 4 * PAIRS
OUT_ROWS = 4 * OUT_UNITS
CELL_COMPS = 10
CELL_PAD = 16
SENT_ROWS = OUT_ROWS + CELL_PAD
OFFSETS = list(range(-RANGE, 0)) + list(range(1, RANGE + 1))

softening_sq = 0.0025
GRID_ROUND = 49152.0
F32 = jnp.float32
BF16 = jnp.bfloat16

H_ROWS = 32
Q_ROWS = 64
V_ROWS = 16
U_ROWS = 48
Q_AT = H_ROWS
V_AT = Q_AT + Q_ROWS
U_AT = V_AT + V_ROWS
CELL_ROWS = U_AT + U_ROWS
M_ROWS = 8


def rounded(value):
    return value.astype(BF16).astype(F32)


def three_parts(value):
    first = rounded(value)
    rest = value - first
    second = rounded(rest)
    return first, second, rest - second


def high_low(value):
    high = rounded(value)
    return high, value - high


def two_parts(value):
    first = value.astype(BF16)
    return first, (value - first.astype(F32)).astype(BF16)


def grid_parts(value):
    high = (value + GRID_ROUND) - GRID_ROUND
    low = value - high
    first = rounded(low)
    return high, low, first, low - first


def norm_parts(parts, extra=None):
    big = sum(high * high for high, _, _, _ in parts)
    small = sum(low * (2.0 * high + low) for high, low, _, _ in parts)
    if extra is not None:
        small = small + extra
    return three_parts(big), three_parts(small)


def put_own(pos_ref, mass_ref, own_ref):
    for pair in range(PAIRS):
        lanes = pl.ds(128 * pair, 128)
        own_ref[4 * pair : 4 * pair + 3, :] = pos_ref[:, lanes]
        own_ref[4 * pair + 3 : 4 * pair + 4, :] = mass_ref[:, lanes]


def pack_kernel(n_dom, *refs):
    ins, outs, scratch, (out_ref, sent_ref, sems) = refs[:9], refs[9:12], refs[12:21], refs[21:]
    results = [
        pltpu.make_async_copy(out_ref.at[pl.ds(0, OWN_ROWS)], outs[0], sems.at[9]),
        pltpu.make_async_copy(sent_ref.at[pl.ds(0, n_dom)], outs[1], sems.at[10]),
        pltpu.make_async_copy(out_ref, outs[2], sems.at[11]),
    ]
    copies = [pltpu.make_async_copy(src, dst, sems.at[at]) for at, (src, dst) in enumerate(zip(ins, scratch))]
    for copy in copies:
        copy.start()
    pos_ref, mass_ref, cmass_ref, center_ref, quad_ref, cl_ref, ll_ref, list_ref, count_ref = scratch
    me = lax.axis_index("dom")
    left = lax.broadcasted_iota(jnp.int32, (4, 128), 1) < LEAF
    sent_ref[...] = jnp.zeros((n_dom + 1, SENT_ROWS, 128), F32)
    for copy in copies:
        copy.wait()
    put_own(pos_ref, mass_ref, out_ref)
    results[0].start()
    out_ref[OWN_ROWS : OWN_ROWS + LEAF_DEV, :] = cl_ref[...].astype(F32)
    out_ref[OWN_ROWS + LEAF_DEV :, :] = ll_ref[...].astype(F32)
    results[2].start()

    def put_cells(target, carry):
        sent_ref[target, OUT_ROWS : OUT_ROWS + 1, :] = cmass_ref[...]
        sent_ref[target, OUT_ROWS + 1 : OUT_ROWS + 4, :] = center_ref[...]
        sent_ref[target, OUT_ROWS + 4 : OUT_ROWS + 10, :] = quad_ref[...]
        return carry

    lax.fori_loop(0, n_dom, put_cells, 0)

    def half(slot, j, right):
        block = list_ref[slot, j]
        value = out_ref[pl.ds(pl.multiple_of(4 * (block // 2), 4), 4), :]
        value = jnp.where(j < count_ref[0, slot], value, 0.0)
        return jnp.where((block & 1) == right, value, pltpu.roll(value, LEAF, 1))

    for slot in range(2 * RANGE):
        target = me + OFFSETS[slot]
        target = jnp.where((target >= 0) & (target < n_dom), target, n_dom)
        for unit in range(OUT_UNITS):
            sent_ref[target, 4 * unit : 4 * unit + 4, :] = jnp.where(left, half(slot, 2 * unit, 0), half(slot, 2 * unit + 1, 1))
    results[1].start()
    for copy in results:
        copy.wait()


def target_h_rows(parts, one, zero):
    big, small = norm_parts(parts, softening_sq)
    minus_high = [-2.0 * part[0] for part in parts]
    minus_one = [-2.0 * part[2] for part in parts]
    minus_two = [-2.0 * part[3] for part in parts]
    rows = minus_high + [one] * 3 + list(big) + minus_high + minus_one + minus_high
    return rows + minus_two + minus_one + [one] * 3 + list(small) + [zero] * 2


def target_features(octet, tg_ref, ce_ref, feat_ref, ah_ref):
    left = lax.broadcasted_iota(jnp.int32, (8, 128), 1) < LEAF
    one = jnp.ones((8, 128), F32)
    zero = jnp.zeros((8, 128), F32)
    parts, centred = [], []
    for comp in range(3):
        rows = pl.ds(octet * 32 + comp, 8, stride=4)
        value = tg_ref[rows, :]
        first = jnp.broadcast_to(value[:, 0:1], (8, 128))
        second = jnp.broadcast_to(value[:, LEAF : LEAF + 1], (8, 128))
        ce_ref[comp, pl.ds(octet * 16, 8, stride=2), :] = first
        ce_ref[comp, pl.ds(octet * 16 + 1, 8, stride=2), :] = second
        value = value - jnp.where(left, first, second)
        tg_ref[rows, :] = value
        centred.append(value)
        parts.append(grid_parts(value))
    rows = target_h_rows(parts, one, zero)
    x, y, z = centred
    split = [three_parts(v) for v in (x, y, z, x * x, y * y, z * z, x * y, x * z, y * z)]
    for which in (0, 0, 1, 0, 1, 2):
        rows += [part[which] for part in split]
    rows += [one] * 3 + [zero] * 7
    for at, value in enumerate(rows):
        feat_ref[8 * at : 8 * at + 8, :] = value
    for sub in range(8):
        features = feat_ref[pl.ds(sub, H_ROWS + Q_ROWS, stride=8), :].T.astype(BF16)
        ah_ref[octet * 8 + sub, :, 0 : H_ROWS + Q_ROWS] = features


def source_h_rows(parts):
    (p1, p2, p3), (s1, s2, s3) = norm_parts(parts)
    high = [part[0] for part in parts]
    one = [part[2] for part in parts]
    two = [part[3] for part in parts]
    rows = dict(enumerate(high + [p1, p2, p3]))
    rows.update(enumerate(one + high + two + high + one + [s1, s2, s3], 9))
    return rows


def put_rows(ref, rows):
    for at, value in rows.items():
        ref[8 * at : 8 * at + 8, :] = value


def fill_constant_rows(ref, count):
    one = jnp.ones((8, 128), F32)
    zero = jnp.zeros((8, 128), F32)
    for at in range(count):
        ones = at in (6, 7, 8, 27, 28, 29) or at == V_AT + 3
        ref[8 * at : 8 * at + 8, :] = one if ones else zero


def cell_features(n_dom, n_sub, octet, cl_ref, spread_ref, ce_ref, cf_ref, cm_ref):
    ids = cl_ref[pl.ds(pl.multiple_of(8 * octet, 8), 8), :]
    lane = ids & 127
    owner = ids >> 7
    me = lax.axis_index("sub")

    def look_up(dom, shift, found):
        here = owner == dom * n_sub + lax.bitwise_xor(me, shift)
        new = []
        for comp in range(CELL_COMPS):
            value = jnp.take_along_axis(spread_ref[dom, shift, comp], lane, axis=1, mode="promise_in_bounds")
            new.append(jnp.where(here, value, found[comp]))
        return tuple(new)

    found = tuple(jnp.zeros((8, 128), F32) for _ in range(CELL_COMPS))
    if n_dom <= 8:
        for dom in range(n_dom):
            for shift in range(n_sub):
                found = look_up(dom, shift, found)
                yield
    else:

        def one_domain(dom, found):
            for shift in range(n_sub):
                found = look_up(dom, shift, found)
            return found

        found = lax.fori_loop(0, n_dom, one_domain, found)
    mass, cx, cy, cz, xx, yy, zz, xy, xz, yz = found
    yield "found"
    cm_ref[...] = mass
    rows8 = pl.ds(pl.multiple_of(8 * octet, 8), 8)
    cx, cy, cz = [value - ce_ref[comp, rows8, :] for comp, value in enumerate((cx, cy, cz))]
    put_rows(cf_ref, source_h_rows([grid_parts(value) for value in (cx, cy, cz)]))
    yield
    qx = xx * cx + xy * cy + xz * cz
    qy = xy * cx + yy * cy + yz * cz
    qz = xz * cx + yz * cy + zz * cz
    const = three_parts(2.5 * (qx * cx + qy * cy + qz * cz))
    linear = [-5.0 * qx, -5.0 * qy, -5.0 * qz]
    square = [2.5 * xx, 2.5 * yy, 2.5 * zz, 5.0 * xy, 5.0 * xz, 5.0 * yz]
    split = [three_parts(value) for value in linear + square]
    rows = []
    for which in (0, 1, 0, 2, 1, 0):
        rows += [part[which] for part in split]
    rows += list(const)
    put_rows(cf_ref, dict(enumerate(rows, Q_AT)))
    yield
    for comp, value in enumerate((cx, cy, cz)):
        for which, part in enumerate(three_parts(value)):
            cf_ref[8 * (V_AT + 4 * which + comp) : 8 * (V_AT + 4 * which + comp) + 8, :] = part
    yield
    columns = {name: three_parts(value) for name, value in dict(xx=xx, yy=yy, zz=zz, xy=xy, xz=xz, yz=yz, cx=qx, cy=qy, cz=qz).items()}
    order = (("xx", "xy", "xz"), ("xy", "yy", "yz"), ("xz", "yz", "zz"), ("cx", "cy", "cz"))
    for which in range(3):
        for column, names in enumerate(order):
            for row, name in enumerate(names):
                at = U_AT + 16 * which + 4 * column + row
                cf_ref[8 * at : 8 * at + 8, :] = columns[name][which]


def source_moments(group, ll_ref, tab_ref, ce_ref, raw_ref, sf_ref):
    left = lax.broadcasted_iota(jnp.int32, (4, 128), 1) < LEAF
    for pair in range(NLEAF // 2):
        first = tab_ref[ll_ref[2 * pair, group]]
        second = tab_ref[ll_ref[2 * pair + 1, group]]
        raw_ref[4 * pair : 4 * pair + 4, :] = jnp.where(left, first, second)
    value = [raw_ref[pl.ds(comp, 8, stride=4), :] for comp in range(4)]
    mass = value[3]
    centred = [value[comp] - ce_ref[comp, pl.ds(group, 1), :] for comp in range(3)]
    for comp, v in enumerate([mass * v for v in centred] + [mass]):
        for which, part in enumerate(high_low(v)):
            at = 4 * which + comp
            sf_ref[8 * at : 8 * at + 8, :] = part


def transposed_dot(rows, weights):
    return lax.dot_general(rows, weights, (((1,), (1,)), ((), ())), preferred_element_type=F32)


def stacked(value):
    return jnp.concatenate(two_parts(value), axis=0)


def cell_group(sub, target, cf_ref, cm_ref):
    def cell_rows(at, count):
        return cf_ref[pl.ds(8 * at + sub, count, stride=8), :].astype(BF16)

    forms = jnp.concatenate(
        [
            jnp.concatenate([cell_rows(0, H_ROWS), jnp.zeros((H_ROWS, 128), BF16)], axis=1),
            jnp.concatenate([jnp.zeros((Q_ROWS, 128), BF16), cell_rows(Q_AT, Q_ROWS)], axis=1),
        ],
        axis=0,
    )
    forms = jnp.dot(target[:, 0 : H_ROWS + Q_ROWS], forms, preferred_element_type=F32)
    yield
    dist_sq, quad_form = forms[:, 0:128], forms[:, 128:256]
    inv = lax.rsqrt(dist_sq)
    inv_two = inv * inv
    inv_three = inv * inv_two
    pull = inv_three * (cm_ref[pl.ds(sub, 1), :] + quad_form * (inv_two * inv_two))
    moments = jnp.concatenate(
        [
            jnp.concatenate([cell_rows(V_AT, V_ROWS), jnp.zeros((V_ROWS, 128), BF16)], axis=1),
            jnp.concatenate([jnp.zeros((U_ROWS, 128), BF16), cell_rows(U_AT, U_ROWS)], axis=1),
        ],
        axis=0,
    )
    return jnp.concatenate([stacked(pull), stacked(inv_three * inv_two)], axis=1), moments


def pair_lanes(pair):
    return pl.ds(pl.multiple_of(128 * pair, 128), 128)


def pair_place(tg_ref, pair):
    return tg_ref[pl.ds(pl.multiple_of(4 * pair, 4), 4), :]


def point_sums(sums, place):
    sums = sums + pltpu.roll(sums, 4, 0)
    return sums[0:3] - place[0:3] * sums[3:4]


def cell_pull(octet, tg_ref, ah_ref, cf_ref, cm_ref, out_ref):
    upper = lax.broadcasted_iota(jnp.int32, (8, 128), 0) < 4
    left = lax.broadcasted_iota(jnp.int32, (LEAF, 128), 1) < LEAF
    for inner in range(4):
        pair = octet * 4 + inner
        first, first_moments = yield from cell_group(2 * inner, ah_ref[pair, 0:LEAF, :], cf_ref, cm_ref)
        second, second_moments = yield from cell_group(2 * inner + 1, ah_ref[pair, LEAF:, :], cf_ref, cm_ref)
        yield
        moments = jnp.concatenate([first_moments, second_moments], axis=0)
        sums = transposed_dot(jnp.concatenate([first, second], axis=0), moments)
        yield
        sums = jnp.where(left, sums[0:64] + sums[64:128], sums[128:192] + sums[192:256]).T
        sums = jnp.concatenate([sums[0:64], sums[64:128]], axis=1)
        place = pair_place(tg_ref, pair)
        x, y, z = [place[comp : comp + 1, :] for comp in range(3)]
        quads = sums[16:32] + sums[32:48] + sums[48:64]
        turned = quads[0:8] * jnp.where(upper, x, y) + quads[8:16] * jnp.where(upper, z, -1.0)
        turned = turned + pltpu.roll(turned, 4, 0)
        out_ref[:, pair_lanes(pair)] = point_sums(sums[0:8] + sums[8:16], place) + turned[0:3]


def put_block_pair(tab_ref, block, value):
    left = lax.broadcasted_iota(jnp.int32, (4, 128), 1) < LEAF
    turned = pltpu.roll(value, LEAF, 1)
    tab_ref[block] = jnp.where(left, value, turned)
    tab_ref[block + 1] = jnp.where(left, turned, value)


def put_eight_pairs(rows_ref, block, coords, feat_ref):
    put_rows(feat_ref, source_h_rows([grid_parts(value) for value in coords]))
    for pair in range(8):
        columns = feat_ref[pl.ds(pair, H_ROWS, stride=8), :].astype(BF16)
        spread = jnp.concatenate([columns] * 4, axis=0).T
        rows_ref[block + 2 * pair] = spread[0:LEAF]
        rows_ref[block + 2 * pair + 1] = spread[LEAF:]


def prepare_kernel(n_dom, n_sub, *refs):
    bundle_ref, near_refs, recv_ref = refs[0], refs[1:n_sub], refs[n_sub]
    tab_ref, rows_ref, at_ref, tg_ref, ce_ref, ah_ref, cl_ref, ll_ref, feat_ref, four_ref = refs[n_sub + 1 :]
    own_ref = bundle_ref.at[0:OWN_ROWS]
    cl_ref[...] = bundle_ref[OWN_ROWS : OWN_ROWS + LEAF_DEV, :].astype(jnp.int32)
    ll_ref[...] = bundle_ref[OWN_ROWS + LEAF_DEV :, :].astype(jnp.int32)
    for at in range(8):
        fill_constant_rows(four_ref.at[at], H_ROWS)
    me = lax.axis_index("sub")

    def near_blocks(shift, near_ref):
        seg = lax.bitwise_xor(me, shift)

        def near(step, carry):
            for at in range(8):
                octet = 8 * step + at
                block = seg * LEAF_DEV + 16 * octet
                first = pl.multiple_of(32 * octet, 32)
                for pair in range(8):
                    put_block_pair(tab_ref, block + 2 * pair, near_ref[pl.ds(pl.multiple_of(first + 4 * pair, 4), 4), :])
                coords = [near_ref[pl.ds(first + comp, 8, stride=4), :] for comp in range(3)]
                put_eight_pairs(rows_ref, block, coords, four_ref.at[at])
            return carry

        lax.fori_loop(0, PAIRS // 64, near, 0)

    for shift in range(1, n_sub):
        near_blocks(shift, near_refs[shift - 1])
    far_tables(n_dom, n_sub * LEAF_DEV, recv_ref, tab_ref, rows_ref, four_ref)
    near_blocks(0, own_ref)
    tg_ref[...] = own_ref[...]

    def targets(step, carry):
        for at in range(2):
            octet = 2 * step + at
            target_features(octet, tg_ref, ce_ref, feat_ref.at[at], ah_ref)
            target_rows(octet, own_ref, four_ref.at[at], at_ref)
        return carry

    lax.fori_loop(0, PAIRS // 16, targets, 0)


def far_tables(n_dom, first_block, recv_ref, tab_ref, rows_ref, four_ref):
    me = lax.axis_index("dom")
    for two in range(RANGE):
        halves = []
        for slot in (2 * two, 2 * two + 1):
            source = me - OFFSETS[slot]
            inside = (source >= 0) & (source < n_dom)
            source = jnp.clip(source, 0, n_dom - 1)
            for unit in range(OUT_UNITS):
                value = jnp.where(inside, recv_ref[source, 4 * unit : 4 * unit + 4, :], 0.0)
                put_block_pair(tab_ref, first_block + slot * CAP + 2 * unit, value)
            halves.append([jnp.where(inside, recv_ref[source, pl.ds(comp, OUT_UNITS, stride=4), :], 0.0) for comp in range(3)])
        coords = [jnp.concatenate([one, other], axis=0) for one, other in zip(*halves)]
        put_eight_pairs(rows_ref, first_block + 2 * two * CAP, coords, four_ref.at[two])


def target_rows(octet, own_ref, feat_ref, at_ref):
    one = jnp.ones((8, 128), F32)
    zero = jnp.zeros((8, 128), F32)
    parts = [grid_parts(own_ref[pl.ds(octet * 32 + comp, 8, stride=4), :]) for comp in range(3)]
    for at, value in enumerate(target_h_rows(parts, one, zero)):
        feat_ref[8 * at : 8 * at + 8, :] = value
    for pair in range(8):
        at_ref[octet * 8 + pair] = feat_ref[pl.ds(pair, H_ROWS, stride=8), :].astype(BF16)


def run(strand, steps=None):
    taken = 0
    while steps is None or taken < steps:
        taken += 1
        if next(strand, "end") == "end":
            return


def pull_kernel(n_dom, n_sub, *refs):
    cell_refs = refs[:n_sub]
    tab_ref, rows_ref, at_ref, tg_ref, ce_ref, ah_ref, cl_ref, ll_in, out_ref = refs[n_sub : n_sub + 9]
    ll_ref, spread_ref, cf_ref, cm_ref, raw_ref, even_ref, odd_ref, dist_even, dist_odd, sem = refs[n_sub + 9 :]
    copy = pltpu.make_async_copy(ll_in, ll_ref, sem)
    copy.start()
    fill_constant_rows(cf_ref, CELL_ROWS)

    def build(octet):
        return cell_features(n_dom, n_sub, octet, cl_ref, spread_ref, ce_ref, cf_ref, cm_ref)

    def spread(dom, carry):
        for shift in range(n_sub):
            for comp in range(CELL_COMPS):
                row = cell_refs[shift][dom, comp : comp + 1, :]
                spread_ref[dom, shift, comp] = jnp.broadcast_to(row, (8, 128))
        return carry

    lax.fori_loop(0, n_dom, spread, 0)

    left = lax.broadcasted_iota(jnp.int32, (M_ROWS, 128), 1) < LEAF
    left_target = lax.broadcasted_iota(jnp.int32, (H_ROWS, 128), 1) < LEAF
    owner = (lax.broadcasted_iota(jnp.int32, (LEAF, 128), 1) // H_ROWS).astype(BF16)
    lower_half, first_own, third_own = owner < 2.0, owner == 0.0, owner == 2.0

    def features(quad, raw_at, slot_ref):
        for group in range(4):
            source_moments(4 * quad + group, ll_ref, tab_ref, ce_ref, raw_ref.at[raw_at + group], slot_ref.at[group])
            yield

    def distances(quad, dist_ref):
        nothing = jnp.zeros((H_ROWS, 128), BF16)
        first, second = at_ref[2 * quad], at_ref[2 * quad + 1]
        targets = jnp.concatenate(
            [
                jnp.concatenate([jnp.where(left_target, first, nothing), nothing], axis=1),
                jnp.concatenate([jnp.where(left_target, nothing, first), nothing], axis=1),
                jnp.concatenate([nothing, jnp.where(left_target, second, nothing)], axis=1),
                jnp.concatenate([nothing, jnp.where(left_target, nothing, second)], axis=1),
            ],
            axis=0,
        )
        sources = []
        for j in range(NLEAF):
            rows = [rows_ref[ll_ref[j, 4 * quad + group]] for group in range(4)]
            low = jnp.where(first_own, rows[0], rows[1])
            high = jnp.where(third_own, rows[2], rows[3])
            sources.append(jnp.where(lower_half, low, high))
            if j % 4 == 3:
                rows = pl.ds(LEAF * (j - 3), 4 * LEAF)
                dist_ref[rows, :] = jnp.dot(jnp.concatenate(sources, axis=0), targets, preferred_element_type=F32)
                sources = []
                yield

    def pull(quad, slot_ref, dist_ref):
        total = jnp.zeros((4 * M_ROWS, 256), F32)
        for chunk in range(8):
            inv = lax.rsqrt(dist_ref[128 * chunk : 128 * chunk + 128, :])
            weights = stacked(inv * inv * inv)
            rows = [slot_ref[group, pl.ds(chunk, M_ROWS, stride=8), :] for group in range(4)]
            rows = jnp.concatenate(rows, axis=0).astype(BF16)
            total += jnp.dot(jnp.concatenate([rows, rows], axis=1), weights, preferred_element_type=F32)
            yield
        for side in range(2):
            pair = 2 * quad + side
            at, columns = 2 * M_ROWS * side, slice(128 * side, 128 * side + 128)
            sums = jnp.where(left, total[at : at + M_ROWS, columns], total[at + M_ROWS : at + 2 * M_ROWS, columns])
            lanes = pair_lanes(pair)
            out_ref[:, lanes] = out_ref[:, lanes] + point_sums(sums, pair_place(tg_ref, pair))

    quads, octets = LEAF_DEV // 4, LEAF_DEV // 8
    run(build(0))
    copy.wait()
    run(features(0, 0, even_ref))
    run(distances(0, dist_even))

    def one_octet(octet, carry):
        quad = 2 * octet
        after = jnp.minimum(quad + 2, quads - 1)
        cells = cell_pull(octet, tg_ref, ah_ref, cf_ref, cm_ref, out_ref)
        coming = build(jnp.minimum(octet + 1, octets - 1))
        for half, (now, slot_ref, dist_ref, ahead, ahead_slot, ahead_dist, raw_at) in enumerate(
            (
                (quad, even_ref, dist_even, quad + 1, odd_ref, dist_odd, 4),
                (quad + 1, odd_ref, dist_odd, after, even_ref, dist_even, 0),
            )
        ):
            direct = pull(now, slot_ref, dist_ref)
            moments, distance = features(ahead, raw_at, ahead_slot), distances(ahead, ahead_dist)
            for step in range(8):
                if step % 2 == 1:
                    run(distance, 1)
                run(direct, 1)
                if step % 2 == 0:
                    run(moments, 1)
                if half == 0 or step < 4:
                    run(coming, 3)
                    run(cells, 2 if half or step % 2 else 1)
                else:
                    run(coming, 1)
            run(moments)
            run(distance)
            run(direct)
        run(coming)
        return carry

    lax.fori_loop(0, octets, one_octet, 0)


def on_device(n_dom, n_sub, positions, masses, cell_mass, cell_center, cell_quad, cell_list, leaf_list, send_list, send_count):
    vmem = pl.BlockSpec(memory_space=pltpu.VMEM)
    smem = pl.BlockSpec(memory_space=pltpu.SMEM)
    anywhere = pl.BlockSpec(memory_space=pl.ANY)

    def limit(mib):
        return pltpu.CompilerParams(vmem_limit_bytes=mib * 1024 * 1024)

    ins = (
        positions,
        masses.reshape(1, -1),
        cell_mass.reshape(1, -1),
        cell_center,
        cell_quad,
        cell_list,
        leaf_list.T,
        send_list.reshape(2 * RANGE, CAP),
        send_count.reshape(1, 2 * RANGE),
    )
    bundle_rows = OWN_ROWS + LEAF_DEV + NLEAF
    packed, sent, bundle = pl.pallas_call(
        functools.partial(pack_kernel, n_dom),
        out_shape=(
            jax.ShapeDtypeStruct((OWN_ROWS, 128), F32),
            jax.ShapeDtypeStruct((n_dom, SENT_ROWS, 128), F32),
            jax.ShapeDtypeStruct((bundle_rows, 128), F32),
        ),
        in_specs=[pl.BlockSpec(memory_space=pltpu.HBM)] * 9,
        out_specs=[anywhere] * 3,
        scratch_shapes=[pltpu.VMEM(array.shape, array.dtype) for array in ins[:7]]
        + [pltpu.SMEM(array.shape, jnp.int32) for array in ins[7:]]
        + [
            pltpu.VMEM((bundle_rows, 128), F32),
            pltpu.VMEM((n_dom + 1, SENT_ROWS, 128), F32),
            pltpu.SemaphoreType.DMA((12,)),
        ],
        compiler_params=limit(63),
        name="pack_own",
    )(*ins)
    received = lax.all_to_all(sent, "dom", split_axis=0, concat_axis=0, tiled=True)

    def across(value, bits):
        return lax.ppermute(value, "sub", [(seg, seg ^ bits) for seg in range(n_sub)])

    nearby = {0: packed}
    bit = n_sub // 2
    while bit:
        nearby.update({at ^ bit: across(value, bit) for at, value in nearby.items()})
        bit //= 2
    nearby = [nearby[at] for at in range(n_sub)]
    own_cells = received[:, OUT_ROWS:]
    cells = [own_cells] + [across(own_cells, bits) for bits in range(1, n_sub)]
    n_blocks = n_sub * LEAF_DEV + 2 * RANGE * CAP
    prepared = pl.pallas_call(
        functools.partial(prepare_kernel, n_dom, n_sub),
        out_shape=(
            jax.ShapeDtypeStruct((n_blocks, 4, 128), F32),
            jax.ShapeDtypeStruct((n_blocks, LEAF, 128), BF16),
            jax.ShapeDtypeStruct((PAIRS, H_ROWS, 128), BF16),
            jax.ShapeDtypeStruct((OWN_ROWS, 128), F32),
            jax.ShapeDtypeStruct((3, LEAF_DEV, 128), F32),
            jax.ShapeDtypeStruct((PAIRS, 128, 128), BF16),
            jax.ShapeDtypeStruct((LEAF_DEV, NCELL), jnp.int32),
            jax.ShapeDtypeStruct((NLEAF, LEAF_DEV), jnp.int32),
        ),
        in_specs=[vmem] * (n_sub + 1),
        out_specs=[vmem] * 8,
        scratch_shapes=[
            pltpu.VMEM((2, 8 * (H_ROWS + Q_ROWS), 128), F32),
            pltpu.VMEM((8, 8 * H_ROWS, 128), F32),
        ],
        compiler_params=limit(24),
        cost_estimate=pl.CostEstimate(flops=0, bytes_accessed=20_000_000, transcendentals=0),
        name="prepare",
    )(bundle, *nearby[1:], received)
    return pl.pallas_call(
        functools.partial(pull_kernel, n_dom, n_sub),
        out_shape=jax.ShapeDtypeStruct((3, LEAF_DEV * LEAF), F32),
        in_specs=[vmem] * (n_sub + 8),
        out_specs=vmem,
        scratch_shapes=[
            pltpu.SMEM((NLEAF, LEAF_DEV), jnp.int32),
            pltpu.VMEM((n_dom, n_sub, CELL_COMPS, 8, 128), F32),
            pltpu.VMEM((8 * CELL_ROWS, 128), F32),
            pltpu.VMEM((8, 128), F32),
            pltpu.VMEM((8, 32, 128), F32),
            pltpu.VMEM((4, 8 * M_ROWS, 128), F32),
            pltpu.VMEM((4, 8 * M_ROWS, 128), F32),
            pltpu.VMEM((NLEAF * LEAF, 256), F32),
            pltpu.VMEM((NLEAF * LEAF, 256), F32),
            pltpu.SemaphoreType.DMA(()),
        ],
        compiler_params=limit(24),
        name="pull",
    )(*cells, *prepared)


def solution(mesh):
    sharded = P(("dom", "sub"))
    return jax.shard_map(
        functools.partial(on_device, mesh.shape["dom"], mesh.shape["sub"]),
        mesh=mesh,
        in_specs=(
            P(None, ("dom", "sub")),
            sharded,
            sharded,
            P(None, ("dom", "sub")),
            P(None, ("dom", "sub")),
            P(("dom", "sub"), None),
            P(("dom", "sub"), None),
            P("dom", "sub", None, None),
            P("dom", "sub", None),
        ),
        out_specs=P(None, ("dom", "sub")),
        check_vma=False,
    )
```

```python
import functools

import jax
import jax.numpy as jnp
from jax import lax
from jax.experimental import pallas as pl
from jax.experimental.pallas import tpu as pltpu
from jax.sharding import PartitionSpec as P

LEAF = 64
LEAF_DEV = 128
NCELL = 128
NLEAF = 16
RANGE = 4
CAP = 8
PAIRS = LEAF_DEV // 2
OUT_UNITS = CAP // 2
OWN_ROWS = 4 * PAIRS
OUT_ROWS = 4 * OUT_UNITS
CELL_COMPS = 10
CELL_PAD = 16
SENT_ROWS = OUT_ROWS + CELL_PAD
OFFSETS = list(range(-RANGE, 0)) + list(range(1, RANGE + 1))

softening_sq = 0.0025
GRID_ROUND = 49152.0
F32 = jnp.float32
BF16 = jnp.bfloat16

H_ROWS = 32
Q_ROWS = 64
V_ROWS = 16
U_ROWS = 48
Q_AT = H_ROWS
V_AT = Q_AT + Q_ROWS
U_AT = V_AT + V_ROWS
CELL_ROWS = U_AT + U_ROWS
M_ROWS = 8


def rounded(value):
    return value.astype(BF16).astype(F32)


def three_parts(value):
    first = rounded(value)
    rest = value - first
    second = rounded(rest)
    return first, second, rest - second


def high_low(value):
    high = rounded(value)
    return high, value - high


def two_parts(value):
    first = value.astype(BF16)
    return first, (value - first.astype(F32)).astype(BF16)


def grid_parts(value):
    high = (value + GRID_ROUND) - GRID_ROUND
    low = value - high
    first = rounded(low)
    return high, low, first, low - first


def norm_parts(parts, extra=None):
    big = sum(high * high for high, _, _, _ in parts)
    small = sum(low * (2.0 * high + low) for high, low, _, _ in parts)
    if extra is not None:
        small = small + extra
    return three_parts(big), three_parts(small)


def put_own(pos_ref, mass_ref, own_ref):
    for pair in range(PAIRS):
        lanes = pl.ds(128 * pair, 128)
        own_ref[4 * pair : 4 * pair + 3, :] = pos_ref[:, lanes]
        own_ref[4 * pair + 3 : 4 * pair + 4, :] = mass_ref[:, lanes]


def pack_kernel(n_dom, *refs):
    ins, outs, scratch, (out_ref, sent_ref, sems) = refs[:9], refs[9:12], refs[12:21], refs[21:]
    results = [
        pltpu.make_async_copy(out_ref.at[pl.ds(0, OWN_ROWS)], outs[0], sems.at[9]),
        pltpu.make_async_copy(sent_ref.at[pl.ds(0, n_dom)], outs[1], sems.at[10]),
        pltpu.make_async_copy(out_ref, outs[2], sems.at[11]),
    ]
    copies = [pltpu.make_async_copy(src, dst, sems.at[at]) for at, (src, dst) in enumerate(zip(ins, scratch))]
    for copy in copies:
        copy.start()
    pos_ref, mass_ref, cmass_ref, center_ref, quad_ref, cl_ref, ll_ref, list_ref, count_ref = scratch
    me = lax.axis_index("dom")
    left = lax.broadcasted_iota(jnp.int32, (4, 128), 1) < LEAF
    sent_ref[...] = jnp.zeros((n_dom + 1, SENT_ROWS, 128), F32)
    for copy in copies:
        copy.wait()
    put_own(pos_ref, mass_ref, out_ref)
    results[0].start()
    out_ref[OWN_ROWS : OWN_ROWS + LEAF_DEV, :] = cl_ref[...].astype(F32)
    out_ref[OWN_ROWS + LEAF_DEV :, :] = ll_ref[...].astype(F32)
    results[2].start()

    def put_cells(target, carry):
        sent_ref[target, OUT_ROWS : OUT_ROWS + 1, :] = cmass_ref[...]
        sent_ref[target, OUT_ROWS + 1 : OUT_ROWS + 4, :] = center_ref[...]
        sent_ref[target, OUT_ROWS + 4 : OUT_ROWS + 10, :] = quad_ref[...]
        return carry

    lax.fori_loop(0, n_dom, put_cells, 0)

    def half(slot, j, right):
        block = list_ref[slot, j]
        value = out_ref[pl.ds(pl.multiple_of(4 * (block // 2), 4), 4), :]
        value = jnp.where(j < count_ref[0, slot], value, 0.0)
        return jnp.where((block & 1) == right, value, pltpu.roll(value, LEAF, 1))

    for slot in range(2 * RANGE):
        target = me + OFFSETS[slot]
        target = jnp.where((target >= 0) & (target < n_dom), target, n_dom)
        for unit in range(OUT_UNITS):
            sent_ref[target, 4 * unit : 4 * unit + 4, :] = jnp.where(left, half(slot, 2 * unit, 0), half(slot, 2 * unit + 1, 1))
    results[1].start()
    for copy in results:
        copy.wait()


def target_h_rows(parts, one, zero):
    big, small = norm_parts(parts, softening_sq)
    minus_high = [-2.0 * part[0] for part in parts]
    minus_one = [-2.0 * part[2] for part in parts]
    minus_two = [-2.0 * part[3] for part in parts]
    rows = minus_high + [one] * 3 + list(big) + minus_high + minus_one + minus_high
    return rows + minus_two + minus_one + [one] * 3 + list(small) + [zero] * 2


def target_features(octet, tg_ref, ce_ref, feat_ref, ah_ref):
    left = lax.broadcasted_iota(jnp.int32, (8, 128), 1) < LEAF
    one = jnp.ones((8, 128), F32)
    zero = jnp.zeros((8, 128), F32)
    parts, centred = [], []
    for comp in range(3):
        rows = pl.ds(octet * 32 + comp, 8, stride=4)
        value = tg_ref[rows, :]
        first = jnp.broadcast_to(value[:, 0:1], (8, 128))
        second = jnp.broadcast_to(value[:, LEAF : LEAF + 1], (8, 128))
        ce_ref[comp, pl.ds(octet * 16, 8, stride=2), :] = first
        ce_ref[comp, pl.ds(octet * 16 + 1, 8, stride=2), :] = second
        value = value - jnp.where(left, first, second)
        tg_ref[rows, :] = value
        centred.append(value)
        parts.append(grid_parts(value))
    rows = target_h_rows(parts, one, zero)
    x, y, z = centred
    split = [three_parts(v) for v in (x, y, z, x * x, y * y, z * z, x * y, x * z, y * z)]
    for which in (0, 0, 1, 0, 1, 2):
        rows += [part[which] for part in split]
    rows += [one] * 3 + [zero] * 7
    for at, value in enumerate(rows):
        feat_ref[8 * at : 8 * at + 8, :] = value
    for sub in range(8):
        features = feat_ref[pl.ds(sub, H_ROWS + Q_ROWS, stride=8), :].T.astype(BF16)
        ah_ref[octet * 8 + sub, :, 0 : H_ROWS + Q_ROWS] = features


def source_h_rows(parts):
    (p1, p2, p3), (s1, s2, s3) = norm_parts(parts)
    high = [part[0] for part in parts]
    one = [part[2] for part in parts]
    two = [part[3] for part in parts]
    rows = dict(enumerate(high + [p1, p2, p3]))
    rows.update(enumerate(one + high + two + high + one + [s1, s2, s3], 9))
    return rows


def put_rows(ref, rows):
    for at, value in rows.items():
        ref[8 * at : 8 * at + 8, :] = value


def fill_constant_rows(ref, count):
    one = jnp.ones((8, 128), F32)
    zero = jnp.zeros((8, 128), F32)
    for at in range(count):
        ones = at in (6, 7, 8, 27, 28, 29) or at == V_AT + 3
        ref[8 * at : 8 * at + 8, :] = one if ones else zero


def cell_features(n_dom, n_sub, octet, cl_ref, spread_ref, ce_ref, cf_ref, cm_ref):
    ids = cl_ref[pl.ds(pl.multiple_of(8 * octet, 8), 8), :]
    lane = ids & 127
    owner = ids >> 7
    me = lax.axis_index("sub")

    def look_up(dom, shift, found):
        here = owner == dom * n_sub + lax.bitwise_xor(me, shift)
        new = []
        for comp in range(CELL_COMPS):
            value = jnp.take_along_axis(spread_ref[dom, shift, comp], lane, axis=1, mode="promise_in_bounds")
            new.append(jnp.where(here, value, found[comp]))
        return tuple(new)

    found = tuple(jnp.zeros((8, 128), F32) for _ in range(CELL_COMPS))
    if n_dom <= 8:
        for dom in range(n_dom):
            for shift in range(n_sub):
                found = look_up(dom, shift, found)
                yield
    else:

        def one_domain(dom, found):
            for shift in range(n_sub):
                found = look_up(dom, shift, found)
            return found

        found = lax.fori_loop(0, n_dom, one_domain, found)
    mass, cx, cy, cz, xx, yy, zz, xy, xz, yz = found
    yield "found"
    cm_ref[...] = mass
    rows8 = pl.ds(pl.multiple_of(8 * octet, 8), 8)
    cx, cy, cz = [value - ce_ref[comp, rows8, :] for comp, value in enumerate((cx, cy, cz))]
    put_rows(cf_ref, source_h_rows([grid_parts(value) for value in (cx, cy, cz)]))
    yield
    qx = xx * cx + xy * cy + xz * cz
    qy = xy * cx + yy * cy + yz * cz
    qz = xz * cx + yz * cy + zz * cz
    const = three_parts(2.5 * (qx * cx + qy * cy + qz * cz))
    linear = [-5.0 * qx, -5.0 * qy, -5.0 * qz]
    square = [2.5 * xx, 2.5 * yy, 2.5 * zz, 5.0 * xy, 5.0 * xz, 5.0 * yz]
    split = [three_parts(value) for value in linear + square]
    rows = []
    for which in (0, 1, 0, 2, 1, 0):
        rows += [part[which] for part in split]
    rows += list(const)
    put_rows(cf_ref, dict(enumerate(rows, Q_AT)))
    yield
    for comp, value in enumerate((cx, cy, cz)):
        for which, part in enumerate(three_parts(value)):
            cf_ref[8 * (V_AT + 4 * which + comp) : 8 * (V_AT + 4 * which + comp) + 8, :] = part
    yield
    columns = {name: three_parts(value) for name, value in dict(xx=xx, yy=yy, zz=zz, xy=xy, xz=xz, yz=yz, cx=qx, cy=qy, cz=qz).items()}
    order = (("xx", "xy", "xz"), ("xy", "yy", "yz"), ("xz", "yz", "zz"), ("cx", "cy", "cz"))
    for which in range(3):
        for column, names in enumerate(order):
            for row, name in enumerate(names):
                at = U_AT + 16 * which + 4 * column + row
                cf_ref[8 * at : 8 * at + 8, :] = columns[name][which]


def source_moments(group, ll_ref, tab_ref, ce_ref, raw_ref, sf_ref):
    left = lax.broadcasted_iota(jnp.int32, (4, 128), 1) < LEAF
    for pair in range(NLEAF // 2):
        first = tab_ref[ll_ref[2 * pair, group]]
        second = tab_ref[ll_ref[2 * pair + 1, group]]
        raw_ref[4 * pair : 4 * pair + 4, :] = jnp.where(left, first, second)
    value = [raw_ref[pl.ds(comp, 8, stride=4), :] for comp in range(4)]
    mass = value[3]
    centred = [value[comp] - ce_ref[comp, pl.ds(group, 1), :] for comp in range(3)]
    for comp, v in enumerate([mass * v for v in centred] + [mass]):
        for which, part in enumerate(high_low(v)):
            at = 4 * which + comp
            sf_ref[8 * at : 8 * at + 8, :] = part


def transposed_dot(rows, weights):
    return lax.dot_general(rows, weights, (((1,), (1,)), ((), ())), preferred_element_type=F32)


def stacked(value):
    return jnp.concatenate(two_parts(value), axis=0)


def cell_group(sub, target, cf_ref, cm_ref):
    def cell_rows(at, count):
        return cf_ref[pl.ds(8 * at + sub, count, stride=8), :].astype(BF16)

    forms = jnp.concatenate(
        [
            jnp.concatenate([cell_rows(0, H_ROWS), jnp.zeros((H_ROWS, 128), BF16)], axis=1),
            jnp.concatenate([jnp.zeros((Q_ROWS, 128), BF16), cell_rows(Q_AT, Q_ROWS)], axis=1),
        ],
        axis=0,
    )
    forms = jnp.dot(target[:, 0 : H_ROWS + Q_ROWS], forms, preferred_element_type=F32)
    yield
    dist_sq, quad_form = forms[:, 0:128], forms[:, 128:256]
    inv = lax.rsqrt(dist_sq)
    inv_two = inv * inv
    inv_three = inv * inv_two
    pull = inv_three * (cm_ref[pl.ds(sub, 1), :] + quad_form * (inv_two * inv_two))
    moments = jnp.concatenate(
        [
            jnp.concatenate([cell_rows(V_AT, V_ROWS), jnp.zeros((V_ROWS, 128), BF16)], axis=1),
            jnp.concatenate([jnp.zeros((U_ROWS, 128), BF16), cell_rows(U_AT, U_ROWS)], axis=1),
        ],
        axis=0,
    )
    return jnp.concatenate([stacked(pull), stacked(inv_three * inv_two)], axis=1), moments


def pair_lanes(pair):
    return pl.ds(pl.multiple_of(128 * pair, 128), 128)


def pair_place(tg_ref, pair):
    return tg_ref[pl.ds(pl.multiple_of(4 * pair, 4), 4), :]


def point_sums(sums, place):
    sums = sums + pltpu.roll(sums, 4, 0)
    return sums[0:3] - place[0:3] * sums[3:4]


def cell_pull(octet, tg_ref, ah_ref, cf_ref, cm_ref, out_ref):
    upper = lax.broadcasted_iota(jnp.int32, (8, 128), 0) < 4
    left = lax.broadcasted_iota(jnp.int32, (LEAF, 128), 1) < LEAF
    for inner in range(4):
        pair = octet * 4 + inner
        first, first_moments = yield from cell_group(2 * inner, ah_ref[pair, 0:LEAF, :], cf_ref, cm_ref)
        second, second_moments = yield from cell_group(2 * inner + 1, ah_ref[pair, LEAF:, :], cf_ref, cm_ref)
        yield
        moments = jnp.concatenate([first_moments, second_moments], axis=0)
        sums = transposed_dot(jnp.concatenate([first, second], axis=0), moments)
        yield
        sums = jnp.where(left, sums[0:64] + sums[64:128], sums[128:192] + sums[192:256]).T
        sums = jnp.concatenate([sums[0:64], sums[64:128]], axis=1)
        place = pair_place(tg_ref, pair)
        x, y, z = [place[comp : comp + 1, :] for comp in range(3)]
        quads = sums[16:32] + sums[32:48] + sums[48:64]
        turned = quads[0:8] * jnp.where(upper, x, y) + quads[8:16] * jnp.where(upper, z, -1.0)
        turned = turned + pltpu.roll(turned, 4, 0)
        out_ref[:, pair_lanes(pair)] = point_sums(sums[0:8] + sums[8:16], place) + turned[0:3]


def put_block_pair(tab_ref, block, value):
    left = lax.broadcasted_iota(jnp.int32, (4, 128), 1) < LEAF
    turned = pltpu.roll(value, LEAF, 1)
    tab_ref[block] = jnp.where(left, value, turned)
    tab_ref[block + 1] = jnp.where(left, turned, value)


def put_eight_pairs(rows_ref, block, coords, feat_ref):
    put_rows(feat_ref, source_h_rows([grid_parts(value) for value in coords]))
    for pair in range(8):
        columns = feat_ref[pl.ds(pair, H_ROWS, stride=8), :].astype(BF16)
        spread = jnp.concatenate([columns] * 4, axis=0).T
        rows_ref[block + 2 * pair] = spread[0:LEAF]
        rows_ref[block + 2 * pair + 1] = spread[LEAF:]


def prepare_kernel(n_dom, n_sub, *refs):
    bundle_ref, near_refs, recv_ref = refs[0], refs[1:n_sub], refs[n_sub]
    tab_ref, rows_ref, at_ref, tg_ref, ce_ref, ah_ref, cl_ref, ll_ref, feat_ref, four_ref = refs[n_sub + 1 :]
    own_ref = bundle_ref.at[0:OWN_ROWS]
    cl_ref[...] = bundle_ref[OWN_ROWS : OWN_ROWS + LEAF_DEV, :].astype(jnp.int32)
    ll_ref[...] = bundle_ref[OWN_ROWS + LEAF_DEV :, :].astype(jnp.int32)
    for at in range(8):
        fill_constant_rows(four_ref.at[at], H_ROWS)
    me = lax.axis_index("sub")

    def near_blocks(shift, near_ref):
        seg = lax.bitwise_xor(me, shift)

        def near(step, carry):
            for at in range(8):
                octet = 8 * step + at
                block = seg * LEAF_DEV + 16 * octet
                first = pl.multiple_of(32 * octet, 32)
                for pair in range(8):
                    put_block_pair(tab_ref, block + 2 * pair, near_ref[pl.ds(pl.multiple_of(first + 4 * pair, 4), 4), :])
                coords = [near_ref[pl.ds(first + comp, 8, stride=4), :] for comp in range(3)]
                put_eight_pairs(rows_ref, block, coords, four_ref.at[at])
            return carry

        lax.fori_loop(0, PAIRS // 64, near, 0)

    for shift in range(1, n_sub):
        near_blocks(shift, near_refs[shift - 1])
    far_tables(n_dom, n_sub * LEAF_DEV, recv_ref, tab_ref, rows_ref, four_ref)
    near_blocks(0, own_ref)
    tg_ref[...] = own_ref[...]

    def targets(step, carry):
        for at in range(2):
            octet = 2 * step + at
            target_features(octet, tg_ref, ce_ref, feat_ref.at[at], ah_ref)
            target_rows(octet, own_ref, four_ref.at[at], at_ref)
        return carry

    lax.fori_loop(0, PAIRS // 16, targets, 0)


def far_tables(n_dom, first_block, recv_ref, tab_ref, rows_ref, four_ref):
    me = lax.axis_index("dom")
    for two in range(RANGE):
        halves = []
        for slot in (2 * two, 2 * two + 1):
            source = me - OFFSETS[slot]
            inside = (source >= 0) & (source < n_dom)
            source = jnp.clip(source, 0, n_dom - 1)
            for unit in range(OUT_UNITS):
                value = jnp.where(inside, recv_ref[source, 4 * unit : 4 * unit + 4, :], 0.0)
                put_block_pair(tab_ref, first_block + slot * CAP + 2 * unit, value)
            halves.append([jnp.where(inside, recv_ref[source, pl.ds(comp, OUT_UNITS, stride=4), :], 0.0) for comp in range(3)])
        coords = [jnp.concatenate([one, other], axis=0) for one, other in zip(*halves)]
        put_eight_pairs(rows_ref, first_block + 2 * two * CAP, coords, four_ref.at[two])


def target_rows(octet, own_ref, feat_ref, at_ref):
    one = jnp.ones((8, 128), F32)
    zero = jnp.zeros((8, 128), F32)
    parts = [grid_parts(own_ref[pl.ds(octet * 32 + comp, 8, stride=4), :]) for comp in range(3)]
    for at, value in enumerate(target_h_rows(parts, one, zero)):
        feat_ref[8 * at : 8 * at + 8, :] = value
    for pair in range(8):
        at_ref[octet * 8 + pair] = feat_ref[pl.ds(pair, H_ROWS, stride=8), :].astype(BF16)


def run(strand, steps=None):
    taken = 0
    while steps is None or taken < steps:
        taken += 1
        if next(strand, "end") == "end":
            return


def pull_kernel(n_dom, n_sub, *refs):
    cell_refs = refs[:n_sub]
    tab_ref, rows_ref, at_ref, tg_ref, ce_ref, ah_ref, cl_ref, ll_in, out_ref = refs[n_sub : n_sub + 9]
    ll_ref, spread_ref, cf_ref, cm_ref, raw_ref, even_ref, odd_ref, dist_even, dist_odd, sem = refs[n_sub + 9 :]
    copy = pltpu.make_async_copy(ll_in, ll_ref, sem)
    copy.start()
    fill_constant_rows(cf_ref, CELL_ROWS)

    def build(octet):
        return cell_features(n_dom, n_sub, octet, cl_ref, spread_ref, ce_ref, cf_ref, cm_ref)

    def spread(dom, carry):
        for shift in range(n_sub):
            for comp in range(CELL_COMPS):
                row = cell_refs[shift][dom, comp : comp + 1, :]
                spread_ref[dom, shift, comp] = jnp.broadcast_to(row, (8, 128))
        return carry

    lax.fori_loop(0, n_dom, spread, 0)

    left = lax.broadcasted_iota(jnp.int32, (M_ROWS, 128), 1) < LEAF
    left_target = lax.broadcasted_iota(jnp.int32, (H_ROWS, 128), 1) < LEAF
    owner = (lax.broadcasted_iota(jnp.int32, (LEAF, 128), 1) // H_ROWS).astype(BF16)
    lower_half, first_own, third_own = owner < 2.0, owner == 0.0, owner == 2.0

    def features(quad, raw_at, slot_ref):
        for group in range(4):
            source_moments(4 * quad + group, ll_ref, tab_ref, ce_ref, raw_ref.at[raw_at + group], slot_ref.at[group])
            yield

    def distances(quad, dist_ref):
        nothing = jnp.zeros((H_ROWS, 128), BF16)
        first, second = at_ref[2 * quad], at_ref[2 * quad + 1]
        targets = jnp.concatenate(
            [
                jnp.concatenate([jnp.where(left_target, first, nothing), nothing], axis=1),
                jnp.concatenate([jnp.where(left_target, nothing, first), nothing], axis=1),
                jnp.concatenate([nothing, jnp.where(left_target, second, nothing)], axis=1),
                jnp.concatenate([nothing, jnp.where(left_target, nothing, second)], axis=1),
            ],
            axis=0,
        )
        sources = []
        for j in range(NLEAF):
            rows = [rows_ref[ll_ref[j, 4 * quad + group]] for group in range(4)]
            low = jnp.where(first_own, rows[0], rows[1])
            high = jnp.where(third_own, rows[2], rows[3])
            sources.append(jnp.where(lower_half, low, high))
            if j % 4 == 3:
                rows = pl.ds(LEAF * (j - 3), 4 * LEAF)
                dist_ref[rows, :] = jnp.dot(jnp.concatenate(sources, axis=0), targets, preferred_element_type=F32)
                sources = []
                yield

    def pull(quad, slot_ref, dist_ref):
        totals = [jnp.zeros((2 * M_ROWS, 128), F32) for _ in range(2)]
        for chunk in range(8):
            for side in range(2):
                inv = lax.rsqrt(dist_ref[128 * chunk : 128 * chunk + 128, 128 * side : 128 * side + 128])
                weights = stacked(inv * inv * inv)
                rows = [slot_ref[2 * side + half, pl.ds(chunk, M_ROWS, stride=8), :] for half in range(2)]
                rows = jnp.concatenate(rows, axis=0).astype(BF16)
                totals[side] += jnp.dot(jnp.concatenate([rows, rows], axis=1), weights, preferred_element_type=F32)
                yield
        for side in range(2):
            pair = 2 * quad + side
            sums = jnp.where(left, totals[side][0:M_ROWS], totals[side][M_ROWS:])
            lanes = pair_lanes(pair)
            out_ref[:, lanes] = out_ref[:, lanes] + point_sums(sums, pair_place(tg_ref, pair))

    quads, octets = LEAF_DEV // 4, LEAF_DEV // 8
    run(build(0))
    copy.wait()
    run(features(0, 0, even_ref))
    run(distances(0, dist_even))

    def one_octet(octet, carry):
        quad = 2 * octet
        after = jnp.minimum(quad + 2, quads - 1)
        cells = cell_pull(octet, tg_ref, ah_ref, cf_ref, cm_ref, out_ref)
        coming = build(jnp.minimum(octet + 1, octets - 1))
        for half, (now, slot_ref, dist_ref, ahead, ahead_slot, ahead_dist, raw_at) in enumerate(
            (
                (quad, even_ref, dist_even, quad + 1, odd_ref, dist_odd, 4),
                (quad + 1, odd_ref, dist_odd, after, even_ref, dist_even, 0),
            )
        ):
            direct = pull(now, slot_ref, dist_ref)
            moments, distance = features(ahead, raw_at, ahead_slot), distances(ahead, ahead_dist)
            for step in range(8):
                if step % 2 == 1:
                    run(distance, 1)
                run(direct, 1)
                if step % 2 == 0:
                    run(moments, 1)
                if half == 0 or step < 4:
                    run(coming, 3)
                    run(cells, 2 if half or step % 2 else 1)
                else:
                    run(coming, 1)
                run(direct, 1)
            run(moments)
            run(distance)
            run(direct)
        run(coming)
        return carry

    lax.fori_loop(0, octets, one_octet, 0)


def on_device(n_dom, n_sub, positions, masses, cell_mass, cell_center, cell_quad, cell_list, leaf_list, send_list, send_count):
    vmem = pl.BlockSpec(memory_space=pltpu.VMEM)
    smem = pl.BlockSpec(memory_space=pltpu.SMEM)
    anywhere = pl.BlockSpec(memory_space=pl.ANY)

    def limit(mib):
        return pltpu.CompilerParams(vmem_limit_bytes=mib * 1024 * 1024)

    ins = (
        positions,
        masses.reshape(1, -1),
        cell_mass.reshape(1, -1),
        cell_center,
        cell_quad,
        cell_list,
        leaf_list.T,
        send_list.reshape(2 * RANGE, CAP),
        send_count.reshape(1, 2 * RANGE),
    )
    bundle_rows = OWN_ROWS + LEAF_DEV + NLEAF
    packed, sent, bundle = pl.pallas_call(
        functools.partial(pack_kernel, n_dom),
        out_shape=(
            jax.ShapeDtypeStruct((OWN_ROWS, 128), F32),
            jax.ShapeDtypeStruct((n_dom, SENT_ROWS, 128), F32),
            jax.ShapeDtypeStruct((bundle_rows, 128), F32),
        ),
        in_specs=[pl.BlockSpec(memory_space=pltpu.HBM)] * 9,
        out_specs=[anywhere] * 3,
        scratch_shapes=[pltpu.VMEM(array.shape, array.dtype) for array in ins[:7]]
        + [pltpu.SMEM(array.shape, jnp.int32) for array in ins[7:]]
        + [
            pltpu.VMEM((bundle_rows, 128), F32),
            pltpu.VMEM((n_dom + 1, SENT_ROWS, 128), F32),
            pltpu.SemaphoreType.DMA((12,)),
        ],
        compiler_params=limit(63),
        name="pack_own",
    )(*ins)
    received = lax.all_to_all(sent, "dom", split_axis=0, concat_axis=0, tiled=True)

    def across(value, bits):
        return lax.ppermute(value, "sub", [(seg, seg ^ bits) for seg in range(n_sub)])

    nearby = {0: packed}
    bit = n_sub // 2
    while bit:
        nearby.update({at ^ bit: across(value, bit) for at, value in nearby.items()})
        bit //= 2
    nearby = [nearby[at] for at in range(n_sub)]
    own_cells = received[:, OUT_ROWS:]
    cells = [own_cells] + [across(own_cells, bits) for bits in range(1, n_sub)]
    n_blocks = n_sub * LEAF_DEV + 2 * RANGE * CAP
    prepared = pl.pallas_call(
        functools.partial(prepare_kernel, n_dom, n_sub),
        out_shape=(
            jax.ShapeDtypeStruct((n_blocks, 4, 128), F32),
            jax.ShapeDtypeStruct((n_blocks, LEAF, 128), BF16),
            jax.ShapeDtypeStruct((PAIRS, H_ROWS, 128), BF16),
            jax.ShapeDtypeStruct((OWN_ROWS, 128), F32),
            jax.ShapeDtypeStruct((3, LEAF_DEV, 128), F32),
            jax.ShapeDtypeStruct((PAIRS, 128, 128), BF16),
            jax.ShapeDtypeStruct((LEAF_DEV, NCELL), jnp.int32),
            jax.ShapeDtypeStruct((NLEAF, LEAF_DEV), jnp.int32),
        ),
        in_specs=[vmem] * (n_sub + 1),
        out_specs=[vmem] * 8,
        scratch_shapes=[
            pltpu.VMEM((2, 8 * (H_ROWS + Q_ROWS), 128), F32),
            pltpu.VMEM((8, 8 * H_ROWS, 128), F32),
        ],
        compiler_params=limit(24),
        cost_estimate=pl.CostEstimate(flops=0, bytes_accessed=20_000_000, transcendentals=0),
        name="prepare",
    )(bundle, *nearby[1:], received)
    return pl.pallas_call(
        functools.partial(pull_kernel, n_dom, n_sub),
        out_shape=jax.ShapeDtypeStruct((3, LEAF_DEV * LEAF), F32),
        in_specs=[vmem] * (n_sub + 8),
        out_specs=vmem,
        scratch_shapes=[
            pltpu.SMEM((NLEAF, LEAF_DEV), jnp.int32),
            pltpu.VMEM((n_dom, n_sub, CELL_COMPS, 8, 128), F32),
            pltpu.VMEM((8 * CELL_ROWS, 128), F32),
            pltpu.VMEM((8, 128), F32),
            pltpu.VMEM((8, 32, 128), F32),
            pltpu.VMEM((4, 8 * M_ROWS, 128), F32),
            pltpu.VMEM((4, 8 * M_ROWS, 128), F32),
            pltpu.VMEM((NLEAF * LEAF, 256), F32),
            pltpu.VMEM((NLEAF * LEAF, 256), F32),
            pltpu.SemaphoreType.DMA(()),
        ],
        compiler_params=limit(24),
        name="pull",
    )(*cells, *prepared)


def solution(mesh):
    sharded = P(("dom", "sub"))
    return jax.shard_map(
        functools.partial(on_device, mesh.shape["dom"], mesh.shape["sub"]),
        mesh=mesh,
        in_specs=(
            P(None, ("dom", "sub")),
            sharded,
            sharded,
            P(None, ("dom", "sub")),
            P(None, ("dom", "sub")),
            P(("dom", "sub"), None),
            P(("dom", "sub"), None),
            P("dom", "sub", None, None),
            P("dom", "sub", None),
        ),
        out_specs=P(None, ("dom", "sub")),
        check_vma=False,
    )
```

```python
import functools

import jax
import jax.numpy as jnp
from jax import lax
from jax.experimental import pallas as pl
from jax.experimental.pallas import tpu as pltpu
from jax.sharding import PartitionSpec as P

LEAF = 64
LEAF_DEV = 128
NCELL = 128
NLEAF = 16
RANGE = 4
CAP = 8
PAIRS = LEAF_DEV // 2
OUT_UNITS = CAP // 2
OWN_ROWS = 4 * PAIRS
OUT_ROWS = 4 * OUT_UNITS
CELL_COMPS = 10
CELL_PAD = 16
SENT_ROWS = OUT_ROWS + CELL_PAD
OFFSETS = list(range(-RANGE, 0)) + list(range(1, RANGE + 1))

softening_sq = 0.0025
GRID_ROUND = 49152.0
F32 = jnp.float32
BF16 = jnp.bfloat16

H_ROWS = 32
Q_ROWS = 64
V_ROWS = 16
U_ROWS = 48
Q_AT = H_ROWS
V_AT = Q_AT + Q_ROWS
U_AT = V_AT + V_ROWS
CELL_ROWS = U_AT + U_ROWS
M_ROWS = 8


def rounded(value):
    return value.astype(BF16).astype(F32)


def three_parts(value):
    first = rounded(value)
    rest = value - first
    second = rounded(rest)
    return first, second, rest - second


def high_low(value):
    high = rounded(value)
    return high, value - high


def two_parts(value):
    first = value.astype(BF16)
    return first, (value - first.astype(F32)).astype(BF16)


def grid_parts(value):
    high = (value + GRID_ROUND) - GRID_ROUND
    low = value - high
    first = rounded(low)
    return high, low, first, low - first


def norm_parts(parts, extra=None):
    big = sum(high * high for high, _, _, _ in parts)
    small = sum(low * (2.0 * high + low) for high, low, _, _ in parts)
    if extra is not None:
        small = small + extra
    return three_parts(big), three_parts(small)


def put_own(pos_ref, mass_ref, own_ref):
    for pair in range(PAIRS):
        lanes = pl.ds(128 * pair, 128)
        own_ref[4 * pair : 4 * pair + 3, :] = pos_ref[:, lanes]
        own_ref[4 * pair + 3 : 4 * pair + 4, :] = mass_ref[:, lanes]


def pack_kernel(n_dom, *refs):
    ins, outs, scratch, (out_ref, sent_ref, sems) = refs[:9], refs[9:12], refs[12:21], refs[21:]
    results = [
        pltpu.make_async_copy(out_ref.at[pl.ds(0, OWN_ROWS)], outs[0], sems.at[9]),
        pltpu.make_async_copy(sent_ref.at[pl.ds(0, n_dom)], outs[1], sems.at[10]),
        pltpu.make_async_copy(out_ref, outs[2], sems.at[11]),
    ]
    copies = [pltpu.make_async_copy(src, dst, sems.at[at]) for at, (src, dst) in enumerate(zip(ins, scratch))]
    for copy in copies:
        copy.start()
    pos_ref, mass_ref, cmass_ref, center_ref, quad_ref, cl_ref, ll_ref, list_ref, count_ref = scratch
    me = lax.axis_index("dom")
    left = lax.broadcasted_iota(jnp.int32, (4, 128), 1) < LEAF
    sent_ref[...] = jnp.zeros((n_dom + 1, SENT_ROWS, 128), F32)
    for copy in copies:
        copy.wait()
    put_own(pos_ref, mass_ref, out_ref)
    results[0].start()
    out_ref[OWN_ROWS : OWN_ROWS + LEAF_DEV, :] = cl_ref[...].astype(F32)
    out_ref[OWN_ROWS + LEAF_DEV :, :] = ll_ref[...].astype(F32)
    results[2].start()

    def put_cells(target, carry):
        sent_ref[target, OUT_ROWS : OUT_ROWS + 1, :] = cmass_ref[...]
        sent_ref[target, OUT_ROWS + 1 : OUT_ROWS + 4, :] = center_ref[...]
        sent_ref[target, OUT_ROWS + 4 : OUT_ROWS + 10, :] = quad_ref[...]
        return carry

    lax.fori_loop(0, n_dom, put_cells, 0)

    def half(slot, j, right):
        block = list_ref[slot, j]
        value = out_ref[pl.ds(pl.multiple_of(4 * (block // 2), 4), 4), :]
        value = jnp.where(j < count_ref[0, slot], value, 0.0)
        return jnp.where((block & 1) == right, value, pltpu.roll(value, LEAF, 1))

    for slot in range(2 * RANGE):
        target = me + OFFSETS[slot]
        target = jnp.where((target >= 0) & (target < n_dom), target, n_dom)
        for unit in range(OUT_UNITS):
            sent_ref[target, 4 * unit : 4 * unit + 4, :] = jnp.where(left, half(slot, 2 * unit, 0), half(slot, 2 * unit + 1, 1))
    results[1].start()
    for copy in results:
        copy.wait()


def target_h_rows(parts, one, zero):
    big, small = norm_parts(parts, softening_sq)
    minus_high = [-2.0 * part[0] for part in parts]
    minus_one = [-2.0 * part[2] for part in parts]
    minus_two = [-2.0 * part[3] for part in parts]
    rows = minus_high + [one] * 3 + list(big) + minus_high + minus_one + minus_high
    return rows + minus_two + minus_one + [one] * 3 + list(small) + [zero] * 2


def target_features(octet, tg_ref, ce_ref, feat_ref, ah_ref):
    left = lax.broadcasted_iota(jnp.int32, (8, 128), 1) < LEAF
    one = jnp.ones((8, 128), F32)
    zero = jnp.zeros((8, 128), F32)
    parts, centred = [], []
    for comp in range(3):
        rows = pl.ds(octet * 32 + comp, 8, stride=4)
        value = tg_ref[rows, :]
        first = jnp.broadcast_to(value[:, 0:1], (8, 128))
        second = jnp.broadcast_to(value[:, LEAF : LEAF + 1], (8, 128))
        ce_ref[comp, pl.ds(octet * 16, 8, stride=2), :] = first
        ce_ref[comp, pl.ds(octet * 16 + 1, 8, stride=2), :] = second
        value = value - jnp.where(left, first, second)
        tg_ref[rows, :] = value
        centred.append(value)
        parts.append(grid_parts(value))
    rows = target_h_rows(parts, one, zero)
    x, y, z = centred
    split = [three_parts(v) for v in (x, y, z, x * x, y * y, z * z, x * y, x * z, y * z)]
    for which in (0, 0, 1, 0, 1, 2):
        rows += [part[which] for part in split]
    rows += [one] * 3 + [zero] * 7
    for at, value in enumerate(rows):
        feat_ref[8 * at : 8 * at + 8, :] = value
    for sub in range(8):
        features = feat_ref[pl.ds(sub, H_ROWS + Q_ROWS, stride=8), :].T.astype(BF16)
        ah_ref[octet * 8 + sub, :, 0 : H_ROWS + Q_ROWS] = features


def source_h_rows(parts):
    (p1, p2, p3), (s1, s2, s3) = norm_parts(parts)
    high = [part[0] for part in parts]
    one = [part[2] for part in parts]
    two = [part[3] for part in parts]
    rows = dict(enumerate(high + [p1, p2, p3]))
    rows.update(enumerate(one + high + two + high + one + [s1, s2, s3], 9))
    return rows


def put_rows(ref, rows):
    for at, value in rows.items():
        ref[8 * at : 8 * at + 8, :] = value


def fill_constant_rows(ref, count):
    one = jnp.ones((8, 128), F32)
    zero = jnp.zeros((8, 128), F32)
    for at in range(count):
        ones = at in (6, 7, 8, 27, 28, 29) or at == V_AT + 3
        ref[8 * at : 8 * at + 8, :] = one if ones else zero


def cell_features(n_dom, n_sub, octet, cl_ref, spread_ref, ce_ref, cf_ref, cm_ref):
    ids = cl_ref[pl.ds(pl.multiple_of(8 * octet, 8), 8), :]
    lane = ids & 127
    owner = ids >> 7
    me = lax.axis_index("sub")

    def look_up(dom, shift, found):
        here = owner == dom * n_sub + lax.bitwise_xor(me, shift)
        new = []
        for comp in range(CELL_COMPS):
            value = jnp.take_along_axis(spread_ref[dom, shift, comp], lane, axis=1, mode="promise_in_bounds")
            new.append(jnp.where(here, value, found[comp]))
        return tuple(new)

    found = tuple(jnp.zeros((8, 128), F32) for _ in range(CELL_COMPS))
    if n_dom <= 8:
        for dom in range(n_dom):
            for shift in range(n_sub):
                found = look_up(dom, shift, found)
                yield
    else:

        def one_domain(dom, found):
            for shift in range(n_sub):
                found = look_up(dom, shift, found)
            return found

        found = lax.fori_loop(0, n_dom, one_domain, found)
    mass, cx, cy, cz, xx, yy, zz, xy, xz, yz = found
    yield "found"
    cm_ref[...] = mass
    rows8 = pl.ds(pl.multiple_of(8 * octet, 8), 8)
    cx, cy, cz = [value - ce_ref[comp, rows8, :] for comp, value in enumerate((cx, cy, cz))]
    put_rows(cf_ref, source_h_rows([grid_parts(value) for value in (cx, cy, cz)]))
    yield
    qx = xx * cx + xy * cy + xz * cz
    qy = xy * cx + yy * cy + yz * cz
    qz = xz * cx + yz * cy + zz * cz
    const = three_parts(2.5 * (qx * cx + qy * cy + qz * cz))
    linear = [-5.0 * qx, -5.0 * qy, -5.0 * qz]
    square = [2.5 * xx, 2.5 * yy, 2.5 * zz, 5.0 * xy, 5.0 * xz, 5.0 * yz]
    split = [three_parts(value) for value in linear + square]
    rows = []
    for which in (0, 1, 0, 2, 1, 0):
        rows += [part[which] for part in split]
    rows += list(const)
    put_rows(cf_ref, dict(enumerate(rows, Q_AT)))
    yield
    for comp, value in enumerate((cx, cy, cz)):
        for which, part in enumerate(three_parts(value)):
            cf_ref[8 * (V_AT + 4 * which + comp) : 8 * (V_AT + 4 * which + comp) + 8, :] = part
    yield
    columns = {name: three_parts(value) for name, value in dict(xx=xx, yy=yy, zz=zz, xy=xy, xz=xz, yz=yz, cx=qx, cy=qy, cz=qz).items()}
    order = (("xx", "xy", "xz"), ("xy", "yy", "yz"), ("xz", "yz", "zz"), ("cx", "cy", "cz"))
    for which in range(3):
        for column, names in enumerate(order):
            for row, name in enumerate(names):
                at = U_AT + 16 * which + 4 * column + row
                cf_ref[8 * at : 8 * at + 8, :] = columns[name][which]


def source_moments(group, ll_ref, tab_ref, ce_ref, raw_ref, sf_ref):
    left = lax.broadcasted_iota(jnp.int32, (4, 128), 1) < LEAF
    for pair in range(NLEAF // 2):
        first = tab_ref[ll_ref[2 * pair, group]]
        second = tab_ref[ll_ref[2 * pair + 1, group]]
        raw_ref[4 * pair : 4 * pair + 4, :] = jnp.where(left, first, second)
    value = [raw_ref[pl.ds(comp, 8, stride=4), :] for comp in range(4)]
    mass = value[3]
    centred = [value[comp] - ce_ref[comp, pl.ds(group, 1), :] for comp in range(3)]
    for comp, v in enumerate([mass * v for v in centred] + [mass]):
        for which, part in enumerate(high_low(v)):
            at = 4 * which + comp
            sf_ref[8 * at : 8 * at + 8, :] = part


def transposed_dot(rows, weights):
    return lax.dot_general(rows, weights, (((1,), (1,)), ((), ())), preferred_element_type=F32)


def stacked(value):
    return jnp.concatenate(two_parts(value), axis=0)


def cell_group(sub, target, cf_ref, cm_ref):
    def cell_rows(at, count):
        return cf_ref[pl.ds(8 * at + sub, count, stride=8), :].astype(BF16)

    forms = jnp.concatenate(
        [
            jnp.concatenate([cell_rows(0, H_ROWS), jnp.zeros((H_ROWS, 128), BF16)], axis=1),
            jnp.concatenate([jnp.zeros((Q_ROWS, 128), BF16), cell_rows(Q_AT, Q_ROWS)], axis=1),
        ],
        axis=0,
    )
    forms = jnp.dot(target[:, 0 : H_ROWS + Q_ROWS], forms, preferred_element_type=F32)
    yield
    dist_sq, quad_form = forms[:, 0:128], forms[:, 128:256]
    inv = lax.rsqrt(dist_sq)
    inv_two = inv * inv
    inv_three = inv * inv_two
    pull = inv_three * (cm_ref[pl.ds(sub, 1), :] + quad_form * (inv_two * inv_two))
    moments = jnp.concatenate(
        [
            jnp.concatenate([cell_rows(V_AT, V_ROWS), jnp.zeros((V_ROWS, 128), BF16)], axis=1),
            jnp.concatenate([jnp.zeros((U_ROWS, 128), BF16), cell_rows(U_AT, U_ROWS)], axis=1),
        ],
        axis=0,
    )
    return jnp.concatenate([stacked(pull), stacked(inv_three * inv_two)], axis=1), moments


def pair_lanes(pair):
    return pl.ds(pl.multiple_of(128 * pair, 128), 128)


def pair_place(tg_ref, pair):
    return tg_ref[pl.ds(pl.multiple_of(4 * pair, 4), 4), :]


def point_sums(sums, place):
    sums = sums + pltpu.roll(sums, 4, 0)
    return sums[0:3] - place[0:3] * sums[3:4]


def cell_pull(octet, tg_ref, ah_ref, cf_ref, cm_ref, out_ref):
    upper = lax.broadcasted_iota(jnp.int32, (8, 128), 0) < 4
    left = lax.broadcasted_iota(jnp.int32, (LEAF, 128), 1) < LEAF
    for inner in range(4):
        pair = octet * 4 + inner
        first, first_moments = yield from cell_group(2 * inner, ah_ref[pair, 0:LEAF, :], cf_ref, cm_ref)
        second, second_moments = yield from cell_group(2 * inner + 1, ah_ref[pair, LEAF:, :], cf_ref, cm_ref)
        yield
        moments = jnp.concatenate([first_moments, second_moments], axis=0)
        sums = transposed_dot(jnp.concatenate([first, second], axis=0), moments)
        yield
        sums = jnp.where(left, sums[0:64] + sums[64:128], sums[128:192] + sums[192:256]).T
        sums = jnp.concatenate([sums[0:64], sums[64:128]], axis=1)
        place = pair_place(tg_ref, pair)
        x, y, z = [place[comp : comp + 1, :] for comp in range(3)]
        quads = sums[16:32] + sums[32:48] + sums[48:64]
        turned = quads[0:8] * jnp.where(upper, x, y) + quads[8:16] * jnp.where(upper, z, -1.0)
        turned = turned + pltpu.roll(turned, 4, 0)
        out_ref[:, pair_lanes(pair)] = point_sums(sums[0:8] + sums[8:16], place) + turned[0:3]


def put_block_pair(tab_ref, block, value):
    left = lax.broadcasted_iota(jnp.int32, (4, 128), 1) < LEAF
    turned = pltpu.roll(value, LEAF, 1)
    tab_ref[block] = jnp.where(left, value, turned)
    tab_ref[block + 1] = jnp.where(left, turned, value)


def put_eight_pairs(rows_ref, block, coords, feat_ref):
    put_rows(feat_ref, source_h_rows([grid_parts(value) for value in coords]))
    for pair in range(8):
        columns = feat_ref[pl.ds(pair, H_ROWS, stride=8), :].astype(BF16)
        spread = jnp.concatenate([columns] * 4, axis=0).T
        rows_ref[block + 2 * pair] = spread[0:LEAF]
        rows_ref[block + 2 * pair + 1] = spread[LEAF:]


def prepare_kernel(n_dom, n_sub, *refs):
    bundle_ref, near_refs, recv_ref = refs[0], refs[1:n_sub], refs[n_sub]
    tab_ref, rows_ref, at_ref, tg_ref, ce_ref, ah_ref, cl_ref, ll_ref, feat_ref, four_ref = refs[n_sub + 1 :]
    own_ref = bundle_ref.at[0:OWN_ROWS]
    cl_ref[...] = bundle_ref[OWN_ROWS : OWN_ROWS + LEAF_DEV, :].astype(jnp.int32)
    ll_ref[...] = bundle_ref[OWN_ROWS + LEAF_DEV :, :].astype(jnp.int32)
    for at in range(8):
        fill_constant_rows(four_ref.at[at], H_ROWS)
    me = lax.axis_index("sub")

    def near_blocks(shift, near_ref):
        seg = lax.bitwise_xor(me, shift)

        def near(step, carry):
            for at in range(8):
                octet = 8 * step + at
                block = seg * LEAF_DEV + 16 * octet
                first = pl.multiple_of(32 * octet, 32)
                for pair in range(8):
                    put_block_pair(tab_ref, block + 2 * pair, near_ref[pl.ds(pl.multiple_of(first + 4 * pair, 4), 4), :])
                coords = [near_ref[pl.ds(first + comp, 8, stride=4), :] for comp in range(3)]
                put_eight_pairs(rows_ref, block, coords, four_ref.at[at])
            return carry

        lax.fori_loop(0, PAIRS // 64, near, 0)

    for shift in range(1, n_sub):
        near_blocks(shift, near_refs[shift - 1])
    far_tables(n_dom, n_sub * LEAF_DEV, recv_ref, tab_ref, rows_ref, four_ref)
    near_blocks(0, own_ref)
    tg_ref[...] = own_ref[...]

    def targets(step, carry):
        for at in range(2):
            octet = 2 * step + at
            target_features(octet, tg_ref, ce_ref, feat_ref.at[at], ah_ref)
            target_rows(octet, own_ref, four_ref.at[at], at_ref)
        return carry

    lax.fori_loop(0, PAIRS // 16, targets, 0)


def far_tables(n_dom, first_block, recv_ref, tab_ref, rows_ref, four_ref):
    me = lax.axis_index("dom")
    for two in range(RANGE):
        halves = []
        for slot in (2 * two, 2 * two + 1):
            source = me - OFFSETS[slot]
            inside = (source >= 0) & (source < n_dom)
            source = jnp.clip(source, 0, n_dom - 1)
            for unit in range(OUT_UNITS):
                value = jnp.where(inside, recv_ref[source, 4 * unit : 4 * unit + 4, :], 0.0)
                put_block_pair(tab_ref, first_block + slot * CAP + 2 * unit, value)
            halves.append([jnp.where(inside, recv_ref[source, pl.ds(comp, OUT_UNITS, stride=4), :], 0.0) for comp in range(3)])
        coords = [jnp.concatenate([one, other], axis=0) for one, other in zip(*halves)]
        put_eight_pairs(rows_ref, first_block + 2 * two * CAP, coords, four_ref.at[two])


def target_rows(octet, own_ref, feat_ref, at_ref):
    one = jnp.ones((8, 128), F32)
    zero = jnp.zeros((8, 128), F32)
    parts = [grid_parts(own_ref[pl.ds(octet * 32 + comp, 8, stride=4), :]) for comp in range(3)]
    for at, value in enumerate(target_h_rows(parts, one, zero)):
        feat_ref[8 * at : 8 * at + 8, :] = value
    for pair in range(8):
        at_ref[octet * 8 + pair] = feat_ref[pl.ds(pair, H_ROWS, stride=8), :].astype(BF16)


def run(strand, steps=None):
    taken = 0
    while steps is None or taken < steps:
        taken += 1
        if next(strand, "end") == "end":
            return


def pull_kernel(n_dom, n_sub, *refs):
    cell_refs = refs[:n_sub]
    tab_ref, rows_ref, at_ref, tg_ref, ce_ref, ah_ref, cl_ref, ll_in, out_ref = refs[n_sub : n_sub + 9]
    ll_ref, spread_ref, cf_ref, cm_ref, raw_ref, even_ref, odd_ref, dist_even, dist_odd, sem = refs[n_sub + 9 :]
    copy = pltpu.make_async_copy(ll_in, ll_ref, sem)
    copy.start()
    fill_constant_rows(cf_ref, CELL_ROWS)

    def build(octet):
        return cell_features(n_dom, n_sub, octet, cl_ref, spread_ref, ce_ref, cf_ref, cm_ref)

    def spread(dom, carry):
        for shift in range(n_sub):
            for comp in range(CELL_COMPS):
                row = cell_refs[shift][dom, comp : comp + 1, :]
                spread_ref[dom, shift, comp] = jnp.broadcast_to(row, (8, 128))
        return carry

    lax.fori_loop(0, n_dom, spread, 0)

    left = lax.broadcasted_iota(jnp.int32, (M_ROWS, 128), 1) < LEAF
    left_target = lax.broadcasted_iota(jnp.int32, (H_ROWS, 128), 1) < LEAF
    owner = (lax.broadcasted_iota(jnp.int32, (LEAF, 128), 1) // H_ROWS).astype(BF16)
    lower_half, first_own, third_own = owner < 2.0, owner == 0.0, owner == 2.0

    def features(quad, raw_at, slot_ref):
        for group in range(4):
            source_moments(4 * quad + group, ll_ref, tab_ref, ce_ref, raw_ref.at[raw_at + group], slot_ref.at[group])
            yield

    def distances(quad, dist_ref):
        nothing = jnp.zeros((H_ROWS, 128), BF16)
        first, second = at_ref[2 * quad], at_ref[2 * quad + 1]
        targets = jnp.concatenate(
            [
                jnp.concatenate([jnp.where(left_target, first, nothing), nothing], axis=1),
                jnp.concatenate([jnp.where(left_target, nothing, first), nothing], axis=1),
                jnp.concatenate([nothing, jnp.where(left_target, second, nothing)], axis=1),
                jnp.concatenate([nothing, jnp.where(left_target, nothing, second)], axis=1),
            ],
            axis=0,
        )
        sources = []
        for j in range(NLEAF):
            rows = [rows_ref[ll_ref[j, 4 * quad + group]] for group in range(4)]
            low = jnp.where(first_own, rows[0], rows[1])
            high = jnp.where(third_own, rows[2], rows[3])
            sources.append(jnp.where(lower_half, low, high))
            if j % 4 == 3:
                rows = pl.ds(LEAF * (j - 3), 4 * LEAF)
                dist_ref[rows, :] = jnp.dot(jnp.concatenate(sources, axis=0), targets, preferred_element_type=F32)
                sources = []
                yield

    def pull(quad, slot_ref, dist_ref):
        totals = [jnp.zeros((2 * M_ROWS, 128), F32) for _ in range(2)]
        for chunk in range(8):
            for side in range(2):
                inv = lax.rsqrt(dist_ref[128 * chunk : 128 * chunk + 128, 128 * side : 128 * side + 128])
                weights = stacked(inv * inv * inv)
                rows = [slot_ref[2 * side + half, pl.ds(chunk, M_ROWS, stride=8), :] for half in range(2)]
                rows = jnp.concatenate(rows, axis=0).astype(BF16)
                totals[side] += jnp.dot(jnp.concatenate([rows, rows], axis=1), weights, preferred_element_type=F32)
                yield
        for side in range(2):
            pair = 2 * quad + side
            sums = jnp.where(left, totals[side][0:M_ROWS], totals[side][M_ROWS:])
            lanes = pair_lanes(pair)
            out_ref[:, lanes] = out_ref[:, lanes] + point_sums(sums, pair_place(tg_ref, pair))

    quads, octets = LEAF_DEV // 4, LEAF_DEV // 8
    run(build(0))
    copy.wait()
    run(features(0, 0, even_ref))
    run(distances(0, dist_even))

    def one_octet(octet, carry):
        quad = 2 * octet
        after = jnp.minimum(quad + 2, quads - 1)
        cells = cell_pull(octet, tg_ref, ah_ref, cf_ref, cm_ref, out_ref)
        coming = build(jnp.minimum(octet + 1, octets - 1))
        for half, (now, slot_ref, dist_ref, ahead, ahead_slot, ahead_dist, raw_at) in enumerate(
            (
                (quad, even_ref, dist_even, quad + 1, odd_ref, dist_odd, 4),
                (quad + 1, odd_ref, dist_odd, after, even_ref, dist_even, 0),
            )
        ):
            direct = pull(now, slot_ref, dist_ref)
            moments, distance = features(ahead, raw_at, ahead_slot), distances(ahead, ahead_dist)
            for step in range(8):
                early = half == 0 or step < 4
                run(direct, 1)
                run(coming, 1)
                if early:
                    run(cells, 1)
                    run(coming, 1)
                if step % 2 == 1:
                    run(distance, 1)
                else:
                    run(moments, 1)
                run(direct, 1)
                if early:
                    run(coming, 1)
                    if half or step % 2:
                        run(cells, 1)
            run(moments)
            run(distance)
            run(direct)
        run(coming)
        return carry

    lax.fori_loop(0, octets, one_octet, 0)


def on_device(n_dom, n_sub, positions, masses, cell_mass, cell_center, cell_quad, cell_list, leaf_list, send_list, send_count):
    vmem = pl.BlockSpec(memory_space=pltpu.VMEM)
    smem = pl.BlockSpec(memory_space=pltpu.SMEM)
    anywhere = pl.BlockSpec(memory_space=pl.ANY)

    def limit(mib):
        return pltpu.CompilerParams(vmem_limit_bytes=mib * 1024 * 1024)

    ins = (
        positions,
        masses.reshape(1, -1),
        cell_mass.reshape(1, -1),
        cell_center,
        cell_quad,
        cell_list,
        leaf_list.T,
        send_list.reshape(2 * RANGE, CAP),
        send_count.reshape(1, 2 * RANGE),
    )
    bundle_rows = OWN_ROWS + LEAF_DEV + NLEAF
    packed, sent, bundle = pl.pallas_call(
        functools.partial(pack_kernel, n_dom),
        out_shape=(
            jax.ShapeDtypeStruct((OWN_ROWS, 128), F32),
            jax.ShapeDtypeStruct((n_dom, SENT_ROWS, 128), F32),
            jax.ShapeDtypeStruct((bundle_rows, 128), F32),
        ),
        in_specs=[pl.BlockSpec(memory_space=pltpu.HBM)] * 9,
        out_specs=[anywhere] * 3,
        scratch_shapes=[pltpu.VMEM(array.shape, array.dtype) for array in ins[:7]]
        + [pltpu.SMEM(array.shape, jnp.int32) for array in ins[7:]]
        + [
            pltpu.VMEM((bundle_rows, 128), F32),
            pltpu.VMEM((n_dom + 1, SENT_ROWS, 128), F32),
            pltpu.SemaphoreType.DMA((12,)),
        ],
        compiler_params=limit(63),
        name="pack_own",
    )(*ins)
    received = lax.all_to_all(sent, "dom", split_axis=0, concat_axis=0, tiled=True)

    def across(value, bits):
        return lax.ppermute(value, "sub", [(seg, seg ^ bits) for seg in range(n_sub)])

    nearby = {0: packed}
    bit = n_sub // 2
    while bit:
        nearby.update({at ^ bit: across(value, bit) for at, value in nearby.items()})
        bit //= 2
    nearby = [nearby[at] for at in range(n_sub)]
    own_cells = received[:, OUT_ROWS:]
    cells = [own_cells] + [across(own_cells, bits) for bits in range(1, n_sub)]
    n_blocks = n_sub * LEAF_DEV + 2 * RANGE * CAP
    prepared = pl.pallas_call(
        functools.partial(prepare_kernel, n_dom, n_sub),
        out_shape=(
            jax.ShapeDtypeStruct((n_blocks, 4, 128), F32),
            jax.ShapeDtypeStruct((n_blocks, LEAF, 128), BF16),
            jax.ShapeDtypeStruct((PAIRS, H_ROWS, 128), BF16),
            jax.ShapeDtypeStruct((OWN_ROWS, 128), F32),
            jax.ShapeDtypeStruct((3, LEAF_DEV, 128), F32),
            jax.ShapeDtypeStruct((PAIRS, 128, 128), BF16),
            jax.ShapeDtypeStruct((LEAF_DEV, NCELL), jnp.int32),
            jax.ShapeDtypeStruct((NLEAF, LEAF_DEV), jnp.int32),
        ),
        in_specs=[vmem] * (n_sub + 1),
        out_specs=[vmem] * 8,
        scratch_shapes=[
            pltpu.VMEM((2, 8 * (H_ROWS + Q_ROWS), 128), F32),
            pltpu.VMEM((8, 8 * H_ROWS, 128), F32),
        ],
        compiler_params=limit(24),
        cost_estimate=pl.CostEstimate(flops=0, bytes_accessed=20_000_000, transcendentals=0),
        name="prepare",
    )(bundle, *nearby[1:], received)
    return pl.pallas_call(
        functools.partial(pull_kernel, n_dom, n_sub),
        out_shape=jax.ShapeDtypeStruct((3, LEAF_DEV * LEAF), F32),
        in_specs=[vmem] * (n_sub + 8),
        out_specs=vmem,
        scratch_shapes=[
            pltpu.SMEM((NLEAF, LEAF_DEV), jnp.int32),
            pltpu.VMEM((n_dom, n_sub, CELL_COMPS, 8, 128), F32),
            pltpu.VMEM((8 * CELL_ROWS, 128), F32),
            pltpu.VMEM((8, 128), F32),
            pltpu.VMEM((8, 32, 128), F32),
            pltpu.VMEM((4, 8 * M_ROWS, 128), F32),
            pltpu.VMEM((4, 8 * M_ROWS, 128), F32),
            pltpu.VMEM((NLEAF * LEAF, 256), F32),
            pltpu.VMEM((NLEAF * LEAF, 256), F32),
            pltpu.SemaphoreType.DMA(()),
        ],
        compiler_params=limit(24),
        name="pull",
    )(*cells, *prepared)


def solution(mesh):
    sharded = P(("dom", "sub"))
    return jax.shard_map(
        functools.partial(on_device, mesh.shape["dom"], mesh.shape["sub"]),
        mesh=mesh,
        in_specs=(
            P(None, ("dom", "sub")),
            sharded,
            sharded,
            P(None, ("dom", "sub")),
            P(None, ("dom", "sub")),
            P(("dom", "sub"), None),
            P(("dom", "sub"), None),
            P("dom", "sub", None, None),
            P("dom", "sub", None),
        ),
        out_specs=P(None, ("dom", "sub")),
        check_vma=False,
    )
```

```python
import functools

import jax
import jax.numpy as jnp
from jax import lax
from jax.experimental import pallas as pl
from jax.experimental.pallas import tpu as pltpu
from jax.sharding import PartitionSpec as P

LEAF = 64
LEAF_DEV = 128
NCELL = 128
NLEAF = 16
RANGE = 4
CAP = 8
PAIRS = LEAF_DEV // 2
OUT_UNITS = CAP // 2
OWN_ROWS = 4 * PAIRS
OUT_ROWS = 4 * OUT_UNITS
CELL_COMPS = 10
CELL_PAD = 16
SENT_ROWS = OUT_ROWS + CELL_PAD
OFFSETS = list(range(-RANGE, 0)) + list(range(1, RANGE + 1))

softening_sq = 0.0025
GRID_ROUND = 49152.0
F32 = jnp.float32
BF16 = jnp.bfloat16

H_ROWS = 32
Q_ROWS = 64
V_ROWS = 16
U_ROWS = 48
Q_AT = H_ROWS
V_AT = Q_AT + Q_ROWS
U_AT = V_AT + V_ROWS
CELL_ROWS = U_AT + U_ROWS
M_ROWS = 8


def rounded(value):
    return value.astype(BF16).astype(F32)


def three_parts(value):
    first = rounded(value)
    rest = value - first
    second = rounded(rest)
    return first, second, rest - second


def high_low(value):
    high = rounded(value)
    return high, value - high


def two_parts(value):
    first = value.astype(BF16)
    return first, (value - first.astype(F32)).astype(BF16)


def grid_parts(value):
    high = (value + GRID_ROUND) - GRID_ROUND
    low = value - high
    first = rounded(low)
    return high, low, first, low - first


def norm_parts(parts, extra=None):
    big = sum(high * high for high, _, _, _ in parts)
    small = sum(low * (2.0 * high + low) for high, low, _, _ in parts)
    if extra is not None:
        small = small + extra
    return three_parts(big), three_parts(small)


def put_own(pos_ref, mass_ref, own_ref):
    for pair in range(PAIRS):
        lanes = pl.ds(128 * pair, 128)
        own_ref[4 * pair : 4 * pair + 3, :] = pos_ref[:, lanes]
        own_ref[4 * pair + 3 : 4 * pair + 4, :] = mass_ref[:, lanes]


def pack_kernel(n_dom, *refs):
    ins, outs, scratch, (out_ref, sent_ref, sems) = refs[:9], refs[9:12], refs[12:21], refs[21:]
    results = [
        pltpu.make_async_copy(out_ref.at[pl.ds(0, OWN_ROWS)], outs[0], sems.at[9]),
        pltpu.make_async_copy(sent_ref.at[pl.ds(0, n_dom)], outs[1], sems.at[10]),
        pltpu.make_async_copy(out_ref, outs[2], sems.at[11]),
    ]
    copies = [pltpu.make_async_copy(src, dst, sems.at[at]) for at, (src, dst) in enumerate(zip(ins, scratch))]
    for copy in copies:
        copy.start()
    pos_ref, mass_ref, cmass_ref, center_ref, quad_ref, cl_ref, ll_ref, list_ref, count_ref = scratch
    me = lax.axis_index("dom")
    left = lax.broadcasted_iota(jnp.int32, (4, 128), 1) < LEAF
    sent_ref[...] = jnp.zeros((n_dom + 1, SENT_ROWS, 128), F32)
    for copy in copies:
        copy.wait()
    put_own(pos_ref, mass_ref, out_ref)
    results[0].start()
    out_ref[OWN_ROWS : OWN_ROWS + LEAF_DEV, :] = cl_ref[...].astype(F32)
    out_ref[OWN_ROWS + LEAF_DEV :, :] = ll_ref[...].astype(F32)
    results[2].start()

    def put_cells(target, carry):
        sent_ref[target, OUT_ROWS : OUT_ROWS + 1, :] = cmass_ref[...]
        sent_ref[target, OUT_ROWS + 1 : OUT_ROWS + 4, :] = center_ref[...]
        sent_ref[target, OUT_ROWS + 4 : OUT_ROWS + 10, :] = quad_ref[...]
        return carry

    lax.fori_loop(0, n_dom, put_cells, 0)

    def half(slot, j, right):
        block = list_ref[slot, j]
        value = out_ref[pl.ds(pl.multiple_of(4 * (block // 2), 4), 4), :]
        value = jnp.where(j < count_ref[0, slot], value, 0.0)
        return jnp.where((block & 1) == right, value, pltpu.roll(value, LEAF, 1))

    for slot in range(2 * RANGE):
        target = me + OFFSETS[slot]
        target = jnp.where((target >= 0) & (target < n_dom), target, n_dom)
        for unit in range(OUT_UNITS):
            sent_ref[target, 4 * unit : 4 * unit + 4, :] = jnp.where(left, half(slot, 2 * unit, 0), half(slot, 2 * unit + 1, 1))
    results[1].start()
    for copy in results:
        copy.wait()


def target_h_rows(parts, one, zero):
    big, small = norm_parts(parts, softening_sq)
    minus_high = [-2.0 * part[0] for part in parts]
    minus_one = [-2.0 * part[2] for part in parts]
    minus_two = [-2.0 * part[3] for part in parts]
    rows = minus_high + [one] * 3 + list(big) + minus_high + minus_one + minus_high
    return rows + minus_two + minus_one + [one] * 3 + list(small) + [zero] * 2


def target_features(octet, tg_ref, ce_ref, feat_ref, ah_ref):
    left = lax.broadcasted_iota(jnp.int32, (8, 128), 1) < LEAF
    one = jnp.ones((8, 128), F32)
    zero = jnp.zeros((8, 128), F32)
    parts, centred = [], []
    for comp in range(3):
        rows = pl.ds(octet * 32 + comp, 8, stride=4)
        value = tg_ref[rows, :]
        first = jnp.broadcast_to(value[:, 0:1], (8, 128))
        second = jnp.broadcast_to(value[:, LEAF : LEAF + 1], (8, 128))
        ce_ref[comp, pl.ds(octet * 16, 8, stride=2), :] = first
        ce_ref[comp, pl.ds(octet * 16 + 1, 8, stride=2), :] = second
        value = value - jnp.where(left, first, second)
        tg_ref[rows, :] = value
        centred.append(value)
        parts.append(grid_parts(value))
    rows = target_h_rows(parts, one, zero)
    x, y, z = centred
    split = [three_parts(v) for v in (x, y, z, x * x, y * y, z * z, x * y, x * z, y * z)]
    for which in (0, 0, 1, 0, 1, 2):
        rows += [part[which] for part in split]
    rows += [one] * 3 + [zero] * 7
    for at, value in enumerate(rows):
        feat_ref[8 * at : 8 * at + 8, :] = value
    for sub in range(8):
        features = feat_ref[pl.ds(sub, H_ROWS + Q_ROWS, stride=8), :].T.astype(BF16)
        ah_ref[octet * 8 + sub, :, 0 : H_ROWS + Q_ROWS] = features


def source_h_rows(parts):
    (p1, p2, p3), (s1, s2, s3) = norm_parts(parts)
    high = [part[0] for part in parts]
    one = [part[2] for part in parts]
    two = [part[3] for part in parts]
    rows = dict(enumerate(high + [p1, p2, p3]))
    rows.update(enumerate(one + high + two + high + one + [s1, s2, s3], 9))
    return rows


def put_rows(ref, rows):
    for at, value in rows.items():
        ref[8 * at : 8 * at + 8, :] = value


def fill_constant_rows(ref, count):
    one = jnp.ones((8, 128), F32)
    zero = jnp.zeros((8, 128), F32)
    for at in range(count):
        ones = at in (6, 7, 8, 27, 28, 29) or at == V_AT + 3
        ref[8 * at : 8 * at + 8, :] = one if ones else zero


def cell_features(n_dom, n_sub, octet, cl_ref, spread_ref, ce_ref, cf_ref, cm_ref):
    ids = cl_ref[pl.ds(pl.multiple_of(8 * octet, 8), 8), :]
    lane = ids & 127
    owner = ids >> 7
    me = lax.axis_index("sub")

    def look_up(dom, shift, found):
        here = owner == dom * n_sub + lax.bitwise_xor(me, shift)
        new = []
        for comp in range(CELL_COMPS):
            value = jnp.take_along_axis(spread_ref[dom, shift, comp], lane, axis=1, mode="promise_in_bounds")
            new.append(jnp.where(here, value, found[comp]))
        return tuple(new)

    found = tuple(jnp.zeros((8, 128), F32) for _ in range(CELL_COMPS))
    if n_dom <= 8:
        for dom in range(n_dom):
            for shift in range(n_sub):
                found = look_up(dom, shift, found)
                yield
    else:

        def one_domain(dom, found):
            for shift in range(n_sub):
                found = look_up(dom, shift, found)
            return found

        found = lax.fori_loop(0, n_dom, one_domain, found)
    mass, cx, cy, cz, xx, yy, zz, xy, xz, yz = found
    yield "found"
    cm_ref[...] = mass
    rows8 = pl.ds(pl.multiple_of(8 * octet, 8), 8)
    cx, cy, cz = [value - ce_ref[comp, rows8, :] for comp, value in enumerate((cx, cy, cz))]
    put_rows(cf_ref, source_h_rows([grid_parts(value) for value in (cx, cy, cz)]))
    yield
    qx = xx * cx + xy * cy + xz * cz
    qy = xy * cx + yy * cy + yz * cz
    qz = xz * cx + yz * cy + zz * cz
    const = three_parts(2.5 * (qx * cx + qy * cy + qz * cz))
    linear = [-5.0 * qx, -5.0 * qy, -5.0 * qz]
    square = [2.5 * xx, 2.5 * yy, 2.5 * zz, 5.0 * xy, 5.0 * xz, 5.0 * yz]
    split = [three_parts(value) for value in linear + square]
    rows = []
    for which in (0, 1, 0, 2, 1, 0):
        rows += [part[which] for part in split]
    rows += list(const)
    put_rows(cf_ref, dict(enumerate(rows, Q_AT)))
    yield
    for comp, value in enumerate((cx, cy, cz)):
        for which, part in enumerate(three_parts(value)):
            cf_ref[8 * (V_AT + 4 * which + comp) : 8 * (V_AT + 4 * which + comp) + 8, :] = part
    yield
    columns = {name: three_parts(value) for name, value in dict(xx=xx, yy=yy, zz=zz, xy=xy, xz=xz, yz=yz, cx=qx, cy=qy, cz=qz).items()}
    order = (("xx", "xy", "xz"), ("xy", "yy", "yz"), ("xz", "yz", "zz"), ("cx", "cy", "cz"))
    for which in range(3):
        for column, names in enumerate(order):
            for row, name in enumerate(names):
                at = U_AT + 16 * which + 4 * column + row
                cf_ref[8 * at : 8 * at + 8, :] = columns[name][which]


def source_moments(group, ll_ref, tab_ref, ce_ref, raw_ref, sf_ref):
    left = lax.broadcasted_iota(jnp.int32, (4, 128), 1) < LEAF
    for pair in range(NLEAF // 2):
        first = tab_ref[ll_ref[2 * pair, group]]
        second = tab_ref[ll_ref[2 * pair + 1, group]]
        raw_ref[4 * pair : 4 * pair + 4, :] = jnp.where(left, first, second)
    value = [raw_ref[pl.ds(comp, 8, stride=4), :] for comp in range(4)]
    mass = value[3]
    centred = [value[comp] - ce_ref[comp, pl.ds(group, 1), :] for comp in range(3)]
    for comp, v in enumerate([mass * v for v in centred] + [mass]):
        for which, part in enumerate(high_low(v)):
            at = 4 * which + comp
            sf_ref[8 * at : 8 * at + 8, :] = part


def transposed_dot(rows, weights):
    return lax.dot_general(rows, weights, (((1,), (1,)), ((), ())), preferred_element_type=F32)


def stacked(value):
    return jnp.concatenate(two_parts(value), axis=0)


def cell_group(sub, target, cf_ref, cm_ref):
    def cell_rows(at, count):
        return cf_ref[pl.ds(8 * at + sub, count, stride=8), :].astype(BF16)

    forms = jnp.concatenate(
        [
            jnp.concatenate([cell_rows(0, H_ROWS), jnp.zeros((H_ROWS, 128), BF16)], axis=1),
            jnp.concatenate([jnp.zeros((Q_ROWS, 128), BF16), cell_rows(Q_AT, Q_ROWS)], axis=1),
        ],
        axis=0,
    )
    forms = jnp.dot(target[:, 0 : H_ROWS + Q_ROWS], forms, preferred_element_type=F32)
    yield
    dist_sq, quad_form = forms[:, 0:128], forms[:, 128:256]
    inv = lax.rsqrt(dist_sq)
    inv_two = inv * inv
    inv_three = inv * inv_two
    pull = inv_three * (cm_ref[pl.ds(sub, 1), :] + quad_form * (inv_two * inv_two))
    moments = jnp.concatenate(
        [
            jnp.concatenate([cell_rows(V_AT, V_ROWS), jnp.zeros((V_ROWS, 128), BF16)], axis=1),
            jnp.concatenate([jnp.zeros((U_ROWS, 128), BF16), cell_rows(U_AT, U_ROWS)], axis=1),
        ],
        axis=0,
    )
    return jnp.concatenate([stacked(pull), stacked(inv_three * inv_two)], axis=1), moments


def pair_lanes(pair):
    return pl.ds(pl.multiple_of(128 * pair, 128), 128)


def pair_place(tg_ref, pair):
    return tg_ref[pl.ds(pl.multiple_of(4 * pair, 4), 4), :]


def point_sums(sums, place):
    sums = sums + pltpu.roll(sums, 4, 0)
    return sums[0:3] - place[0:3] * sums[3:4]


def cell_pull(octet, tg_ref, ah_ref, cf_ref, cm_ref, out_ref):
    upper = lax.broadcasted_iota(jnp.int32, (8, 128), 0) < 4
    left = lax.broadcasted_iota(jnp.int32, (LEAF, 128), 1) < LEAF
    for inner in range(4):
        pair = octet * 4 + inner
        first, first_moments = yield from cell_group(2 * inner, ah_ref[pair, 0:LEAF, :], cf_ref, cm_ref)
        second, second_moments = yield from cell_group(2 * inner + 1, ah_ref[pair, LEAF:, :], cf_ref, cm_ref)
        yield
        moments = jnp.concatenate([first_moments, second_moments], axis=0)
        sums = transposed_dot(jnp.concatenate([first, second], axis=0), moments)
        yield
        sums = jnp.where(left, sums[0:64] + sums[64:128], sums[128:192] + sums[192:256]).T
        sums = jnp.concatenate([sums[0:64], sums[64:128]], axis=1)
        place = pair_place(tg_ref, pair)
        x, y, z = [place[comp : comp + 1, :] for comp in range(3)]
        quads = sums[16:32] + sums[32:48] + sums[48:64]
        turned = quads[0:8] * jnp.where(upper, x, y) + quads[8:16] * jnp.where(upper, z, -1.0)
        turned = turned + pltpu.roll(turned, 4, 0)
        out_ref[:, pair_lanes(pair)] = point_sums(sums[0:8] + sums[8:16], place) + turned[0:3]


def put_block_pair(tab_ref, block, value):
    left = lax.broadcasted_iota(jnp.int32, (4, 128), 1) < LEAF
    turned = pltpu.roll(value, LEAF, 1)
    tab_ref[block] = jnp.where(left, value, turned)
    tab_ref[block + 1] = jnp.where(left, turned, value)


def put_eight_pairs(rows_ref, block, coords, feat_ref):
    put_rows(feat_ref, source_h_rows([grid_parts(value) for value in coords]))
    for pair in range(8):
        columns = feat_ref[pl.ds(pair, H_ROWS, stride=8), :].astype(BF16)
        spread = jnp.concatenate([columns] * 4, axis=0).T
        rows_ref[block + 2 * pair] = spread[0:LEAF]
        rows_ref[block + 2 * pair + 1] = spread[LEAF:]


def prepare_kernel(n_dom, n_sub, *refs):
    bundle_ref, near_refs, recv_ref = refs[0], refs[1:n_sub], refs[n_sub]
    tab_ref, rows_ref, at_ref, tg_ref, ce_ref, ah_ref, cl_ref, ll_ref, feat_ref, four_ref = refs[n_sub + 1 :]
    own_ref = bundle_ref.at[0:OWN_ROWS]
    cl_ref[...] = bundle_ref[OWN_ROWS : OWN_ROWS + LEAF_DEV, :].astype(jnp.int32)
    ll_ref[...] = bundle_ref[OWN_ROWS + LEAF_DEV :, :].astype(jnp.int32)
    for at in range(8):
        fill_constant_rows(four_ref.at[at], H_ROWS)
    me = lax.axis_index("sub")

    def near_blocks(shift, near_ref):
        seg = lax.bitwise_xor(me, shift)

        def near(step, carry):
            for at in range(8):
                octet = 8 * step + at
                block = seg * LEAF_DEV + 16 * octet
                first = pl.multiple_of(32 * octet, 32)
                for pair in range(8):
                    put_block_pair(tab_ref, block + 2 * pair, near_ref[pl.ds(pl.multiple_of(first + 4 * pair, 4), 4), :])
                coords = [near_ref[pl.ds(first + comp, 8, stride=4), :] for comp in range(3)]
                put_eight_pairs(rows_ref, block, coords, four_ref.at[at])
            return carry

        lax.fori_loop(0, PAIRS // 64, near, 0)

    for shift in range(1, n_sub):
        near_blocks(shift, near_refs[shift - 1])
    far_tables(n_dom, n_sub * LEAF_DEV, recv_ref, tab_ref, rows_ref, four_ref)
    near_blocks(0, own_ref)
    tg_ref[...] = own_ref[...]

    def targets(step, carry):
        for at in range(2):
            octet = 2 * step + at
            target_features(octet, tg_ref, ce_ref, feat_ref.at[at], ah_ref)
            target_rows(octet, own_ref, four_ref.at[at], at_ref)
        return carry

    lax.fori_loop(0, PAIRS // 16, targets, 0)


def far_tables(n_dom, first_block, recv_ref, tab_ref, rows_ref, four_ref):
    me = lax.axis_index("dom")
    for two in range(RANGE):
        halves = []
        for slot in (2 * two, 2 * two + 1):
            source = me - OFFSETS[slot]
            inside = (source >= 0) & (source < n_dom)
            source = jnp.clip(source, 0, n_dom - 1)
            for unit in range(OUT_UNITS):
                value = jnp.where(inside, recv_ref[source, 4 * unit : 4 * unit + 4, :], 0.0)
                put_block_pair(tab_ref, first_block + slot * CAP + 2 * unit, value)
            halves.append([jnp.where(inside, recv_ref[source, pl.ds(comp, OUT_UNITS, stride=4), :], 0.0) for comp in range(3)])
        coords = [jnp.concatenate([one, other], axis=0) for one, other in zip(*halves)]
        put_eight_pairs(rows_ref, first_block + 2 * two * CAP, coords, four_ref.at[two])


def target_rows(octet, own_ref, feat_ref, at_ref):
    one = jnp.ones((8, 128), F32)
    zero = jnp.zeros((8, 128), F32)
    parts = [grid_parts(own_ref[pl.ds(octet * 32 + comp, 8, stride=4), :]) for comp in range(3)]
    for at, value in enumerate(target_h_rows(parts, one, zero)):
        feat_ref[8 * at : 8 * at + 8, :] = value
    for pair in range(8):
        at_ref[octet * 8 + pair] = feat_ref[pl.ds(pair, H_ROWS, stride=8), :].astype(BF16)


def run(strand, steps=None):
    taken = 0
    while steps is None or taken < steps:
        taken += 1
        if next(strand, "end") == "end":
            return


def pull_kernel(n_dom, n_sub, *refs):
    cell_refs = refs[:n_sub]
    tab_ref, rows_ref, at_ref, tg_ref, ce_ref, ah_ref, cl_ref, ll_in, out_ref = refs[n_sub : n_sub + 9]
    ll_ref, spread_ref, cf_ref, cm_ref, raw_ref, even_ref, odd_ref, dist_even, dist_odd, sem = refs[n_sub + 9 :]
    copy = pltpu.make_async_copy(ll_in, ll_ref, sem)
    copy.start()
    fill_constant_rows(cf_ref, CELL_ROWS)

    def build(octet):
        return cell_features(n_dom, n_sub, octet, cl_ref, spread_ref, ce_ref, cf_ref, cm_ref)

    def spread(dom, carry):
        for shift in range(n_sub):
            for comp in range(CELL_COMPS):
                row = cell_refs[shift][dom, comp : comp + 1, :]
                spread_ref[dom, shift, comp] = jnp.broadcast_to(row, (8, 128))
        return carry

    lax.fori_loop(0, n_dom, spread, 0)

    left = lax.broadcasted_iota(jnp.int32, (M_ROWS, 128), 1) < LEAF
    left_target = lax.broadcasted_iota(jnp.int32, (H_ROWS, 128), 1) < LEAF
    owner = (lax.broadcasted_iota(jnp.int32, (LEAF, 128), 1) // H_ROWS).astype(BF16)
    lower_half, first_own, third_own = owner < 2.0, owner == 0.0, owner == 2.0

    def features(quad, raw_at, slot_ref):
        for group in range(4):
            source_moments(4 * quad + group, ll_ref, tab_ref, ce_ref, raw_ref.at[raw_at + group], slot_ref.at[group])
            yield

    def distances(quad, dist_ref):
        nothing = jnp.zeros((H_ROWS, 128), BF16)
        first, second = at_ref[2 * quad], at_ref[2 * quad + 1]
        targets = jnp.concatenate(
            [
                jnp.concatenate([jnp.where(left_target, first, nothing), nothing], axis=1),
                jnp.concatenate([jnp.where(left_target, nothing, first), nothing], axis=1),
                jnp.concatenate([nothing, jnp.where(left_target, second, nothing)], axis=1),
                jnp.concatenate([nothing, jnp.where(left_target, nothing, second)], axis=1),
            ],
            axis=0,
        )
        sources = []
        for j in range(NLEAF):
            rows = [rows_ref[ll_ref[j, 4 * quad + group]] for group in range(4)]
            low = jnp.where(first_own, rows[0], rows[1])
            high = jnp.where(third_own, rows[2], rows[3])
            sources.append(jnp.where(lower_half, low, high))
            if j % 4 == 3:
                rows = pl.ds(LEAF * (j - 3), 4 * LEAF)
                dist_ref[rows, :] = jnp.dot(jnp.concatenate(sources, axis=0), targets, preferred_element_type=F32)
                sources = []
                yield

    def pull(quad, slot_ref, dist_ref):
        totals = [jnp.zeros((2 * M_ROWS, 128), F32) for _ in range(2)]
        for chunk in range(8):
            for side in range(2):
                inv = lax.rsqrt(dist_ref[128 * chunk : 128 * chunk + 128, 128 * side : 128 * side + 128])
                weights = stacked(inv * inv * inv)
                rows = [slot_ref[2 * side + half, pl.ds(chunk, M_ROWS, stride=8), :] for half in range(2)]
                rows = jnp.concatenate(rows, axis=0).astype(BF16)
                totals[side] += jnp.dot(jnp.concatenate([rows, rows], axis=1), weights, preferred_element_type=F32)
                yield
        for side in range(2):
            pair = 2 * quad + side
            sums = jnp.where(left, totals[side][0:M_ROWS], totals[side][M_ROWS:])
            lanes = pair_lanes(pair)
            out_ref[:, lanes] = out_ref[:, lanes] + point_sums(sums, pair_place(tg_ref, pair))

    quads, octets = LEAF_DEV // 4, LEAF_DEV // 8
    run(build(0))
    copy.wait()
    run(features(0, 0, even_ref))
    run(distances(0, dist_even))

    def one_octet(octet, carry):
        quad = 2 * octet
        after = jnp.minimum(quad + 2, quads - 1)
        cells = cell_pull(octet, tg_ref, ah_ref, cf_ref, cm_ref, out_ref)
        coming = build(jnp.minimum(octet + 1, octets - 1))
        for half, (now, slot_ref, dist_ref, ahead, ahead_slot, ahead_dist, raw_at) in enumerate(
            (
                (quad, even_ref, dist_even, quad + 1, odd_ref, dist_odd, 4),
                (quad + 1, odd_ref, dist_odd, after, even_ref, dist_even, 0),
            )
        ):
            direct = pull(now, slot_ref, dist_ref)
            moments, distance = features(ahead, raw_at, ahead_slot), distances(ahead, ahead_dist)
            for step in range(8):
                if step % 2 == 1:
                    run(distance, 1)
                run(direct, 1)
                if step % 2 == 0:
                    run(moments, 1)
                if half == 0 or step < 4:
                    if step % 2 == 0:
                        run(coming, 3 if half and step else 6)
                    run(cells, 2 if half or step % 2 else 1)
                else:
                    run(coming, 1)
                run(direct, 1)
            run(moments)
            run(distance)
            run(direct)
        run(coming)
        return carry

    lax.fori_loop(0, octets, one_octet, 0)


def on_device(n_dom, n_sub, positions, masses, cell_mass, cell_center, cell_quad, cell_list, leaf_list, send_list, send_count):
    vmem = pl.BlockSpec(memory_space=pltpu.VMEM)
    smem = pl.BlockSpec(memory_space=pltpu.SMEM)
    anywhere = pl.BlockSpec(memory_space=pl.ANY)

    def limit(mib):
        return pltpu.CompilerParams(vmem_limit_bytes=mib * 1024 * 1024)

    ins = (
        positions,
        masses.reshape(1, -1),
        cell_mass.reshape(1, -1),
        cell_center,
        cell_quad,
        cell_list,
        leaf_list.T,
        send_list.reshape(2 * RANGE, CAP),
        send_count.reshape(1, 2 * RANGE),
    )
    bundle_rows = OWN_ROWS + LEAF_DEV + NLEAF
    packed, sent, bundle = pl.pallas_call(
        functools.partial(pack_kernel, n_dom),
        out_shape=(
            jax.ShapeDtypeStruct((OWN_ROWS, 128), F32),
            jax.ShapeDtypeStruct((n_dom, SENT_ROWS, 128), F32),
            jax.ShapeDtypeStruct((bundle_rows, 128), F32),
        ),
        in_specs=[pl.BlockSpec(memory_space=pltpu.HBM)] * 9,
        out_specs=[anywhere] * 3,
        scratch_shapes=[pltpu.VMEM(array.shape, array.dtype) for array in ins[:7]]
        + [pltpu.SMEM(array.shape, jnp.int32) for array in ins[7:]]
        + [
            pltpu.VMEM((bundle_rows, 128), F32),
            pltpu.VMEM((n_dom + 1, SENT_ROWS, 128), F32),
            pltpu.SemaphoreType.DMA((12,)),
        ],
        compiler_params=limit(63),
        name="pack_own",
    )(*ins)
    received = lax.all_to_all(sent, "dom", split_axis=0, concat_axis=0, tiled=True)

    def across(value, bits):
        return lax.ppermute(value, "sub", [(seg, seg ^ bits) for seg in range(n_sub)])

    nearby = {0: packed}
    bit = n_sub // 2
    while bit:
        nearby.update({at ^ bit: across(value, bit) for at, value in nearby.items()})
        bit //= 2
    nearby = [nearby[at] for at in range(n_sub)]
    own_cells = received[:, OUT_ROWS:]
    cells = [own_cells] + [across(own_cells, bits) for bits in range(1, n_sub)]
    n_blocks = n_sub * LEAF_DEV + 2 * RANGE * CAP
    prepared = pl.pallas_call(
        functools.partial(prepare_kernel, n_dom, n_sub),
        out_shape=(
            jax.ShapeDtypeStruct((n_blocks, 4, 128), F32),
            jax.ShapeDtypeStruct((n_blocks, LEAF, 128), BF16),
            jax.ShapeDtypeStruct((PAIRS, H_ROWS, 128), BF16),
            jax.ShapeDtypeStruct((OWN_ROWS, 128), F32),
            jax.ShapeDtypeStruct((3, LEAF_DEV, 128), F32),
            jax.ShapeDtypeStruct((PAIRS, 128, 128), BF16),
            jax.ShapeDtypeStruct((LEAF_DEV, NCELL), jnp.int32),
            jax.ShapeDtypeStruct((NLEAF, LEAF_DEV), jnp.int32),
        ),
        in_specs=[vmem] * (n_sub + 1),
        out_specs=[vmem] * 8,
        scratch_shapes=[
            pltpu.VMEM((2, 8 * (H_ROWS + Q_ROWS), 128), F32),
            pltpu.VMEM((8, 8 * H_ROWS, 128), F32),
        ],
        compiler_params=limit(24),
        cost_estimate=pl.CostEstimate(flops=0, bytes_accessed=20_000_000, transcendentals=0),
        name="prepare",
    )(bundle, *nearby[1:], received)
    return pl.pallas_call(
        functools.partial(pull_kernel, n_dom, n_sub),
        out_shape=jax.ShapeDtypeStruct((3, LEAF_DEV * LEAF), F32),
        in_specs=[vmem] * (n_sub + 8),
        out_specs=vmem,
        scratch_shapes=[
            pltpu.SMEM((NLEAF, LEAF_DEV), jnp.int32),
            pltpu.VMEM((n_dom, n_sub, CELL_COMPS, 8, 128), F32),
            pltpu.VMEM((8 * CELL_ROWS, 128), F32),
            pltpu.VMEM((8, 128), F32),
            pltpu.VMEM((8, 32, 128), F32),
            pltpu.VMEM((4, 8 * M_ROWS, 128), F32),
            pltpu.VMEM((4, 8 * M_ROWS, 128), F32),
            pltpu.VMEM((NLEAF * LEAF, 256), F32),
            pltpu.VMEM((NLEAF * LEAF, 256), F32),
            pltpu.SemaphoreType.DMA(()),
        ],
        compiler_params=limit(24),
        name="pull",
    )(*cells, *prepared)


def solution(mesh):
    sharded = P(("dom", "sub"))
    return jax.shard_map(
        functools.partial(on_device, mesh.shape["dom"], mesh.shape["sub"]),
        mesh=mesh,
        in_specs=(
            P(None, ("dom", "sub")),
            sharded,
            sharded,
            P(None, ("dom", "sub")),
            P(None, ("dom", "sub")),
            P(("dom", "sub"), None),
            P(("dom", "sub"), None),
            P("dom", "sub", None, None),
            P("dom", "sub", None),
        ),
        out_specs=P(None, ("dom", "sub")),
        check_vma=False,
    )
```
